32 devices in a mesh: replica: 2 (over core), seq: 4 (over z), tensor: 4 (over y, x).
Axes of the slice: x: 2, y: 2, z: 4, core: 2. Of those that a mesh axis runs over, the one named last changes fastest.
Arguments:
- values: bfloat16 [2, 1024, 4096], P('replica', 'seq', 'tensor'), may hold values from -6 to 6
- gate_in: bfloat16 [2, 1024, 4096], P('replica', 'seq', 'tensor'), may hold values from -6 to 6
- in_b: bfloat16 [2, 1024, 128], P('replica', 'seq'), may hold values from -0.03125 to 0.03125
- in_c: bfloat16 [2, 1024, 128], P('replica', 'seq'), may hold values from -6 to 6
- step_sizes: float32 [2, 64, 1024], P('replica', 'tensor', 'seq'), may hold values from 0.2 to 1028
- log_rates: float32 [64], P('tensor'), as said below
- skip_gain: float32 [64], P('tensor'), may hold values from 0.5 to 1.5
- grad_out: bfloat16 [2, 1024, 4096], P('replica', 'seq', 'tensor'), may hold values from -6 to 6
Outputs:
- grad_values: bfloat16 [2, 1024, 4096], P('replica', 'seq', 'tensor')
- grad_gate: bfloat16 [2, 1024, 4096], P('replica', 'seq', 'tensor')
- grad_b: float32 [2, 1024, 128], P('replica', 'seq')
- grad_c: float32 [2, 1024, 128], P('replica', 'seq')
- grad_step_sizes: float32 [2, 64, 1024], P('replica', 'tensor', 'seq')
- grad_log_rates: float32 [64], P('tensor')
- derivative_bypass_weight: float32 [64], P('tensor')
The draws below stay inside these ranges and needn't reach their ends.
Inputs may be any that keep to these rules, and one draw needn't show every extreme that they name: `log_rates`: each entry is at least log(0.1 / 1024).
All inputs are finite; a program needn't handle non-finite values.
Results may differ from the reference program's by a relative error of at most 0.0047.
Values sent between devices are 32-bit elements; how exact they have to be, the bound alone decides.
No kernel may reach another device: no remote copies, remote signals or barrier semaphores. Data moves between devices by JAX's collectives and lax.ppermute only.
A program may use at most 64 MiB of HBM per device.

```python
import math
import jax
import jax.numpy as jnp
from jax import lax

HEADS = 64
HEAD_DIM = 64
STATE = 128
TOK_DEV = 256
RUNS_IN_TOTAL = 2
TOKENS_PER_RUN = 1024


def draw_step_sizes(key, part):
    key_base = jax.random.fold_in(key, 11)
    key_factor = jax.random.fold_in(key, 12)
    key_spots = jax.random.fold_in(key, 13)
    random_seed_number = jax.random.fold_in(key, 14)
    baseline_steps = jax.random.uniform(key_base, (RUNS_IN_TOTAL, HEADS, TOKENS_PER_RUN), jnp.float32, 0.5, 1.5)
    block_count = TOKENS_PER_RUN // TOK_DEV
    rising = 3.0 ** (jnp.arange(block_count, dtype=jnp.float32) / max(block_count - 1, 1)) / math.sqrt(3.0)
    spike_factor = jax.random.uniform(key_factor, (RUNS_IN_TOTAL, HEADS, block_count), jnp.float32, 0.7, 1.4) * rising
    spike_factor = jnp.broadcast_to(spike_factor[:, :, :, None], (RUNS_IN_TOTAL, HEADS, block_count, TOK_DEV)).reshape(RUNS_IN_TOTAL, HEADS, TOKENS_PER_RUN)
    spike_positions = jax.random.randint(key_spots, (RUNS_IN_TOTAL, 3), 0, TOKENS_PER_RUN)
    outlier_indicator = jnp.any(jnp.arange(TOKENS_PER_RUN)[None, None, :] == spike_positions[:, :, None], axis=1)
    outlier_number = jax.random.uniform(random_seed_number, (RUNS_IN_TOTAL, TOKENS_PER_RUN), jnp.float32, 0.5, 1.0) * TOKENS_PER_RUN
    outlier_magnitudes = jnp.where(outlier_indicator, outlier_number, 0.0)
    return baseline_steps * spike_factor + outlier_magnitudes[:, None, :]


def draw_log_rates(key, part):
    key_pick = jax.random.fold_in(key, 21)
    key_slow = jax.random.fold_in(key, 22)
    key_fast = jax.random.fold_in(key, 23)
    share = 0.5
    slow_pick = jax.random.uniform(key_pick, (HEADS,), jnp.float32) < share
    slow_rate = jax.random.uniform(key_slow, (HEADS,), jnp.float32, 0.1, 0.5) / TOKENS_PER_RUN
    fast_rate = jnp.exp(jax.random.uniform(key_fast, (HEADS,), jnp.float32, math.log(0.02), math.log(0.06)))
    return jnp.log(jnp.where(slow_pick, slow_rate, fast_rate))


def block_scale(own_key, shape, shards, low, top_value):
    gain = 1.0
    for position, parts in shards:
        heights = jax.random.uniform(jax.random.fold_in(jax.random.fold_in(own_key, 6), position), (parts,), jnp.float32, low / len(shards), top_value / len(shards))
        gain = gain * jnp.repeat(jnp.exp(heights), shape[position] // parts).reshape((-1,) + (1,) * (len(shape) - 1 - position))
    return gain


def noise(own_key, shape, scale, most, cuts=(), held_as=jnp.bfloat16):
    array = scale * jax.random.normal(own_key, shape, jnp.float32)
    if cuts:
        array = array * block_scale(own_key, shape, cuts, -0.22, 0.18)
    return jnp.clip(array, -most, most).astype(held_as)


def setup_inputs(seed: int = 0) -> dict:
    arg_keys = jax.random.split(jax.random.key(seed), 9)
    return {
        "values": noise(arg_keys[0], (RUNS_IN_TOTAL, TOKENS_PER_RUN, HEADS * HEAD_DIM), 1.0, 6.0, ((0, 2), (1, 4), (2, 4))),
        "gate_in": noise(arg_keys[1], (RUNS_IN_TOTAL, TOKENS_PER_RUN, HEADS * HEAD_DIM), 1.0, 6.0, ((0, 2), (1, 4), (2, 4))),
        "in_b": noise(arg_keys[2], (RUNS_IN_TOTAL, TOKENS_PER_RUN, STATE), (STATE * TOK_DEV) ** -0.5, 0.03125, ((0, 2), (1, 4))),
        "in_c": noise(arg_keys[3], (RUNS_IN_TOTAL, TOKENS_PER_RUN, STATE), 1.0, 6.0, ((0, 2), (1, 4))),
        "step_sizes": draw_step_sizes(jax.random.fold_in(arg_keys[8], 71), 0),
        "log_rates": draw_log_rates(jax.random.fold_in(arg_keys[8], 71), 0),
        "skip_gain": jnp.clip(0.5 + 1.0 * jax.random.uniform(arg_keys[6], (HEADS,), jnp.float32) ** block_scale(arg_keys[6], (HEADS,), ((0, 4),), -0.2, 0.2), 0.5, 1.5),
        "grad_out": noise(arg_keys[7], (RUNS_IN_TOTAL, TOKENS_PER_RUN, HEADS * HEAD_DIM), 1.0, 6.0, ((0, 2), (1, 4), (2, 4))),
    }


def spread(per_head, head_width):
    head_count, length = per_head.shape
    return jnp.broadcast_to(per_head.T[:, :, None], (length, head_count, head_width)).reshape(length, head_count * head_width)


def head_sums(wide_rows, head_count):
    length = wide_rows.shape[0]
    return jnp.sum(wide_rows.reshape(length, head_count, -1), axis=2).T


def causal_decay(head_cum):
    length = head_cum.shape[0]
    row_ids = lax.broadcasted_iota(jnp.int32, (length, length), 0)
    col_ids = lax.broadcasted_iota(jnp.int32, (length, length), 1)
    causal = row_ids >= col_ids
    return jnp.where(causal, jnp.exp(jnp.where(causal, head_cum[:, None] - head_cum[None, :], 0.0)), 0.0)


def local_forward(block_vals, block_b, block_c, block_steps, decay_rates):
    head_count = block_steps.shape[0]
    head_width = block_vals.shape[1] // head_count
    logdecay = -decay_rates[:, None] * block_steps
    cumulative = jnp.cumsum(logdecay, axis=1)
    block_total = cumulative[:, -1]
    scores = jnp.dot(block_c, block_b.T, preferred_element_type=jnp.float32)

    def head_forward(head_index, intra_out):
        decay_mask = causal_decay(cumulative[head_index])
        mixing = (scores * decay_mask).astype(jnp.bfloat16)
        head_vals = lax.dynamic_slice_in_dim(block_vals, head_index * head_width, head_width, 1)
        piece_out = jnp.dot(mixing, head_vals, preferred_element_type=jnp.float32)
        return lax.dynamic_update_slice_in_dim(intra_out, piece_out, head_index * head_width, 1)

    intra_out = lax.fori_loop(0, head_count, head_forward, jnp.zeros(block_vals.shape, jnp.float32))
    scaled_exact = spread(jnp.exp(block_total[:, None] - cumulative), head_width) * block_vals
    scaled = scaled_exact.astype(jnp.bfloat16)
    device_hidden_memory = jnp.dot(scaled.T, block_b, preferred_element_type=jnp.float32).reshape(head_count, head_width, -1)
    return cumulative, block_total, scores, intra_out, scaled_exact, scaled, device_hidden_memory


def local_pull(block_c, block_gate, block_grad, cumulative, head_width):
    head_count = cumulative.shape[0]
    gate_wide = block_gate.astype(jnp.float32)
    gate_sigmoid = jax.nn.sigmoid(gate_wide)
    grad_y = block_grad.astype(jnp.float32) * (gate_wide * gate_sigmoid)
    growth = spread(jnp.exp(cumulative), head_width)
    grad_inter = growth * grad_y
    pulled = jnp.dot(grad_inter.T, block_c.astype(jnp.float32), precision=lax.Precision.HIGHEST)
    return gate_wide, gate_sigmoid, grad_y, growth, grad_inter, pulled.reshape(head_count, head_width, -1)


def local_rest(block_vals, block_b, block_c, block_grad, block_steps, decay_rates, skip_gain, forward_parts, pull_parts, entering, after):
    cumulative, block_total, scores, intra_out, scaled_exact, scaled, device_hidden_memory = forward_parts
    gate_wide, gate_sigmoid, grad_y, growth, grad_inter, pulled = pull_parts
    head_count, length = block_steps.shape
    head_width = block_vals.shape[1] // head_count
    entering_flat = entering.reshape(head_count * head_width, -1)
    after_flat = after.reshape(head_count * head_width, -1)
    inter_part = jnp.dot(block_c.astype(jnp.float32), entering_flat.T, precision=lax.Precision.HIGHEST)
    skip_wide = spread(jnp.broadcast_to(skip_gain[:, None], (head_count, length)), head_width)
    mamba_out = intra_out + growth * inter_part + skip_wide * block_vals
    grad_gate = (block_grad.astype(jnp.float32) * mamba_out * gate_sigmoid * (1.0 + gate_wide * (1.0 - gate_sigmoid))).astype(jnp.bfloat16)
    grad_y_b = grad_y.astype(jnp.bfloat16)

    def head_backward(head_index, carried):
        grad_inner, intra_cum, sum_c, sum_b = carried
        decay_mask = causal_decay(cumulative[head_index])
        mix_exact = scores * decay_mask
        mixing = mix_exact.astype(jnp.bfloat16)
        head_vals = lax.dynamic_slice_in_dim(block_vals, head_index * head_width, head_width, 1)
        head_grad = lax.dynamic_slice_in_dim(grad_y_b, head_index * head_width, head_width, 1)
        grad_mixing = jnp.dot(head_grad, head_vals.T, preferred_element_type=jnp.float32)
        grad_scores = (grad_mixing * decay_mask).astype(jnp.bfloat16)
        weighted = grad_mixing * mix_exact
        piece_grad = jnp.dot(mixing.T, head_grad, preferred_element_type=jnp.float32)
        grad_inner = lax.dynamic_update_slice_in_dim(grad_inner, piece_grad, head_index * head_width, 1)
        cum_row = jnp.sum(weighted, axis=1) - jnp.sum(weighted, axis=0)
        intra_cum = lax.dynamic_update_slice_in_dim(intra_cum, cum_row[None, :], head_index, 0)
        sum_c = sum_c + jnp.dot(grad_scores, block_b, preferred_element_type=jnp.float32)
        sum_b = sum_b + jnp.dot(grad_scores.T, block_c, preferred_element_type=jnp.float32)
        return grad_inner, intra_cum, sum_c, sum_b

    state_zeros = jnp.zeros(block_b.shape, jnp.float32)
    start = (jnp.zeros(block_vals.shape, jnp.float32), jnp.zeros((head_count, length), jnp.float32), state_zeros, state_zeros)
    grad_inner, intra_cum, sum_c, sum_b = lax.fori_loop(0, head_count, head_backward, start)
    grad_scaled = jnp.dot(block_b.astype(jnp.float32), after_flat.T, precision=lax.Precision.HIGHEST)
    out_decay = spread(jnp.exp(block_total[:, None] - cumulative), head_width)
    grad_values = (grad_inner + out_decay * grad_scaled + skip_wide * grad_y).astype(jnp.bfloat16)
    grad_c = sum_c + jnp.dot(grad_inter, entering_flat, precision=lax.Precision.HIGHEST)
    grad_b = sum_b + jnp.dot(scaled.astype(jnp.float32), after_flat, precision=lax.Precision.HIGHEST)
    from_inter = head_sums(grad_y * growth * inter_part, head_count)
    from_scaled = head_sums(grad_scaled * scaled_exact, head_count)
    grad_total = jnp.sum(from_scaled, axis=1) + jnp.exp(block_total) * jnp.sum(after * entering, axis=(1, 2))
    last_token = lax.broadcasted_iota(jnp.int32, (head_count, length), 1) == length - 1
    grad_cum = intra_cum + from_inter - from_scaled + jnp.where(last_token, grad_total[:, None], 0.0)
    grad_log = jnp.flip(jnp.cumsum(jnp.flip(grad_cum, axis=1), axis=1), axis=1)
    grad_steps = -decay_rates[:, None] * grad_log
    rate_part = -decay_rates * jnp.sum(block_steps * grad_log, axis=1)
    skip_part = jnp.sum(head_sums(grad_y * block_vals, head_count), axis=1)
    return grad_values, grad_gate, grad_b, grad_c, grad_steps, rate_part, skip_part


def reference(values, gate_in, in_b, in_c, step_sizes, log_rates, skip_gain, grad_out):
    block_count = TOKENS_PER_RUN // TOK_DEV
    decay_rates = jnp.exp(log_rates)
    collected = []
    for sequence in range(RUNS_IN_TOTAL):
        value_blocks = values[sequence].reshape(block_count, TOK_DEV, -1)
        gate_blocks = gate_in[sequence].reshape(block_count, TOK_DEV, -1)
        grad_blocks = grad_out[sequence].reshape(block_count, TOK_DEV, -1)
        b_blocks = in_b[sequence].reshape(block_count, TOK_DEV, STATE)
        c_blocks = in_c[sequence].reshape(block_count, TOK_DEV, STATE)
        step_blocks = step_sizes[sequence].reshape(HEADS, block_count, TOK_DEV).transpose(1, 0, 2)

        def first_section(pieces):
            block_vals, block_b, block_c, block_steps, block_gate, block_grad = pieces
            forward_parts = local_forward(block_vals, block_b, block_c, block_steps, decay_rates)
            pull_parts = local_pull(block_c, block_gate, block_grad, forward_parts[0], HEAD_DIM)
            return forward_parts[1], forward_parts[6], pull_parts[5]

        totals, local_states, pulls = lax.map(first_section, (value_blocks, b_blocks, c_blocks, step_blocks, gate_blocks, grad_blocks))

        def forward_link(carried, pieces):
            block_total, block_state = pieces
            return jnp.exp(block_total)[:, None, None] * carried + block_state, carried

        def backward_link(carried, pieces):
            block_total, block_pull = pieces
            return block_pull + jnp.exp(block_total)[:, None, None] * carried, carried

        state_zeros = jnp.zeros((HEADS, HEAD_DIM, STATE), jnp.float32)
        ignored, entering = lax.scan(forward_link, state_zeros, (totals, local_states))
        ignored, after = lax.scan(backward_link, state_zeros, (totals, pulls), reverse=True)

        def last_section(pieces):
            block_vals, block_b, block_c, block_steps, block_gate, block_grad, block_enter, block_after = pieces
            forward_parts = local_forward(block_vals, block_b, block_c, block_steps, decay_rates)
            pull_parts = local_pull(block_c, block_gate, block_grad, forward_parts[0], HEAD_DIM)
            return local_rest(block_vals, block_b, block_c, block_grad, block_steps, decay_rates, skip_gain, forward_parts, pull_parts, block_enter, block_after)

        block_results = lax.map(last_section, (value_blocks, b_blocks, c_blocks, step_blocks, gate_blocks, grad_blocks, entering, after))
        collected.append((
            block_results[0].reshape(TOKENS_PER_RUN, -1),
            block_results[1].reshape(TOKENS_PER_RUN, -1),
            block_results[2].reshape(TOKENS_PER_RUN, STATE),
            block_results[3].reshape(TOKENS_PER_RUN, STATE),
            block_results[4].transpose(1, 0, 2).reshape(HEADS, TOKENS_PER_RUN),
            jnp.sum(block_results[5], axis=0),
            jnp.sum(block_results[6], axis=0),
        ))
    grad_values = jnp.stack([entry[0] for entry in collected])
    grad_gate = jnp.stack([entry[1] for entry in collected])
    grad_b = jnp.stack([entry[2] for entry in collected])
    grad_c = jnp.stack([entry[3] for entry in collected])
    grad_step_sizes = jnp.stack([entry[4] for entry in collected])
    grad_log_rates = jnp.sum(jnp.stack([entry[5] for entry in collected]), axis=0)
    derivative_bypass_weight = jnp.sum(jnp.stack([entry[6] for entry in collected]), axis=0)
    return (grad_values, grad_gate, grad_b, grad_c, grad_step_sizes, grad_log_rates, derivative_bypass_weight)
```

```python
import functools

import jax
import jax.numpy as jnp
from jax import lax
from jax.experimental import pallas as pl
from jax.experimental.pallas import tpu as pltpu
from jax.sharding import PartitionSpec as P

F32 = jnp.float32
BF16 = jnp.bfloat16
VMEM_LIMIT = 24 * 1024 * 1024
LANES = 256


def split(x, parts):
    terms = []
    for _ in range(parts - 1):
        term = x.astype(BF16)
        terms.append(term)
        x = x - term.astype(F32)
    terms.append(x.astype(BF16))
    return terms


def mm(a, b):
    return lax.dot_general(a, b, (((1,), (0,)), ((), ())), preferred_element_type=F32)


def mm_nt(a, b):
    return lax.dot_general(a, b, (((1,), (1,)), ((), ())), preferred_element_type=F32)


def mm_tn(a, b):
    return lax.dot_general(a, b, (((0,), (0,)), ((), ())), preferred_element_type=F32)


def iota(shape, dim):
    return lax.broadcasted_iota(jnp.int32, shape, dim)


def to_column(row):
    n = row.shape[1]
    eye = iota((n, n), 0) == iota((n, n), 1)
    return jnp.sum(jnp.where(eye, row, 0.0), axis=1, keepdims=True)


def to_row(column):
    n = column.shape[0]
    eye = iota((n, n), 0) == iota((n, n), 1)
    return jnp.sum(jnp.where(eye, column, 0.0), axis=0, keepdims=True)


def head_map(heads, width, first, lanes):
    low = iota((heads, lanes), 0) * width
    channel = iota((heads, lanes), 1) + first
    return (channel >= low) & (channel < low + width)


def spread_map(heads, width, first, lanes):
    one = jnp.where(head_map(heads, width, first, lanes), 1.0, 0.0).astype(BF16)
    return jnp.concatenate([one, one, one], axis=0)


def rows_of_three(per_head):
    return jnp.concatenate(split(per_head, 3), axis=0)


def spread(three, first, lanes, width):
    heads = three.shape[0] // 3
    return mm_tn(three, spread_map(heads, width, first, lanes))


def scan_tokens(per_head, backward):
    heads, length = per_head.shape
    source = iota((length, length), 0)
    target = iota((length, length), 1)
    keep = source >= target if backward else source <= target
    sums = mm(rows_of_three(per_head), jnp.where(keep, 1.0, 0.0).astype(BF16))
    return sums[:heads] + sums[heads : 2 * heads] + sums[2 * heads :]


def decays(steps, log_rates):
    rates = jnp.exp(to_column(log_rates))
    logdecay = -rates * steps
    cumulative = scan_tokens(logdecay, False)
    total = cumulative[:, -1:]
    return rates, logdecay, cumulative, total


def gate_parts(gate, grad):
    wide = gate.astype(F32)
    sigmoid = 1.0 / (1.0 + jnp.exp(-wide))
    return wide, sigmoid, grad.astype(F32) * (wide * sigmoid)


def states_kernel(v_ref, gate_ref, go_ref, b_ref, c_ref, steps_ref, lr_ref, local_ref, pulled_ref, decay_ref):
    length, channels = v_ref.shape
    heads = steps_ref.shape[0]
    width = channels // heads
    _, _, cumulative, total = decays(steps_ref[...], lr_ref[...])
    growth = rows_of_three(jnp.exp(cumulative))
    fall = rows_of_three(jnp.exp(total - cumulative))
    decay = jnp.exp(total)
    b_t = b_ref[...].astype(F32).T.astype(BF16)
    c_t = c_ref[...].astype(F32).T.astype(BF16)
    for first in range(0, channels, LANES):
        here = pl.ds(first, LANES)
        _, _, grad_y = gate_parts(gate_ref[:, here], go_ref[:, here])
        grad_inter = spread(growth, first, LANES, width) * grad_y
        high, low = split(grad_inter, 2)
        pulled_ref[:, here] = mm(c_t, high) + mm(c_t, low)
        scaled = (spread(fall, first, LANES, width) * v_ref[:, here].astype(F32)).astype(BF16)
        local_ref[:, here] = mm(b_t, scaled)
        decay_ref[:, here] = jnp.sum(
            jnp.where(head_map(heads, width, first, LANES), decay, 0.0), axis=0, keepdims=True
        )


def intra_kernel(
    v_ref, gate_ref, go_ref, b_ref, c_ref, steps_ref, lr_ref,
    intra_ref, inner_ref, sum_b_ref, sum_c_ref,
    grad_t_ref, inner_t_ref, acc_ref,
):
    length, channels = v_ref.shape
    heads = steps_ref.shape[0]
    width = channels // heads
    half = length // 2
    pair = 2 * width
    _, _, cumulative, _ = decays(steps_ref[...], lr_ref[...])
    columns = cumulative.T
    scores = mm_nt(c_ref[...], b_ref[...])
    causal = iota((half, half), 0) >= iota((half, half), 1)
    left = iota((1, pair), 1) < width
    acc_ref[...] = jnp.zeros_like(acc_ref)

    def blocks(x):
        return x[:half, :half], x[half:, :half], x[half:, half:]

    scores_00, scores_10, scores_11 = blocks(scores)
    for first in range(0, channels, pair):
        here = pl.ds(first, pair)
        _, _, grad_y = gate_parts(gate_ref[:, here], go_ref[:, here])
        grad_t_ref[here, :] = grad_y.T.astype(BF16)
        vals = v_ref[:, here]
        pieces = []
        for side in range(2):
            head = first // width + side
            own = left if side == 0 else jnp.logical_not(left)
            row = cumulative[head : head + 1, :]
            column = columns[:, head : head + 1]
            row_0, row_1 = row[:, :half], row[:, half:]
            column_0, column_1 = column[:half], column[half:]
            decay_00 = jnp.exp(jnp.where(causal, column_0 - row_0, -1e30))
            decay_10 = jnp.exp(column_1 - row_0)
            decay_11 = jnp.exp(jnp.where(causal, column_1 - row_1, -1e30))
            mix_00 = (scores_00 * decay_00).astype(BF16)
            mix_10 = (scores_10 * decay_10).astype(BF16)
            mix_11 = (scores_11 * decay_11).astype(BF16)
            low_rows = jnp.concatenate([mix_10, mix_11], axis=1)
            pieces.append((mm(mix_00, vals[:half]), mm(low_rows, vals)))
            head_grad = jnp.where(own, grad_y, 0.0).astype(BF16)
            mixed_0 = mm_nt(head_grad[:half], vals[:half])
            mixed_1 = mm_nt(head_grad[half:], vals)
            acc_ref[:half, :half] += mixed_0 * decay_00
            acc_ref[half:, :half] += mixed_1[:, :half] * decay_10
            acc_ref[half:, half:] += mixed_1[:, half:] * decay_11
            mine = pl.ds(first + side * width, width)
            grad_t = grad_t_ref[mine, :]
            inner_t_ref[mine, :half] = mm(grad_t[:, :half], mix_00) + mm(grad_t[:, half:], mix_10)
            inner_t_ref[mine, half:] = mm(grad_t[:, half:], mix_11)
        intra_ref[:half, here] = jnp.where(left, pieces[0][0], pieces[1][0])
        intra_ref[half:, here] = jnp.where(left, pieces[0][1], pieces[1][1])
        inner_ref[:, here] = inner_t_ref[here, :].T
    shares = acc_ref[...]
    high, low = split(shares, 2)
    sum_c_ref[...] = mm(high, b_ref[...]) + mm(low, b_ref[...])
    high, low = split(shares.T, 2)
    sum_b_ref[...] = mm(high, c_ref[...]) + mm(low, c_ref[...])


def rest_kernel(
    v_ref, gate_ref, go_ref, b_ref, c_ref, steps_ref, lr_ref, skip_ref,
    intra_ref, inner_ref, sum_b_ref, sum_c_ref, entering_ref, after_ref, decay_ref,
    gv_ref, gg_ref, gb_ref, gc_ref, gs_ref, parts_ref,
):
    length, channels = v_ref.shape
    heads = steps_ref.shape[0]
    width = channels // heads
    rates, logdecay, cumulative, total = decays(steps_ref[...], lr_ref[...])
    growth_three = rows_of_three(jnp.exp(cumulative))
    fall_three = rows_of_three(jnp.exp(total - cumulative))
    skip_column = to_column(skip_ref[...])
    block_b = b_ref[...]
    block_c = c_ref[...]
    grad_b = sum_b_ref[...]
    grad_c = sum_c_ref[...]
    grad_cum = jnp.zeros((heads, length), F32)
    grad_total = jnp.zeros((heads, 1), F32)
    skip_part = jnp.zeros((heads, 1), F32)
    for first in range(0, channels, LANES):
        here = pl.ds(first, LANES)
        mine = head_map(heads, width, first, LANES)
        head_rows = jnp.where(mine, 1.0, 0.0).astype(BF16)
        skip = jnp.sum(jnp.where(mine, skip_column, 0.0), axis=0, keepdims=True)
        grad_out = go_ref[:, here].astype(F32)
        wide, sigmoid, grad_y = gate_parts(gate_ref[:, here], go_ref[:, here])
        vals = v_ref[:, here].astype(F32)
        growth = spread(growth_three, first, LANES, width)
        fall = spread(fall_three, first, LANES, width)
        entering = entering_ref[:, here]
        after = after_ref[:, here]
        enter_high, enter_low = split(entering, 2)
        after_high, after_low = split(after, 2)
        inter = growth * (mm(block_c, enter_high) + mm(block_c, enter_low))
        outer = fall * (mm(block_b, after_high) + mm(block_b, after_low))
        intra = intra_ref[:, here]
        inner = inner_ref[:, here]
        mamba = intra + inter + skip * vals
        gg_ref[:, here] = (grad_out * mamba * sigmoid * (1.0 + wide * (1.0 - sigmoid))).astype(BF16)
        gv_ref[:, here] = (inner + outer + skip * grad_y).astype(BF16)
        inter_high, inter_low = split(growth * grad_y, 2)
        grad_c = grad_c + mm_nt(inter_high, enter_high) + (
            mm_nt(inter_high, enter_low) + mm_nt(inter_low, enter_high)
        )
        scaled = (fall * vals).astype(BF16)
        grad_b = grad_b + mm_nt(scaled, after_high) + mm_nt(scaled, after_low)
        grad_y_b = grad_y.astype(BF16).astype(F32)
        cum_terms = grad_y_b * intra + grad_y * inter - vals * (inner + outer)
        cum_high, cum_low = split(cum_terms, 2)
        grad_cum = grad_cum + mm_nt(head_rows, cum_high) + mm_nt(head_rows, cum_low)
        total_row = jnp.sum(vals * outer, axis=0, keepdims=True) + decay_ref[:, here] * jnp.sum(
            after * entering, axis=0, keepdims=True
        )
        skip_row = jnp.sum(grad_y * vals, axis=0, keepdims=True)
        grad_total = grad_total + jnp.sum(jnp.where(mine, total_row, 0.0), axis=1, keepdims=True)
        skip_part = skip_part + jnp.sum(jnp.where(mine, skip_row, 0.0), axis=1, keepdims=True)
    gb_ref[...] = grad_b
    gc_ref[...] = grad_c
    grad_log = scan_tokens(grad_cum, True) + grad_total
    gs_ref[...] = -rates * grad_log
    rate_part = jnp.sum(logdecay * grad_log, axis=1, keepdims=True)
    parts_ref[...] = jnp.concatenate([to_row(rate_part), to_row(skip_part)], axis=0)


def call(kernel, outs, scratch=(), flops=0):
    def run(*args):
        size = sum(a.size * a.dtype.itemsize for a in (*args, *outs))
        return pl.pallas_call(
            kernel,
            out_shape=tuple(outs),
            in_specs=[pl.BlockSpec(memory_space=pltpu.VMEM)] * len(args),
            out_specs=tuple(pl.BlockSpec(memory_space=pltpu.VMEM) for _ in outs),
            scratch_shapes=list(scratch),
            compiler_params=pltpu.CompilerParams(vmem_limit_bytes=VMEM_LIMIT),
            cost_estimate=pl.CostEstimate(flops=flops, bytes_accessed=size, transcendentals=0),
        )(*args)

    return run


def shift(x, axis, size, by):
    pairs = [(i, i + by) for i in range(size) if 0 <= i + by < size]
    return lax.ppermute(x, axis, pairs)


def swap(x, axis, size, bit):
    return lax.ppermute(x, axis, [(i, i ^ bit) for i in range(size)])


def sum_over(x, axis, size):
    if size == 4:
        near = x + swap(x, axis, size, 1)
        return near + (swap(x, axis, size, 2) + swap(x, axis, size, 3))
    if size & (size - 1):
        return lax.psum(x, axis)
    bit = 1
    while bit < size:
        x = x + swap(x, axis, size, bit)
        bit *= 2
    return x


def sum_both(x, y, axis, size):
    if size & (size - 1):
        return lax.psum((x, y), axis)
    bits = [1 << k for k in range(size.bit_length() - 1)]
    for up, down in zip(bits, bits[::-1]):
        x, y = x + swap(x, axis, size, up), y + swap(y, axis, size, down)
    return x, y


def shards(sizes, values, gate_in, in_b, in_c, step_sizes, log_rates, skip_gain, grad_out):
    vals, gate, grad = values[0], gate_in[0], grad_out[0]
    block_b, block_c, steps = in_b[0], in_c[0], step_sizes[0]
    length, channels = vals.shape
    heads = steps.shape[0]
    state = block_b.shape[1]
    rates_row = log_rates.reshape(1, heads)
    skip_row = skip_gain.reshape(1, heads)
    common = (vals, gate, grad, block_b, block_c, steps, rates_row)
    like = jax.ShapeDtypeStruct
    state_like = like((state, channels), F32)
    wide_like = like((length, channels), F32)
    share_like = like((length, state), F32)

    local, pulled, decay = call(
        states_kernel,
        [state_like, state_like, like((1, channels), F32)],
        flops=8 * length * channels * state,
    )(*common)

    seq = sizes["seq"]
    entering = jnp.zeros_like(local)
    after = jnp.zeros_like(pulled)
    for hop in range(seq - 1):
        entering = shift(decay * entering + local if hop else local, "seq", seq, 1)
        after = shift(decay * after + pulled if hop else pulled, "seq", seq, -1)

    intra, inner, sum_b, sum_c = call(
        intra_kernel,
        [wide_like, wide_like, share_like, share_like],
        [
            pltpu.VMEM((channels, length), BF16),
            pltpu.VMEM((channels, length), F32),
            pltpu.VMEM((length, length), F32),
        ],
        flops=16 * length * length * channels,
    )(*common)

    grad_values, grad_gate, grad_b, grad_c, grad_steps, parts = call(
        rest_kernel,
        [
            like((length, channels), BF16),
            like((length, channels), BF16),
            share_like,
            share_like,
            like((heads, length), F32),
            like((2, heads), F32),
        ],
        flops=20 * length * channels * state,
    )(*common, skip_row, intra, inner, sum_b, sum_c, entering, after, decay)

    grad_b, grad_c = sum_both(grad_b, grad_c, "tensor", sizes["tensor"])
    parts = sum_over(sum_over(parts, "seq", seq), "replica", sizes["replica"])
    return (
        grad_values[None],
        grad_gate[None],
        grad_b[None],
        grad_c[None],
        grad_steps[None],
        parts[0],
        parts[1],
    )


def solution(mesh):
    in_specs = (
        P("replica", "seq", "tensor"),
        P("replica", "seq", "tensor"),
        P("replica", "seq", None),
        P("replica", "seq", None),
        P("replica", "tensor", "seq"),
        P("tensor"),
        P("tensor"),
        P("replica", "seq", "tensor"),
    )
    out_specs = (
        P("replica", "seq", "tensor"),
        P("replica", "seq", "tensor"),
        P("replica", "seq", None),
        P("replica", "seq", None),
        P("replica", "tensor", "seq"),
        P("tensor"),
        P("tensor"),
    )
    body = functools.partial(shards, dict(mesh.shape))
    return jax.shard_map(body, mesh=mesh, in_specs=in_specs, out_specs=out_specs, check_vma=False)
```

```python
import functools

import jax
import jax.numpy as jnp
from jax import lax
from jax.experimental import pallas as pl
from jax.experimental.pallas import tpu as pltpu
from jax.sharding import PartitionSpec as P

F32 = jnp.float32
BF16 = jnp.bfloat16
VMEM_LIMIT = 24 * 1024 * 1024
LANES = 256
CHUNKS = 2


def split(x, parts):
    terms = []
    for _ in range(parts - 1):
        term = x.astype(BF16)
        terms.append(term)
        x = x - term.astype(F32)
    terms.append(x.astype(BF16))
    return terms


def mm(a, b):
    return lax.dot_general(a, b, (((1,), (0,)), ((), ())), preferred_element_type=F32)


def mm_nt(a, b):
    return lax.dot_general(a, b, (((1,), (1,)), ((), ())), preferred_element_type=F32)


def mm_tn(a, b):
    return lax.dot_general(a, b, (((0,), (0,)), ((), ())), preferred_element_type=F32)


def iota(shape, dim):
    return lax.broadcasted_iota(jnp.int32, shape, dim)


def to_column(row):
    n = row.shape[1]
    eye = iota((n, n), 0) == iota((n, n), 1)
    return jnp.sum(jnp.where(eye, row, 0.0), axis=1, keepdims=True)


def to_row(column):
    n = column.shape[0]
    eye = iota((n, n), 0) == iota((n, n), 1)
    return jnp.sum(jnp.where(eye, column, 0.0), axis=0, keepdims=True)


def head_map(heads, width, first, lanes):
    low = iota((heads, lanes), 0) * width
    channel = iota((heads, lanes), 1) + first
    return (channel >= low) & (channel < low + width)


def spread_map(heads, width, first, lanes):
    one = jnp.where(head_map(heads, width, first, lanes), 1.0, 0.0).astype(BF16)
    return jnp.concatenate([one, one, one], axis=0)


def rows_of_three(per_head):
    return jnp.concatenate(split(per_head, 3), axis=0)


def spread(three, first, lanes, width):
    heads = three.shape[0] // 3
    return mm_tn(three, spread_map(heads, width, first, lanes))


def scan_tokens(per_head, backward):
    heads, length = per_head.shape
    source = iota((length, length), 0)
    target = iota((length, length), 1)
    keep = source >= target if backward else source <= target
    sums = mm(rows_of_three(per_head), jnp.where(keep, 1.0, 0.0).astype(BF16))
    return sums[:heads] + sums[heads : 2 * heads] + sums[2 * heads :]


def channel_row(column, heads, width, first):
    mine = head_map(heads, width, first, LANES)
    return jnp.sum(jnp.where(mine, column, 0.0), axis=0, keepdims=True)


def head_column(row, heads, width, first):
    mine = head_map(heads, width, first, LANES)
    return jnp.sum(jnp.where(mine, row, 0.0), axis=1, keepdims=True)


def gate_parts(gate, grad):
    wide = gate.astype(F32)
    sigmoid = 1.0 / (1.0 + jnp.exp(-wide))
    return wide, sigmoid, grad.astype(F32) * (wide * sigmoid)


def states_kernel(chunks, size, *refs):
    sources, outs, (steps_ref, lr_ref, sems) = refs[:7], refs[7:-3], refs[-3:]
    v_ref, gate_ref, go_ref, b_ref, c_ref = outs[:5]
    cum_ref, neg_ref, decay_ref, slope_ref = outs[5:9]
    mine_refs, other_refs = outs[9 : 9 + chunks], outs[9 + chunks :]
    targets = (v_ref, gate_ref, go_ref, b_ref, c_ref, steps_ref, lr_ref)
    copies = [
        pltpu.make_async_copy(source, target, sems.at[i])
        for i, (source, target) in enumerate(zip(sources, targets))
    ]
    for i in (6, 5, 3, 4, 0, 1, 2):
        copies[i].start()
    copies[6].wait()
    copies[5].wait()
    length, channels = v_ref.shape
    heads = steps_ref.shape[0]
    width = channels // heads
    lower = lax.axis_index("seq") < size // 2 if size > 1 else True
    rates = jnp.exp(to_column(lr_ref[...]))
    cumulative = scan_tokens(-rates * steps_ref[...], False)
    total = cumulative[:, -1:]
    decay = jnp.exp(total)
    cum_ref[...] = cumulative
    neg_ref[...] = jnp.broadcast_to(-rates, (heads, length))
    growth = rows_of_three(jnp.exp(cumulative))
    fall = rows_of_three(jnp.exp(total - cumulative))
    copies[3].wait()
    copies[4].wait()
    b_t = b_ref[...].astype(F32).T.astype(BF16)
    c_t = c_ref[...].astype(F32).T.astype(BF16)
    for i in range(3):
        copies[i].wait()
    rows = b_t.shape[0] // chunks
    for first in range(0, channels, LANES):
        here = pl.ds(first, LANES)
        _, _, grad_y = gate_parts(gate_ref[:, here], go_ref[:, here])
        high, low = split(spread(growth, first, LANES, width) * grad_y, 2)
        pulled = mm(c_t, high) + mm(c_t, low)
        scaled = (spread(fall, first, LANES, width) * v_ref[:, here].astype(F32)).astype(BF16)
        local = mm(b_t, scaled)
        mine = jnp.where(lower, local, pulled)
        other = jnp.where(lower, pulled, local)
        for i in range(chunks):
            mine_refs[i][:, here] = mine[i * rows : (i + 1) * rows]
            other_refs[i][:, here] = other[i * rows : (i + 1) * rows]
        decay_ref[:, here] = channel_row(decay, heads, width, first)
        slope_ref[:, here] = channel_row(total * decay, heads, width, first)


def intra_kernel(
    v_ref, gate_ref, go_ref, b_ref, c_ref, cum_ref, skip_ref,
    coef_ref, mamba_ref, inner_ref, growth_ref, fall_ref, gy_ref,
    high_ref, low_ref, scaled_ref, q_ref, r_ref, sum_b_ref, sum_c_ref, gcum_ref, parts_ref,
    grad_t_ref, inner_t_ref, acc_ref,
):
    length, channels = v_ref.shape
    heads = cum_ref.shape[0]
    width = channels // heads
    half = length // 2
    pair = 2 * width
    cumulative = cum_ref[...]
    columns = cumulative.T
    scores = mm_nt(c_ref[...], b_ref[...])
    causal = iota((half, half), 0) >= iota((half, half), 1)
    left = iota((1, pair), 1) < width
    acc_ref[...] = jnp.zeros_like(acc_ref)

    def blocks(x):
        return x[:half, :half], x[half:, :half], x[half:, half:]

    scores_00, scores_10, scores_11 = blocks(scores)
    for first in range(0, channels, pair):
        here = pl.ds(first, pair)
        _, _, grad_y = gate_parts(gate_ref[:, here], go_ref[:, here])
        grad_t_ref[here, :] = grad_y.T.astype(BF16)
        vals = v_ref[:, here]
        pieces = []
        for side in range(2):
            head = first // width + side
            own = left if side == 0 else jnp.logical_not(left)
            row = cumulative[head : head + 1, :]
            column = columns[:, head : head + 1]
            row_0, row_1 = row[:, :half], row[:, half:]
            column_0, column_1 = column[:half], column[half:]
            decay_00 = jnp.exp(jnp.where(causal, column_0 - row_0, -1e30))
            decay_10 = jnp.exp(column_1 - row_0)
            decay_11 = jnp.exp(jnp.where(causal, column_1 - row_1, -1e30))
            mix_00 = (scores_00 * decay_00).astype(BF16)
            mix_10 = (scores_10 * decay_10).astype(BF16)
            mix_11 = (scores_11 * decay_11).astype(BF16)
            low_rows = jnp.concatenate([mix_10, mix_11], axis=1)
            pieces.append((mm(mix_00, vals[:half]), mm(low_rows, vals)))
            head_grad = jnp.where(own, grad_y, 0.0).astype(BF16)
            mixed_0 = mm_nt(head_grad[:half], vals[:half])
            mixed_1 = mm_nt(head_grad[half:], vals)
            acc_ref[:half, :half] += mixed_0 * decay_00
            acc_ref[half:, :half] += mixed_1[:, :half] * decay_10
            acc_ref[half:, half:] += mixed_1[:, half:] * decay_11
            mine = pl.ds(first + side * width, width)
            grad_t = grad_t_ref[mine, :]
            inner_t_ref[mine, :half] = mm(grad_t[:, :half], mix_00) + mm(grad_t[:, half:], mix_10)
            inner_t_ref[mine, half:] = mm(grad_t[:, half:], mix_11)
        mamba_ref[:half, here] = jnp.where(left, pieces[0][0], pieces[1][0])
        mamba_ref[half:, here] = jnp.where(left, pieces[0][1], pieces[1][1])
        inner_ref[:, here] = inner_t_ref[here, :].T
    shares = acc_ref[...]
    high, low = split(shares, 2)
    sum_c_ref[...] = mm(high, b_ref[...]) + mm(low, b_ref[...])
    high, low = split(shares.T, 2)
    sum_b_ref[...] = mm(high, c_ref[...]) + mm(low, c_ref[...])

    total = cumulative[:, -1:]
    left_over = total - cumulative
    growth_three = rows_of_three(jnp.exp(cumulative))
    fall_three = rows_of_three(jnp.exp(left_over))
    growth_slope = rows_of_three(cumulative * jnp.exp(cumulative))
    fall_slope = rows_of_three(left_over * jnp.exp(left_over))
    b_t = b_ref[...].astype(F32).T.astype(BF16)
    c_t = c_ref[...].astype(F32).T.astype(BF16)
    skip_column = to_column(skip_ref[...])
    grad_cum = jnp.zeros((heads, length), F32)
    skip_part = jnp.zeros((heads, 1), F32)
    for first in range(0, channels, LANES):
        here = pl.ds(first, LANES)
        wide, sigmoid, grad_y = gate_parts(gate_ref[:, here], go_ref[:, here])
        vals = v_ref[:, here].astype(F32)
        skip = channel_row(skip_column, heads, width, first)
        growth = spread(growth_three, first, LANES, width)
        fall = spread(fall_three, first, LANES, width)
        growth_ref[:, here] = growth
        fall_ref[:, here] = fall
        gy_ref[:, here] = grad_y
        coef_ref[:, here] = go_ref[:, here].astype(F32) * sigmoid * (1.0 + wide * (1.0 - sigmoid))
        high, low = split(growth * grad_y, 2)
        high_ref[:, here] = high
        low_ref[:, here] = low
        scaled_ref[:, here] = (fall * vals).astype(BF16)
        intra = mamba_ref[:, here]
        inner = inner_ref[:, here]
        mamba_ref[:, here] = intra + skip * vals
        inner_ref[:, here] = inner + skip * grad_y
        high, low = split(grad_y.astype(BF16).astype(F32) * intra - vals * inner, 2)
        head_rows = jnp.where(head_map(heads, width, first, LANES), 1.0, 0.0).astype(BF16)
        grad_cum = grad_cum + mm_nt(head_rows, high) + mm_nt(head_rows, low)
        skip_row = jnp.sum(grad_y * vals, axis=0, keepdims=True)
        skip_part = skip_part + head_column(skip_row, heads, width, first)
        high, low = split(spread(growth_slope, first, LANES, width) * grad_y, 2)
        q_ref[:, here] = mm(c_t, high) + mm(c_t, low)
        high, low = split(spread(fall_slope, first, LANES, width) * vals, 2)
        r_ref[:, here] = mm(b_t, high) + mm(b_t, low)
    gcum_ref[...] = grad_cum
    rate_part = jnp.sum(grad_cum * cumulative, axis=1, keepdims=True)
    parts_ref[...] = jnp.concatenate([to_row(rate_part), to_row(skip_part)], axis=0)


def pick(size, first, second, last):
    if size == 1:
        return jnp.zeros_like(first), jnp.zeros_like(first)
    if size % 2:
        return first, second
    index = lax.axis_index("seq")
    lower = index < size // 2
    edge = jnp.logical_or(index == 0, index == size - 1)
    first = jnp.where(edge, 0.0, first)
    second = jnp.where(edge, last, second)
    return jnp.where(lower, first, second), jnp.where(lower, second, first)


def share_kernel(
    size, start, heads, final,
    first_ref, second_ref, last_ref, high_ref, low_ref, scaled_ref, q_ref, r_ref,
    sum_b_ref, sum_c_ref, decay_ref, slope_ref, row_ref, parts_ref, top_ref, bottom_ref, out_ref,
):
    rows, channels = first_ref.shape
    length = scaled_ref.shape[0]
    width = channels // heads
    half = length // 2
    here = slice(start, start + rows)
    grad_b = sum_b_ref[:, here]
    grad_c = sum_c_ref[:, here]
    rate_part = jnp.zeros((heads, 1), F32)
    for begin in range(0, channels, LANES):
        lanes = pl.ds(begin, LANES)
        entering, after = pick(size, first_ref[:, lanes], second_ref[:, lanes], last_ref[:, lanes])
        enter_high, enter_low = split(entering, 2)
        after_high, after_low = split(after, 2)
        high, low, scaled = high_ref[:, lanes], low_ref[:, lanes], scaled_ref[:, lanes]
        grad_c = grad_c + mm_nt(high, enter_high) + (mm_nt(high, enter_low) + mm_nt(low, enter_high))
        grad_b = grad_b + mm_nt(scaled, after_high) + mm_nt(scaled, after_low)
        terms = entering * q_ref[here, lanes] + after * (
            r_ref[here, lanes] + slope_ref[:, lanes] * entering
        )
        row = row_ref[:, lanes] + jnp.sum(terms, axis=0, keepdims=True)
        if final:
            rate_part = rate_part + head_column(row, heads, width, begin)
        else:
            out_ref[:, lanes] = row
    both = jnp.concatenate([grad_b, grad_c], axis=1)
    top_ref[...] = both[:half]
    bottom_ref[...] = both[half:]
    if final:
        base = parts_ref[...]
        out_ref[...] = jnp.concatenate([base[:1] + to_row(rate_part), base[1:]], axis=0)


def rest_kernel(size, chunks, *refs):
    states, refs = [refs[3 * i : 3 * i + 3] for i in range(chunks)], refs[3 * chunks :]
    (
        v_ref, b_ref, c_ref, coef_ref, mamba_ref, inner_ref, growth_ref, fall_ref, gy_ref,
        gcum_ref, decay_ref, neg_ref, gv_ref, gg_ref, gs_ref,
    ) = refs
    length, channels = v_ref.shape
    heads = gcum_ref.shape[0]
    width = channels // heads
    block_b, block_c = b_ref[...], c_ref[...]
    grad_cum = gcum_ref[...]
    grad_total = jnp.zeros((heads, 1), F32)
    for first in range(0, channels, LANES):
        here = pl.ds(first, LANES)
        picked = [pick(size, *(ref[:, here] for ref in state)) for state in states]
        entering = jnp.concatenate([one[0] for one in picked], axis=0)
        after = jnp.concatenate([one[1] for one in picked], axis=0)
        enter_high, enter_low = split(entering, 2)
        after_high, after_low = split(after, 2)
        inter = growth_ref[:, here] * (mm(block_c, enter_high) + mm(block_c, enter_low))
        outer = fall_ref[:, here] * (mm(block_b, after_high) + mm(block_b, after_low))
        gg_ref[0, :, here] = (coef_ref[:, here] * (mamba_ref[:, here] + inter)).astype(BF16)
        gv_ref[0, :, here] = (inner_ref[:, here] + outer).astype(BF16)
        pulled = v_ref[:, here].astype(F32) * outer
        high, low = split(gy_ref[:, here] * inter - pulled, 2)
        head_rows = jnp.where(head_map(heads, width, first, LANES), 1.0, 0.0).astype(BF16)
        grad_cum = grad_cum + mm_nt(head_rows, high) + mm_nt(head_rows, low)
        total_row = jnp.sum(pulled, axis=0, keepdims=True) + decay_ref[:, here] * jnp.sum(
            after * entering, axis=0, keepdims=True
        )
        grad_total = grad_total + head_column(total_row, heads, width, first)
    gs_ref[0] = neg_ref[...] * (scan_tokens(grad_cum, True) + grad_total)


def tree(values):
    while len(values) > 1:
        values = [sum(values[i + 1 : i + 2], values[i]) for i in range(0, len(values), 2)]
    return values[0]


def last_kernel(chunks, smalls, *refs):
    refs, (gb_ref, gc_ref, rate_ref, skip_ref) = refs[:-4], refs[-4:]
    half = gb_ref.shape[1] // 2
    tops = [refs[4 * i][...] + refs[4 * i + 1][...] for i in range(chunks)]
    bottoms = [refs[4 * i + 2][...] + refs[4 * i + 3][...] for i in range(chunks)]
    rows = tops[0].shape[1] // 2
    for place, parts in ((slice(0, half), tops), (slice(half, 2 * half), bottoms)):
        gb_ref[0, place, :] = jnp.concatenate([part[:, :rows] for part in parts], axis=1)
        gc_ref[0, place, :] = jnp.concatenate([part[:, rows:] for part in parts], axis=1)
    small = tree([ref[...] for ref in refs[4 * chunks :]])
    rate_ref[...] = small[:1]
    skip_ref[...] = small[1:]


def call(kernel, outs, scratch=(), flops=0, space=pltpu.VMEM):
    def run(*args):
        size = sum(a.size * a.dtype.itemsize for a in (*args, *outs))
        return pl.pallas_call(
            kernel,
            out_shape=tuple(outs),
            in_specs=[pl.BlockSpec(memory_space=space)] * len(args),
            out_specs=tuple(pl.BlockSpec(memory_space=pltpu.VMEM) for _ in outs),
            scratch_shapes=list(scratch),
            compiler_params=pltpu.CompilerParams(vmem_limit_bytes=VMEM_LIMIT),
            cost_estimate=pl.CostEstimate(flops=flops, bytes_accessed=size, transcendentals=0),
        )(*args)

    return run


def swap(x, axis, size, bit):
    return lax.ppermute(x, axis, [(i, i ^ bit) for i in range(size)])


def hop_pairs(size, hop):
    to = list(range(size))
    to[hop], to[hop + 1] = hop + 1, hop
    to[size - 1 - hop], to[size - 2 - hop] = size - 2 - hop, size - 1 - hop
    return list(enumerate(to))


def chain(size, mine, other, decay):
    if size == 1:
        return mine, mine, mine
    if size % 2:
        raise NotImplementedError
    index = lax.axis_index("seq")
    place = jnp.minimum(index, size - 1 - index)
    first = second = got = None
    for hop in range(size - 1):
        base = mine if hop < size // 2 else other
        got = lax.ppermute(base if got is None else decay * got + base, "seq", hop_pairs(size, hop))
        if hop < size // 2 - 1:
            first = got if first is None else jnp.where(place == hop + 1, got, first)
        elif hop < size - 2:
            second = got if second is None else jnp.where(place == size - 2 - hop, got, second)
    return got if first is None else first, got if second is None else second, got


def last_sums(x, axis, size, order):
    if size == 1:
        return [x]
    if size & (size - 1):
        return [lax.psum(x, axis)]
    bits = [1 << k for k in range(size.bit_length() - 1)][::order]
    for bit in bits[:-1]:
        x = x + swap(x, axis, size, bit)
    return [x, swap(x, axis, size, bits[-1])]


def shards(sizes, values, gate_in, in_b, in_c, step_sizes, log_rates, skip_gain, grad_out):
    like = jax.ShapeDtypeStruct
    length, channels = values.shape[1:]
    heads = step_sizes.shape[1]
    state = in_b.shape[2]
    seq = sizes["seq"]
    rows = state // CHUNKS
    wide = like((length, channels), F32)
    wide_b = like((length, channels), BF16)
    share = like((length, state), F32)
    small = like((heads, length), F32)
    row = like((1, channels), F32)
    piece = like((rows, channels), F32)
    maps = like((length, state), BF16)

    out = call(
        functools.partial(states_kernel, CHUNKS, seq),
        [wide_b, wide_b, wide_b, maps, maps, small, small, row, row] + [piece] * (2 * CHUNKS),
        [
            pltpu.VMEM((heads, length), F32),
            pltpu.VMEM((1, heads), F32),
            pltpu.SemaphoreType.DMA((7,)),
        ],
        flops=8 * length * channels * state,
        space=pltpu.HBM,
    )(
        values[0], gate_in[0], grad_out[0], in_b[0], in_c[0], step_sizes[0],
        log_rates.reshape(1, heads),
    )
    vals, gate, grad, block_b, block_c, cumulative, negative, decay, slope = out[:9]
    mine, other = out[9 : 9 + CHUNKS], out[9 + CHUNKS :]

    (
        coef, mamba, inner, growth, fall, grad_y, high, low, scaled, q, r,
        sum_b, sum_c, grad_cum, parts,
    ) = call(
        intra_kernel,
        [wide] * 6 + [wide_b] * 3 + [like((state, channels), F32)] * 2 + [share, share, small]
        + [like((2, heads), F32)],
        [
            pltpu.VMEM((channels, length), BF16),
            pltpu.VMEM((channels, length), F32),
            pltpu.VMEM((length, length), F32),
        ],
        flops=16 * length * length * channels,
    )(vals, gate, grad, block_b, block_c, cumulative, skip_gain.reshape(1, heads))

    states = [chain(seq, mine[i], other[i], decay) for i in range(CHUNKS)]
    rate_row = jnp.zeros((1, channels), F32)
    payload = like((length // 2, 2 * rows), F32)
    halves = []
    for i in range(CHUNKS):
        final = i == CHUNKS - 1
        top, bottom, rate_row = call(
            functools.partial(share_kernel, seq, i * rows, heads, final),
            [payload, payload, like((2, heads), F32) if final else row],
            flops=10 * length * channels * rows,
        )(*states[i], high, low, scaled, q, r, sum_b, sum_c, decay, slope, rate_row, parts)
        halves.append((top, bottom))
    tensor = sizes["tensor"]
    sums = []
    for top, bottom in halves:
        for x, order in ((top, 1), (bottom, -1)):
            terms = last_sums(x, "tensor", tensor, order)
            sums += terms if len(terms) == 2 else [terms[0], jnp.zeros_like(x)]
    parts = functools.reduce(jnp.add, last_sums(rate_row, "replica", sizes["replica"], 1))
    if seq == 4:
        smalls = [parts] + [swap(parts, "seq", seq, bit) for bit in (1, 2, 3)]
    else:
        smalls = last_sums(parts, "seq", seq, 1)

    grad_values, grad_gate, grad_steps = call(
        functools.partial(rest_kernel, seq, CHUNKS),
        [like((1, length, channels), BF16)] * 2 + [like((1, heads, length), F32)],
        flops=10 * length * channels * state,
    )(
        *(x for group in states for x in group),
        vals, block_b, block_c, coef, mamba, inner, growth, fall, grad_y, grad_cum, decay, negative,
    )
    grad_b, grad_c, rate_sum, skip_sum = call(
        functools.partial(last_kernel, CHUNKS, len(smalls)),
        [like((1, length, state), F32)] * 2 + [like((1, heads), F32)] * 2,
    )(*sums, *smalls)
    return (
        grad_values,
        grad_gate,
        grad_b,
        grad_c,
        grad_steps,
        rate_sum.reshape(heads),
        skip_sum.reshape(heads),
    )


def solution(mesh):
    in_specs = (
        P("replica", "seq", "tensor"),
        P("replica", "seq", "tensor"),
        P("replica", "seq", None),
        P("replica", "seq", None),
        P("replica", "tensor", "seq"),
        P("tensor"),
        P("tensor"),
        P("replica", "seq", "tensor"),
    )
    out_specs = (
        P("replica", "seq", "tensor"),
        P("replica", "seq", "tensor"),
        P("replica", "seq", None),
        P("replica", "seq", None),
        P("replica", "tensor", "seq"),
        P("tensor"),
        P("tensor"),
    )
    body = functools.partial(shards, dict(mesh.shape))
    return jax.shard_map(body, mesh=mesh, in_specs=in_specs, out_specs=out_specs, check_vma=False)
```

```python
import functools

import jax
import jax.numpy as jnp
from jax import lax
from jax.experimental import pallas as pl
from jax.experimental.pallas import tpu as pltpu
from jax.sharding import PartitionSpec as P

F32 = jnp.float32
BF16 = jnp.bfloat16
VMEM_LIMIT = 24 * 1024 * 1024
LANES = 256
CHUNKS = 2
STREAMS = 2


def split(x, parts):
    terms = []
    for _ in range(parts - 1):
        term = x.astype(BF16)
        terms.append(term)
        x = x - term.astype(F32)
    terms.append(x.astype(BF16))
    return terms


def mm(a, b):
    return lax.dot_general(a, b, (((1,), (0,)), ((), ())), preferred_element_type=F32)


def mm_nt(a, b):
    return lax.dot_general(a, b, (((1,), (1,)), ((), ())), preferred_element_type=F32)


def mm_tn(a, b):
    return lax.dot_general(a, b, (((0,), (0,)), ((), ())), preferred_element_type=F32)


def iota(shape, dim):
    return lax.broadcasted_iota(jnp.int32, shape, dim)


def to_column(row):
    n = row.shape[1]
    eye = iota((n, n), 0) == iota((n, n), 1)
    return jnp.sum(jnp.where(eye, row, 0.0), axis=1, keepdims=True)


def to_row(column):
    n = column.shape[0]
    eye = iota((n, n), 0) == iota((n, n), 1)
    return jnp.sum(jnp.where(eye, column, 0.0), axis=0, keepdims=True)


def head_map(heads, width, first, lanes):
    low = iota((heads, lanes), 0) * width
    channel = iota((heads, lanes), 1) + first
    return (channel >= low) & (channel < low + width)


def spread_map(heads, width, first, lanes):
    one = jnp.where(head_map(heads, width, first, lanes), 1.0, 0.0).astype(BF16)
    return jnp.concatenate([one, one, one], axis=0)


def rows_of_three(per_head):
    return jnp.concatenate(split(per_head, 3), axis=0)


def spread(three, first, lanes, width):
    heads = three.shape[0] // 3
    return mm_tn(three, spread_map(heads, width, first, lanes))


def scan_tokens(per_head, backward):
    heads, length = per_head.shape
    source = iota((length, length), 0)
    target = iota((length, length), 1)
    keep = source >= target if backward else source <= target
    sums = mm(rows_of_three(per_head), jnp.where(keep, 1.0, 0.0).astype(BF16))
    return sums[:heads] + sums[heads : 2 * heads] + sums[2 * heads :]


def channel_row(column, heads, width, first):
    mine = head_map(heads, width, first, LANES)
    return jnp.sum(jnp.where(mine, column, 0.0), axis=0, keepdims=True)


def head_column(row, heads, width, first):
    mine = head_map(heads, width, first, LANES)
    return jnp.sum(jnp.where(mine, row, 0.0), axis=1, keepdims=True)


def gate_parts(gate, grad):
    wide = gate.astype(F32)
    sigmoid = 1.0 / (1.0 + jnp.exp(-wide))
    return wide, sigmoid, grad.astype(F32) * (wide * sigmoid)


def states_kernel(chunks, size, *refs):
    sources, outs, (steps_ref, lr_ref, sems) = refs[:7], refs[7:-3], refs[-3:]
    v_ref, gate_ref, go_ref, b_ref, c_ref = outs[:5]
    cum_ref, neg_ref, decay_ref, slope_ref = outs[5:9]
    mine_refs, other_refs = outs[9 : 9 + chunks], outs[9 + chunks :]
    targets = (v_ref, gate_ref, go_ref, b_ref, c_ref, steps_ref, lr_ref)
    copies = [
        pltpu.make_async_copy(source, target, sems.at[i])
        for i, (source, target) in enumerate(zip(sources, targets))
    ]
    for i in (6, 5, 3, 4, 0, 1, 2):
        copies[i].start()
    copies[6].wait()
    copies[5].wait()
    length, channels = v_ref.shape
    heads = steps_ref.shape[0]
    width = channels // heads
    lower = lax.axis_index("seq") < size // 2 if size > 1 else True
    rates = jnp.exp(to_column(lr_ref[...]))
    cumulative = scan_tokens(-rates * steps_ref[...], False)
    total = cumulative[:, -1:]
    decay = jnp.exp(total)
    cum_ref[...] = cumulative
    neg_ref[...] = jnp.broadcast_to(-rates, (heads, length))
    growth = rows_of_three(jnp.exp(cumulative))
    fall = rows_of_three(jnp.exp(total - cumulative))
    copies[3].wait()
    copies[4].wait()
    b_t = b_ref[...].astype(F32).T.astype(BF16)
    c_t = c_ref[...].astype(F32).T.astype(BF16)
    for i in range(3):
        copies[i].wait()
    rows = b_t.shape[0] // chunks
    for first in range(0, channels, LANES):
        here = pl.ds(first, LANES)
        _, _, grad_y = gate_parts(gate_ref[:, here], go_ref[:, here])
        high, low = split(spread(growth, first, LANES, width) * grad_y, 2)
        pulled = mm(c_t, high) + mm(c_t, low)
        scaled = (spread(fall, first, LANES, width) * v_ref[:, here].astype(F32)).astype(BF16)
        local = mm(b_t, scaled)
        mine = jnp.where(lower, local, pulled)
        other = jnp.where(lower, pulled, local)
        for i in range(chunks):
            mine_refs[i][:, here] = mine[i * rows : (i + 1) * rows]
            other_refs[i][:, here] = other[i * rows : (i + 1) * rows]
        decay_ref[:, here] = channel_row(decay, heads, width, first)
        slope_ref[:, here] = channel_row(total * decay, heads, width, first)


def intra_kernel(
    v_ref, gate_ref, go_ref, b_ref, c_ref, cum_ref,
    intra_ref, inner_ref, sum_b_ref, sum_c_ref, grad_t_ref, inner_t_ref, acc_ref,
):
    length, channels = v_ref.shape
    heads = cum_ref.shape[0]
    width = channels // heads
    half = length // 2
    pair = 2 * width
    cumulative = cum_ref[...]
    columns = cumulative.T
    scores = mm_nt(c_ref[...], b_ref[...])
    causal = iota((half, half), 0) >= iota((half, half), 1)
    left = iota((1, pair), 1) < width
    acc_ref[...] = jnp.zeros_like(acc_ref)

    def blocks(x):
        return x[:half, :half], x[half:, :half], x[half:, half:]

    scores_00, scores_10, scores_11 = blocks(scores)
    for first in range(0, channels, pair):
        here = pl.ds(first, pair)
        _, _, grad_y = gate_parts(gate_ref[:, here], go_ref[:, here])
        grad_t_ref[here, :] = grad_y.T.astype(BF16)
        vals = v_ref[:, here]
        pieces = []
        for side in range(2):
            head = first // width + side
            own = left if side == 0 else jnp.logical_not(left)
            row = cumulative[head : head + 1, :]
            column = columns[:, head : head + 1]
            row_0, row_1 = row[:, :half], row[:, half:]
            column_0, column_1 = column[:half], column[half:]
            decay_00 = jnp.exp(jnp.where(causal, column_0 - row_0, -1e30))
            decay_10 = jnp.exp(column_1 - row_0)
            decay_11 = jnp.exp(jnp.where(causal, column_1 - row_1, -1e30))
            mix_00 = (scores_00 * decay_00).astype(BF16)
            mix_10 = (scores_10 * decay_10).astype(BF16)
            mix_11 = (scores_11 * decay_11).astype(BF16)
            low_rows = jnp.concatenate([mix_10, mix_11], axis=1)
            pieces.append((mm(mix_00, vals[:half]), mm(low_rows, vals)))
            head_grad = jnp.where(own, grad_y, 0.0).astype(BF16)
            mixed_0 = mm_nt(head_grad[:half], vals[:half])
            mixed_1 = mm_nt(head_grad[half:], vals)
            acc_ref[:half, :half] += mixed_0 * decay_00
            acc_ref[half:, :half] += mixed_1[:, :half] * decay_10
            acc_ref[half:, half:] += mixed_1[:, half:] * decay_11
            mine = pl.ds(first + side * width, width)
            grad_t = grad_t_ref[mine, :]
            inner_t_ref[mine, :half] = mm(grad_t[:, :half], mix_00) + mm(grad_t[:, half:], mix_10)
            inner_t_ref[mine, half:] = mm(grad_t[:, half:], mix_11)
        intra_ref[:half, here] = jnp.where(left, pieces[0][0], pieces[1][0])
        intra_ref[half:, here] = jnp.where(left, pieces[0][1], pieces[1][1])
        inner_ref[:, here] = inner_t_ref[here, :].T
    shares = acc_ref[...]
    high, low = split(shares, 2)
    sum_c_ref[...] = mm(high, b_ref[...]) + mm(low, b_ref[...])
    high, low = split(shares.T, 2)
    sum_b_ref[...] = mm(high, c_ref[...]) + mm(low, c_ref[...])


def prepare_kernel(
    v_ref, gate_ref, go_ref, b_ref, c_ref, cum_ref, skip_ref, intra_ref, in_inner_ref, after_ref,
    coef_ref, mamba_ref, inner_ref, growth_ref, fall_ref, gy_ref,
    high_ref, low_ref, scaled_ref, q_ref, r_ref, gcum_ref, parts_ref,
):
    length, channels = v_ref.shape
    heads = cum_ref.shape[0]
    width = channels // heads
    cumulative = cum_ref[...]
    total = cumulative[:, -1:]
    left_over = total - cumulative
    growth_three = rows_of_three(jnp.exp(cumulative))
    fall_three = rows_of_three(jnp.exp(left_over))
    growth_slope = rows_of_three(cumulative * jnp.exp(cumulative))
    fall_slope = rows_of_three(left_over * jnp.exp(left_over))
    b_t = b_ref[...].astype(F32).T.astype(BF16)
    c_t = c_ref[...].astype(F32).T.astype(BF16)
    skip_column = to_column(skip_ref[...])
    grad_cum = jnp.zeros((heads, length), F32)
    skip_part = jnp.zeros((heads, 1), F32)
    for first in range(0, channels, LANES):
        here = pl.ds(first, LANES)
        wide, sigmoid, grad_y = gate_parts(gate_ref[:, here], go_ref[:, here])
        vals = v_ref[:, here].astype(F32)
        skip = channel_row(skip_column, heads, width, first)
        growth = spread(growth_three, first, LANES, width)
        fall = spread(fall_three, first, LANES, width)
        growth_ref[:, here] = growth
        fall_ref[:, here] = fall
        gy_ref[:, here] = grad_y
        coef_ref[:, here] = go_ref[:, here].astype(F32) * sigmoid * (1.0 + wide * (1.0 - sigmoid))
        high, low = split(growth * grad_y, 2)
        high_ref[:, here] = high
        low_ref[:, here] = low
        scaled_ref[:, here] = (fall * vals).astype(BF16)
        intra = intra_ref[:, here]
        inner = in_inner_ref[:, here]
        mamba_ref[:, here] = intra + skip * vals
        inner_ref[:, here] = inner + skip * grad_y
        high, low = split(grad_y.astype(BF16).astype(F32) * intra - vals * inner, 2)
        head_rows = jnp.where(head_map(heads, width, first, LANES), 1.0, 0.0).astype(BF16)
        grad_cum = grad_cum + mm_nt(head_rows, high) + mm_nt(head_rows, low)
        skip_row = jnp.sum(grad_y * vals, axis=0, keepdims=True)
        skip_part = skip_part + head_column(skip_row, heads, width, first)
        high, low = split(spread(growth_slope, first, LANES, width) * grad_y, 2)
        q_ref[:, here] = mm(c_t, high) + mm(c_t, low)
        high, low = split(spread(fall_slope, first, LANES, width) * vals, 2)
        r_ref[:, here] = mm(b_t, high) + mm(b_t, low)
    gcum_ref[...] = grad_cum
    rate_part = jnp.sum(grad_cum * cumulative, axis=1, keepdims=True)
    parts_ref[...] = jnp.concatenate([to_row(rate_part), to_row(skip_part)], axis=0)


def pick(size, first, second, last):
    if size == 1:
        return jnp.zeros_like(first), jnp.zeros_like(first)
    if size % 2:
        return first, second
    index = lax.axis_index("seq")
    lower = index < size // 2
    edge = jnp.logical_or(index == 0, index == size - 1)
    first = jnp.where(edge, 0.0, first)
    second = jnp.where(edge, last, second)
    return jnp.where(lower, first, second), jnp.where(lower, second, first)


def picked(size, states, here):
    both = [pick(size, *(ref[:, here] for ref in state)) for state in states]
    return jnp.concatenate([x[0] for x in both], axis=0), jnp.concatenate([x[1] for x in both], axis=0)


def share_kernel(size, streams, start, heads, final, *refs):
    states, refs = [refs[3 * i : 3 * i + 3] for i in range(streams)], refs[3 * streams :]
    (
        high_ref, low_ref, scaled_ref, q_ref, r_ref, sum_b_ref, sum_c_ref, decay_ref, slope_ref,
        row_ref, parts_ref,
    ) = refs[:11]
    both_refs, out_ref = refs[11:-1], refs[-1]
    rows = streams * states[0][0].shape[0]
    length, channels = scaled_ref.shape
    width = channels // heads
    here = slice(start, start + rows)
    grad_b = sum_b_ref[:, here]
    grad_c = sum_c_ref[:, here]
    rate_part = jnp.zeros((heads, 1), F32)
    for begin in range(0, channels, LANES):
        lanes = pl.ds(begin, LANES)
        entering, after = picked(size, states, lanes)
        enter_high, enter_low = split(entering, 2)
        after_high, after_low = split(after, 2)
        high, low, scaled = high_ref[:, lanes], low_ref[:, lanes], scaled_ref[:, lanes]
        grad_c = grad_c + mm_nt(high, enter_high) + (mm_nt(high, enter_low) + mm_nt(low, enter_high))
        grad_b = grad_b + mm_nt(scaled, after_high) + mm_nt(scaled, after_low)
        terms = entering * q_ref[here, lanes] + after * (
            r_ref[here, lanes] + slope_ref[:, lanes] * entering
        )
        row = row_ref[:, lanes] + jnp.sum(terms, axis=0, keepdims=True)
        if final:
            rate_part = rate_part + head_column(row, heads, width, begin)
        else:
            out_ref[:, lanes] = row
    both = jnp.concatenate([grad_b, grad_c], axis=1)
    part = length // len(both_refs)
    for i, ref in enumerate(both_refs):
        ref[...] = both[i * part : (i + 1) * part]
    if final:
        base = parts_ref[...]
        out_ref[...] = jnp.concatenate([base[:1] + to_row(rate_part), base[1:]], axis=0)


def rest_kernel(size, pieces, *refs):
    states, refs = [refs[3 * i : 3 * i + 3] for i in range(pieces)], refs[3 * pieces :]
    (
        v_ref, b_ref, c_ref, coef_ref, mamba_ref, inner_ref, growth_ref, fall_ref, gy_ref,
        gcum_ref, decay_ref, neg_ref, gv_ref, gg_ref, gs_ref,
    ) = refs
    length, channels = v_ref.shape
    heads = gcum_ref.shape[0]
    width = channels // heads
    block_b, block_c = b_ref[...], c_ref[...]
    grad_cum = gcum_ref[...]
    grad_total = jnp.zeros((heads, 1), F32)
    for first in range(0, channels, LANES):
        here = pl.ds(first, LANES)
        entering, after = picked(size, states, here)
        enter_high, enter_low = split(entering, 2)
        after_high, after_low = split(after, 2)
        inter = growth_ref[:, here] * (mm(block_c, enter_high) + mm(block_c, enter_low))
        outer = fall_ref[:, here] * (mm(block_b, after_high) + mm(block_b, after_low))
        gg_ref[0, :, here] = (coef_ref[:, here] * (mamba_ref[:, here] + inter)).astype(BF16)
        gv_ref[0, :, here] = (inner_ref[:, here] + outer).astype(BF16)
        pulled = v_ref[:, here].astype(F32) * outer
        high, low = split(gy_ref[:, here] * inter - pulled, 2)
        head_rows = jnp.where(head_map(heads, width, first, LANES), 1.0, 0.0).astype(BF16)
        grad_cum = grad_cum + mm_nt(head_rows, high) + mm_nt(head_rows, low)
        total_row = jnp.sum(pulled, axis=0, keepdims=True) + decay_ref[:, here] * jnp.sum(
            after * entering, axis=0, keepdims=True
        )
        grad_total = grad_total + head_column(total_row, heads, width, first)
    gs_ref[0] = neg_ref[...] * (scan_tokens(grad_cum, True) + grad_total)


def tree(values):
    while len(values) > 1:
        values = [sum(values[i + 1 : i + 2], values[i]) for i in range(0, len(values), 2)]
    return values[0]


def last_kernel(parts, smalls, *refs):
    refs, (gb_ref, gc_ref, rate_ref, skip_ref) = refs[:-4], refs[-4:]
    length = gb_ref.shape[1]
    start = 0
    for count in parts:
        part = length // count
        for i in range(count):
            both = refs[0][...] + refs[1][...]
            refs = refs[2:]
            rows = both.shape[1] // 2
            gb_ref[0, i * part : (i + 1) * part, start : start + rows] = both[:, :rows]
            gc_ref[0, i * part : (i + 1) * part, start : start + rows] = both[:, rows:]
        start += rows
    small = tree([ref[...] for ref in refs])
    rate_ref[...] = small[:1]
    skip_ref[...] = small[1:]


def call(kernel, outs, scratch=(), flops=0, space=pltpu.VMEM, after=()):
    def run(*args):
        if space == pltpu.HBM:
            args = [pltpu.with_memory_space_constraint(a, space) for a in args]
        specs = [pl.BlockSpec(memory_space=space)] * len(args)
        specs += [pl.BlockSpec(memory_space=pl.ANY)] * len(after)
        args = (*args, *after)
        size = sum(a.size * a.dtype.itemsize for a in (*args, *outs))
        return pl.pallas_call(
            kernel,
            out_shape=tuple(outs),
            in_specs=specs,
            out_specs=tuple(pl.BlockSpec(memory_space=pltpu.VMEM) for _ in outs),
            scratch_shapes=list(scratch),
            compiler_params=pltpu.CompilerParams(vmem_limit_bytes=VMEM_LIMIT),
            cost_estimate=pl.CostEstimate(flops=flops, bytes_accessed=size, transcendentals=0),
        )(*args)

    return run


def swap(x, axis, size, bit):
    return lax.ppermute(x, axis, [(i, i ^ bit) for i in range(size)])


def link_pairs(size, group):
    to = list(range(size))
    for low in (group, size - 2 - group):
        to[low], to[low + 1] = low + 1, low
    return list(enumerate(to))


def pass_kernel(*refs):
    got_ref, base_ref, decay_ref = refs[:3]
    refs[-1][...] = decay_ref[...] * got_ref[...] + base_ref[...]


def pass_on(got, base, decay, after):
    return call(pass_kernel, [jax.ShapeDtypeStruct(base.shape, F32)], flops=2 * base.size, after=after)(
        got, base, decay
    )[0]


def chain(size, chunks, streams, mine, other, decay, work):
    if size == 1:
        for k in sorted(work):
            work[k](())
        return [(x, x, x) for x in mine]
    if size % 2:
        raise NotImplementedError
    index = lax.axis_index("seq")
    place = jnp.minimum(index, size - 1 - index)
    middle = size // 2 - 1
    pieces = range(chunks * streams)
    first, second, last = [[None for _ in pieces] for _ in range(3)]
    token = ()
    count = 0

    def add(got, base):
        nonlocal token, count
        if count in work:
            token = work[count](token)
        count += 1
        token = (pass_on(got, base, decay, token),)
        return token[0]

    def keep(old, new, where):
        return new if old is None else jnp.where(place == where, new, old)

    for stage in range(chunks + size - 2):
        for stream in range(streams):
            sends = []
            for group in range(middle + 1):
                out, back = ([
                    c * streams + stream for c in (stage - hop,) if 0 <= c < chunks
                ] for hop in (group, size - 2 - group))
                back = back if group < middle else []
                pays = [mine[p] if group == 0 else add(first[p], mine[p]) for p in out]
                pays += [add(second[p], other[p]) for p in back]
                if pays:
                    pay = pays[0] if len(pays) == 1 else jnp.where(place == group, *pays)
                    sends.append((group, out, back, pay))
            for group, out, back, pay in sends:
                got = lax.ppermute(pay, "seq", link_pairs(size, group))
                for p in out:
                    if group == size - 2:
                        last[p] = got
                    elif group == middle:
                        second[p] = got
                    else:
                        first[p] = keep(first[p], got, group + 1)
                for p in back:
                    if group == 0:
                        last[p] = got
                    else:
                        second[p] = keep(second[p], got, group)
    for k in sorted(work):
        if k >= count:
            token = work[k](token)
    return [
        (last[p] if first[p] is None else first[p], last[p] if second[p] is None else second[p], last[p])
        for p in pieces
    ]


def last_sums(x, axis, size, order):
    if size == 1:
        return [x]
    if size & (size - 1):
        return [lax.psum(x, axis)]
    bits = [1 << k for k in range(size.bit_length() - 1)][::order]
    for bit in bits[:-1]:
        x = x + swap(x, axis, size, bit)
    return [x, swap(x, axis, size, bits[-1])]


def shards(sizes, values, gate_in, in_b, in_c, step_sizes, log_rates, skip_gain, grad_out):
    like = jax.ShapeDtypeStruct
    length, channels = values.shape[1:]
    heads = step_sizes.shape[1]
    state = in_b.shape[2]
    seq = sizes["seq"]
    pieces = CHUNKS * STREAMS
    rows = state // pieces
    wide = like((length, channels), F32)
    wide_b = like((length, channels), BF16)
    share = like((length, state), F32)
    small = like((heads, length), F32)
    row = like((1, channels), F32)
    piece = like((rows, channels), F32)
    maps = like((length, state), BF16)

    out = call(
        functools.partial(states_kernel, pieces, seq),
        [wide_b, wide_b, wide_b, maps, maps, small, small, row, row] + [piece] * (2 * pieces),
        [
            pltpu.VMEM((heads, length), F32),
            pltpu.VMEM((1, heads), F32),
            pltpu.SemaphoreType.DMA((7,)),
        ],
        flops=8 * length * channels * state,
        space=pltpu.HBM,
    )(
        values[0], gate_in[0], grad_out[0], in_b[0], in_c[0], step_sizes[0],
        log_rates.reshape(1, heads),
    )
    vals, gate, grad, block_b, block_c, cumulative, negative, decay, slope = out[:9]
    mine, other = out[9 : 9 + pieces], out[9 + pieces :]

    made = {}

    def intra(after):
        made["intra"] = call(
            intra_kernel,
            [wide, wide, share, share],
            [
                pltpu.VMEM((channels, length), BF16),
                pltpu.VMEM((channels, length), F32),
                pltpu.VMEM((length, length), F32),
            ],
            flops=16 * length * length * channels,
        )(vals, gate, grad, block_b, block_c, cumulative)
        return (made["intra"][2],)

    def prepare(after):
        made["prepare"] = call(
            prepare_kernel,
            [wide] * 6 + [wide_b] * 3 + [like((state, channels), F32)] * 2 + [small, like((2, heads), F32)],
            flops=16 * length * state * channels,
        )(
            vals, gate, grad, block_b, block_c, cumulative, skip_gain.reshape(1, heads),
            *made["intra"][:2], *(after if after else made["intra"][2:3]),
        )
        return (made["prepare"][-2],)

    states = chain(seq, CHUNKS, STREAMS, mine, other, decay, {0: intra, 2: prepare})
    sum_b, sum_c = made["intra"][2:]
    (
        coef, mamba, inner, growth, fall, grad_y, high, low, scaled, q, r, grad_cum, parts,
    ) = made["prepare"]
    tensor = sizes["tensor"]
    rate_row = jnp.zeros((1, channels), F32)
    sums, counts = [], []
    for i in range(CHUNKS):
        final = i == CHUNKS - 1
        counts.append(2 if final else 1)
        payload = like((length // counts[-1], 2 * rows * STREAMS), F32)
        *shares, rate_row = call(
            functools.partial(share_kernel, seq, STREAMS, i * rows * STREAMS, heads, final),
            [payload] * counts[-1] + [like((2, heads), F32) if final else row],
            flops=10 * length * channels * rows * STREAMS,
        )(
            *(x for group in states[i * STREAMS : (i + 1) * STREAMS] for x in group),
            high, low, scaled, q, r, sum_b, sum_c, decay, slope, rate_row, parts,
        )
        for k, x in enumerate(shares):
            terms = last_sums(x, "tensor", tensor, 1 - 2 * k)
            sums += terms if len(terms) == 2 else [terms[0], jnp.zeros_like(x)]
    parts = functools.reduce(jnp.add, last_sums(rate_row, "replica", sizes["replica"], 1))
    if seq == 4:
        smalls = [parts] + [swap(parts, "seq", seq, bit) for bit in (1, 2, 3)]
    else:
        smalls = last_sums(parts, "seq", seq, 1)

    grad_values, grad_gate, grad_steps = call(
        functools.partial(rest_kernel, seq, pieces),
        [like((1, length, channels), BF16)] * 2 + [like((1, heads, length), F32)],
        flops=10 * length * channels * state,
    )(
        *(x for group in states for x in group),
        vals, block_b, block_c, coef, mamba, inner, growth, fall, grad_y, grad_cum, decay, negative,
    )
    grad_b, grad_c, rate_sum, skip_sum = call(
        functools.partial(last_kernel, tuple(counts), len(smalls)),
        [like((1, length, state), F32)] * 2 + [like((1, heads), F32)] * 2,
    )(*sums, *smalls)
    return (
        grad_values,
        grad_gate,
        grad_b,
        grad_c,
        grad_steps,
        rate_sum.reshape(heads),
        skip_sum.reshape(heads),
    )


def solution(mesh):
    in_specs = (
        P("replica", "seq", "tensor"),
        P("replica", "seq", "tensor"),
        P("replica", "seq", None),
        P("replica", "seq", None),
        P("replica", "tensor", "seq"),
        P("tensor"),
        P("tensor"),
        P("replica", "seq", "tensor"),
    )
    out_specs = (
        P("replica", "seq", "tensor"),
        P("replica", "seq", "tensor"),
        P("replica", "seq", None),
        P("replica", "seq", None),
        P("replica", "tensor", "seq"),
        P("tensor"),
        P("tensor"),
    )
    body = functools.partial(shards, dict(mesh.shape))
    return jax.shard_map(body, mesh=mesh, in_specs=in_specs, out_specs=out_specs, check_vma=False)
```

```python
import functools

import jax
import jax.numpy as jnp
from jax import lax
from jax.experimental import pallas as pl
from jax.experimental.pallas import tpu as pltpu
from jax.sharding import PartitionSpec as P

F32 = jnp.float32
BF16 = jnp.bfloat16
VMEM_LIMIT = 24 * 1024 * 1024
LANES = 256
CHUNKS = 4
PARTS = 2
LAG = 1


def split(x, parts):
    terms = []
    for _ in range(parts - 1):
        term = x.astype(BF16)
        terms.append(term)
        x = x - term.astype(F32)
    terms.append(x.astype(BF16))
    return terms


def mm(a, b):
    return lax.dot_general(a, b, (((1,), (0,)), ((), ())), preferred_element_type=F32)


def mm_nt(a, b):
    return lax.dot_general(a, b, (((1,), (1,)), ((), ())), preferred_element_type=F32)


def mm_tn(a, b):
    return lax.dot_general(a, b, (((0,), (0,)), ((), ())), preferred_element_type=F32)


def iota(shape, dim):
    return lax.broadcasted_iota(jnp.int32, shape, dim)


def to_column(row):
    n = row.shape[1]
    eye = iota((n, n), 0) == iota((n, n), 1)
    return jnp.sum(jnp.where(eye, row, 0.0), axis=1, keepdims=True)


def to_row(column):
    n = column.shape[0]
    eye = iota((n, n), 0) == iota((n, n), 1)
    return jnp.sum(jnp.where(eye, column, 0.0), axis=0, keepdims=True)


def head_map(heads, width, first, lanes):
    low = iota((heads, lanes), 0) * width
    channel = iota((heads, lanes), 1) + first
    return (channel >= low) & (channel < low + width)


def spread_map(heads, width, first, lanes):
    one = jnp.where(head_map(heads, width, first, lanes), 1.0, 0.0).astype(BF16)
    return jnp.concatenate([one, one, one], axis=0)


def rows_of_three(per_head):
    return jnp.concatenate(split(per_head, 3), axis=0)


def spread(three, first, lanes, width):
    heads = three.shape[0] // 3
    return mm_tn(three, spread_map(heads, width, first, lanes))


def scan_tokens(per_head, backward):
    heads, length = per_head.shape
    source = iota((length, length), 0)
    target = iota((length, length), 1)
    keep = source >= target if backward else source <= target
    sums = mm(rows_of_three(per_head), jnp.where(keep, 1.0, 0.0).astype(BF16))
    return sums[:heads] + sums[heads : 2 * heads] + sums[2 * heads :]


def channel_row(column, heads, width, first):
    mine = head_map(heads, width, first, LANES)
    return jnp.sum(jnp.where(mine, column, 0.0), axis=0, keepdims=True)


def head_column(row, heads, width, first):
    mine = head_map(heads, width, first, LANES)
    return jnp.sum(jnp.where(mine, row, 0.0), axis=1, keepdims=True)


def gate_parts(gate, grad):
    wide = gate.astype(F32)
    sigmoid = 1.0 / (1.0 + jnp.exp(-wide))
    return wide, sigmoid, grad.astype(F32) * (wide * sigmoid)


def states_kernel(chunks, size, *refs):
    sources, outs, (steps_ref, lr_ref, sems) = refs[:8], refs[8:-3], refs[-3:]
    v_ref, gate_ref, go_ref, b_ref, c_ref = outs[:5]
    cum_ref, neg_ref, decay_ref, slope_ref, skip_ref = outs[5:10]
    mine_refs, other_refs = outs[10 : 10 + chunks], outs[10 + chunks :]
    targets = (v_ref, gate_ref, go_ref, b_ref, c_ref, steps_ref, lr_ref, skip_ref)
    copies = [
        pltpu.make_async_copy(source, target, sems.at[i])
        for i, (source, target) in enumerate(zip(sources, targets))
    ]
    for i in (6, 5, 3, 4, 0, 1, 2, 7):
        copies[i].start()
    copies[6].wait()
    copies[5].wait()
    length, channels = v_ref.shape
    heads = steps_ref.shape[0]
    width = channels // heads
    lower = lax.axis_index("seq") < size // 2 if size > 1 else True
    rates = jnp.exp(to_column(lr_ref[...]))
    cumulative = scan_tokens(-rates * steps_ref[...], False)
    total = cumulative[:, -1:]
    decay = jnp.exp(total)
    cum_ref[...] = cumulative
    neg_ref[...] = jnp.broadcast_to(-rates, (heads, length))
    growth = rows_of_three(jnp.exp(cumulative))
    fall = rows_of_three(jnp.exp(total - cumulative))
    copies[3].wait()
    copies[4].wait()
    b_t = b_ref[...].astype(F32).T.astype(BF16)
    c_t = c_ref[...].astype(F32).T.astype(BF16)
    for i in (0, 1, 2, 7):
        copies[i].wait()
    rows = b_t.shape[0] // chunks
    for first in range(0, channels, LANES):
        here = pl.ds(first, LANES)
        _, _, grad_y = gate_parts(gate_ref[:, here], go_ref[:, here])
        high, low = split(spread(growth, first, LANES, width) * grad_y, 2)
        pulled = mm(c_t, high) + mm(c_t, low)
        scaled = (spread(fall, first, LANES, width) * v_ref[:, here].astype(F32)).astype(BF16)
        local = mm(b_t, scaled)
        mine = jnp.where(lower, local, pulled)
        other = jnp.where(lower, pulled, local)
        for i in range(chunks):
            mine_refs[i][:, here] = mine[i * rows : (i + 1) * rows]
            other_refs[i][:, here] = other[i * rows : (i + 1) * rows]
        decay_ref[:, here] = channel_row(decay, heads, width, first)
        slope_ref[:, here] = channel_row(total * decay, heads, width, first)


def intra_kernel(
    v_ref, gate_ref, go_ref, b_ref, c_ref, cum_ref,
    intra_ref, inner_ref, sum_b_ref, sum_c_ref, grad_t_ref, inner_t_ref, acc_ref,
):
    length, channels = v_ref.shape
    heads = cum_ref.shape[0]
    width = channels // heads
    half = length // 2
    pair = 2 * width
    cumulative = cum_ref[...]
    columns = cumulative.T
    scores = mm_nt(c_ref[...], b_ref[...])
    causal = iota((half, half), 0) >= iota((half, half), 1)
    left = iota((1, pair), 1) < width
    acc_ref[...] = jnp.zeros_like(acc_ref)

    def blocks(x):
        return x[:half, :half], x[half:, :half], x[half:, half:]

    scores_00, scores_10, scores_11 = blocks(scores)
    for first in range(0, channels, pair):
        here = pl.ds(first, pair)
        _, _, grad_y = gate_parts(gate_ref[:, here], go_ref[:, here])
        grad_t_ref[here, :] = grad_y.T.astype(BF16)
        vals = v_ref[:, here]
        pieces = []
        for side in range(2):
            head = first // width + side
            own = left if side == 0 else jnp.logical_not(left)
            row = cumulative[head : head + 1, :]
            column = columns[:, head : head + 1]
            row_0, row_1 = row[:, :half], row[:, half:]
            column_0, column_1 = column[:half], column[half:]
            decay_00 = jnp.exp(jnp.where(causal, column_0 - row_0, -1e30))
            decay_10 = jnp.exp(column_1 - row_0)
            decay_11 = jnp.exp(jnp.where(causal, column_1 - row_1, -1e30))
            mix_00 = (scores_00 * decay_00).astype(BF16)
            mix_10 = (scores_10 * decay_10).astype(BF16)
            mix_11 = (scores_11 * decay_11).astype(BF16)
            low_rows = jnp.concatenate([mix_10, mix_11], axis=1)
            pieces.append((mm(mix_00, vals[:half]), mm(low_rows, vals)))
            head_grad = jnp.where(own, grad_y, 0.0).astype(BF16)
            mixed_0 = mm_nt(head_grad[:half], vals[:half])
            mixed_1 = mm_nt(head_grad[half:], vals)
            acc_ref[:half, :half] += mixed_0 * decay_00
            acc_ref[half:, :half] += mixed_1[:, :half] * decay_10
            acc_ref[half:, half:] += mixed_1[:, half:] * decay_11
            mine = pl.ds(first + side * width, width)
            grad_t = grad_t_ref[mine, :]
            inner_t_ref[mine, :half] = mm(grad_t[:, :half], mix_00) + mm(grad_t[:, half:], mix_10)
            inner_t_ref[mine, half:] = mm(grad_t[:, half:], mix_11)
        intra_ref[:half, here] = jnp.where(left, pieces[0][0], pieces[1][0])
        intra_ref[half:, here] = jnp.where(left, pieces[0][1], pieces[1][1])
        inner_ref[:, here] = inner_t_ref[here, :].T
    shares = acc_ref[...]
    high, low = split(shares, 2)
    sum_c_ref[...] = mm(high, b_ref[...]) + mm(low, b_ref[...])
    high, low = split(shares.T, 2)
    sum_b_ref[...] = mm(high, c_ref[...]) + mm(low, c_ref[...])


def prepare_kernel(
    v_ref, gate_ref, go_ref, b_ref, c_ref, cum_ref, skip_ref, intra_ref, in_inner_ref, after_ref,
    coef_ref, mamba_ref, inner_ref, growth_ref, fall_ref, gy_ref,
    high_ref, low_ref, scaled_ref, q_ref, r_ref, gcum_ref, parts_ref,
):
    length, channels = v_ref.shape
    heads = cum_ref.shape[0]
    width = channels // heads
    cumulative = cum_ref[...]
    total = cumulative[:, -1:]
    left_over = total - cumulative
    growth_three = rows_of_three(jnp.exp(cumulative))
    fall_three = rows_of_three(jnp.exp(left_over))
    growth_slope = rows_of_three(cumulative * jnp.exp(cumulative))
    fall_slope = rows_of_three(left_over * jnp.exp(left_over))
    b_t = b_ref[...].astype(F32).T.astype(BF16)
    c_t = c_ref[...].astype(F32).T.astype(BF16)
    skip_column = to_column(skip_ref[...])
    grad_cum = jnp.zeros((heads, length), F32)
    skip_part = jnp.zeros((heads, 1), F32)
    for first in range(0, channels, LANES):
        here = pl.ds(first, LANES)
        wide, sigmoid, grad_y = gate_parts(gate_ref[:, here], go_ref[:, here])
        vals = v_ref[:, here].astype(F32)
        skip = channel_row(skip_column, heads, width, first)
        growth = spread(growth_three, first, LANES, width)
        fall = spread(fall_three, first, LANES, width)
        growth_ref[:, here] = growth
        fall_ref[:, here] = fall
        gy_ref[:, here] = grad_y
        coef_ref[:, here] = go_ref[:, here].astype(F32) * sigmoid * (1.0 + wide * (1.0 - sigmoid))
        high, low = split(growth * grad_y, 2)
        high_ref[:, here] = high
        low_ref[:, here] = low
        scaled_ref[:, here] = (fall * vals).astype(BF16)
        intra = intra_ref[:, here]
        inner = in_inner_ref[:, here]
        mamba_ref[:, here] = intra + skip * vals
        inner_ref[:, here] = inner + skip * grad_y
        high, low = split(grad_y.astype(BF16).astype(F32) * intra - vals * inner, 2)
        head_rows = jnp.where(head_map(heads, width, first, LANES), 1.0, 0.0).astype(BF16)
        grad_cum = grad_cum + mm_nt(head_rows, high) + mm_nt(head_rows, low)
        skip_row = jnp.sum(grad_y * vals, axis=0, keepdims=True)
        skip_part = skip_part + head_column(skip_row, heads, width, first)
        high, low = split(spread(growth_slope, first, LANES, width) * grad_y, 2)
        q_ref[:, here] = mm(c_t, high) + mm(c_t, low)
        high, low = split(spread(fall_slope, first, LANES, width) * vals, 2)
        r_ref[:, here] = mm(b_t, high) + mm(b_t, low)
    gcum_ref[...] = grad_cum
    rate_part = jnp.sum(grad_cum * cumulative, axis=1, keepdims=True)
    parts_ref[...] = jnp.concatenate([to_row(rate_part), to_row(skip_part)], axis=0)


def pick(size, first, second, last):
    if size == 1:
        return jnp.zeros_like(first), jnp.zeros_like(first)
    if size % 2:
        return first, second
    index = lax.axis_index("seq")
    lower = index < size // 2
    edge = jnp.logical_or(index == 0, index == size - 1)
    first = jnp.where(edge, 0.0, first)
    second = jnp.where(edge, last, second)
    return jnp.where(lower, first, second), jnp.where(lower, second, first)


def picked(size, states, here):
    both = [pick(size, *(ref[:, here] for ref in state)) for state in states]
    return jnp.concatenate([x[0] for x in both], axis=0), jnp.concatenate([x[1] for x in both], axis=0)


def rate_kernel(size, pieces, start, heads, final, *refs):
    states, refs = [refs[3 * i : 3 * i + 3] for i in range(pieces)], refs[3 * pieces :]
    q_ref, r_ref, slope_ref, row_ref, parts_ref, out_ref = *refs[:5], refs[-1]
    rows, channels = pieces * states[0][0].shape[0], q_ref.shape[1]
    here = slice(start, start + rows)
    rate_part = jnp.zeros((heads, 1), F32)
    for begin in range(0, channels, LANES):
        lanes = pl.ds(begin, LANES)
        entering, after = picked(size, states, lanes)
        terms = entering * q_ref[here, lanes] + after * (
            r_ref[here, lanes] + slope_ref[:, lanes] * entering
        )
        row = row_ref[:, lanes] + jnp.sum(terms, axis=0, keepdims=True)
        if final:
            rate_part = rate_part + head_column(row, heads, channels // heads, begin)
        else:
            out_ref[:, lanes] = row
    if final:
        base = parts_ref[...]
        out_ref[...] = jnp.concatenate([base[:1] + to_row(rate_part), base[1:]], axis=0)


def share_kernel(size, pieces, start, *refs):
    states, refs = [refs[3 * i : 3 * i + 3] for i in range(pieces)], refs[3 * pieces :]
    high_ref, low_ref, scaled_ref, sum_b_ref, sum_c_ref = refs[:5]
    rows, channels = pieces * states[0][0].shape[0], scaled_ref.shape[1]
    here = slice(start, start + rows)
    grad_b = sum_b_ref[:, here]
    grad_c = sum_c_ref[:, here]
    for begin in range(0, channels, LANES):
        lanes = pl.ds(begin, LANES)
        entering, after = picked(size, states, lanes)
        enter_high, enter_low = split(entering, 2)
        after_high, after_low = split(after, 2)
        high, low, scaled = high_ref[:, lanes], low_ref[:, lanes], scaled_ref[:, lanes]
        grad_c = grad_c + mm_nt(high, enter_high) + (mm_nt(high, enter_low) + mm_nt(low, enter_high))
        grad_b = grad_b + mm_nt(scaled, after_high) + mm_nt(scaled, after_low)
    refs[-1][...] = jnp.concatenate([grad_b, grad_c], axis=1)


def rest_kernel(size, pieces, *refs):
    states, refs = [refs[3 * i : 3 * i + 3] for i in range(pieces)], refs[3 * pieces :]
    (
        v_ref, b_ref, c_ref, coef_ref, mamba_ref, inner_ref, growth_ref, fall_ref, gy_ref,
        gcum_ref, decay_ref, neg_ref, _, gv_ref, gg_ref, gs_ref, total_ref,
    ) = refs
    length, channels = v_ref.shape
    heads = gcum_ref.shape[0]
    width = channels // heads
    block_b, block_c = b_ref[...], c_ref[...]
    grad_cum = gcum_ref[...]
    grad_total = jnp.zeros((heads, 1), F32)
    for first in range(0, channels, LANES):
        here = pl.ds(first, LANES)
        entering, after = picked(size, states, here)
        enter_high, enter_low = split(entering, 2)
        after_high, after_low = split(after, 2)
        inter = growth_ref[:, here] * (mm(block_c, enter_high) + mm(block_c, enter_low))
        outer = fall_ref[:, here] * (mm(block_b, after_high) + mm(block_b, after_low))
        gg_ref[0, :, here] = (coef_ref[:, here] * (mamba_ref[:, here] + inter)).astype(BF16)
        gv_ref[0, :, here] = (inner_ref[:, here] + outer).astype(BF16)
        pulled = v_ref[:, here].astype(F32) * outer
        high, low = split(gy_ref[:, here] * inter - pulled, 2)
        head_rows = jnp.where(head_map(heads, width, first, LANES), 1.0, 0.0).astype(BF16)
        grad_cum = grad_cum + mm_nt(head_rows, high) + mm_nt(head_rows, low)
        total_row = jnp.sum(pulled, axis=0, keepdims=True) + decay_ref[:, here] * jnp.sum(
            after * entering, axis=0, keepdims=True
        )
        grad_total = grad_total + head_column(total_row, heads, width, first)
    gs_ref[0] = neg_ref[...] * (scan_tokens(grad_cum, True) + grad_total)
    total_ref[...] = to_row(grad_total)


def tree(values):
    while len(values) > 1:
        values = [sum(values[i + 1 : i + 2], values[i]) for i in range(0, len(values), 2)]
    return values[0]


def add_kernel(x_ref, y_ref, *refs):
    refs[-1][...] = x_ref[...] + y_ref[...]


def last_kernel(counts, *refs):
    refs, (gb_ref, gc_ref, rate_ref, skip_ref) = refs[:-4], refs[-4:]
    sums = []
    for count in counts:
        sums.append(tree([ref[...] for ref in refs[:count]]))
        refs = refs[count:]
    *shares, small = sums
    start = 0
    for both in shares:
        rows = both.shape[1] // 2
        gb_ref[0, :, start : start + rows] = both[:, :rows]
        gc_ref[0, :, start : start + rows] = both[:, rows:]
        start += rows
    rate_ref[...] = small[:1]
    skip_ref[...] = small[1:]


def call(kernel, outs, scratch=(), flops=0, space=pltpu.VMEM, after=()):
    def run(*args):
        if space == pltpu.HBM:
            args = [pltpu.with_memory_space_constraint(a, space) for a in args]
        specs = [pl.BlockSpec(memory_space=space)] * len(args)
        specs += [pl.BlockSpec(memory_space=pl.ANY)] * len(after)
        args = (*args, *after)
        size = sum(a.size * a.dtype.itemsize for a in (*args, *outs))
        return pl.pallas_call(
            kernel,
            out_shape=tuple(outs),
            in_specs=specs,
            out_specs=tuple(pl.BlockSpec(memory_space=pltpu.VMEM) for _ in outs),
            scratch_shapes=list(scratch),
            compiler_params=pltpu.CompilerParams(vmem_limit_bytes=VMEM_LIMIT),
            cost_estimate=pl.CostEstimate(flops=flops, bytes_accessed=size, transcendentals=0),
        )(*args)

    return run


def swap(x, axis, size, bit):
    return lax.ppermute(x, axis, [(i, i ^ bit) for i in range(size)])


def hop_pairs(size, hop):
    to = list(range(size))
    for low in (hop, size - 2 - hop):
        to[low], to[low + 1] = low + 1, low
    return list(enumerate(to))


def pass_kernel(*refs):
    got_ref, base_ref, decay_ref = refs[:3]
    refs[-1][...] = decay_ref[...] * got_ref[...] + base_ref[...]


def pass_on(got, base, decay, after):
    return call(pass_kernel, [jax.ShapeDtypeStruct(base.shape, F32)], flops=2 * base.size, after=after)(
        got, base, decay
    )[0]


def chain(size, mine, other, decay, work):
    chunks = len(mine)
    if size == 1:
        for k in sorted(work):
            work[k](())
        return [(x, x, x) for x in mine]
    if size % 2:
        raise NotImplementedError
    index = lax.axis_index("seq")
    place = jnp.minimum(index, size - 1 - index)
    middle = size // 2 - 1
    got = {(0, c): lax.ppermute(mine[c], "seq", hop_pairs(size, 0)) for c in range(chunks)}
    steps = [
        (hop + c + (LAG if hop > middle else 0), hop, c) for hop in range(1, size - 1) for c in range(chunks)
    ]
    token = ()
    for count, (_, hop, c) in enumerate(sorted(steps)):
        if count in work:
            token = work[count](token)
        if hop > middle and c > 1:
            token = (*token, got[hop, c - 2])
        base = mine[c] if hop <= middle else other[c]
        pay = pass_on(got[hop - 1, c], base, decay, token)
        got[hop, c] = lax.ppermute(pay, "seq", hop_pairs(size, hop))
        token = (pay,)
    for k in sorted(work):
        if k >= len(steps):
            token = work[k](token)
    states = []
    for c in range(chunks):
        first, second, last = got[0, c], got[middle, c], got[size - 2, c]
        for hop in range(1, middle):
            first = jnp.where(place == hop + 1, got[hop, c], first)
        for hop in range(middle + 1, size - 2):
            second = jnp.where(place == size - 2 - hop, got[hop, c], second)
        states.append((first, second, last))
    return states


def sum_terms(x, axis, size):
    if size == 1:
        return [x]
    if size == 4:
        return [x] + [swap(x, axis, size, bit) for bit in (1, 2, 3)]
    if size & (size - 1):
        return [lax.psum(x, axis)]
    bit = 1
    while 2 * bit < size:
        x = x + swap(x, axis, size, bit)
        bit *= 2
    return [x, swap(x, axis, size, bit)]


def small_terms(x, axes, sizes, between):
    bits = [(axis, 1 << k) for axis in axes for k in range(sizes[axis].bit_length() - 1)]
    if any(sizes[axis] & (sizes[axis] - 1) for axis in axes):
        x = lax.psum(x, tuple(axes))
        between((x,))
        return [x]
    after = ()
    for count, (axis, bit) in enumerate(bits):
        theirs = swap(x, axis, sizes[axis], bit)
        if count == len(bits) - 1:
            break
        x = call(add_kernel, [jax.ShapeDtypeStruct(x.shape, F32)], after=after)(x, theirs)[0]
        after = between((x,)) if count == 0 else ()
    if len(bits) < 2:
        between((x,))
    return [x, theirs] if bits else [x]


def shards(sizes, values, gate_in, in_b, in_c, step_sizes, log_rates, skip_gain, grad_out):
    like = jax.ShapeDtypeStruct
    length, channels = values.shape[1:]
    heads = step_sizes.shape[1]
    state = in_b.shape[2]
    seq = sizes["seq"]
    rows = state // CHUNKS
    wide = like((length, channels), F32)
    wide_b = like((length, channels), BF16)
    share = like((length, state), F32)
    small = like((heads, length), F32)
    row = like((1, channels), F32)
    piece = like((rows, channels), F32)
    maps = like((length, state), BF16)

    out = call(
        functools.partial(states_kernel, CHUNKS, seq),
        [wide_b, wide_b, wide_b, maps, maps, small, small, row, row, like((1, heads), F32)]
        + [piece] * (2 * CHUNKS),
        [
            pltpu.VMEM((heads, length), F32),
            pltpu.VMEM((1, heads), F32),
            pltpu.SemaphoreType.DMA((8,)),
        ],
        flops=8 * length * channels * state,
        space=pltpu.HBM,
    )(
        values[0], gate_in[0], grad_out[0], in_b[0], in_c[0], step_sizes[0],
        log_rates.reshape(1, heads), skip_gain.reshape(1, heads),
    )
    vals, gate, grad, block_b, block_c, cumulative, negative, decay, slope, skip = out[:10]
    mine, other = out[10 : 10 + CHUNKS], out[10 + CHUNKS :]

    made = {}

    def intra(after):
        made["intra"] = call(
            intra_kernel,
            [wide, wide, share, share],
            [
                pltpu.VMEM((channels, length), BF16),
                pltpu.VMEM((channels, length), F32),
                pltpu.VMEM((length, length), F32),
            ],
            flops=16 * length * length * channels,
        )(vals, gate, grad, block_b, block_c, cumulative)
        return (made["intra"][2],)

    def prepare(after):
        made["prepare"] = call(
            prepare_kernel,
            [wide] * 6 + [wide_b] * 3 + [like((state, channels), F32)] * 2 + [small, like((2, heads), F32)],
            flops=16 * length * state * channels,
        )(
            vals, gate, grad, block_b, block_c, cumulative, skip,
            *made["intra"][:2], *(after if after else made["intra"][2:3]),
        )
        return (made["prepare"][-2],)

    hops = max(seq - 2, 0) * CHUNKS
    states = chain(seq, mine, other, decay, {0: intra, max(hops - 1, 1): prepare})
    sum_b, sum_c = made["intra"][2:]
    (
        coef, mamba, inner, growth, fall, grad_y, high, low, scaled, q, r, grad_cum, parts,
    ) = made["prepare"]

    rate_row = jnp.zeros((1, channels), F32)
    terms, counts = [], []
    for i in range(PARTS):
        final = i == PARTS - 1
        count = CHUNKS // PARTS
        own = [x for group in states[i * count : (i + 1) * count] for x in group]
        rate_row = call(
            functools.partial(rate_kernel, seq, count, i * rows * count, heads, final),
            [like((2, heads), F32) if final else row],
        )(*own, q, r, slope, rate_row, parts)[0]
        share_of = call(
            functools.partial(share_kernel, seq, count, i * rows * count),
            [like((length, 2 * rows * count), F32)],
            flops=10 * length * channels * rows * count,
            after=(rate_row,),
        )(*own, high, low, scaled, sum_b, sum_c)[0]
        own = sum_terms(share_of, "tensor", sizes["tensor"])
        terms += own
        counts.append(len(own))

    def rest(after):
        made["rest"] = call(
            functools.partial(rest_kernel, seq, CHUNKS),
            [like((1, length, channels), BF16)] * 2
            + [like((1, heads, length), F32), like((1, heads), F32)],
            flops=10 * length * channels * state,
            after=after,
        )(
            *(x for group in states for x in group),
            vals, block_b, block_c, coef, mamba, inner, growth, fall, grad_y, grad_cum, decay, negative,
        )
        return (made["rest"][3],)

    own = small_terms(rate_row, ("replica", "seq"), sizes, rest)
    terms += own
    counts.append(len(own))
    grad_values, grad_gate, grad_steps, _ = made["rest"]
    grad_b, grad_c, rate_sum, skip_sum = call(
        functools.partial(last_kernel, tuple(counts)),
        [like((1, length, state), F32)] * 2 + [like((1, heads), F32)] * 2,
    )(*terms)
    return (
        grad_values,
        grad_gate,
        grad_b,
        grad_c,
        grad_steps,
        rate_sum.reshape(heads),
        skip_sum.reshape(heads),
    )


def solution(mesh):
    in_specs = (
        P("replica", "seq", "tensor"),
        P("replica", "seq", "tensor"),
        P("replica", "seq", None),
        P("replica", "seq", None),
        P("replica", "tensor", "seq"),
        P("tensor"),
        P("tensor"),
        P("replica", "seq", "tensor"),
    )
    out_specs = (
        P("replica", "seq", "tensor"),
        P("replica", "seq", "tensor"),
        P("replica", "seq", None),
        P("replica", "seq", None),
        P("replica", "tensor", "seq"),
        P("tensor"),
        P("tensor"),
    )
    body = functools.partial(shards, dict(mesh.shape))
    return jax.shard_map(body, mesh=mesh, in_specs=in_specs, out_specs=out_specs, check_vma=False)
```

```python
import functools

import jax
import jax.numpy as jnp
from jax import lax
from jax.experimental import pallas as pl
from jax.experimental.pallas import tpu as pltpu
from jax.sharding import PartitionSpec as P

F32 = jnp.float32
BF16 = jnp.bfloat16
VMEM_LIMIT = 24 * 1024 * 1024
LANES = 256
CHUNKS = 2
PARTS = 2
LAG = 1


def split(x, parts):
    terms = []
    for _ in range(parts - 1):
        term = x.astype(BF16)
        terms.append(term)
        x = x - term.astype(F32)
    terms.append(x.astype(BF16))
    return terms


def mm(a, b):
    return lax.dot_general(a, b, (((1,), (0,)), ((), ())), preferred_element_type=F32)


def mm_nt(a, b):
    return lax.dot_general(a, b, (((1,), (1,)), ((), ())), preferred_element_type=F32)


def mm_tn(a, b):
    return lax.dot_general(a, b, (((0,), (0,)), ((), ())), preferred_element_type=F32)


def iota(shape, dim):
    return lax.broadcasted_iota(jnp.int32, shape, dim)


def to_column(row):
    n = row.shape[1]
    eye = iota((n, n), 0) == iota((n, n), 1)
    return jnp.sum(jnp.where(eye, row, 0.0), axis=1, keepdims=True)


def to_row(column):
    n = column.shape[0]
    eye = iota((n, n), 0) == iota((n, n), 1)
    return jnp.sum(jnp.where(eye, column, 0.0), axis=0, keepdims=True)


def head_map(heads, width, first, lanes):
    low = iota((heads, lanes), 0) * width
    channel = iota((heads, lanes), 1) + first
    return (channel >= low) & (channel < low + width)


def spread_map(heads, width, first, lanes):
    one = jnp.where(head_map(heads, width, first, lanes), 1.0, 0.0).astype(BF16)
    return jnp.concatenate([one, one, one], axis=0)


def rows_of_three(per_head):
    return jnp.concatenate(split(per_head, 3), axis=0)


def spread(three, first, lanes, width):
    heads = three.shape[0] // 3
    return mm_tn(three, spread_map(heads, width, first, lanes))


def scan_tokens(per_head, backward):
    heads, length = per_head.shape
    source = iota((length, length), 0)
    target = iota((length, length), 1)
    keep = source >= target if backward else source <= target
    sums = mm(rows_of_three(per_head), jnp.where(keep, 1.0, 0.0).astype(BF16))
    return sums[:heads] + sums[heads : 2 * heads] + sums[2 * heads :]


def channel_row(column, heads, width, first):
    mine = head_map(heads, width, first, LANES)
    return jnp.sum(jnp.where(mine, column, 0.0), axis=0, keepdims=True)


def head_column(row, heads, width, first):
    mine = head_map(heads, width, first, LANES)
    return jnp.sum(jnp.where(mine, row, 0.0), axis=1, keepdims=True)


def gate_parts(gate, grad):
    wide = gate.astype(F32)
    sigmoid = 1.0 / (1.0 + jnp.exp(-wide))
    return wide, sigmoid, grad.astype(F32) * (wide * sigmoid)


def states_kernel(chunks, size, *refs):
    sources, outs, (steps_ref, lr_ref, sems) = refs[:8], refs[8:-3], refs[-3:]
    v_ref, gate_ref, go_ref, b_ref, c_ref = outs[:5]
    cum_ref, neg_ref, decay_ref, slope_ref, skip_ref = outs[5:10]
    mine_refs, other_refs = outs[10 : 10 + chunks], outs[10 + chunks :]
    targets = (v_ref, gate_ref, go_ref, b_ref, c_ref, steps_ref, lr_ref, skip_ref)
    copies = [
        pltpu.make_async_copy(source, target, sems.at[i])
        for i, (source, target) in enumerate(zip(sources, targets))
    ]
    for i in (6, 5, 3, 4, 0, 1, 2, 7):
        copies[i].start()
    copies[6].wait()
    copies[5].wait()
    length, channels = v_ref.shape
    heads = steps_ref.shape[0]
    width = channels // heads
    lower = lax.axis_index("seq") < size // 2 if size > 1 else True
    rates = jnp.exp(to_column(lr_ref[...]))
    cumulative = scan_tokens(-rates * steps_ref[...], False)
    total = cumulative[:, -1:]
    decay = jnp.exp(total)
    cum_ref[...] = cumulative
    neg_ref[...] = jnp.broadcast_to(-rates, (heads, length))
    growth = rows_of_three(jnp.exp(cumulative))
    fall = rows_of_three(jnp.exp(total - cumulative))
    copies[3].wait()
    copies[4].wait()
    b_t = b_ref[...].astype(F32).T.astype(BF16)
    c_t = c_ref[...].astype(F32).T.astype(BF16)
    for i in (0, 1, 2, 7):
        copies[i].wait()
    rows = b_t.shape[0] // chunks
    for first in range(0, channels, LANES):
        here = pl.ds(first, LANES)
        _, _, grad_y = gate_parts(gate_ref[:, here], go_ref[:, here])
        high, low = split(spread(growth, first, LANES, width) * grad_y, 2)
        pulled = mm(c_t, high) + mm(c_t, low)
        scaled = (spread(fall, first, LANES, width) * v_ref[:, here].astype(F32)).astype(BF16)
        local = mm(b_t, scaled)
        mine = jnp.where(lower, local, pulled)
        other = jnp.where(lower, pulled, local)
        for i in range(chunks):
            mine_refs[i][:, here] = mine[i * rows : (i + 1) * rows]
            other_refs[i][:, here] = other[i * rows : (i + 1) * rows]
        decay_ref[:, here] = channel_row(decay, heads, width, first)
        slope_ref[:, here] = channel_row(total * decay, heads, width, first)


def intra_kernel(
    v_ref, gate_ref, go_ref, b_ref, c_ref, cum_ref,
    intra_ref, inner_ref, sum_b_ref, sum_c_ref, grad_t_ref, inner_t_ref, acc_ref,
):
    length, channels = v_ref.shape
    heads = cum_ref.shape[0]
    width = channels // heads
    half = length // 2
    pair = 2 * width
    cumulative = cum_ref[...]
    columns = cumulative.T
    scores = mm_nt(c_ref[...], b_ref[...])
    causal = iota((half, half), 0) >= iota((half, half), 1)
    left = iota((1, pair), 1) < width
    acc_ref[...] = jnp.zeros_like(acc_ref)

    def blocks(x):
        return x[:half, :half], x[half:, :half], x[half:, half:]

    scores_00, scores_10, scores_11 = blocks(scores)
    for first in range(0, channels, pair):
        here = pl.ds(first, pair)
        _, _, grad_y = gate_parts(gate_ref[:, here], go_ref[:, here])
        grad_t_ref[here, :] = grad_y.T.astype(BF16)
        vals = v_ref[:, here]
        pieces = []
        for side in range(2):
            head = first // width + side
            own = left if side == 0 else jnp.logical_not(left)
            row = cumulative[head : head + 1, :]
            column = columns[:, head : head + 1]
            row_0, row_1 = row[:, :half], row[:, half:]
            column_0, column_1 = column[:half], column[half:]
            decay_00 = jnp.exp(jnp.where(causal, column_0 - row_0, -1e30))
            decay_10 = jnp.exp(column_1 - row_0)
            decay_11 = jnp.exp(jnp.where(causal, column_1 - row_1, -1e30))
            mix_00 = (scores_00 * decay_00).astype(BF16)
            mix_10 = (scores_10 * decay_10).astype(BF16)
            mix_11 = (scores_11 * decay_11).astype(BF16)
            low_rows = jnp.concatenate([mix_10, mix_11], axis=1)
            pieces.append((mm(mix_00, vals[:half]), mm(low_rows, vals)))
            head_grad = jnp.where(own, grad_y, 0.0).astype(BF16)
            mixed_0 = mm_nt(head_grad[:half], vals[:half])
            mixed_1 = mm_nt(head_grad[half:], vals)
            acc_ref[:half, :half] += mixed_0 * decay_00
            acc_ref[half:, :half] += mixed_1[:, :half] * decay_10
            acc_ref[half:, half:] += mixed_1[:, half:] * decay_11
            mine = pl.ds(first + side * width, width)
            grad_t = grad_t_ref[mine, :]
            inner_t_ref[mine, :half] = mm(grad_t[:, :half], mix_00) + mm(grad_t[:, half:], mix_10)
            inner_t_ref[mine, half:] = mm(grad_t[:, half:], mix_11)
        intra_ref[:half, here] = jnp.where(left, pieces[0][0], pieces[1][0])
        intra_ref[half:, here] = jnp.where(left, pieces[0][1], pieces[1][1])
        inner_ref[:, here] = inner_t_ref[here, :].T
    shares = acc_ref[...]
    high, low = split(shares, 2)
    sum_c_ref[...] = mm(high, b_ref[...]) + mm(low, b_ref[...])
    high, low = split(shares.T, 2)
    sum_b_ref[...] = mm(high, c_ref[...]) + mm(low, c_ref[...])


def prepare_kernel(
    v_ref, gate_ref, go_ref, b_ref, c_ref, cum_ref, skip_ref, intra_ref, in_inner_ref, after_ref,
    coef_ref, mamba_ref, inner_ref, growth_ref, fall_ref, gy_ref,
    high_ref, low_ref, scaled_ref, q_ref, r_ref, gcum_ref, parts_ref,
):
    length, channels = v_ref.shape
    heads = cum_ref.shape[0]
    width = channels // heads
    cumulative = cum_ref[...]
    total = cumulative[:, -1:]
    left_over = total - cumulative
    growth_three = rows_of_three(jnp.exp(cumulative))
    fall_three = rows_of_three(jnp.exp(left_over))
    growth_slope = rows_of_three(cumulative * jnp.exp(cumulative))
    fall_slope = rows_of_three(left_over * jnp.exp(left_over))
    b_t = b_ref[...].astype(F32).T.astype(BF16)
    c_t = c_ref[...].astype(F32).T.astype(BF16)
    skip_column = to_column(skip_ref[...])
    grad_cum = jnp.zeros((heads, length), F32)
    skip_part = jnp.zeros((heads, 1), F32)
    for first in range(0, channels, LANES):
        here = pl.ds(first, LANES)
        wide, sigmoid, grad_y = gate_parts(gate_ref[:, here], go_ref[:, here])
        vals = v_ref[:, here].astype(F32)
        skip = channel_row(skip_column, heads, width, first)
        growth = spread(growth_three, first, LANES, width)
        fall = spread(fall_three, first, LANES, width)
        growth_ref[:, here] = growth
        fall_ref[:, here] = fall
        gy_ref[:, here] = grad_y
        coef_ref[:, here] = go_ref[:, here].astype(F32) * sigmoid * (1.0 + wide * (1.0 - sigmoid))
        high, low = split(growth * grad_y, 2)
        high_ref[:, here] = high
        low_ref[:, here] = low
        scaled_ref[:, here] = (fall * vals).astype(BF16)
        intra = intra_ref[:, here]
        inner = in_inner_ref[:, here]
        mamba_ref[:, here] = intra + skip * vals
        inner_ref[:, here] = inner + skip * grad_y
        high, low = split(grad_y.astype(BF16).astype(F32) * intra - vals * inner, 2)
        head_rows = jnp.where(head_map(heads, width, first, LANES), 1.0, 0.0).astype(BF16)
        grad_cum = grad_cum + mm_nt(head_rows, high) + mm_nt(head_rows, low)
        skip_row = jnp.sum(grad_y * vals, axis=0, keepdims=True)
        skip_part = skip_part + head_column(skip_row, heads, width, first)
        high, low = split(spread(growth_slope, first, LANES, width) * grad_y, 2)
        q_ref[:, here] = mm(c_t, high) + mm(c_t, low)
        high, low = split(spread(fall_slope, first, LANES, width) * vals, 2)
        r_ref[:, here] = mm(b_t, high) + mm(b_t, low)
    gcum_ref[...] = grad_cum
    rate_part = jnp.sum(grad_cum * cumulative, axis=1, keepdims=True)
    parts_ref[...] = jnp.concatenate([to_row(rate_part), to_row(skip_part)], axis=0)


def pick(size, first, second, last):
    if size == 1:
        return jnp.zeros_like(first), jnp.zeros_like(first)
    if size % 2:
        return first, second
    index = lax.axis_index("seq")
    lower = index < size // 2
    edge = jnp.logical_or(index == 0, index == size - 1)
    first = jnp.where(edge, 0.0, first)
    second = jnp.where(edge, last, second)
    return jnp.where(lower, first, second), jnp.where(lower, second, first)


def picked(size, states, here):
    both = [pick(size, *(ref[:, here] for ref in state)) for state in states]
    return jnp.concatenate([x[0] for x in both], axis=0), jnp.concatenate([x[1] for x in both], axis=0)


def rate_kernel(size, pieces, start, heads, final, *refs):
    states, refs = [refs[3 * i : 3 * i + 3] for i in range(pieces)], refs[3 * pieces :]
    q_ref, r_ref, slope_ref, row_ref, parts_ref, out_ref = *refs[:5], refs[-1]
    rows, channels = pieces * states[0][0].shape[0], q_ref.shape[1]
    here = slice(start, start + rows)
    rate_part = jnp.zeros((heads, 1), F32)
    for begin in range(0, channels, LANES):
        lanes = pl.ds(begin, LANES)
        entering, after = picked(size, states, lanes)
        terms = entering * q_ref[here, lanes] + after * (
            r_ref[here, lanes] + slope_ref[:, lanes] * entering
        )
        row = row_ref[:, lanes] + jnp.sum(terms, axis=0, keepdims=True)
        if final:
            rate_part = rate_part + head_column(row, heads, channels // heads, begin)
        else:
            out_ref[:, lanes] = row
    if final:
        base = parts_ref[...]
        out_ref[...] = jnp.concatenate([base[:1] + to_row(rate_part), base[1:]], axis=0)


def share_kernel(size, pieces, start, *refs):
    states, refs = [refs[3 * i : 3 * i + 3] for i in range(pieces)], refs[3 * pieces :]
    high_ref, low_ref, scaled_ref, sum_b_ref, sum_c_ref = refs[:5]
    rows, channels = pieces * states[0][0].shape[0], scaled_ref.shape[1]
    here = slice(start, start + rows)
    grad_b = sum_b_ref[:, here]
    grad_c = sum_c_ref[:, here]
    for begin in range(0, channels, LANES):
        lanes = pl.ds(begin, LANES)
        entering, after = picked(size, states, lanes)
        enter_high, enter_low = split(entering, 2)
        after_high, after_low = split(after, 2)
        high, low, scaled = high_ref[:, lanes], low_ref[:, lanes], scaled_ref[:, lanes]
        grad_c = grad_c + mm_nt(high, enter_high) + (mm_nt(high, enter_low) + mm_nt(low, enter_high))
        grad_b = grad_b + mm_nt(scaled, after_high) + mm_nt(scaled, after_low)
    refs[-1][...] = jnp.concatenate([grad_b, grad_c], axis=1)


def rest_kernel(size, pieces, *refs):
    states, refs = [refs[3 * i : 3 * i + 3] for i in range(pieces)], refs[3 * pieces :]
    (
        v_ref, b_ref, c_ref, coef_ref, mamba_ref, inner_ref, growth_ref, fall_ref, gy_ref,
        gcum_ref, decay_ref, neg_ref, _, gv_ref, gg_ref, gs_ref, total_ref,
    ) = refs
    length, channels = v_ref.shape
    heads = gcum_ref.shape[0]
    width = channels // heads
    block_b, block_c = b_ref[...], c_ref[...]
    grad_cum = gcum_ref[...]
    grad_total = jnp.zeros((heads, 1), F32)
    for first in range(0, channels, LANES):
        here = pl.ds(first, LANES)
        entering, after = picked(size, states, here)
        enter_high, enter_low = split(entering, 2)
        after_high, after_low = split(after, 2)
        inter = growth_ref[:, here] * (mm(block_c, enter_high) + mm(block_c, enter_low))
        outer = fall_ref[:, here] * (mm(block_b, after_high) + mm(block_b, after_low))
        gg_ref[0, :, here] = (coef_ref[:, here] * (mamba_ref[:, here] + inter)).astype(BF16)
        gv_ref[0, :, here] = (inner_ref[:, here] + outer).astype(BF16)
        pulled = v_ref[:, here].astype(F32) * outer
        high, low = split(gy_ref[:, here] * inter - pulled, 2)
        head_rows = jnp.where(head_map(heads, width, first, LANES), 1.0, 0.0).astype(BF16)
        grad_cum = grad_cum + mm_nt(head_rows, high) + mm_nt(head_rows, low)
        total_row = jnp.sum(pulled, axis=0, keepdims=True) + decay_ref[:, here] * jnp.sum(
            after * entering, axis=0, keepdims=True
        )
        grad_total = grad_total + head_column(total_row, heads, width, first)
    gs_ref[0] = neg_ref[...] * (scan_tokens(grad_cum, True) + grad_total)
    total_ref[...] = to_row(grad_total)


def tree(values):
    while len(values) > 1:
        values = [sum(values[i + 1 : i + 2], values[i]) for i in range(0, len(values), 2)]
    return values[0]


def add_kernel(x_ref, y_ref, *refs):
    refs[-1][...] = x_ref[...] + y_ref[...]


def last_kernel(counts, *refs):
    refs, (gb_ref, gc_ref, rate_ref, skip_ref) = refs[:-4], refs[-4:]
    sums = []
    for count in counts:
        sums.append(tree([ref[...] for ref in refs[:count]]))
        refs = refs[count:]
    *shares, small = sums
    start = 0
    for both in shares:
        rows = both.shape[1] // 2
        gb_ref[0, :, start : start + rows] = both[:, :rows]
        gc_ref[0, :, start : start + rows] = both[:, rows:]
        start += rows
    rate_ref[...] = small[:1]
    skip_ref[...] = small[1:]


def call(kernel, outs, scratch=(), flops=0, space=pltpu.VMEM, after=()):
    def run(*args):
        if space == pltpu.HBM:
            args = [pltpu.with_memory_space_constraint(a, space) for a in args]
        specs = [pl.BlockSpec(memory_space=space)] * len(args)
        specs += [pl.BlockSpec(memory_space=pl.ANY)] * len(after)
        args = (*args, *after)
        size = sum(a.size * a.dtype.itemsize for a in (*args, *outs))
        return pl.pallas_call(
            kernel,
            out_shape=tuple(outs),
            in_specs=specs,
            out_specs=tuple(pl.BlockSpec(memory_space=pltpu.VMEM) for _ in outs),
            scratch_shapes=list(scratch),
            compiler_params=pltpu.CompilerParams(vmem_limit_bytes=VMEM_LIMIT),
            cost_estimate=pl.CostEstimate(flops=flops, bytes_accessed=size, transcendentals=0),
        )(*args)

    return run


def swap(x, axis, size, bit):
    return lax.ppermute(x, axis, [(i, i ^ bit) for i in range(size)])


def hop_pairs(size, hop):
    return [(hop, hop + 1), (size - 1 - hop, size - 2 - hop)]


def pass_kernel(*refs):
    got_ref, base_ref, decay_ref = refs[:3]
    refs[-1][...] = decay_ref[...] * got_ref[...] + base_ref[...]


def pass_on(got, base, decay, after):
    return call(pass_kernel, [jax.ShapeDtypeStruct(base.shape, F32)], flops=2 * base.size, after=after)(
        got, base, decay
    )[0]


def chain(size, mine, other, decay, work):
    chunks = len(mine)
    if size == 1:
        for k in sorted(work):
            work[k](())
        return [(x, x, x) for x in mine]
    if size % 2:
        raise NotImplementedError
    index = lax.axis_index("seq")
    place = jnp.minimum(index, size - 1 - index)
    middle = size // 2 - 1
    got = {(0, c): lax.ppermute(mine[c], "seq", hop_pairs(size, 0)) for c in range(chunks)}
    steps = [
        (hop + c + (LAG if hop > middle else 0), hop, c) for hop in range(1, size - 1) for c in range(chunks)
    ]
    token = ()
    for count, (_, hop, c) in enumerate(sorted(steps)):
        if count in work:
            token = work[count](token)
        if hop > middle and c > 1:
            token = (*token, got[hop, c - 2])
        base = mine[c] if hop <= middle else other[c]
        pay = pass_on(got[hop - 1, c], base, decay, token)
        got[hop, c] = lax.ppermute(pay, "seq", hop_pairs(size, hop))
        token = (pay,)
    for k in sorted(work):
        if k >= len(steps):
            token = work[k](token)
    states = []
    for c in range(chunks):
        first, second, last = got[0, c], got[middle, c], got[size - 2, c]
        for hop in range(1, middle):
            first = jnp.where(place == hop + 1, got[hop, c], first)
        for hop in range(middle + 1, size - 2):
            second = jnp.where(place == size - 2 - hop, got[hop, c], second)
        states.append((first, second, last))
    return states


def sum_terms(x, axis, size):
    if size == 1:
        return [x]
    if size == 4:
        return [x] + [swap(x, axis, size, bit) for bit in (1, 2, 3)]
    if size & (size - 1):
        return [lax.psum(x, axis)]
    bit = 1
    while 2 * bit < size:
        x = x + swap(x, axis, size, bit)
        bit *= 2
    return [x, swap(x, axis, size, bit)]


def small_terms(x, axes, sizes, between):
    bits = [(axis, 1 << k) for axis in axes for k in range(sizes[axis].bit_length() - 1)]
    if any(sizes[axis] & (sizes[axis] - 1) for axis in axes):
        x = lax.psum(x, tuple(axes))
        between((x,))
        return [x]
    after = ()
    for count, (axis, bit) in enumerate(bits):
        theirs = swap(x, axis, sizes[axis], bit)
        if count == len(bits) - 1:
            break
        x = call(add_kernel, [jax.ShapeDtypeStruct(x.shape, F32)], after=after)(x, theirs)[0]
        after = between((x,)) if count == 0 else ()
    if len(bits) < 2:
        between((x,))
    return [x, theirs] if bits else [x]


def shards(sizes, values, gate_in, in_b, in_c, step_sizes, log_rates, skip_gain, grad_out):
    like = jax.ShapeDtypeStruct
    length, channels = values.shape[1:]
    heads = step_sizes.shape[1]
    state = in_b.shape[2]
    seq = sizes["seq"]
    rows = state // CHUNKS
    wide = like((length, channels), F32)
    wide_b = like((length, channels), BF16)
    share = like((length, state), F32)
    small = like((heads, length), F32)
    row = like((1, channels), F32)
    piece = like((rows, channels), F32)
    maps = like((length, state), BF16)

    out = call(
        functools.partial(states_kernel, CHUNKS, seq),
        [wide_b, wide_b, wide_b, maps, maps, small, small, row, row, like((1, heads), F32)]
        + [piece] * (2 * CHUNKS),
        [
            pltpu.VMEM((heads, length), F32),
            pltpu.VMEM((1, heads), F32),
            pltpu.SemaphoreType.DMA((8,)),
        ],
        flops=8 * length * channels * state,
        space=pltpu.HBM,
    )(
        values[0], gate_in[0], grad_out[0], in_b[0], in_c[0], step_sizes[0],
        log_rates.reshape(1, heads), skip_gain.reshape(1, heads),
    )
    vals, gate, grad, block_b, block_c, cumulative, negative, decay, slope, skip = out[:10]
    mine, other = out[10 : 10 + CHUNKS], out[10 + CHUNKS :]

    made = {}

    def intra(after):
        made["intra"] = call(
            intra_kernel,
            [wide, wide, share, share],
            [
                pltpu.VMEM((channels, length), BF16),
                pltpu.VMEM((channels, length), F32),
                pltpu.VMEM((length, length), F32),
            ],
            flops=16 * length * length * channels,
        )(vals, gate, grad, block_b, block_c, cumulative)
        return (made["intra"][2],)

    def prepare(after):
        made["prepare"] = call(
            prepare_kernel,
            [wide] * 6 + [wide_b] * 3 + [like((state, channels), F32)] * 2 + [small, like((2, heads), F32)],
            flops=16 * length * state * channels,
        )(
            vals, gate, grad, block_b, block_c, cumulative, skip,
            *made["intra"][:2], *(after if after else made["intra"][2:3]),
        )
        return (made["prepare"][-2],)

    states = chain(seq, mine, other, decay, {0: intra, 1: prepare})
    sum_b, sum_c = made["intra"][2:]
    (
        coef, mamba, inner, growth, fall, grad_y, high, low, scaled, q, r, grad_cum, parts,
    ) = made["prepare"]

    rate_row = jnp.zeros((1, channels), F32)
    terms, counts = [], []
    for i in range(PARTS):
        final = i == PARTS - 1
        count = CHUNKS // PARTS
        own = [x for group in states[i * count : (i + 1) * count] for x in group]
        rate_row = call(
            functools.partial(rate_kernel, seq, count, i * rows * count, heads, final),
            [like((2, heads), F32) if final else row],
        )(*own, q, r, slope, rate_row, parts)[0]
        share_of = call(
            functools.partial(share_kernel, seq, count, i * rows * count),
            [like((length, 2 * rows * count), F32)],
            flops=10 * length * channels * rows * count,
            after=(rate_row,),
        )(*own, high, low, scaled, sum_b, sum_c)[0]
        own = sum_terms(share_of, "tensor", sizes["tensor"])
        terms += own
        counts.append(len(own))

    def rest(after):
        made["rest"] = call(
            functools.partial(rest_kernel, seq, CHUNKS),
            [like((1, length, channels), BF16)] * 2
            + [like((1, heads, length), F32), like((1, heads), F32)],
            flops=10 * length * channels * state,
            after=after,
        )(
            *(x for group in states for x in group),
            vals, block_b, block_c, coef, mamba, inner, growth, fall, grad_y, grad_cum, decay, negative,
        )
        return (made["rest"][3],)

    own = small_terms(rate_row, ("replica", "seq"), sizes, rest)
    terms += own
    counts.append(len(own))
    grad_values, grad_gate, grad_steps, _ = made["rest"]
    grad_b, grad_c, rate_sum, skip_sum = call(
        functools.partial(last_kernel, tuple(counts)),
        [like((1, length, state), F32)] * 2 + [like((1, heads), F32)] * 2,
    )(*terms)
    return (
        grad_values,
        grad_gate,
        grad_b,
        grad_c,
        grad_steps,
        rate_sum.reshape(heads),
        skip_sum.reshape(heads),
    )


def solution(mesh):
    in_specs = (
        P("replica", "seq", "tensor"),
        P("replica", "seq", "tensor"),
        P("replica", "seq", None),
        P("replica", "seq", None),
        P("replica", "tensor", "seq"),
        P("tensor"),
        P("tensor"),
        P("replica", "seq", "tensor"),
    )
    out_specs = (
        P("replica", "seq", "tensor"),
        P("replica", "seq", "tensor"),
        P("replica", "seq", None),
        P("replica", "seq", None),
        P("replica", "tensor", "seq"),
        P("tensor"),
        P("tensor"),
    )
    body = functools.partial(shards, dict(mesh.shape))
    return jax.shard_map(body, mesh=mesh, in_specs=in_specs, out_specs=out_specs, check_vma=False)
```

```python
import functools

import jax
import jax.numpy as jnp
from jax import lax
from jax.experimental import pallas as pl
from jax.experimental.pallas import tpu as pltpu
from jax.sharding import PartitionSpec as P

F32 = jnp.float32
BF16 = jnp.bfloat16
VMEM_LIMIT = 24 * 1024 * 1024
LANES = 256
CHUNKS = 4
PARTS = 2
LAG = 2


def split(x, parts):
    terms = []
    for _ in range(parts - 1):
        term = x.astype(BF16)
        terms.append(term)
        x = x - term.astype(F32)
    terms.append(x.astype(BF16))
    return terms


def mm(a, b):
    return lax.dot_general(a, b, (((1,), (0,)), ((), ())), preferred_element_type=F32)


def mm_nt(a, b):
    return lax.dot_general(a, b, (((1,), (1,)), ((), ())), preferred_element_type=F32)


def mm_tn(a, b):
    return lax.dot_general(a, b, (((0,), (0,)), ((), ())), preferred_element_type=F32)


def iota(shape, dim):
    return lax.broadcasted_iota(jnp.int32, shape, dim)


def to_column(row):
    n = row.shape[1]
    eye = iota((n, n), 0) == iota((n, n), 1)
    return jnp.sum(jnp.where(eye, row, 0.0), axis=1, keepdims=True)


def to_row(column):
    n = column.shape[0]
    eye = iota((n, n), 0) == iota((n, n), 1)
    return jnp.sum(jnp.where(eye, column, 0.0), axis=0, keepdims=True)


def head_map(heads, width, first, lanes):
    low = iota((heads, lanes), 0) * width
    channel = iota((heads, lanes), 1) + first
    return (channel >= low) & (channel < low + width)


def spread_map(heads, width, first, lanes):
    one = jnp.where(head_map(heads, width, first, lanes), 1.0, 0.0).astype(BF16)
    return jnp.concatenate([one, one, one], axis=0)


def rows_of_three(per_head):
    return jnp.concatenate(split(per_head, 3), axis=0)


def spread(three, first, lanes, width):
    heads = three.shape[0] // 3
    return mm_tn(three, spread_map(heads, width, first, lanes))


def scan_tokens(per_head, backward):
    heads, length = per_head.shape
    source = iota((length, length), 0)
    target = iota((length, length), 1)
    keep = source >= target if backward else source <= target
    sums = mm(rows_of_three(per_head), jnp.where(keep, 1.0, 0.0).astype(BF16))
    return sums[:heads] + sums[heads : 2 * heads] + sums[2 * heads :]


def channel_row(column, heads, width, first):
    mine = head_map(heads, width, first, LANES)
    return jnp.sum(jnp.where(mine, column, 0.0), axis=0, keepdims=True)


def head_column(row, heads, width, first):
    mine = head_map(heads, width, first, LANES)
    return jnp.sum(jnp.where(mine, row, 0.0), axis=1, keepdims=True)


def gate_parts(gate, grad):
    wide = gate.astype(F32)
    sigmoid = 1.0 / (1.0 + jnp.exp(-wide))
    return wide, sigmoid, grad.astype(F32) * (wide * sigmoid)


def states_kernel(chunks, size, *refs):
    sources, outs, (steps_ref, lr_ref, sems) = refs[:8], refs[8:-3], refs[-3:]
    v_ref, gate_ref, go_ref, b_ref, c_ref = outs[:5]
    cum_ref, neg_ref, decay_ref, slope_ref, skip_ref = outs[5:10]
    mine_refs, other_refs = outs[10 : 10 + chunks], outs[10 + chunks :]
    targets = (v_ref, gate_ref, go_ref, b_ref, c_ref, steps_ref, lr_ref, skip_ref)
    copies = [
        pltpu.make_async_copy(source, target, sems.at[i])
        for i, (source, target) in enumerate(zip(sources, targets))
    ]
    for i in (6, 5, 3, 4, 0, 1, 2, 7):
        copies[i].start()
    copies[6].wait()
    copies[5].wait()
    length, channels = v_ref.shape
    heads = steps_ref.shape[0]
    width = channels // heads
    lower = lax.axis_index("seq") < size // 2 if size > 1 else True
    rates = jnp.exp(to_column(lr_ref[...]))
    cumulative = scan_tokens(-rates * steps_ref[...], False)
    total = cumulative[:, -1:]
    decay = jnp.exp(total)
    cum_ref[...] = cumulative
    neg_ref[...] = jnp.broadcast_to(-rates, (heads, length))
    growth = rows_of_three(jnp.exp(cumulative))
    fall = rows_of_three(jnp.exp(total - cumulative))
    copies[3].wait()
    copies[4].wait()
    b_t = b_ref[...].astype(F32).T.astype(BF16)
    c_t = c_ref[...].astype(F32).T.astype(BF16)
    for i in (0, 1, 2, 7):
        copies[i].wait()
    rows = b_t.shape[0] // chunks
    for first in range(0, channels, LANES):
        here = pl.ds(first, LANES)
        _, _, grad_y = gate_parts(gate_ref[:, here], go_ref[:, here])
        high, low = split(spread(growth, first, LANES, width) * grad_y, 2)
        pulled = mm(c_t, high) + mm(c_t, low)
        scaled = (spread(fall, first, LANES, width) * v_ref[:, here].astype(F32)).astype(BF16)
        local = mm(b_t, scaled)
        mine = jnp.where(lower, local, pulled)
        other = jnp.where(lower, pulled, local)
        for i in range(chunks):
            mine_refs[i][:, here] = mine[i * rows : (i + 1) * rows]
            other_refs[i][:, here] = other[i * rows : (i + 1) * rows]
        decay_ref[:, here] = channel_row(decay, heads, width, first)
        slope_ref[:, here] = channel_row(total * decay, heads, width, first)


def intra_kernel(
    v_ref, gate_ref, go_ref, b_ref, c_ref, cum_ref,
    intra_ref, inner_ref, sum_b_ref, sum_c_ref, grad_t_ref, inner_t_ref, acc_ref,
):
    length, channels = v_ref.shape
    heads = cum_ref.shape[0]
    width = channels // heads
    half = length // 2
    pair = 2 * width
    cumulative = cum_ref[...]
    columns = cumulative.T
    scores = mm_nt(c_ref[...], b_ref[...])
    causal = iota((half, half), 0) >= iota((half, half), 1)
    left = iota((1, pair), 1) < width
    acc_ref[...] = jnp.zeros_like(acc_ref)

    def blocks(x):
        return x[:half, :half], x[half:, :half], x[half:, half:]

    scores_00, scores_10, scores_11 = blocks(scores)
    for first in range(0, channels, pair):
        here = pl.ds(first, pair)
        _, _, grad_y = gate_parts(gate_ref[:, here], go_ref[:, here])
        grad_t_ref[here, :] = grad_y.T.astype(BF16)
        vals = v_ref[:, here]
        pieces = []
        for side in range(2):
            head = first // width + side
            own = left if side == 0 else jnp.logical_not(left)
            row = cumulative[head : head + 1, :]
            column = columns[:, head : head + 1]
            row_0, row_1 = row[:, :half], row[:, half:]
            column_0, column_1 = column[:half], column[half:]
            decay_00 = jnp.exp(jnp.where(causal, column_0 - row_0, -1e30))
            decay_10 = jnp.exp(column_1 - row_0)
            decay_11 = jnp.exp(jnp.where(causal, column_1 - row_1, -1e30))
            mix_00 = (scores_00 * decay_00).astype(BF16)
            mix_10 = (scores_10 * decay_10).astype(BF16)
            mix_11 = (scores_11 * decay_11).astype(BF16)
            low_rows = jnp.concatenate([mix_10, mix_11], axis=1)
            pieces.append((mm(mix_00, vals[:half]), mm(low_rows, vals)))
            head_grad = jnp.where(own, grad_y, 0.0).astype(BF16)
            mixed_0 = mm_nt(head_grad[:half], vals[:half])
            mixed_1 = mm_nt(head_grad[half:], vals)
            acc_ref[:half, :half] += mixed_0 * decay_00
            acc_ref[half:, :half] += mixed_1[:, :half] * decay_10
            acc_ref[half:, half:] += mixed_1[:, half:] * decay_11
            mine = pl.ds(first + side * width, width)
            grad_t = grad_t_ref[mine, :]
            inner_t_ref[mine, :half] = mm(grad_t[:, :half], mix_00) + mm(grad_t[:, half:], mix_10)
            inner_t_ref[mine, half:] = mm(grad_t[:, half:], mix_11)
        intra_ref[:half, here] = jnp.where(left, pieces[0][0], pieces[1][0])
        intra_ref[half:, here] = jnp.where(left, pieces[0][1], pieces[1][1])
        inner_ref[:, here] = inner_t_ref[here, :].T
    shares = acc_ref[...]
    high, low = split(shares, 2)
    sum_c_ref[...] = mm(high, b_ref[...]) + mm(low, b_ref[...])
    high, low = split(shares.T, 2)
    sum_b_ref[...] = mm(high, c_ref[...]) + mm(low, c_ref[...])


def prepare_kernel(
    v_ref, gate_ref, go_ref, b_ref, c_ref, cum_ref, skip_ref, intra_ref, in_inner_ref, after_ref,
    coef_ref, mamba_ref, inner_ref, growth_ref, fall_ref, gy_ref,
    high_ref, low_ref, scaled_ref, q_ref, r_ref, gcum_ref, parts_ref,
):
    length, channels = v_ref.shape
    heads = cum_ref.shape[0]
    width = channels // heads
    cumulative = cum_ref[...]
    total = cumulative[:, -1:]
    left_over = total - cumulative
    growth_three = rows_of_three(jnp.exp(cumulative))
    fall_three = rows_of_three(jnp.exp(left_over))
    growth_slope = rows_of_three(cumulative * jnp.exp(cumulative))
    fall_slope = rows_of_three(left_over * jnp.exp(left_over))
    b_t = b_ref[...].astype(F32).T.astype(BF16)
    c_t = c_ref[...].astype(F32).T.astype(BF16)
    skip_column = to_column(skip_ref[...])
    grad_cum = jnp.zeros((heads, length), F32)
    skip_part = jnp.zeros((heads, 1), F32)
    for first in range(0, channels, LANES):
        here = pl.ds(first, LANES)
        wide, sigmoid, grad_y = gate_parts(gate_ref[:, here], go_ref[:, here])
        vals = v_ref[:, here].astype(F32)
        skip = channel_row(skip_column, heads, width, first)
        growth = spread(growth_three, first, LANES, width)
        fall = spread(fall_three, first, LANES, width)
        growth_ref[:, here] = growth
        fall_ref[:, here] = fall
        gy_ref[:, here] = grad_y
        coef_ref[:, here] = go_ref[:, here].astype(F32) * sigmoid * (1.0 + wide * (1.0 - sigmoid))
        high, low = split(growth * grad_y, 2)
        high_ref[:, here] = high
        low_ref[:, here] = low
        scaled_ref[:, here] = (fall * vals).astype(BF16)
        intra = intra_ref[:, here]
        inner = in_inner_ref[:, here]
        mamba_ref[:, here] = intra + skip * vals
        inner_ref[:, here] = inner + skip * grad_y
        high, low = split(grad_y.astype(BF16).astype(F32) * intra - vals * inner, 2)
        head_rows = jnp.where(head_map(heads, width, first, LANES), 1.0, 0.0).astype(BF16)
        grad_cum = grad_cum + mm_nt(head_rows, high) + mm_nt(head_rows, low)
        skip_row = jnp.sum(grad_y * vals, axis=0, keepdims=True)
        skip_part = skip_part + head_column(skip_row, heads, width, first)
        high, low = split(spread(growth_slope, first, LANES, width) * grad_y, 2)
        q_ref[:, here] = mm(c_t, high) + mm(c_t, low)
        high, low = split(spread(fall_slope, first, LANES, width) * vals, 2)
        r_ref[:, here] = mm(b_t, high) + mm(b_t, low)
    gcum_ref[...] = grad_cum
    rate_part = jnp.sum(grad_cum * cumulative, axis=1, keepdims=True)
    parts_ref[...] = jnp.concatenate([to_row(rate_part), to_row(skip_part)], axis=0)


def pick(size, first, second, last):
    if size == 1:
        return jnp.zeros_like(first), jnp.zeros_like(first)
    if size % 2:
        return first, second
    index = lax.axis_index("seq")
    lower = index < size // 2
    edge = jnp.logical_or(index == 0, index == size - 1)
    first = jnp.where(edge, 0.0, first)
    second = jnp.where(edge, last, second)
    return jnp.where(lower, first, second), jnp.where(lower, second, first)


def picked(size, states, here):
    both = [pick(size, *(ref[:, here] for ref in state)) for state in states]
    return jnp.concatenate([x[0] for x in both], axis=0), jnp.concatenate([x[1] for x in both], axis=0)


def rate_kernel(size, pieces, start, heads, final, *refs):
    states, refs = [refs[3 * i : 3 * i + 3] for i in range(pieces)], refs[3 * pieces :]
    q_ref, r_ref, slope_ref, row_ref, parts_ref, out_ref = *refs[:5], refs[-1]
    rows, channels = pieces * states[0][0].shape[0], q_ref.shape[1]
    here = slice(start, start + rows)
    rate_part = jnp.zeros((heads, 1), F32)
    for begin in range(0, channels, LANES):
        lanes = pl.ds(begin, LANES)
        entering, after = picked(size, states, lanes)
        terms = entering * q_ref[here, lanes] + after * (
            r_ref[here, lanes] + slope_ref[:, lanes] * entering
        )
        row = row_ref[:, lanes] + jnp.sum(terms, axis=0, keepdims=True)
        if final:
            rate_part = rate_part + head_column(row, heads, channels // heads, begin)
        else:
            out_ref[:, lanes] = row
    if final:
        base = parts_ref[...]
        out_ref[...] = jnp.concatenate([base[:1] + to_row(rate_part), base[1:]], axis=0)


def share_kernel(size, pieces, start, *refs):
    states, refs = [refs[3 * i : 3 * i + 3] for i in range(pieces)], refs[3 * pieces :]
    high_ref, low_ref, scaled_ref, sum_b_ref, sum_c_ref = refs[:5]
    rows, channels = pieces * states[0][0].shape[0], scaled_ref.shape[1]
    here = slice(start, start + rows)
    grad_b = sum_b_ref[:, here]
    grad_c = sum_c_ref[:, here]
    for begin in range(0, channels, LANES):
        lanes = pl.ds(begin, LANES)
        entering, after = picked(size, states, lanes)
        enter_high, enter_low = split(entering, 2)
        after_high, after_low = split(after, 2)
        high, low, scaled = high_ref[:, lanes], low_ref[:, lanes], scaled_ref[:, lanes]
        grad_c = grad_c + mm_nt(high, enter_high) + (mm_nt(high, enter_low) + mm_nt(low, enter_high))
        grad_b = grad_b + mm_nt(scaled, after_high) + mm_nt(scaled, after_low)
    refs[-1][...] = jnp.concatenate([grad_b, grad_c], axis=1)


def rest_kernel(size, pieces, *refs):
    states, refs = [refs[3 * i : 3 * i + 3] for i in range(pieces)], refs[3 * pieces :]
    (
        v_ref, b_ref, c_ref, coef_ref, mamba_ref, inner_ref, growth_ref, fall_ref, gy_ref,
        gcum_ref, decay_ref, neg_ref, _, gv_ref, gg_ref, gs_ref, total_ref,
    ) = refs
    length, channels = v_ref.shape
    heads = gcum_ref.shape[0]
    width = channels // heads
    block_b, block_c = b_ref[...], c_ref[...]
    grad_cum = gcum_ref[...]
    grad_total = jnp.zeros((heads, 1), F32)
    for first in range(0, channels, LANES):
        here = pl.ds(first, LANES)
        entering, after = picked(size, states, here)
        enter_high, enter_low = split(entering, 2)
        after_high, after_low = split(after, 2)
        inter = growth_ref[:, here] * (mm(block_c, enter_high) + mm(block_c, enter_low))
        outer = fall_ref[:, here] * (mm(block_b, after_high) + mm(block_b, after_low))
        gg_ref[0, :, here] = (coef_ref[:, here] * (mamba_ref[:, here] + inter)).astype(BF16)
        gv_ref[0, :, here] = (inner_ref[:, here] + outer).astype(BF16)
        pulled = v_ref[:, here].astype(F32) * outer
        high, low = split(gy_ref[:, here] * inter - pulled, 2)
        head_rows = jnp.where(head_map(heads, width, first, LANES), 1.0, 0.0).astype(BF16)
        grad_cum = grad_cum + mm_nt(head_rows, high) + mm_nt(head_rows, low)
        total_row = jnp.sum(pulled, axis=0, keepdims=True) + decay_ref[:, here] * jnp.sum(
            after * entering, axis=0, keepdims=True
        )
        grad_total = grad_total + head_column(total_row, heads, width, first)
    gs_ref[0] = neg_ref[...] * (scan_tokens(grad_cum, True) + grad_total)
    total_ref[...] = to_row(grad_total)


def tree(values):
    while len(values) > 1:
        values = [sum(values[i + 1 : i + 2], values[i]) for i in range(0, len(values), 2)]
    return values[0]


def add_kernel(x_ref, y_ref, *refs):
    refs[-1][...] = x_ref[...] + y_ref[...]


def last_kernel(counts, *refs):
    refs, (gb_ref, gc_ref, rate_ref, skip_ref) = refs[:-4], refs[-4:]
    sums = []
    for count in counts:
        sums.append(tree([ref[...] for ref in refs[:count]]))
        refs = refs[count:]
    *shares, small = sums
    start = 0
    for both in shares:
        rows = both.shape[1] // 2
        gb_ref[0, :, start : start + rows] = both[:, :rows]
        gc_ref[0, :, start : start + rows] = both[:, rows:]
        start += rows
    rate_ref[...] = small[:1]
    skip_ref[...] = small[1:]


def call(kernel, outs, scratch=(), flops=0, space=pltpu.VMEM, after=()):
    def run(*args):
        if space == pltpu.HBM:
            args = [pltpu.with_memory_space_constraint(a, space) for a in args]
        specs = [pl.BlockSpec(memory_space=space)] * len(args)
        specs += [pl.BlockSpec(memory_space=pl.ANY)] * len(after)
        args = (*args, *after)
        size = sum(a.size * a.dtype.itemsize for a in (*args, *outs))
        return pl.pallas_call(
            kernel,
            out_shape=tuple(outs),
            in_specs=specs,
            out_specs=tuple(pl.BlockSpec(memory_space=pltpu.VMEM) for _ in outs),
            scratch_shapes=list(scratch),
            compiler_params=pltpu.CompilerParams(vmem_limit_bytes=VMEM_LIMIT),
            cost_estimate=pl.CostEstimate(flops=flops, bytes_accessed=size, transcendentals=0),
        )(*args)

    return run


def swap(x, axis, size, bit):
    return lax.ppermute(x, axis, [(i, i ^ bit) for i in range(size)])


def hop(x, sizes, step):
    size, copies = sizes["seq"], sizes["replica"]
    pairs = []
    for copy in range(copies):
        for place in range(size):
            to = (copy ^ 1 if copies % 2 == 0 else copy, place)
            for low in (step, size - 2 - step):
                if place in (low, low + 1):
                    to = (copy, 2 * low + 1 - place)
            pairs.append((copy * size + place, to[0] * size + to[1]))
    return lax.ppermute(x, ("replica", "seq"), pairs)


def pass_kernel(*refs):
    got_ref, base_ref, decay_ref = refs[:3]
    refs[-1][...] = decay_ref[...] * got_ref[...] + base_ref[...]


def pass_on(got, base, decay, after):
    return call(pass_kernel, [jax.ShapeDtypeStruct(base.shape, F32)], flops=2 * base.size, after=after)(
        got, base, decay
    )[0]


def chain(sizes, mine, other, decay, work):
    chunks = len(mine)
    size = sizes["seq"]
    if size == 1:
        for k in sorted(work):
            work[k](())
        return [(x, x, x) for x in mine]
    if size % 2:
        raise NotImplementedError
    index = lax.axis_index("seq")
    place = jnp.minimum(index, size - 1 - index)
    middle = size // 2 - 1
    got = {(0, c): hop(mine[c], sizes, 0) for c in range(chunks)}
    steps = [
        (at + c + (LAG if at > middle else 0), at, c) for at in range(1, size - 1) for c in range(chunks)
    ]
    token = ()
    for count, (_, at, c) in enumerate(sorted(steps)):
        if count in work:
            token = work[count](token)
        if at > middle and c > 1:
            token = (*token, got[at, c - 2])
        base = mine[c] if at <= middle else other[c]
        pay = pass_on(got[at - 1, c], base, decay, token)
        got[at, c] = hop(pay, sizes, at)
        token = (pay,)
    for k in sorted(work):
        if k >= len(steps):
            token = work[k](token)
    states = []
    for c in range(chunks):
        first, second, last = got[0, c], got[middle, c], got[size - 2, c]
        for at in range(1, middle):
            first = jnp.where(place == at + 1, got[at, c], first)
        for at in range(middle + 1, size - 2):
            second = jnp.where(place == size - 2 - at, got[at, c], second)
        states.append((first, second, last))
    return states


def sum_terms(x, axis, size):
    if size == 1:
        return [x]
    if size == 4:
        return [x] + [swap(x, axis, size, bit) for bit in (1, 2, 3)]
    if size & (size - 1):
        return [lax.psum(x, axis)]
    bit = 1
    while 2 * bit < size:
        x = x + swap(x, axis, size, bit)
        bit *= 2
    return [x, swap(x, axis, size, bit)]


def small_terms(x, axes, sizes, between):
    bits = [(axis, 1 << k) for axis in axes for k in range(sizes[axis].bit_length() - 1)]
    if any(sizes[axis] & (sizes[axis] - 1) for axis in axes):
        x = lax.psum(x, tuple(axes))
        between((x,))
        return [x]
    after = ()
    for count, (axis, bit) in enumerate(bits):
        theirs = swap(x, axis, sizes[axis], bit)
        if count == len(bits) - 1:
            break
        x = call(add_kernel, [jax.ShapeDtypeStruct(x.shape, F32)], after=after)(x, theirs)[0]
        after = between((x,)) if count == 0 else ()
    if len(bits) < 2:
        between((x,))
    return [x, theirs] if bits else [x]


def shards(sizes, values, gate_in, in_b, in_c, step_sizes, log_rates, skip_gain, grad_out):
    like = jax.ShapeDtypeStruct
    length, channels = values.shape[1:]
    heads = step_sizes.shape[1]
    state = in_b.shape[2]
    seq = sizes["seq"]
    rows = state // CHUNKS
    wide = like((length, channels), F32)
    wide_b = like((length, channels), BF16)
    share = like((length, state), F32)
    small = like((heads, length), F32)
    row = like((1, channels), F32)
    piece = like((rows, channels), F32)
    maps = like((length, state), BF16)

    out = call(
        functools.partial(states_kernel, CHUNKS, seq),
        [wide_b, wide_b, wide_b, maps, maps, small, small, row, row, like((1, heads), F32)]
        + [piece] * (2 * CHUNKS),
        [
            pltpu.VMEM((heads, length), F32),
            pltpu.VMEM((1, heads), F32),
            pltpu.SemaphoreType.DMA((8,)),
        ],
        flops=8 * length * channels * state,
        space=pltpu.HBM,
    )(
        values[0], gate_in[0], grad_out[0], in_b[0], in_c[0], step_sizes[0],
        log_rates.reshape(1, heads), skip_gain.reshape(1, heads),
    )
    vals, gate, grad, block_b, block_c, cumulative, negative, decay, slope, skip = out[:10]
    mine, other = out[10 : 10 + CHUNKS], out[10 + CHUNKS :]

    made = {}

    def intra(after):
        made["intra"] = call(
            intra_kernel,
            [wide, wide, share, share],
            [
                pltpu.VMEM((channels, length), BF16),
                pltpu.VMEM((channels, length), F32),
                pltpu.VMEM((length, length), F32),
            ],
            flops=16 * length * length * channels,
        )(vals, gate, grad, block_b, block_c, cumulative)
        return (made["intra"][2],)

    def prepare(after):
        made["prepare"] = call(
            prepare_kernel,
            [wide] * 6 + [wide_b] * 3 + [like((state, channels), F32)] * 2 + [small, like((2, heads), F32)],
            flops=16 * length * state * channels,
        )(
            vals, gate, grad, block_b, block_c, cumulative, skip,
            *made["intra"][:2], *(after if after else made["intra"][2:3]),
        )
        return (made["prepare"][-2],)

    states = chain(sizes, mine, other, decay, {0: intra, max(seq - 2, 0) * CHUNKS - 1: prepare})
    sum_b, sum_c = made["intra"][2:]
    (
        coef, mamba, inner, growth, fall, grad_y, high, low, scaled, q, r, grad_cum, parts,
    ) = made["prepare"]

    rate_row = jnp.zeros((1, channels), F32)
    terms, counts = [], []
    for i in range(PARTS):
        final = i == PARTS - 1
        count = CHUNKS // PARTS
        own = [x for group in states[i * count : (i + 1) * count] for x in group]
        rate_row = call(
            functools.partial(rate_kernel, seq, count, i * rows * count, heads, final),
            [like((2, heads), F32) if final else row],
        )(*own, q, r, slope, rate_row, parts)[0]
        share_of = call(
            functools.partial(share_kernel, seq, count, i * rows * count),
            [like((length, 2 * rows * count), F32)],
            flops=10 * length * channels * rows * count,
            after=(rate_row,),
        )(*own, high, low, scaled, sum_b, sum_c)[0]
        own = sum_terms(share_of, "tensor", sizes["tensor"])
        terms += own
        counts.append(len(own))

    def rest(after):
        made["rest"] = call(
            functools.partial(rest_kernel, seq, CHUNKS),
            [like((1, length, channels), BF16)] * 2
            + [like((1, heads, length), F32), like((1, heads), F32)],
            flops=10 * length * channels * state,
            after=after,
        )(
            *(x for group in states for x in group),
            vals, block_b, block_c, coef, mamba, inner, growth, fall, grad_y, grad_cum, decay, negative,
        )
        return (made["rest"][3],)

    own = small_terms(rate_row, ("replica", "seq"), sizes, rest)
    terms += own
    counts.append(len(own))
    grad_values, grad_gate, grad_steps, _ = made["rest"]
    grad_b, grad_c, rate_sum, skip_sum = call(
        functools.partial(last_kernel, tuple(counts)),
        [like((1, length, state), F32)] * 2 + [like((1, heads), F32)] * 2,
    )(*terms)
    return (
        grad_values,
        grad_gate,
        grad_b,
        grad_c,
        grad_steps,
        rate_sum.reshape(heads),
        skip_sum.reshape(heads),
    )


def solution(mesh):
    in_specs = (
        P("replica", "seq", "tensor"),
        P("replica", "seq", "tensor"),
        P("replica", "seq", None),
        P("replica", "seq", None),
        P("replica", "tensor", "seq"),
        P("tensor"),
        P("tensor"),
        P("replica", "seq", "tensor"),
    )
    out_specs = (
        P("replica", "seq", "tensor"),
        P("replica", "seq", "tensor"),
        P("replica", "seq", None),
        P("replica", "seq", None),
        P("replica", "tensor", "seq"),
        P("tensor"),
        P("tensor"),
    )
    body = functools.partial(shards, dict(mesh.shape))
    return jax.shard_map(body, mesh=mesh, in_specs=in_specs, out_specs=out_specs, check_vma=False)
```

```python
import functools

import jax
import jax.numpy as jnp
from jax import lax
from jax.experimental import pallas as pl
from jax.experimental.pallas import tpu as pltpu
from jax.sharding import PartitionSpec as P

F32 = jnp.float32
BF16 = jnp.bfloat16
VMEM_LIMIT = 24 * 1024 * 1024
LANES = 256
CHUNKS = 4
PARTS = 2
LAG = 1


def split(x, parts):
    terms = []
    for _ in range(parts - 1):
        term = x.astype(BF16)
        terms.append(term)
        x = x - term.astype(F32)
    terms.append(x.astype(BF16))
    return terms


def mm(a, b):
    return lax.dot_general(a, b, (((1,), (0,)), ((), ())), preferred_element_type=F32)


def mm_nt(a, b):
    return lax.dot_general(a, b, (((1,), (1,)), ((), ())), preferred_element_type=F32)


def mm_tn(a, b):
    return lax.dot_general(a, b, (((0,), (0,)), ((), ())), preferred_element_type=F32)


def iota(shape, dim):
    return lax.broadcasted_iota(jnp.int32, shape, dim)


def to_column(row):
    n = row.shape[1]
    eye = iota((n, n), 0) == iota((n, n), 1)
    return jnp.sum(jnp.where(eye, row, 0.0), axis=1, keepdims=True)


def to_row(column):
    n = column.shape[0]
    eye = iota((n, n), 0) == iota((n, n), 1)
    return jnp.sum(jnp.where(eye, column, 0.0), axis=0, keepdims=True)


def head_map(heads, width, first, lanes):
    low = iota((heads, lanes), 0) * width
    channel = iota((heads, lanes), 1) + first
    return (channel >= low) & (channel < low + width)


def spread_map(heads, width, first, lanes):
    one = jnp.where(head_map(heads, width, first, lanes), 1.0, 0.0).astype(BF16)
    return jnp.concatenate([one, one, one], axis=0)


def rows_of_three(per_head):
    return jnp.concatenate(split(per_head, 3), axis=0)


def spread(three, first, lanes, width):
    heads = three.shape[0] // 3
    return mm_tn(three, spread_map(heads, width, first, lanes))


def scan_tokens(per_head, backward):
    heads, length = per_head.shape
    source = iota((length, length), 0)
    target = iota((length, length), 1)
    keep = source >= target if backward else source <= target
    sums = mm(rows_of_three(per_head), jnp.where(keep, 1.0, 0.0).astype(BF16))
    return sums[:heads] + sums[heads : 2 * heads] + sums[2 * heads :]


def channel_row(column, heads, width, first):
    mine = head_map(heads, width, first, LANES)
    return jnp.sum(jnp.where(mine, column, 0.0), axis=0, keepdims=True)


def head_column(row, heads, width, first):
    mine = head_map(heads, width, first, LANES)
    return jnp.sum(jnp.where(mine, row, 0.0), axis=1, keepdims=True)


def gate_parts(gate, grad):
    wide = gate.astype(F32)
    sigmoid = 1.0 / (1.0 + jnp.exp(-wide))
    return wide, sigmoid, grad.astype(F32) * (wide * sigmoid)


def states_kernel(chunks, size, *refs):
    sources, outs, (steps_ref, lr_ref, sems) = refs[:8], refs[8:-3], refs[-3:]
    v_ref, gate_ref, go_ref, b_ref, c_ref = outs[:5]
    cum_ref, neg_ref, decay_ref, slope_ref, skip_ref = outs[5:10]
    mine_refs, other_refs = outs[10 : 10 + chunks], outs[10 + chunks :]
    targets = (v_ref, gate_ref, go_ref, b_ref, c_ref, steps_ref, lr_ref, skip_ref)
    copies = [
        pltpu.make_async_copy(source, target, sems.at[i])
        for i, (source, target) in enumerate(zip(sources, targets))
    ]
    for i in (6, 5, 3, 4, 0, 1, 2, 7):
        copies[i].start()
    copies[6].wait()
    copies[5].wait()
    length, channels = v_ref.shape
    heads = steps_ref.shape[0]
    width = channels // heads
    lower = lax.axis_index("seq") < size // 2 if size > 1 else True
    rates = jnp.exp(to_column(lr_ref[...]))
    cumulative = scan_tokens(-rates * steps_ref[...], False)
    total = cumulative[:, -1:]
    decay = jnp.exp(total)
    cum_ref[...] = cumulative
    neg_ref[...] = jnp.broadcast_to(-rates, (heads, length))
    growth = rows_of_three(jnp.exp(cumulative))
    fall = rows_of_three(jnp.exp(total - cumulative))
    copies[3].wait()
    copies[4].wait()
    b_t = b_ref[...].astype(F32).T.astype(BF16)
    c_t = c_ref[...].astype(F32).T.astype(BF16)
    for i in (0, 1, 2, 7):
        copies[i].wait()
    rows = b_t.shape[0] // chunks
    for first in range(0, channels, LANES):
        here = pl.ds(first, LANES)
        _, _, grad_y = gate_parts(gate_ref[:, here], go_ref[:, here])
        high, low = split(spread(growth, first, LANES, width) * grad_y, 2)
        pulled = mm(c_t, high) + mm(c_t, low)
        scaled = (spread(fall, first, LANES, width) * v_ref[:, here].astype(F32)).astype(BF16)
        local = mm(b_t, scaled)
        mine = jnp.where(lower, local, pulled)
        other = jnp.where(lower, pulled, local)
        for i in range(chunks):
            mine_refs[i][:, here] = mine[i * rows : (i + 1) * rows]
            other_refs[i][:, here] = other[i * rows : (i + 1) * rows]
        decay_ref[:, here] = channel_row(decay, heads, width, first)
        slope_ref[:, here] = channel_row(total * decay, heads, width, first)


def intra_kernel(
    v_ref, gate_ref, go_ref, b_ref, c_ref, cum_ref,
    intra_ref, inner_ref, sum_b_ref, sum_c_ref, grad_t_ref, inner_t_ref, acc_ref,
):
    length, channels = v_ref.shape
    heads = cum_ref.shape[0]
    width = channels // heads
    half = length // 2
    pair = 2 * width
    cumulative = cum_ref[...]
    columns = cumulative.T
    scores = mm_nt(c_ref[...], b_ref[...])
    causal = iota((half, half), 0) >= iota((half, half), 1)
    left = iota((1, pair), 1) < width
    acc_ref[...] = jnp.zeros_like(acc_ref)

    def blocks(x):
        return x[:half, :half], x[half:, :half], x[half:, half:]

    scores_00, scores_10, scores_11 = blocks(scores)
    for first in range(0, channels, pair):
        here = pl.ds(first, pair)
        _, _, grad_y = gate_parts(gate_ref[:, here], go_ref[:, here])
        grad_t_ref[here, :] = grad_y.T.astype(BF16)
        vals = v_ref[:, here]
        pieces = []
        for side in range(2):
            head = first // width + side
            own = left if side == 0 else jnp.logical_not(left)
            row = cumulative[head : head + 1, :]
            column = columns[:, head : head + 1]
            row_0, row_1 = row[:, :half], row[:, half:]
            column_0, column_1 = column[:half], column[half:]
            decay_00 = jnp.exp(jnp.where(causal, column_0 - row_0, -1e30))
            decay_10 = jnp.exp(column_1 - row_0)
            decay_11 = jnp.exp(jnp.where(causal, column_1 - row_1, -1e30))
            mix_00 = (scores_00 * decay_00).astype(BF16)
            mix_10 = (scores_10 * decay_10).astype(BF16)
            mix_11 = (scores_11 * decay_11).astype(BF16)
            low_rows = jnp.concatenate([mix_10, mix_11], axis=1)
            pieces.append((mm(mix_00, vals[:half]), mm(low_rows, vals)))
            head_grad = jnp.where(own, grad_y, 0.0).astype(BF16)
            mixed_0 = mm_nt(head_grad[:half], vals[:half])
            mixed_1 = mm_nt(head_grad[half:], vals)
            acc_ref[:half, :half] += mixed_0 * decay_00
            acc_ref[half:, :half] += mixed_1[:, :half] * decay_10
            acc_ref[half:, half:] += mixed_1[:, half:] * decay_11
            mine = pl.ds(first + side * width, width)
            grad_t = grad_t_ref[mine, :]
            inner_t_ref[mine, :half] = mm(grad_t[:, :half], mix_00) + mm(grad_t[:, half:], mix_10)
            inner_t_ref[mine, half:] = mm(grad_t[:, half:], mix_11)
        intra_ref[:half, here] = jnp.where(left, pieces[0][0], pieces[1][0])
        intra_ref[half:, here] = jnp.where(left, pieces[0][1], pieces[1][1])
        inner_ref[:, here] = inner_t_ref[here, :].T
    shares = acc_ref[...]
    high, low = split(shares, 2)
    sum_c_ref[...] = mm(high, b_ref[...]) + mm(low, b_ref[...])
    high, low = split(shares.T, 2)
    sum_b_ref[...] = mm(high, c_ref[...]) + mm(low, c_ref[...])


def factors_kernel(
    v_ref, gate_ref, go_ref, b_ref, c_ref, cum_ref, after_ref,
    high_ref, low_ref, scaled_ref, q_ref, r_ref,
):
    length, channels = v_ref.shape
    heads = cum_ref.shape[0]
    width = channels // heads
    cumulative = cum_ref[...]
    left_over = cumulative[:, -1:] - cumulative
    growth = rows_of_three(jnp.exp(cumulative))
    fall = rows_of_three(jnp.exp(left_over))
    growth_slope = rows_of_three(cumulative * jnp.exp(cumulative))
    fall_slope = rows_of_three(left_over * jnp.exp(left_over))
    b_t = b_ref[...].astype(F32).T.astype(BF16)
    c_t = c_ref[...].astype(F32).T.astype(BF16)
    for first in range(0, channels, LANES):
        here = pl.ds(first, LANES)
        _, _, grad_y = gate_parts(gate_ref[:, here], go_ref[:, here])
        vals = v_ref[:, here].astype(F32)
        high, low = split(spread(growth, first, LANES, width) * grad_y, 2)
        high_ref[:, here] = high
        low_ref[:, here] = low
        scaled_ref[:, here] = (spread(fall, first, LANES, width) * vals).astype(BF16)
        high, low = split(spread(growth_slope, first, LANES, width) * grad_y, 2)
        q_ref[:, here] = mm(c_t, high) + mm(c_t, low)
        high, low = split(spread(fall_slope, first, LANES, width) * vals, 2)
        r_ref[:, here] = mm(b_t, high) + mm(b_t, low)


def prepare_kernel(
    v_ref, gate_ref, go_ref, cum_ref, skip_ref, intra_ref, in_inner_ref, after_ref,
    coef_ref, mamba_ref, inner_ref, growth_ref, fall_ref, gy_ref, gcum_ref, parts_ref,
):
    length, channels = v_ref.shape
    heads = cum_ref.shape[0]
    width = channels // heads
    cumulative = cum_ref[...]
    growth_three = rows_of_three(jnp.exp(cumulative))
    fall_three = rows_of_three(jnp.exp(cumulative[:, -1:] - cumulative))
    skip_column = to_column(skip_ref[...])
    grad_cum = jnp.zeros((heads, length), F32)
    skip_part = jnp.zeros((heads, 1), F32)
    for first in range(0, channels, LANES):
        here = pl.ds(first, LANES)
        wide, sigmoid, grad_y = gate_parts(gate_ref[:, here], go_ref[:, here])
        vals = v_ref[:, here].astype(F32)
        skip = channel_row(skip_column, heads, width, first)
        growth_ref[:, here] = spread(growth_three, first, LANES, width)
        fall_ref[:, here] = spread(fall_three, first, LANES, width)
        gy_ref[:, here] = grad_y
        coef_ref[:, here] = go_ref[:, here].astype(F32) * sigmoid * (1.0 + wide * (1.0 - sigmoid))
        intra = intra_ref[:, here]
        inner = in_inner_ref[:, here]
        mamba_ref[:, here] = intra + skip * vals
        inner_ref[:, here] = inner + skip * grad_y
        high, low = split(grad_y.astype(BF16).astype(F32) * intra - vals * inner, 2)
        head_rows = jnp.where(head_map(heads, width, first, LANES), 1.0, 0.0).astype(BF16)
        grad_cum = grad_cum + mm_nt(head_rows, high) + mm_nt(head_rows, low)
        skip_row = jnp.sum(grad_y * vals, axis=0, keepdims=True)
        skip_part = skip_part + head_column(skip_row, heads, width, first)
    gcum_ref[...] = grad_cum
    rate_part = jnp.sum(grad_cum * cumulative, axis=1, keepdims=True)
    parts_ref[...] = jnp.concatenate([to_row(rate_part), to_row(skip_part)], axis=0)


def pick(size, first, second, last):
    if size == 1:
        return jnp.zeros_like(first), jnp.zeros_like(first)
    if size % 2:
        return first, second
    index = lax.axis_index("seq")
    lower = index < size // 2
    edge = jnp.logical_or(index == 0, index == size - 1)
    first = jnp.where(edge, 0.0, first)
    second = jnp.where(edge, last, second)
    return jnp.where(lower, first, second), jnp.where(lower, second, first)


def picked(size, states, here):
    both = [pick(size, *(ref[:, here] for ref in state)) for state in states]
    return jnp.concatenate([x[0] for x in both], axis=0), jnp.concatenate([x[1] for x in both], axis=0)


def rate_kernel(size, pieces, start, heads, final, *refs):
    states, refs = [refs[3 * i : 3 * i + 3] for i in range(pieces)], refs[3 * pieces :]
    q_ref, r_ref, slope_ref, row_ref, parts_ref, out_ref = *refs[:5], refs[-1]
    rows, channels = pieces * states[0][0].shape[0], q_ref.shape[1]
    here = slice(start, start + rows)
    rate_part = jnp.zeros((heads, 1), F32)
    for begin in range(0, channels, LANES):
        lanes = pl.ds(begin, LANES)
        entering, after = picked(size, states, lanes)
        terms = entering * q_ref[here, lanes] + after * (
            r_ref[here, lanes] + slope_ref[:, lanes] * entering
        )
        row = row_ref[:, lanes] + jnp.sum(terms, axis=0, keepdims=True)
        if final:
            rate_part = rate_part + head_column(row, heads, channels // heads, begin)
        else:
            out_ref[:, lanes] = row
    if final:
        base = parts_ref[...]
        out_ref[...] = jnp.concatenate([base[:1] + to_row(rate_part), base[1:]], axis=0)


def share_kernel(size, pieces, start, *refs):
    states, refs = [refs[3 * i : 3 * i + 3] for i in range(pieces)], refs[3 * pieces :]
    high_ref, low_ref, scaled_ref, sum_b_ref, sum_c_ref = refs[:5]
    rows, channels = pieces * states[0][0].shape[0], scaled_ref.shape[1]
    here = slice(start, start + rows)
    grad_b = sum_b_ref[:, here]
    grad_c = sum_c_ref[:, here]
    for begin in range(0, channels, LANES):
        lanes = pl.ds(begin, LANES)
        entering, after = picked(size, states, lanes)
        enter_high, enter_low = split(entering, 2)
        after_high, after_low = split(after, 2)
        high, low, scaled = high_ref[:, lanes], low_ref[:, lanes], scaled_ref[:, lanes]
        grad_c = grad_c + mm_nt(high, enter_high) + (mm_nt(high, enter_low) + mm_nt(low, enter_high))
        grad_b = grad_b + mm_nt(scaled, after_high) + mm_nt(scaled, after_low)
    refs[-1][...] = jnp.concatenate([grad_b, grad_c], axis=1)


def rest_kernel(size, pieces, *refs):
    states, refs = [refs[3 * i : 3 * i + 3] for i in range(pieces)], refs[3 * pieces :]
    (
        v_ref, b_ref, c_ref, coef_ref, mamba_ref, inner_ref, growth_ref, fall_ref, gy_ref,
        gcum_ref, decay_ref, neg_ref, _, gv_ref, gg_ref, gs_ref, total_ref,
    ) = refs
    length, channels = v_ref.shape
    heads = gcum_ref.shape[0]
    width = channels // heads
    block_b, block_c = b_ref[...], c_ref[...]
    grad_cum = gcum_ref[...]
    grad_total = jnp.zeros((heads, 1), F32)
    for first in range(0, channels, LANES):
        here = pl.ds(first, LANES)
        entering, after = picked(size, states, here)
        enter_high, enter_low = split(entering, 2)
        after_high, after_low = split(after, 2)
        inter = growth_ref[:, here] * (mm(block_c, enter_high) + mm(block_c, enter_low))
        outer = fall_ref[:, here] * (mm(block_b, after_high) + mm(block_b, after_low))
        gg_ref[0, :, here] = (coef_ref[:, here] * (mamba_ref[:, here] + inter)).astype(BF16)
        gv_ref[0, :, here] = (inner_ref[:, here] + outer).astype(BF16)
        pulled = v_ref[:, here].astype(F32) * outer
        high, low = split(gy_ref[:, here] * inter - pulled, 2)
        head_rows = jnp.where(head_map(heads, width, first, LANES), 1.0, 0.0).astype(BF16)
        grad_cum = grad_cum + mm_nt(head_rows, high) + mm_nt(head_rows, low)
        total_row = jnp.sum(pulled, axis=0, keepdims=True) + decay_ref[:, here] * jnp.sum(
            after * entering, axis=0, keepdims=True
        )
        grad_total = grad_total + head_column(total_row, heads, width, first)
    gs_ref[0] = neg_ref[...] * (scan_tokens(grad_cum, True) + grad_total)
    total_ref[...] = to_row(grad_total)


def tree(values):
    while len(values) > 1:
        values = [sum(values[i + 1 : i + 2], values[i]) for i in range(0, len(values), 2)]
    return values[0]


def add_kernel(x_ref, y_ref, *refs):
    refs[-1][...] = x_ref[...] + y_ref[...]


def last_kernel(counts, *refs):
    refs, (gb_ref, gc_ref, rate_ref, skip_ref) = refs[:-4], refs[-4:]
    sums = []
    for count in counts:
        sums.append(tree([ref[...] for ref in refs[:count]]))
        refs = refs[count:]
    *shares, small = sums
    start = 0
    for both in shares:
        rows = both.shape[1] // 2
        gb_ref[0, :, start : start + rows] = both[:, :rows]
        gc_ref[0, :, start : start + rows] = both[:, rows:]
        start += rows
    rate_ref[...] = small[:1]
    skip_ref[...] = small[1:]


def call(kernel, outs, scratch=(), flops=0, space=pltpu.VMEM, after=()):
    def run(*args):
        if space == pltpu.HBM:
            args = [pltpu.with_memory_space_constraint(a, space) for a in args]
        specs = [pl.BlockSpec(memory_space=space)] * len(args)
        specs += [pl.BlockSpec(memory_space=pl.ANY)] * len(after)
        args = (*args, *after)
        size = sum(a.size * a.dtype.itemsize for a in (*args, *outs))
        return pl.pallas_call(
            kernel,
            out_shape=tuple(outs),
            in_specs=specs,
            out_specs=tuple(pl.BlockSpec(memory_space=pltpu.VMEM) for _ in outs),
            scratch_shapes=list(scratch),
            compiler_params=pltpu.CompilerParams(vmem_limit_bytes=VMEM_LIMIT),
            cost_estimate=pl.CostEstimate(flops=flops, bytes_accessed=size, transcendentals=0),
        )(*args)

    return run


def swap(x, axis, size, bit):
    return lax.ppermute(x, axis, [(i, i ^ bit) for i in range(size)])


def hop(x, sizes, step):
    size, copies = sizes["seq"], sizes["replica"]
    pairs = []
    for copy in range(copies):
        for place in range(size):
            to = (copy ^ 1 if copies % 2 == 0 else copy, place)
            for low in (step, size - 2 - step):
                if place in (low, low + 1):
                    to = (copy, 2 * low + 1 - place)
            pairs.append((copy * size + place, to[0] * size + to[1]))
    return lax.ppermute(x, ("replica", "seq"), pairs)


def pass_kernel(*refs):
    got_ref, base_ref, decay_ref = refs[:3]
    refs[-1][...] = decay_ref[...] * got_ref[...] + base_ref[...]


def pass_on(got, base, decay, after):
    return call(pass_kernel, [jax.ShapeDtypeStruct(base.shape, F32)], flops=2 * base.size, after=after)(
        got, base, decay
    )[0]


def chain(sizes, mine, other, decay, work):
    chunks = len(mine)
    size = sizes["seq"]
    if size == 1:
        for k in sorted(work):
            work[k](())
        return [(x, x, x) for x in mine]
    if size % 2:
        raise NotImplementedError
    index = lax.axis_index("seq")
    place = jnp.minimum(index, size - 1 - index)
    middle = size // 2 - 1
    got = {(0, c): hop(mine[c], sizes, 0) for c in range(chunks)}
    steps = [
        (at + c + (LAG if at > middle else 0), at, c) for at in range(1, size - 1) for c in range(chunks)
    ]
    token = ()
    for count, (_, at, c) in enumerate(sorted(steps)):
        if count in work:
            token = work[count](token)
        if at > middle and c > 2:
            token = (*token, got[at, c - 3])
        base = mine[c] if at <= middle else other[c]
        pay = pass_on(got[at - 1, c], base, decay, token)
        got[at, c] = hop(pay, sizes, at)
        token = (pay,)
    for k in sorted(work):
        if k >= len(steps):
            token = work[k](token)
    states = []
    for c in range(chunks):
        first, second, last = got[0, c], got[middle, c], got[size - 2, c]
        for at in range(1, middle):
            first = jnp.where(place == at + 1, got[at, c], first)
        for at in range(middle + 1, size - 2):
            second = jnp.where(place == size - 2 - at, got[at, c], second)
        states.append((first, second, last))
    return states


def sum_terms(x, axis, size):
    if size == 1:
        return [x]
    if size == 4:
        return [x] + [swap(x, axis, size, bit) for bit in (1, 2, 3)]
    if size & (size - 1):
        return [lax.psum(x, axis)]
    bit = 1
    while 2 * bit < size:
        x = x + swap(x, axis, size, bit)
        bit *= 2
    return [x, swap(x, axis, size, bit)]


def small_terms(x, axes, sizes, between):
    bits = [(axis, 1 << k) for axis in axes for k in range(sizes[axis].bit_length() - 1)]
    if any(sizes[axis] & (sizes[axis] - 1) for axis in axes):
        x = lax.psum(x, tuple(axes))
        between((x,))
        return [x]
    after = ()
    for count, (axis, bit) in enumerate(bits):
        theirs = swap(x, axis, sizes[axis], bit)
        if count == len(bits) - 1:
            break
        x = call(add_kernel, [jax.ShapeDtypeStruct(x.shape, F32)], after=after)(x, theirs)[0]
        after = between((x,)) if count == 0 else ()
    if len(bits) < 2:
        between((x,))
    return [x, theirs] if bits else [x]


def shards(sizes, values, gate_in, in_b, in_c, step_sizes, log_rates, skip_gain, grad_out):
    like = jax.ShapeDtypeStruct
    length, channels = values.shape[1:]
    heads = step_sizes.shape[1]
    state = in_b.shape[2]
    seq = sizes["seq"]
    rows = state // CHUNKS
    wide = like((length, channels), F32)
    wide_b = like((length, channels), BF16)
    share = like((length, state), F32)
    small = like((heads, length), F32)
    row = like((1, channels), F32)
    piece = like((rows, channels), F32)
    maps = like((length, state), BF16)

    out = call(
        functools.partial(states_kernel, CHUNKS, seq),
        [wide_b, wide_b, wide_b, maps, maps, small, small, row, row, like((1, heads), F32)]
        + [piece] * (2 * CHUNKS),
        [
            pltpu.VMEM((heads, length), F32),
            pltpu.VMEM((1, heads), F32),
            pltpu.SemaphoreType.DMA((8,)),
        ],
        flops=8 * length * channels * state,
        space=pltpu.HBM,
    )(
        values[0], gate_in[0], grad_out[0], in_b[0], in_c[0], step_sizes[0],
        log_rates.reshape(1, heads), skip_gain.reshape(1, heads),
    )
    vals, gate, grad, block_b, block_c, cumulative, negative, decay, slope, skip = out[:10]
    mine, other = out[10 : 10 + CHUNKS], out[10 + CHUNKS :]

    made = {}

    def intra(after):
        made["intra"] = call(
            intra_kernel,
            [wide, wide, share, share],
            [
                pltpu.VMEM((channels, length), BF16),
                pltpu.VMEM((channels, length), F32),
                pltpu.VMEM((length, length), F32),
            ],
            flops=16 * length * length * channels,
        )(vals, gate, grad, block_b, block_c, cumulative)
        return (made["intra"][2],)

    def factors(after):
        made["factors"] = call(
            factors_kernel,
            [wide_b] * 3 + [like((state, channels), F32)] * 2,
            flops=8 * length * state * channels,
        )(vals, gate, grad, block_b, block_c, cumulative, *(after if after else made["intra"][2:3]))
        return (made["factors"][-1],)

    def prepare(after):
        made["prepare"] = call(
            prepare_kernel,
            [wide] * 6 + [small, like((2, heads), F32)],
            flops=8 * length * state * channels,
        )(
            vals, gate, grad, cumulative, skip,
            *made["intra"][:2], *(after if after else made["intra"][2:3]),
        )
        return (made["prepare"][-1],)

    last_middle = (max(seq // 2 - 1, 1) - 1) * CHUNKS + CHUNKS
    states = chain(sizes, mine, other, decay, {0: intra, 1: factors, last_middle + LAG: prepare})
    sum_b, sum_c = made["intra"][2:]
    high, low, scaled, q, r = made["factors"]
    coef, mamba, inner, growth, fall, grad_y, grad_cum, parts = made["prepare"]

    rate_row = jnp.zeros((1, channels), F32)
    terms, counts = [], []
    for i in range(PARTS):
        final = i == PARTS - 1
        count = CHUNKS // PARTS
        own = [x for group in states[i * count : (i + 1) * count] for x in group]
        rate_row = call(
            functools.partial(rate_kernel, seq, count, i * rows * count, heads, final),
            [like((2, heads), F32) if final else row],
        )(*own, q, r, slope, rate_row, parts)[0]
        share_of = call(
            functools.partial(share_kernel, seq, count, i * rows * count),
            [like((length, 2 * rows * count), F32)],
            flops=10 * length * channels * rows * count,
            after=(rate_row,),
        )(*own, high, low, scaled, sum_b, sum_c)[0]
        own = sum_terms(share_of, "tensor", sizes["tensor"])
        terms += own
        counts.append(len(own))

    def rest(after):
        made["rest"] = call(
            functools.partial(rest_kernel, seq, CHUNKS),
            [like((1, length, channels), BF16)] * 2
            + [like((1, heads, length), F32), like((1, heads), F32)],
            flops=10 * length * channels * state,
            after=after,
        )(
            *(x for group in states for x in group),
            vals, block_b, block_c, coef, mamba, inner, growth, fall, grad_y, grad_cum, decay, negative,
        )
        return (made["rest"][3],)

    own = small_terms(rate_row, ("replica", "seq"), sizes, rest)
    terms += own
    counts.append(len(own))
    grad_values, grad_gate, grad_steps, _ = made["rest"]
    grad_b, grad_c, rate_sum, skip_sum = call(
        functools.partial(last_kernel, tuple(counts)),
        [like((1, length, state), F32)] * 2 + [like((1, heads), F32)] * 2,
    )(*terms)
    return (
        grad_values,
        grad_gate,
        grad_b,
        grad_c,
        grad_steps,
        rate_sum.reshape(heads),
        skip_sum.reshape(heads),
    )


def solution(mesh):
    in_specs = (
        P("replica", "seq", "tensor"),
        P("replica", "seq", "tensor"),
        P("replica", "seq", None),
        P("replica", "seq", None),
        P("replica", "tensor", "seq"),
        P("tensor"),
        P("tensor"),
        P("replica", "seq", "tensor"),
    )
    out_specs = (
        P("replica", "seq", "tensor"),
        P("replica", "seq", "tensor"),
        P("replica", "seq", None),
        P("replica", "seq", None),
        P("replica", "tensor", "seq"),
        P("tensor"),
        P("tensor"),
    )
    body = functools.partial(shards, dict(mesh.shape))
    return jax.shard_map(body, mesh=mesh, in_specs=in_specs, out_specs=out_specs, check_vma=False)
```

```python
import functools

import jax
import jax.numpy as jnp
from jax import lax
from jax.experimental import pallas as pl
from jax.experimental.pallas import tpu as pltpu
from jax.sharding import PartitionSpec as P

F32 = jnp.float32
BF16 = jnp.bfloat16
VMEM_LIMIT = 24 * 1024 * 1024
LANES = 256
CHUNKS = 4
PARTS = 2
LAG = 1


def split(x, parts):
    terms = []
    for _ in range(parts - 1):
        term = x.astype(BF16)
        terms.append(term)
        x = x - term.astype(F32)
    terms.append(x.astype(BF16))
    return terms


def mm(a, b):
    return lax.dot_general(a, b, (((1,), (0,)), ((), ())), preferred_element_type=F32)


def mm_nt(a, b):
    return lax.dot_general(a, b, (((1,), (1,)), ((), ())), preferred_element_type=F32)


def mm_tn(a, b):
    return lax.dot_general(a, b, (((0,), (0,)), ((), ())), preferred_element_type=F32)


def iota(shape, dim):
    return lax.broadcasted_iota(jnp.int32, shape, dim)


def to_column(row):
    n = row.shape[1]
    eye = iota((n, n), 0) == iota((n, n), 1)
    return jnp.sum(jnp.where(eye, row, 0.0), axis=1, keepdims=True)


def to_row(column):
    n = column.shape[0]
    eye = iota((n, n), 0) == iota((n, n), 1)
    return jnp.sum(jnp.where(eye, column, 0.0), axis=0, keepdims=True)


def head_map(heads, width, first, lanes):
    low = iota((heads, lanes), 0) * width
    channel = iota((heads, lanes), 1) + first
    return (channel >= low) & (channel < low + width)


def spread_map(heads, width, first, lanes):
    one = jnp.where(head_map(heads, width, first, lanes), 1.0, 0.0).astype(BF16)
    return jnp.concatenate([one, one, one], axis=0)


def rows_of_three(per_head):
    return jnp.concatenate(split(per_head, 3), axis=0)


def spread(three, first, lanes, width):
    heads = three.shape[0] // 3
    return mm_tn(three, spread_map(heads, width, first, lanes))


def scan_tokens(per_head, backward):
    heads, length = per_head.shape
    source = iota((length, length), 0)
    target = iota((length, length), 1)
    keep = source >= target if backward else source <= target
    sums = mm(rows_of_three(per_head), jnp.where(keep, 1.0, 0.0).astype(BF16))
    return sums[:heads] + sums[heads : 2 * heads] + sums[2 * heads :]


def channel_row(column, heads, width, first):
    mine = head_map(heads, width, first, LANES)
    return jnp.sum(jnp.where(mine, column, 0.0), axis=0, keepdims=True)


def head_column(row, heads, width, first):
    mine = head_map(heads, width, first, LANES)
    return jnp.sum(jnp.where(mine, row, 0.0), axis=1, keepdims=True)


def gate_parts(gate, grad):
    wide = gate.astype(F32)
    sigmoid = 1.0 / (1.0 + jnp.exp(-wide))
    return wide, sigmoid, grad.astype(F32) * (wide * sigmoid)


def states_kernel(chunks, size, *refs):
    sources, outs, (steps_ref, lr_ref, sems) = refs[:8], refs[8:-3], refs[-3:]
    v_ref, gate_ref, go_ref, b_ref, c_ref = outs[:5]
    cum_ref, neg_ref, decay_ref, slope_ref, skip_ref = outs[5:10]
    mine_refs, other_refs = outs[10 : 10 + chunks], outs[10 + chunks :]
    targets = (v_ref, gate_ref, go_ref, b_ref, c_ref, steps_ref, lr_ref, skip_ref)
    copies = [
        pltpu.make_async_copy(source, target, sems.at[i])
        for i, (source, target) in enumerate(zip(sources, targets))
    ]
    for i in (6, 5, 3, 4, 0, 1, 2, 7):
        copies[i].start()
    copies[6].wait()
    copies[5].wait()
    length, channels = v_ref.shape
    heads = steps_ref.shape[0]
    width = channels // heads
    lower = lax.axis_index("seq") < size // 2 if size > 1 else True
    rates = jnp.exp(to_column(lr_ref[...]))
    cumulative = scan_tokens(-rates * steps_ref[...], False)
    total = cumulative[:, -1:]
    decay = jnp.exp(total)
    cum_ref[...] = cumulative
    neg_ref[...] = jnp.broadcast_to(-rates, (heads, length))
    growth = rows_of_three(jnp.exp(cumulative))
    fall = rows_of_three(jnp.exp(total - cumulative))
    copies[3].wait()
    copies[4].wait()
    b_t = b_ref[...].astype(F32).T.astype(BF16)
    c_t = c_ref[...].astype(F32).T.astype(BF16)
    for i in (0, 1, 2, 7):
        copies[i].wait()
    rows = b_t.shape[0] // chunks
    for first in range(0, channels, LANES):
        here = pl.ds(first, LANES)
        _, _, grad_y = gate_parts(gate_ref[:, here], go_ref[:, here])
        high, low = split(spread(growth, first, LANES, width) * grad_y, 2)
        pulled = mm(c_t, high) + mm(c_t, low)
        scaled = (spread(fall, first, LANES, width) * v_ref[:, here].astype(F32)).astype(BF16)
        local = mm(b_t, scaled)
        mine = jnp.where(lower, local, pulled)
        other = jnp.where(lower, pulled, local)
        for i in range(chunks):
            mine_refs[i][:, here] = mine[i * rows : (i + 1) * rows]
            other_refs[i][:, here] = other[i * rows : (i + 1) * rows]
        decay_ref[:, here] = channel_row(decay, heads, width, first)
        slope_ref[:, here] = channel_row(total * decay, heads, width, first)


def intra_kernel(
    v_ref, gate_ref, go_ref, b_ref, c_ref, cum_ref,
    intra_ref, inner_ref, sum_b_ref, sum_c_ref, grad_t_ref, inner_t_ref, acc_ref,
):
    length, channels = v_ref.shape
    heads = cum_ref.shape[0]
    width = channels // heads
    half = length // 2
    pair = 2 * width
    cumulative = cum_ref[...]
    columns = cumulative.T
    scores = mm_nt(c_ref[...], b_ref[...])
    causal = iota((half, half), 0) >= iota((half, half), 1)
    left = iota((1, pair), 1) < width
    acc_ref[...] = jnp.zeros_like(acc_ref)

    def blocks(x):
        return x[:half, :half], x[half:, :half], x[half:, half:]

    scores_00, scores_10, scores_11 = blocks(scores)
    for first in range(0, channels, pair):
        here = pl.ds(first, pair)
        _, _, grad_y = gate_parts(gate_ref[:, here], go_ref[:, here])
        grad_t_ref[here, :] = grad_y.T.astype(BF16)
        vals = v_ref[:, here]
        pieces = []
        for side in range(2):
            head = first // width + side
            own = left if side == 0 else jnp.logical_not(left)
            row = cumulative[head : head + 1, :]
            column = columns[:, head : head + 1]
            row_0, row_1 = row[:, :half], row[:, half:]
            column_0, column_1 = column[:half], column[half:]
            decay_00 = jnp.exp(jnp.where(causal, column_0 - row_0, -1e30))
            decay_10 = jnp.exp(column_1 - row_0)
            decay_11 = jnp.exp(jnp.where(causal, column_1 - row_1, -1e30))
            mix_00 = (scores_00 * decay_00).astype(BF16)
            mix_10 = (scores_10 * decay_10).astype(BF16)
            mix_11 = (scores_11 * decay_11).astype(BF16)
            low_rows = jnp.concatenate([mix_10, mix_11], axis=1)
            pieces.append((mm(mix_00, vals[:half]), mm(low_rows, vals)))
            head_grad = jnp.where(own, grad_y, 0.0).astype(BF16)
            mixed_0 = mm_nt(head_grad[:half], vals[:half])
            mixed_1 = mm_nt(head_grad[half:], vals)
            acc_ref[:half, :half] += mixed_0 * decay_00
            acc_ref[half:, :half] += mixed_1[:, :half] * decay_10
            acc_ref[half:, half:] += mixed_1[:, half:] * decay_11
            mine = pl.ds(first + side * width, width)
            grad_t = grad_t_ref[mine, :]
            inner_t_ref[mine, :half] = mm(grad_t[:, :half], mix_00) + mm(grad_t[:, half:], mix_10)
            inner_t_ref[mine, half:] = mm(grad_t[:, half:], mix_11)
        intra_ref[:half, here] = jnp.where(left, pieces[0][0], pieces[1][0])
        intra_ref[half:, here] = jnp.where(left, pieces[0][1], pieces[1][1])
        inner_ref[:, here] = inner_t_ref[here, :].T
    shares = acc_ref[...]
    high, low = split(shares, 2)
    sum_c_ref[...] = mm(high, b_ref[...]) + mm(low, b_ref[...])
    high, low = split(shares.T, 2)
    sum_b_ref[...] = mm(high, c_ref[...]) + mm(low, c_ref[...])


def factors_kernel(
    v_ref, gate_ref, go_ref, b_ref, c_ref, cum_ref, after_ref,
    high_ref, low_ref, scaled_ref, q_ref, r_ref,
):
    length, channels = v_ref.shape
    heads = cum_ref.shape[0]
    width = channels // heads
    cumulative = cum_ref[...]
    left_over = cumulative[:, -1:] - cumulative
    growth = rows_of_three(jnp.exp(cumulative))
    fall = rows_of_three(jnp.exp(left_over))
    growth_slope = rows_of_three(cumulative * jnp.exp(cumulative))
    fall_slope = rows_of_three(left_over * jnp.exp(left_over))
    b_t = b_ref[...].astype(F32).T.astype(BF16)
    c_t = c_ref[...].astype(F32).T.astype(BF16)
    for first in range(0, channels, LANES):
        here = pl.ds(first, LANES)
        _, _, grad_y = gate_parts(gate_ref[:, here], go_ref[:, here])
        vals = v_ref[:, here].astype(F32)
        high, low = split(spread(growth, first, LANES, width) * grad_y, 2)
        high_ref[:, here] = high
        low_ref[:, here] = low
        scaled_ref[:, here] = (spread(fall, first, LANES, width) * vals).astype(BF16)
        high, low = split(spread(growth_slope, first, LANES, width) * grad_y, 2)
        q_ref[:, here] = mm(c_t, high) + mm(c_t, low)
        high, low = split(spread(fall_slope, first, LANES, width) * vals, 2)
        r_ref[:, here] = mm(b_t, high) + mm(b_t, low)


def prepare_kernel(
    v_ref, gate_ref, go_ref, cum_ref, skip_ref, intra_ref, in_inner_ref, after_ref,
    coef_ref, mamba_ref, inner_ref, growth_ref, fall_ref, gy_ref, gcum_ref, parts_ref,
):
    length, channels = v_ref.shape
    heads = cum_ref.shape[0]
    width = channels // heads
    cumulative = cum_ref[...]
    growth_three = rows_of_three(jnp.exp(cumulative))
    fall_three = rows_of_three(jnp.exp(cumulative[:, -1:] - cumulative))
    skip_column = to_column(skip_ref[...])
    grad_cum = jnp.zeros((heads, length), F32)
    skip_part = jnp.zeros((heads, 1), F32)
    for first in range(0, channels, LANES):
        here = pl.ds(first, LANES)
        wide, sigmoid, grad_y = gate_parts(gate_ref[:, here], go_ref[:, here])
        vals = v_ref[:, here].astype(F32)
        skip = channel_row(skip_column, heads, width, first)
        growth_ref[:, here] = spread(growth_three, first, LANES, width)
        fall_ref[:, here] = spread(fall_three, first, LANES, width)
        gy_ref[:, here] = grad_y
        coef_ref[:, here] = go_ref[:, here].astype(F32) * sigmoid * (1.0 + wide * (1.0 - sigmoid))
        intra = intra_ref[:, here]
        inner = in_inner_ref[:, here]
        mamba_ref[:, here] = intra + skip * vals
        inner_ref[:, here] = inner + skip * grad_y
        high, low = split(grad_y.astype(BF16).astype(F32) * intra - vals * inner, 2)
        head_rows = jnp.where(head_map(heads, width, first, LANES), 1.0, 0.0).astype(BF16)
        grad_cum = grad_cum + mm_nt(head_rows, high) + mm_nt(head_rows, low)
        skip_row = jnp.sum(grad_y * vals, axis=0, keepdims=True)
        skip_part = skip_part + head_column(skip_row, heads, width, first)
    gcum_ref[...] = grad_cum
    rate_part = jnp.sum(grad_cum * cumulative, axis=1, keepdims=True)
    parts_ref[...] = jnp.concatenate([to_row(rate_part), to_row(skip_part)], axis=0)


def pick(size, first, second, last):
    if size == 1:
        return jnp.zeros_like(first), jnp.zeros_like(first)
    if size % 2:
        return first, second
    index = lax.axis_index("seq")
    lower = index < size // 2
    edge = jnp.logical_or(index == 0, index == size - 1)
    first = jnp.where(edge, 0.0, first)
    second = jnp.where(edge, last, second)
    return jnp.where(lower, first, second), jnp.where(lower, second, first)


def picked(size, states, here):
    both = [pick(size, *(ref[:, here] for ref in state)) for state in states]
    return jnp.concatenate([x[0] for x in both], axis=0), jnp.concatenate([x[1] for x in both], axis=0)


def rate_kernel(size, pieces, start, heads, final, *refs):
    states, refs = [refs[3 * i : 3 * i + 3] for i in range(pieces)], refs[3 * pieces :]
    q_ref, r_ref, slope_ref, row_ref, parts_ref, out_ref = *refs[:5], refs[-1]
    rows, channels = pieces * states[0][0].shape[0], q_ref.shape[1]
    here = slice(start, start + rows)
    rate_part = jnp.zeros((heads, 1), F32)
    for begin in range(0, channels, LANES):
        lanes = pl.ds(begin, LANES)
        entering, after = picked(size, states, lanes)
        terms = entering * q_ref[here, lanes] + after * (
            r_ref[here, lanes] + slope_ref[:, lanes] * entering
        )
        row = row_ref[:, lanes] + jnp.sum(terms, axis=0, keepdims=True)
        if final:
            rate_part = rate_part + head_column(row, heads, channels // heads, begin)
        else:
            out_ref[:, lanes] = row
    if final:
        base = parts_ref[...]
        out_ref[...] = jnp.concatenate([base[:1] + to_row(rate_part), base[1:]], axis=0)


def share_kernel(size, pieces, start, *refs):
    states, refs = [refs[3 * i : 3 * i + 3] for i in range(pieces)], refs[3 * pieces :]
    high_ref, low_ref, scaled_ref, sum_b_ref, sum_c_ref = refs[:5]
    rows, channels = pieces * states[0][0].shape[0], scaled_ref.shape[1]
    here = slice(start, start + rows)
    grad_b = sum_b_ref[:, here]
    grad_c = sum_c_ref[:, here]
    for begin in range(0, channels, LANES):
        lanes = pl.ds(begin, LANES)
        entering, after = picked(size, states, lanes)
        enter_high, enter_low = split(entering, 2)
        after_high, after_low = split(after, 2)
        high, low, scaled = high_ref[:, lanes], low_ref[:, lanes], scaled_ref[:, lanes]
        grad_c = grad_c + mm_nt(high, enter_high) + (mm_nt(high, enter_low) + mm_nt(low, enter_high))
        grad_b = grad_b + mm_nt(scaled, after_high) + mm_nt(scaled, after_low)
    refs[-1][...] = jnp.concatenate([grad_b, grad_c], axis=1)


def rest_kernel(size, pieces, *refs):
    states, refs = [refs[3 * i : 3 * i + 3] for i in range(pieces)], refs[3 * pieces :]
    (
        v_ref, b_ref, c_ref, coef_ref, mamba_ref, inner_ref, growth_ref, fall_ref, gy_ref,
        gcum_ref, decay_ref, neg_ref, *_, gv_ref, gg_ref, gs_ref,
    ) = refs
    length, channels = v_ref.shape
    heads = gcum_ref.shape[0]
    width = channels // heads
    block_b, block_c = b_ref[...], c_ref[...]
    grad_cum = gcum_ref[...]
    grad_total = jnp.zeros((heads, 1), F32)
    for first in range(0, channels, LANES):
        here = pl.ds(first, LANES)
        entering, after = picked(size, states, here)
        enter_high, enter_low = split(entering, 2)
        after_high, after_low = split(after, 2)
        inter = growth_ref[:, here] * (mm(block_c, enter_high) + mm(block_c, enter_low))
        outer = fall_ref[:, here] * (mm(block_b, after_high) + mm(block_b, after_low))
        gg_ref[0, :, here] = (coef_ref[:, here] * (mamba_ref[:, here] + inter)).astype(BF16)
        gv_ref[0, :, here] = (inner_ref[:, here] + outer).astype(BF16)
        pulled = v_ref[:, here].astype(F32) * outer
        high, low = split(gy_ref[:, here] * inter - pulled, 2)
        head_rows = jnp.where(head_map(heads, width, first, LANES), 1.0, 0.0).astype(BF16)
        grad_cum = grad_cum + mm_nt(head_rows, high) + mm_nt(head_rows, low)
        total_row = jnp.sum(pulled, axis=0, keepdims=True) + decay_ref[:, here] * jnp.sum(
            after * entering, axis=0, keepdims=True
        )
        grad_total = grad_total + head_column(total_row, heads, width, first)
    gs_ref[0] = neg_ref[...] * (scan_tokens(grad_cum, True) + grad_total)


def tree(values):
    while len(values) > 1:
        values = [sum(values[i + 1 : i + 2], values[i]) for i in range(0, len(values), 2)]
    return values[0]


def add_kernel(x_ref, y_ref, *refs):
    refs[-1][...] = x_ref[...] + y_ref[...]


def sum_kernel(*refs):
    refs[-1][...] = tree([ref[...] for ref in refs[:-1]])


def last_kernel(counts, *refs):
    refs, (gb_ref, gc_ref, rate_ref, skip_ref) = refs[:-4], refs[-4:]
    sums = []
    for count in counts:
        sums.append(tree([ref[...] for ref in refs[:count]]))
        refs = refs[count:]
    *shares, small = sums
    start = 0
    for both in shares:
        rows = both.shape[1] // 2
        gb_ref[0, :, start : start + rows] = both[:, :rows]
        gc_ref[0, :, start : start + rows] = both[:, rows:]
        start += rows
    rate_ref[...] = small[:1]
    skip_ref[...] = small[1:]


def call(kernel, outs, scratch=(), flops=0, space=pltpu.VMEM, after=()):
    def run(*args):
        if space == pltpu.HBM:
            args = [pltpu.with_memory_space_constraint(a, space) for a in args]
        specs = [pl.BlockSpec(memory_space=space)] * len(args)
        specs += [pl.BlockSpec(memory_space=pl.ANY)] * len(after)
        args = (*args, *after)
        size = sum(a.size * a.dtype.itemsize for a in (*args, *outs))
        return pl.pallas_call(
            kernel,
            out_shape=tuple(outs),
            in_specs=specs,
            out_specs=tuple(pl.BlockSpec(memory_space=pltpu.VMEM) for _ in outs),
            scratch_shapes=list(scratch),
            compiler_params=pltpu.CompilerParams(vmem_limit_bytes=VMEM_LIMIT),
            cost_estimate=pl.CostEstimate(flops=flops, bytes_accessed=size, transcendentals=0),
        )(*args)

    return run


def swap(x, axis, size, bit):
    return lax.ppermute(x, axis, [(i, i ^ bit) for i in range(size)])


def hop(x, sizes, step):
    size, copies = sizes["seq"], sizes["replica"]
    pairs = []
    for copy in range(copies):
        for place in range(size):
            to = (copy ^ 1 if copies % 2 == 0 else copy, place)
            for low in (step, size - 2 - step):
                if place in (low, low + 1):
                    to = (copy, 2 * low + 1 - place)
            pairs.append((copy * size + place, to[0] * size + to[1]))
    return lax.ppermute(x, ("replica", "seq"), pairs)


def pass_kernel(*refs):
    got_ref, base_ref, decay_ref = refs[:3]
    refs[-1][...] = decay_ref[...] * got_ref[...] + base_ref[...]


def pass_on(got, base, decay, after):
    return call(pass_kernel, [jax.ShapeDtypeStruct(base.shape, F32)], flops=2 * base.size, after=after)(
        got, base, decay
    )[0]


def chain(sizes, mine, other, decay, work):
    chunks = len(mine)
    size = sizes["seq"]
    if size == 1:
        for k in sorted(work):
            work[k](())
        return [(x, x, x) for x in mine]
    if size % 2:
        raise NotImplementedError
    index = lax.axis_index("seq")
    place = jnp.minimum(index, size - 1 - index)
    middle = size // 2 - 1
    got = {(0, c): hop(mine[c], sizes, 0) for c in range(chunks)}
    steps = [
        (at + c + (LAG if at > middle else 0), at, c) for at in range(1, size - 1) for c in range(chunks)
    ]
    token = ()
    for count, (_, at, c) in enumerate(sorted(steps)):
        if count in work:
            token = work[count](token)
        if at > middle and c > 2:
            token = (*token, got[at, c - 3])
        base = mine[c] if at <= middle else other[c]
        pay = pass_on(got[at - 1, c], base, decay, token)
        got[at, c] = hop(pay, sizes, at)
        token = (pay,)
    for k in sorted(work):
        if k >= len(steps):
            token = work[k](token)
    states = []
    for c in range(chunks):
        first, second, last = got[0, c], got[middle, c], got[size - 2, c]
        for at in range(1, middle):
            first = jnp.where(place == at + 1, got[at, c], first)
        for at in range(middle + 1, size - 2):
            second = jnp.where(place == size - 2 - at, got[at, c], second)
        states.append((first, second, last))
    return states


def sum_terms(x, axis, size):
    if size == 1:
        return [x]
    if size == 4:
        return [x] + [swap(x, axis, size, bit) for bit in (1, 2, 3)]
    if size & (size - 1):
        return [lax.psum(x, axis)]
    bit = 1
    while 2 * bit < size:
        x = x + swap(x, axis, size, bit)
        bit *= 2
    return [x, swap(x, axis, size, bit)]


def small_terms(x, axes, sizes, between):
    bits = [(axis, 1 << k) for axis in axes for k in range(sizes[axis].bit_length() - 1)]
    if any(sizes[axis] & (sizes[axis] - 1) for axis in axes):
        x = lax.psum(x, tuple(axes))
        between((x,))
        return [x]
    for count, (axis, bit) in enumerate(bits):
        theirs = swap(x, axis, sizes[axis], bit)
        if count == len(bits) - 1:
            break
        x = call(add_kernel, [jax.ShapeDtypeStruct(x.shape, F32)])(x, theirs)[0]
    between((x,))
    return [x, theirs] if bits else [x]


def shards(sizes, values, gate_in, in_b, in_c, step_sizes, log_rates, skip_gain, grad_out):
    like = jax.ShapeDtypeStruct
    length, channels = values.shape[1:]
    heads = step_sizes.shape[1]
    state = in_b.shape[2]
    seq = sizes["seq"]
    rows = state // CHUNKS
    wide = like((length, channels), F32)
    wide_b = like((length, channels), BF16)
    share = like((length, state), F32)
    small = like((heads, length), F32)
    row = like((1, channels), F32)
    piece = like((rows, channels), F32)
    maps = like((length, state), BF16)

    out = call(
        functools.partial(states_kernel, CHUNKS, seq),
        [wide_b, wide_b, wide_b, maps, maps, small, small, row, row, like((1, heads), F32)]
        + [piece] * (2 * CHUNKS),
        [
            pltpu.VMEM((heads, length), F32),
            pltpu.VMEM((1, heads), F32),
            pltpu.SemaphoreType.DMA((8,)),
        ],
        flops=8 * length * channels * state,
        space=pltpu.HBM,
    )(
        values[0], gate_in[0], grad_out[0], in_b[0], in_c[0], step_sizes[0],
        log_rates.reshape(1, heads), skip_gain.reshape(1, heads),
    )
    vals, gate, grad, block_b, block_c, cumulative, negative, decay, slope, skip = out[:10]
    mine, other = out[10 : 10 + CHUNKS], out[10 + CHUNKS :]

    made = {}

    def intra(after):
        made["intra"] = call(
            intra_kernel,
            [wide, wide, share, share],
            [
                pltpu.VMEM((channels, length), BF16),
                pltpu.VMEM((channels, length), F32),
                pltpu.VMEM((length, length), F32),
            ],
            flops=16 * length * length * channels,
        )(vals, gate, grad, block_b, block_c, cumulative)
        return (made["intra"][2],)

    def factors(after):
        made["factors"] = call(
            factors_kernel,
            [wide_b] * 3 + [like((state, channels), F32)] * 2,
            flops=8 * length * state * channels,
        )(vals, gate, grad, block_b, block_c, cumulative, *(after if after else made["intra"][2:3]))
        return (made["factors"][-1],)

    def prepare(after):
        made["prepare"] = call(
            prepare_kernel,
            [wide] * 6 + [small, like((2, heads), F32)],
            flops=8 * length * state * channels,
        )(
            vals, gate, grad, cumulative, skip,
            *made["intra"][:2], *(after if after else made["intra"][2:3]),
        )
        return (made["prepare"][-1],)

    last_middle = (max(seq // 2 - 1, 1) - 1) * CHUNKS + CHUNKS
    states = chain(sizes, mine, other, decay, {0: intra, 1: factors, last_middle + LAG: prepare})
    sum_b, sum_c = made["intra"][2:]
    high, low, scaled, q, r = made["factors"]
    coef, mamba, inner, growth, fall, grad_y, grad_cum, parts = made["prepare"]

    rate_row = jnp.zeros((1, channels), F32)
    terms, counts, done = [], [], []
    for i in range(PARTS):
        final = i == PARTS - 1
        count = CHUNKS // PARTS
        own = [x for group in states[i * count : (i + 1) * count] for x in group]
        rate_row = call(
            functools.partial(rate_kernel, seq, count, i * rows * count, heads, final),
            [like((2, heads), F32) if final else row],
        )(*own, q, r, slope, rate_row, parts)[0]
        share_of = call(
            functools.partial(share_kernel, seq, count, i * rows * count),
            [like((length, 2 * rows * count), F32)],
            flops=10 * length * channels * rows * count,
            after=(rate_row,),
        )(*own, high, low, scaled, sum_b, sum_c)[0]
        own = sum_terms(share_of, "tensor", sizes["tensor"])
        if not final:
            own = [call(sum_kernel, [like(share_of.shape, F32)])(*own)[0]]
            done += own
        terms += own
        counts.append(len(own))

    def rest(after):
        made["rest"] = call(
            functools.partial(rest_kernel, seq, CHUNKS),
            [like((1, length, channels), BF16)] * 2 + [like((1, heads, length), F32)],
            flops=10 * length * channels * state,
            after=(*after, *done),
        )(
            *(x for group in states for x in group),
            vals, block_b, block_c, coef, mamba, inner, growth, fall, grad_y, grad_cum, decay, negative,
        )

    own = small_terms(rate_row, ("replica", "seq"), sizes, rest)
    terms += own
    counts.append(len(own))
    grad_values, grad_gate, grad_steps = made["rest"]
    grad_b, grad_c, rate_sum, skip_sum = call(
        functools.partial(last_kernel, tuple(counts)),
        [like((1, length, state), F32)] * 2 + [like((1, heads), F32)] * 2,
    )(*terms)
    return (
        grad_values,
        grad_gate,
        grad_b,
        grad_c,
        grad_steps,
        rate_sum.reshape(heads),
        skip_sum.reshape(heads),
    )


def solution(mesh):
    in_specs = (
        P("replica", "seq", "tensor"),
        P("replica", "seq", "tensor"),
        P("replica", "seq", None),
        P("replica", "seq", None),
        P("replica", "tensor", "seq"),
        P("tensor"),
        P("tensor"),
        P("replica", "seq", "tensor"),
    )
    out_specs = (
        P("replica", "seq", "tensor"),
        P("replica", "seq", "tensor"),
        P("replica", "seq", None),
        P("replica", "seq", None),
        P("replica", "tensor", "seq"),
        P("tensor"),
        P("tensor"),
    )
    body = functools.partial(shards, dict(mesh.shape))
    return jax.shard_map(body, mesh=mesh, in_specs=in_specs, out_specs=out_specs, check_vma=False)
```

```python
import functools

import jax
import jax.numpy as jnp
from jax import lax
from jax.experimental import pallas as pl
from jax.experimental.pallas import tpu as pltpu
from jax.sharding import PartitionSpec as P

F32 = jnp.float32
BF16 = jnp.bfloat16
VMEM_LIMIT = 24 * 1024 * 1024
LANES = 256
CHUNKS = 4
PARTS = 2
LAG = 1


def split(x, parts):
    terms = []
    for _ in range(parts - 1):
        term = x.astype(BF16)
        terms.append(term)
        x = x - term.astype(F32)
    terms.append(x.astype(BF16))
    return terms


def mm(a, b):
    return lax.dot_general(a, b, (((1,), (0,)), ((), ())), preferred_element_type=F32)


def mm_nt(a, b):
    return lax.dot_general(a, b, (((1,), (1,)), ((), ())), preferred_element_type=F32)


def mm_tn(a, b):
    return lax.dot_general(a, b, (((0,), (0,)), ((), ())), preferred_element_type=F32)


def iota(shape, dim):
    return lax.broadcasted_iota(jnp.int32, shape, dim)


def to_column(row):
    n = row.shape[1]
    eye = iota((n, n), 0) == iota((n, n), 1)
    return jnp.sum(jnp.where(eye, row, 0.0), axis=1, keepdims=True)


def to_row(column):
    n = column.shape[0]
    eye = iota((n, n), 0) == iota((n, n), 1)
    return jnp.sum(jnp.where(eye, column, 0.0), axis=0, keepdims=True)


def head_map(heads, width, first, lanes):
    low = iota((heads, lanes), 0) * width
    channel = iota((heads, lanes), 1) + first
    return (channel >= low) & (channel < low + width)


def spread_map(heads, width, first, lanes):
    one = jnp.where(head_map(heads, width, first, lanes), 1.0, 0.0).astype(BF16)
    return jnp.concatenate([one, one, one], axis=0)


def rows_of_three(per_head):
    return jnp.concatenate(split(per_head, 3), axis=0)


def spread(three, first, lanes, width):
    heads = three.shape[0] // 3
    return mm_tn(three, spread_map(heads, width, first, lanes))


def scan_tokens(per_head, backward):
    heads, length = per_head.shape
    source = iota((length, length), 0)
    target = iota((length, length), 1)
    keep = source >= target if backward else source <= target
    sums = mm(rows_of_three(per_head), jnp.where(keep, 1.0, 0.0).astype(BF16))
    return sums[:heads] + sums[heads : 2 * heads] + sums[2 * heads :]


def channel_row(column, heads, width, first):
    mine = head_map(heads, width, first, LANES)
    return jnp.sum(jnp.where(mine, column, 0.0), axis=0, keepdims=True)


def head_column(row, heads, width, first):
    mine = head_map(heads, width, first, LANES)
    return jnp.sum(jnp.where(mine, row, 0.0), axis=1, keepdims=True)


def gate_parts(gate, grad):
    wide = gate.astype(F32)
    sigmoid = 1.0 / (1.0 + jnp.exp(-wide))
    return wide, sigmoid, grad.astype(F32) * (wide * sigmoid)


def states_kernel(chunks, size, *refs):
    sources, outs, (steps_ref, lr_ref, sems) = refs[:8], refs[8:-3], refs[-3:]
    v_ref, gate_ref, go_ref, b_ref, c_ref = outs[:5]
    cum_ref, neg_ref, decay_ref, slope_ref, skip_ref = outs[5:10]
    mine_refs, other_refs = outs[10 : 10 + chunks], outs[10 + chunks :]
    targets = (v_ref, gate_ref, go_ref, b_ref, c_ref, steps_ref, lr_ref, skip_ref)
    copies = [
        pltpu.make_async_copy(source, target, sems.at[i])
        for i, (source, target) in enumerate(zip(sources, targets))
    ]
    for i in (6, 5, 3, 4, 0, 1, 2, 7):
        copies[i].start()
    copies[6].wait()
    copies[5].wait()
    length, channels = v_ref.shape
    heads = steps_ref.shape[0]
    width = channels // heads
    lower = lax.axis_index("seq") < size // 2 if size > 1 else True
    rates = jnp.exp(to_column(lr_ref[...]))
    cumulative = scan_tokens(-rates * steps_ref[...], False)
    total = cumulative[:, -1:]
    decay = jnp.exp(total)
    cum_ref[...] = cumulative
    neg_ref[...] = jnp.broadcast_to(-rates, (heads, length))
    growth = rows_of_three(jnp.exp(cumulative))
    fall = rows_of_three(jnp.exp(total - cumulative))
    copies[3].wait()
    copies[4].wait()
    b_t = b_ref[...].astype(F32).T.astype(BF16)
    c_t = c_ref[...].astype(F32).T.astype(BF16)
    for i in (0, 1, 2, 7):
        copies[i].wait()
    rows = b_t.shape[0] // chunks
    for first in range(0, channels, LANES):
        here = pl.ds(first, LANES)
        _, _, grad_y = gate_parts(gate_ref[:, here], go_ref[:, here])
        high, low = split(spread(growth, first, LANES, width) * grad_y, 2)
        pulled = mm(c_t, high) + mm(c_t, low)
        scaled = (spread(fall, first, LANES, width) * v_ref[:, here].astype(F32)).astype(BF16)
        local = mm(b_t, scaled)
        mine = jnp.where(lower, local, pulled)
        other = jnp.where(lower, pulled, local)
        for i in range(chunks):
            mine_refs[i][:, here] = mine[i * rows : (i + 1) * rows]
            other_refs[i][:, here] = other[i * rows : (i + 1) * rows]
        decay_ref[:, here] = channel_row(decay, heads, width, first)
        slope_ref[:, here] = channel_row(total * decay, heads, width, first)


def intra_kernel(
    v_ref, gate_ref, go_ref, b_ref, c_ref, cum_ref,
    intra_ref, inner_ref, sum_b_ref, sum_c_ref, grad_t_ref, inner_t_ref, acc_ref,
):
    length, channels = v_ref.shape
    heads = cum_ref.shape[0]
    width = channels // heads
    half = length // 2
    pair = 2 * width
    cumulative = cum_ref[...]
    columns = cumulative.T
    scores = mm_nt(c_ref[...], b_ref[...])
    causal = iota((half, half), 0) >= iota((half, half), 1)
    left = iota((1, pair), 1) < width
    acc_ref[...] = jnp.zeros_like(acc_ref)

    def blocks(x):
        return x[:half, :half], x[half:, :half], x[half:, half:]

    scores_00, scores_10, scores_11 = blocks(scores)
    for first in range(0, channels, pair):
        here = pl.ds(first, pair)
        _, _, grad_y = gate_parts(gate_ref[:, here], go_ref[:, here])
        grad_t_ref[here, :] = grad_y.T.astype(BF16)
        vals = v_ref[:, here]
        pieces = []
        for side in range(2):
            head = first // width + side
            own = left if side == 0 else jnp.logical_not(left)
            row = cumulative[head : head + 1, :]
            column = columns[:, head : head + 1]
            row_0, row_1 = row[:, :half], row[:, half:]
            column_0, column_1 = column[:half], column[half:]
            decay_00 = jnp.exp(jnp.where(causal, column_0 - row_0, -1e30))
            decay_10 = jnp.exp(column_1 - row_0)
            decay_11 = jnp.exp(jnp.where(causal, column_1 - row_1, -1e30))
            mix_00 = (scores_00 * decay_00).astype(BF16)
            mix_10 = (scores_10 * decay_10).astype(BF16)
            mix_11 = (scores_11 * decay_11).astype(BF16)
            low_rows = jnp.concatenate([mix_10, mix_11], axis=1)
            pieces.append((mm(mix_00, vals[:half]), mm(low_rows, vals)))
            head_grad = jnp.where(own, grad_y, 0.0).astype(BF16)
            mixed_0 = mm_nt(head_grad[:half], vals[:half])
            mixed_1 = mm_nt(head_grad[half:], vals)
            acc_ref[:half, :half] += mixed_0 * decay_00
            acc_ref[half:, :half] += mixed_1[:, :half] * decay_10
            acc_ref[half:, half:] += mixed_1[:, half:] * decay_11
            mine = pl.ds(first + side * width, width)
            grad_t = grad_t_ref[mine, :]
            inner_t_ref[mine, :half] = mm(grad_t[:, :half], mix_00) + mm(grad_t[:, half:], mix_10)
            inner_t_ref[mine, half:] = mm(grad_t[:, half:], mix_11)
        intra_ref[:half, here] = jnp.where(left, pieces[0][0], pieces[1][0])
        intra_ref[half:, here] = jnp.where(left, pieces[0][1], pieces[1][1])
        inner_ref[:, here] = inner_t_ref[here, :].T
    shares = acc_ref[...]
    high, low = split(shares, 2)
    sum_c_ref[...] = mm(high, b_ref[...]) + mm(low, b_ref[...])
    high, low = split(shares.T, 2)
    sum_b_ref[...] = mm(high, c_ref[...]) + mm(low, c_ref[...])


def factors_kernel(
    v_ref, gate_ref, go_ref, b_ref, c_ref, cum_ref, after_ref,
    high_ref, low_ref, scaled_ref, q_ref, r_ref,
):
    length, channels = v_ref.shape
    heads = cum_ref.shape[0]
    width = channels // heads
    cumulative = cum_ref[...]
    left_over = cumulative[:, -1:] - cumulative
    growth = rows_of_three(jnp.exp(cumulative))
    fall = rows_of_three(jnp.exp(left_over))
    growth_slope = rows_of_three(cumulative * jnp.exp(cumulative))
    fall_slope = rows_of_three(left_over * jnp.exp(left_over))
    b_t = b_ref[...].astype(F32).T.astype(BF16)
    c_t = c_ref[...].astype(F32).T.astype(BF16)
    for first in range(0, channels, LANES):
        here = pl.ds(first, LANES)
        _, _, grad_y = gate_parts(gate_ref[:, here], go_ref[:, here])
        vals = v_ref[:, here].astype(F32)
        high, low = split(spread(growth, first, LANES, width) * grad_y, 2)
        high_ref[:, here] = high
        low_ref[:, here] = low
        scaled_ref[:, here] = (spread(fall, first, LANES, width) * vals).astype(BF16)
        high, low = split(spread(growth_slope, first, LANES, width) * grad_y, 2)
        q_ref[:, here] = mm(c_t, high) + mm(c_t, low)
        high, low = split(spread(fall_slope, first, LANES, width) * vals, 2)
        r_ref[:, here] = mm(b_t, high) + mm(b_t, low)


def prepare_kernel(
    v_ref, gate_ref, go_ref, cum_ref, skip_ref, intra_ref, in_inner_ref, after_ref,
    coef_ref, mamba_ref, inner_ref, growth_ref, fall_ref, gy_ref, gcum_ref, parts_ref,
):
    length, channels = v_ref.shape
    heads = cum_ref.shape[0]
    width = channels // heads
    cumulative = cum_ref[...]
    growth_three = rows_of_three(jnp.exp(cumulative))
    fall_three = rows_of_three(jnp.exp(cumulative[:, -1:] - cumulative))
    skip_column = to_column(skip_ref[...])
    grad_cum = jnp.zeros((heads, length), F32)
    skip_part = jnp.zeros((heads, 1), F32)
    for first in range(0, channels, LANES):
        here = pl.ds(first, LANES)
        wide, sigmoid, grad_y = gate_parts(gate_ref[:, here], go_ref[:, here])
        vals = v_ref[:, here].astype(F32)
        skip = channel_row(skip_column, heads, width, first)
        growth_ref[:, here] = spread(growth_three, first, LANES, width)
        fall_ref[:, here] = spread(fall_three, first, LANES, width)
        gy_ref[:, here] = grad_y
        coef_ref[:, here] = go_ref[:, here].astype(F32) * sigmoid * (1.0 + wide * (1.0 - sigmoid))
        intra = intra_ref[:, here]
        inner = in_inner_ref[:, here]
        mamba_ref[:, here] = intra + skip * vals
        inner_ref[:, here] = inner + skip * grad_y
        high, low = split(grad_y.astype(BF16).astype(F32) * intra - vals * inner, 2)
        head_rows = jnp.where(head_map(heads, width, first, LANES), 1.0, 0.0).astype(BF16)
        grad_cum = grad_cum + mm_nt(head_rows, high) + mm_nt(head_rows, low)
        skip_row = jnp.sum(grad_y * vals, axis=0, keepdims=True)
        skip_part = skip_part + head_column(skip_row, heads, width, first)
    gcum_ref[...] = grad_cum
    rate_part = jnp.sum(grad_cum * cumulative, axis=1, keepdims=True)
    parts_ref[...] = jnp.concatenate([to_row(rate_part), to_row(skip_part)], axis=0)


def pick(size, first, second, last):
    if size == 1:
        return jnp.zeros_like(first), jnp.zeros_like(first)
    if size % 2:
        return first, second
    index = lax.axis_index("seq")
    lower = index < size // 2
    edge = jnp.logical_or(index == 0, index == size - 1)
    first = jnp.where(edge, 0.0, first)
    second = jnp.where(edge, last, second)
    return jnp.where(lower, first, second), jnp.where(lower, second, first)


def picked(size, states, here):
    both = [pick(size, *(ref[:, here] for ref in state)) for state in states]
    return jnp.concatenate([x[0] for x in both], axis=0), jnp.concatenate([x[1] for x in both], axis=0)


def rate_kernel(size, pieces, start, heads, final, *refs):
    states, refs = [refs[3 * i : 3 * i + 3] for i in range(pieces)], refs[3 * pieces :]
    q_ref, r_ref, slope_ref, row_ref, parts_ref, out_ref = *refs[:5], refs[-1]
    rows, channels = pieces * states[0][0].shape[0], q_ref.shape[1]
    here = slice(start, start + rows)
    rate_part = jnp.zeros((heads, 1), F32)
    for begin in range(0, channels, LANES):
        lanes = pl.ds(begin, LANES)
        entering, after = picked(size, states, lanes)
        terms = entering * q_ref[here, lanes] + after * (
            r_ref[here, lanes] + slope_ref[:, lanes] * entering
        )
        row = row_ref[:, lanes] + jnp.sum(terms, axis=0, keepdims=True)
        if final:
            rate_part = rate_part + head_column(row, heads, channels // heads, begin)
        else:
            out_ref[:, lanes] = row
    if final:
        base = parts_ref[...]
        out_ref[...] = jnp.concatenate([base[:1] + to_row(rate_part), base[1:]], axis=0)


def share_kernel(size, pieces, start, *refs):
    states, refs = [refs[3 * i : 3 * i + 3] for i in range(pieces)], refs[3 * pieces :]
    high_ref, low_ref, scaled_ref, sum_b_ref, sum_c_ref = refs[:5]
    rows, channels = pieces * states[0][0].shape[0], scaled_ref.shape[1]
    here = slice(start, start + rows)
    grad_b = sum_b_ref[:, here]
    grad_c = sum_c_ref[:, here]
    for begin in range(0, channels, LANES):
        lanes = pl.ds(begin, LANES)
        entering, after = picked(size, states, lanes)
        enter_high, enter_low = split(entering, 2)
        after_high, after_low = split(after, 2)
        high, low, scaled = high_ref[:, lanes], low_ref[:, lanes], scaled_ref[:, lanes]
        grad_c = grad_c + mm_nt(high, enter_high) + (mm_nt(high, enter_low) + mm_nt(low, enter_high))
        grad_b = grad_b + mm_nt(scaled, after_high) + mm_nt(scaled, after_low)
    refs[-1][...] = jnp.concatenate([grad_b, grad_c], axis=1)


def rest_kernel(size, pieces, *refs):
    states, refs = [refs[3 * i : 3 * i + 3] for i in range(pieces)], refs[3 * pieces :]
    (
        v_ref, b_ref, c_ref, coef_ref, mamba_ref, inner_ref, growth_ref, fall_ref, gy_ref,
        gcum_ref, decay_ref, neg_ref, *_, gv_ref, gg_ref, gs_ref, total_ref,
    ) = refs
    length, channels = v_ref.shape
    heads = gcum_ref.shape[0]
    width = channels // heads
    block_b, block_c = b_ref[...], c_ref[...]
    grad_cum = gcum_ref[...]
    grad_total = jnp.zeros((heads, 1), F32)
    for first in range(0, channels, LANES):
        here = pl.ds(first, LANES)
        entering, after = picked(size, states, here)
        enter_high, enter_low = split(entering, 2)
        after_high, after_low = split(after, 2)
        inter = growth_ref[:, here] * (mm(block_c, enter_high) + mm(block_c, enter_low))
        outer = fall_ref[:, here] * (mm(block_b, after_high) + mm(block_b, after_low))
        gg_ref[0, :, here] = (coef_ref[:, here] * (mamba_ref[:, here] + inter)).astype(BF16)
        gv_ref[0, :, here] = (inner_ref[:, here] + outer).astype(BF16)
        pulled = v_ref[:, here].astype(F32) * outer
        high, low = split(gy_ref[:, here] * inter - pulled, 2)
        head_rows = jnp.where(head_map(heads, width, first, LANES), 1.0, 0.0).astype(BF16)
        grad_cum = grad_cum + mm_nt(head_rows, high) + mm_nt(head_rows, low)
        total_row = jnp.sum(pulled, axis=0, keepdims=True) + decay_ref[:, here] * jnp.sum(
            after * entering, axis=0, keepdims=True
        )
        grad_total = grad_total + head_column(total_row, heads, width, first)
    gs_ref[0] = neg_ref[...] * (scan_tokens(grad_cum, True) + grad_total)
    total_ref[...] = to_row(grad_total)


def tree(values):
    while len(values) > 1:
        values = [sum(values[i + 1 : i + 2], values[i]) for i in range(0, len(values), 2)]
    return values[0]


def add_kernel(x_ref, y_ref, *refs):
    refs[-1][...] = x_ref[...] + y_ref[...]


def sum_kernel(*refs):
    refs[-1][...] = tree([ref[...] for ref in refs[:-1]])


def last_kernel(counts, *refs):
    refs, (gb_ref, gc_ref, rate_ref, skip_ref) = refs[:-4], refs[-4:]
    sums = []
    for count in counts:
        sums.append(tree([ref[...] for ref in refs[:count]]))
        refs = refs[count:]
    *shares, small = sums
    start = 0
    for both in shares:
        rows = both.shape[1] // 2
        gb_ref[0, :, start : start + rows] = both[:, :rows]
        gc_ref[0, :, start : start + rows] = both[:, rows:]
        start += rows
    rate_ref[...] = small[:1]
    skip_ref[...] = small[1:]


def call(kernel, outs, scratch=(), flops=0, space=pltpu.VMEM, after=()):
    def run(*args):
        if space == pltpu.HBM:
            args = [pltpu.with_memory_space_constraint(a, space) for a in args]
        specs = [pl.BlockSpec(memory_space=space)] * len(args)
        specs += [pl.BlockSpec(memory_space=pl.ANY)] * len(after)
        args = (*args, *after)
        size = sum(a.size * a.dtype.itemsize for a in (*args, *outs))
        return pl.pallas_call(
            kernel,
            out_shape=tuple(outs),
            in_specs=specs,
            out_specs=tuple(pl.BlockSpec(memory_space=pltpu.VMEM) for _ in outs),
            scratch_shapes=list(scratch),
            compiler_params=pltpu.CompilerParams(vmem_limit_bytes=VMEM_LIMIT),
            cost_estimate=pl.CostEstimate(flops=flops, bytes_accessed=size, transcendentals=0),
        )(*args)

    return run


def swap(x, axis, size, bit):
    return lax.ppermute(x, axis, [(i, i ^ bit) for i in range(size)])


def hop(x, sizes, step):
    size, copies = sizes["seq"], sizes["replica"]
    pairs = []
    for copy in range(copies):
        for place in range(size):
            to = (copy ^ 1 if copies % 2 == 0 else copy, place)
            for low in (step, size - 2 - step):
                if place in (low, low + 1):
                    to = (copy, 2 * low + 1 - place)
            pairs.append((copy * size + place, to[0] * size + to[1]))
    return lax.ppermute(x, ("replica", "seq"), pairs)


def pass_kernel(*refs):
    got_ref, base_ref, decay_ref = refs[:3]
    refs[-1][...] = decay_ref[...] * got_ref[...] + base_ref[...]


def pass_on(got, base, decay, after):
    return call(pass_kernel, [jax.ShapeDtypeStruct(base.shape, F32)], flops=2 * base.size, after=after)(
        got, base, decay
    )[0]


def chain(sizes, mine, other, decay, work):
    chunks = len(mine)
    size = sizes["seq"]
    if size == 1:
        for k in sorted(work):
            work[k](())
        return [(x, x, x) for x in mine]
    if size % 2:
        raise NotImplementedError
    index = lax.axis_index("seq")
    place = jnp.minimum(index, size - 1 - index)
    middle = size // 2 - 1
    got = {(0, c): hop(mine[c], sizes, 0) for c in range(chunks)}
    steps = [
        (at + c + (LAG if at > middle else 0), at, c) for at in range(1, size - 1) for c in range(chunks)
    ]
    token = ()
    for count, (_, at, c) in enumerate(sorted(steps)):
        if count in work:
            token = work[count](token)
        if at > middle and c > 2:
            token = (*token, got[at, c - 3])
        base = mine[c] if at <= middle else other[c]
        pay = pass_on(got[at - 1, c], base, decay, token)
        got[at, c] = hop(pay, sizes, at)
        token = (pay,)
    for k in sorted(work):
        if k >= len(steps):
            token = work[k](token)
    states = []
    for c in range(chunks):
        first, second, last = got[0, c], got[middle, c], got[size - 2, c]
        for at in range(1, middle):
            first = jnp.where(place == at + 1, got[at, c], first)
        for at in range(middle + 1, size - 2):
            second = jnp.where(place == size - 2 - at, got[at, c], second)
        states.append((first, second, last))
    return states


def sum_terms(x, axis, size):
    if size == 1:
        return [x]
    if size == 4:
        return [x] + [swap(x, axis, size, bit) for bit in (1, 2, 3)]
    if size & (size - 1):
        return [lax.psum(x, axis)]
    bit = 1
    while 2 * bit < size:
        x = x + swap(x, axis, size, bit)
        bit *= 2
    return [x, swap(x, axis, size, bit)]


def small_terms(x, axes, sizes, between):
    bits = [(axis, 1 << k) for axis in axes for k in range(sizes[axis].bit_length() - 1)]
    if any(sizes[axis] & (sizes[axis] - 1) for axis in axes):
        x = lax.psum(x, tuple(axes))
        between((x,))
        return [x]
    after = ()
    for count, (axis, bit) in enumerate(bits):
        theirs = swap(x, axis, sizes[axis], bit)
        if count == len(bits) - 1:
            break
        x = call(add_kernel, [jax.ShapeDtypeStruct(x.shape, F32)], after=after)(x, theirs)[0]
        after = between((x,)) if count == 0 else ()
    if len(bits) < 2:
        between((x,))
    return [x, theirs] if bits else [x]


def shards(sizes, values, gate_in, in_b, in_c, step_sizes, log_rates, skip_gain, grad_out):
    like = jax.ShapeDtypeStruct
    length, channels = values.shape[1:]
    heads = step_sizes.shape[1]
    state = in_b.shape[2]
    seq = sizes["seq"]
    rows = state // CHUNKS
    wide = like((length, channels), F32)
    wide_b = like((length, channels), BF16)
    share = like((length, state), F32)
    small = like((heads, length), F32)
    row = like((1, channels), F32)
    piece = like((rows, channels), F32)
    maps = like((length, state), BF16)

    out = call(
        functools.partial(states_kernel, CHUNKS, seq),
        [wide_b, wide_b, wide_b, maps, maps, small, small, row, row, like((1, heads), F32)]
        + [piece] * (2 * CHUNKS),
        [
            pltpu.VMEM((heads, length), F32),
            pltpu.VMEM((1, heads), F32),
            pltpu.SemaphoreType.DMA((8,)),
        ],
        flops=8 * length * channels * state,
        space=pltpu.HBM,
    )(
        values[0], gate_in[0], grad_out[0], in_b[0], in_c[0], step_sizes[0],
        log_rates.reshape(1, heads), skip_gain.reshape(1, heads),
    )
    vals, gate, grad, block_b, block_c, cumulative, negative, decay, slope, skip = out[:10]
    mine, other = out[10 : 10 + CHUNKS], out[10 + CHUNKS :]

    made = {}

    def intra(after):
        made["intra"] = call(
            intra_kernel,
            [wide, wide, share, share],
            [
                pltpu.VMEM((channels, length), BF16),
                pltpu.VMEM((channels, length), F32),
                pltpu.VMEM((length, length), F32),
            ],
            flops=16 * length * length * channels,
        )(vals, gate, grad, block_b, block_c, cumulative)
        return (made["intra"][2],)

    def factors(after):
        made["factors"] = call(
            factors_kernel,
            [wide_b] * 3 + [like((state, channels), F32)] * 2,
            flops=8 * length * state * channels,
        )(vals, gate, grad, block_b, block_c, cumulative, *(after if after else made["intra"][2:3]))
        return (made["factors"][-1],)

    def prepare(after):
        made["prepare"] = call(
            prepare_kernel,
            [wide] * 6 + [small, like((2, heads), F32)],
            flops=8 * length * state * channels,
        )(
            vals, gate, grad, cumulative, skip,
            *made["intra"][:2], *(after if after else made["intra"][2:3]),
        )
        return (made["prepare"][-1],)

    last_middle = (max(seq // 2 - 1, 1) - 1) * CHUNKS + CHUNKS
    states = chain(sizes, mine, other, decay, {0: intra, 1: factors, last_middle + LAG: prepare})
    sum_b, sum_c = made["intra"][2:]
    high, low, scaled, q, r = made["factors"]
    coef, mamba, inner, growth, fall, grad_y, grad_cum, parts = made["prepare"]

    rate_row = jnp.zeros((1, channels), F32)
    terms, counts, done = [], [], []
    for i in range(PARTS):
        final = i == PARTS - 1
        count = CHUNKS // PARTS
        own = [x for group in states[i * count : (i + 1) * count] for x in group]
        rate_row = call(
            functools.partial(rate_kernel, seq, count, i * rows * count, heads, final),
            [like((2, heads), F32) if final else row],
        )(*own, q, r, slope, rate_row, parts)[0]
        share_of = call(
            functools.partial(share_kernel, seq, count, i * rows * count),
            [like((length, 2 * rows * count), F32)],
            flops=10 * length * channels * rows * count,
            after=(rate_row,),
        )(*own, high, low, scaled, sum_b, sum_c)[0]
        own = sum_terms(share_of, "tensor", sizes["tensor"])
        if not final:
            own = [call(sum_kernel, [like(share_of.shape, F32)])(*own)[0]]
            done += own
        terms += own
        counts.append(len(own))

    def rest(after):
        made["rest"] = call(
            functools.partial(rest_kernel, seq, CHUNKS),
            [like((1, length, channels), BF16)] * 2
            + [like((1, heads, length), F32), like((1, heads), F32)],
            flops=10 * length * channels * state,
            after=(*after, *done),
        )(
            *(x for group in states for x in group),
            vals, block_b, block_c, coef, mamba, inner, growth, fall, grad_y, grad_cum, decay, negative,
        )
        return (made["rest"][3],)

    own = small_terms(rate_row, ("seq", "replica"), sizes, rest)
    terms += own
    counts.append(len(own))
    grad_values, grad_gate, grad_steps, _ = made["rest"]
    grad_b, grad_c, rate_sum, skip_sum = call(
        functools.partial(last_kernel, tuple(counts)),
        [like((1, length, state), F32)] * 2 + [like((1, heads), F32)] * 2,
    )(*terms)
    return (
        grad_values,
        grad_gate,
        grad_b,
        grad_c,
        grad_steps,
        rate_sum.reshape(heads),
        skip_sum.reshape(heads),
    )


def solution(mesh):
    in_specs = (
        P("replica", "seq", "tensor"),
        P("replica", "seq", "tensor"),
        P("replica", "seq", None),
        P("replica", "seq", None),
        P("replica", "tensor", "seq"),
        P("tensor"),
        P("tensor"),
        P("replica", "seq", "tensor"),
    )
    out_specs = (
        P("replica", "seq", "tensor"),
        P("replica", "seq", "tensor"),
        P("replica", "seq", None),
        P("replica", "seq", None),
        P("replica", "tensor", "seq"),
        P("tensor"),
        P("tensor"),
    )
    body = functools.partial(shards, dict(mesh.shape))
    return jax.shard_map(body, mesh=mesh, in_specs=in_specs, out_specs=out_specs, check_vma=False)
```

```python
import functools
import math

import jax
import jax.numpy as jnp
from jax import lax
from jax.experimental import pallas as pl
from jax.experimental.pallas import tpu as pltpu
from jax.sharding import PartitionSpec as P

F32 = jnp.float32
BF16 = jnp.bfloat16
VMEM_LIMIT = 24 * 1024 * 1024
LANES = 256
CHUNKS = 4
PARTS = 2
LAG = 1


def split(x, parts):
    terms = []
    for _ in range(parts - 1):
        term = x.astype(BF16)
        terms.append(term)
        x = x - term.astype(F32)
    terms.append(x.astype(BF16))
    return terms


def mm(a, b):
    return lax.dot_general(a, b, (((1,), (0,)), ((), ())), preferred_element_type=F32)


def mm_nt(a, b):
    return lax.dot_general(a, b, (((1,), (1,)), ((), ())), preferred_element_type=F32)


def mm_tn(a, b):
    return lax.dot_general(a, b, (((0,), (0,)), ((), ())), preferred_element_type=F32)


def iota(shape, dim):
    return lax.broadcasted_iota(jnp.int32, shape, dim)


def to_column(row):
    n = row.shape[1]
    eye = iota((n, n), 0) == iota((n, n), 1)
    return jnp.sum(jnp.where(eye, row, 0.0), axis=1, keepdims=True)


def to_row(column):
    n = column.shape[0]
    eye = iota((n, n), 0) == iota((n, n), 1)
    return jnp.sum(jnp.where(eye, column, 0.0), axis=0, keepdims=True)


def head_map(heads, width, first, lanes):
    low = iota((heads, lanes), 0) * width
    channel = iota((heads, lanes), 1) + first
    return (channel >= low) & (channel < low + width)


def spread_map(heads, width, first, lanes):
    one = jnp.where(head_map(heads, width, first, lanes), 1.0, 0.0).astype(BF16)
    return jnp.concatenate([one, one, one], axis=0)


def rows_of_three(per_head):
    return jnp.concatenate(split(per_head, 3), axis=0)


def spread(three, first, lanes, width):
    heads = three.shape[0] // 3
    return mm_tn(three, spread_map(heads, width, first, lanes))


def scan_tokens(per_head, backward):
    heads, length = per_head.shape
    source = iota((length, length), 0)
    target = iota((length, length), 1)
    keep = source >= target if backward else source <= target
    sums = mm(rows_of_three(per_head), jnp.where(keep, 1.0, 0.0).astype(BF16))
    return sums[:heads] + sums[heads : 2 * heads] + sums[2 * heads :]


def channel_row(column, heads, width, first):
    mine = head_map(heads, width, first, LANES)
    return jnp.sum(jnp.where(mine, column, 0.0), axis=0, keepdims=True)


def head_column(row, heads, width, first):
    mine = head_map(heads, width, first, LANES)
    return jnp.sum(jnp.where(mine, row, 0.0), axis=1, keepdims=True)


def gate_parts(gate, grad):
    wide = gate.astype(F32)
    sigmoid = 1.0 / (1.0 + jnp.exp(-wide))
    return wide, sigmoid, grad.astype(F32) * (wide * sigmoid)


def states_kernel(chunks, size, *refs):
    sources, outs, (steps_ref, lr_ref, sems) = refs[:8], refs[8:-3], refs[-3:]
    v_ref, gate_ref, go_ref, b_ref, c_ref = outs[:5]
    cum_ref, neg_ref, decay_ref, slope_ref, skip_ref = outs[5:10]
    mine_refs, other_refs = outs[10 : 10 + chunks], outs[10 + chunks :]
    targets = (v_ref, gate_ref, go_ref, b_ref, c_ref, steps_ref, lr_ref, skip_ref)
    copies = [
        pltpu.make_async_copy(source, target, sems.at[i])
        for i, (source, target) in enumerate(zip(sources, targets))
    ]
    for i in (6, 5, 3, 4, 0, 1, 2, 7):
        copies[i].start()
    copies[6].wait()
    copies[5].wait()
    length, channels = v_ref.shape
    heads = steps_ref.shape[0]
    width = channels // heads
    lower = lax.axis_index("seq") < size // 2 if size > 1 else True
    rates = jnp.exp(to_column(lr_ref[...]))
    cumulative = scan_tokens(-rates * steps_ref[...], False)
    total = cumulative[:, -1:]
    decay = jnp.exp(total)
    cum_ref[...] = cumulative
    neg_ref[...] = jnp.broadcast_to(-rates, (heads, length))
    growth = rows_of_three(jnp.exp(cumulative))
    fall = rows_of_three(jnp.exp(total - cumulative))
    copies[3].wait()
    copies[4].wait()
    b_t = b_ref[...].astype(F32).T.astype(BF16)
    c_t = c_ref[...].astype(F32).T.astype(BF16)
    for i in (0, 1, 2, 7):
        copies[i].wait()
    rows = b_t.shape[0] // chunks
    for first in range(0, channels, LANES):
        here = pl.ds(first, LANES)
        _, _, grad_y = gate_parts(gate_ref[:, here], go_ref[:, here])
        high, low = split(spread(growth, first, LANES, width) * grad_y, 2)
        pulled = mm(c_t, high) + mm(c_t, low)
        scaled = (spread(fall, first, LANES, width) * v_ref[:, here].astype(F32)).astype(BF16)
        local = mm(b_t, scaled)
        mine = jnp.where(lower, local, pulled)
        other = jnp.where(lower, pulled, local)
        for i in range(chunks):
            mine_refs[i][:, here] = mine[i * rows : (i + 1) * rows]
            other_refs[i][:, here] = other[i * rows : (i + 1) * rows]
        decay_ref[:, here] = channel_row(decay, heads, width, first)
        slope_ref[:, here] = channel_row(total * decay, heads, width, first)


def intra_kernel(
    v_ref, gate_ref, go_ref, b_ref, c_ref, cum_ref,
    intra_ref, inner_ref, sum_b_ref, sum_c_ref, grad_t_ref, inner_t_ref, acc_ref,
):
    length, channels = v_ref.shape
    heads = cum_ref.shape[0]
    width = channels // heads
    half = length // 2
    pair = 2 * width
    cumulative = cum_ref[...]
    columns = cumulative.T
    scores = mm_nt(c_ref[...], b_ref[...])
    causal = iota((half, half), 0) >= iota((half, half), 1)
    left = iota((1, pair), 1) < width
    acc_ref[...] = jnp.zeros_like(acc_ref)

    def blocks(x):
        return x[:half, :half], x[half:, :half], x[half:, half:]

    scores_00, scores_10, scores_11 = blocks(scores)
    for first in range(0, channels, pair):
        here = pl.ds(first, pair)
        _, _, grad_y = gate_parts(gate_ref[:, here], go_ref[:, here])
        grad_t_ref[here, :] = grad_y.T.astype(BF16)
        vals = v_ref[:, here]
        pieces = []
        for side in range(2):
            head = first // width + side
            own = left if side == 0 else jnp.logical_not(left)
            row = cumulative[head : head + 1, :]
            column = columns[:, head : head + 1]
            row_0, row_1 = row[:, :half], row[:, half:]
            column_0, column_1 = column[:half], column[half:]
            decay_00 = jnp.exp(jnp.where(causal, column_0 - row_0, -1e30))
            decay_10 = jnp.exp(column_1 - row_0)
            decay_11 = jnp.exp(jnp.where(causal, column_1 - row_1, -1e30))
            mix_00 = (scores_00 * decay_00).astype(BF16)
            mix_10 = (scores_10 * decay_10).astype(BF16)
            mix_11 = (scores_11 * decay_11).astype(BF16)
            low_rows = jnp.concatenate([mix_10, mix_11], axis=1)
            pieces.append((mm(mix_00, vals[:half]), mm(low_rows, vals)))
            head_grad = jnp.where(own, grad_y, 0.0).astype(BF16)
            mixed_0 = mm_nt(head_grad[:half], vals[:half])
            mixed_1 = mm_nt(head_grad[half:], vals)
            acc_ref[:half, :half] += mixed_0 * decay_00
            acc_ref[half:, :half] += mixed_1[:, :half] * decay_10
            acc_ref[half:, half:] += mixed_1[:, half:] * decay_11
            mine = pl.ds(first + side * width, width)
            grad_t = grad_t_ref[mine, :]
            inner_t_ref[mine, :half] = mm(grad_t[:, :half], mix_00) + mm(grad_t[:, half:], mix_10)
            inner_t_ref[mine, half:] = mm(grad_t[:, half:], mix_11)
        intra_ref[:half, here] = jnp.where(left, pieces[0][0], pieces[1][0])
        intra_ref[half:, here] = jnp.where(left, pieces[0][1], pieces[1][1])
        inner_ref[:, here] = inner_t_ref[here, :].T
    shares = acc_ref[...]
    high, low = split(shares, 2)
    sum_c_ref[...] = mm(high, b_ref[...]) + mm(low, b_ref[...])
    high, low = split(shares.T, 2)
    sum_b_ref[...] = mm(high, c_ref[...]) + mm(low, c_ref[...])


def factors_kernel(
    v_ref, gate_ref, go_ref, b_ref, c_ref, cum_ref, after_ref,
    high_ref, low_ref, scaled_ref, q_ref, r_ref,
):
    length, channels = v_ref.shape
    heads = cum_ref.shape[0]
    width = channels // heads
    cumulative = cum_ref[...]
    left_over = cumulative[:, -1:] - cumulative
    growth = rows_of_three(jnp.exp(cumulative))
    fall = rows_of_three(jnp.exp(left_over))
    growth_slope = rows_of_three(cumulative * jnp.exp(cumulative))
    fall_slope = rows_of_three(left_over * jnp.exp(left_over))
    b_t = b_ref[...].astype(F32).T.astype(BF16)
    c_t = c_ref[...].astype(F32).T.astype(BF16)
    for first in range(0, channels, LANES):
        here = pl.ds(first, LANES)
        _, _, grad_y = gate_parts(gate_ref[:, here], go_ref[:, here])
        vals = v_ref[:, here].astype(F32)
        high, low = split(spread(growth, first, LANES, width) * grad_y, 2)
        high_ref[:, here] = high
        low_ref[:, here] = low
        scaled_ref[:, here] = (spread(fall, first, LANES, width) * vals).astype(BF16)
        high, low = split(spread(growth_slope, first, LANES, width) * grad_y, 2)
        q_ref[:, here] = mm(c_t, high) + mm(c_t, low)
        high, low = split(spread(fall_slope, first, LANES, width) * vals, 2)
        r_ref[:, here] = mm(b_t, high) + mm(b_t, low)


def prepare_kernel(
    v_ref, gate_ref, go_ref, cum_ref, skip_ref, intra_ref, in_inner_ref, after_ref,
    coef_ref, mamba_ref, inner_ref, growth_ref, fall_ref, gy_ref, gcum_ref, parts_ref,
):
    length, channels = v_ref.shape
    heads = cum_ref.shape[0]
    width = channels // heads
    cumulative = cum_ref[...]
    growth_three = rows_of_three(jnp.exp(cumulative))
    fall_three = rows_of_three(jnp.exp(cumulative[:, -1:] - cumulative))
    skip_column = to_column(skip_ref[...])
    grad_cum = jnp.zeros((heads, length), F32)
    skip_part = jnp.zeros((heads, 1), F32)
    for first in range(0, channels, LANES):
        here = pl.ds(first, LANES)
        wide, sigmoid, grad_y = gate_parts(gate_ref[:, here], go_ref[:, here])
        vals = v_ref[:, here].astype(F32)
        skip = channel_row(skip_column, heads, width, first)
        growth_ref[:, here] = spread(growth_three, first, LANES, width)
        fall_ref[:, here] = spread(fall_three, first, LANES, width)
        gy_ref[:, here] = grad_y
        coef_ref[:, here] = go_ref[:, here].astype(F32) * sigmoid * (1.0 + wide * (1.0 - sigmoid))
        intra = intra_ref[:, here]
        inner = in_inner_ref[:, here]
        mamba_ref[:, here] = intra + skip * vals
        inner_ref[:, here] = inner + skip * grad_y
        high, low = split(grad_y.astype(BF16).astype(F32) * intra - vals * inner, 2)
        head_rows = jnp.where(head_map(heads, width, first, LANES), 1.0, 0.0).astype(BF16)
        grad_cum = grad_cum + mm_nt(head_rows, high) + mm_nt(head_rows, low)
        skip_row = jnp.sum(grad_y * vals, axis=0, keepdims=True)
        skip_part = skip_part + head_column(skip_row, heads, width, first)
    gcum_ref[...] = grad_cum
    rate_part = jnp.sum(grad_cum * cumulative, axis=1, keepdims=True)
    parts_ref[...] = jnp.concatenate([to_row(rate_part), to_row(skip_part)], axis=0)


def pick(size, first, second, last):
    if size == 1:
        return jnp.zeros_like(first), jnp.zeros_like(first)
    if size % 2:
        return first, second
    index = lax.axis_index("seq")
    lower = index < size // 2
    edge = jnp.logical_or(index == 0, index == size - 1)
    first = jnp.where(edge, 0.0, first)
    second = jnp.where(edge, last, second)
    return jnp.where(lower, first, second), jnp.where(lower, second, first)


def picked(size, states, here):
    both = [pick(size, *(ref[:, here] for ref in state)) for state in states]
    return jnp.concatenate([x[0] for x in both], axis=0), jnp.concatenate([x[1] for x in both], axis=0)


def rate_kernel(size, pieces, start, heads, final, *refs):
    states, refs = [refs[3 * i : 3 * i + 3] for i in range(pieces)], refs[3 * pieces :]
    q_ref, r_ref, slope_ref, row_ref, parts_ref, out_ref = *refs[:5], refs[-1]
    rows, channels = pieces * states[0][0].shape[0], q_ref.shape[1]
    here = slice(start, start + rows)
    rate_part = jnp.zeros((heads, 1), F32)
    for begin in range(0, channels, LANES):
        lanes = pl.ds(begin, LANES)
        entering, after = picked(size, states, lanes)
        terms = entering * q_ref[here, lanes] + after * (
            r_ref[here, lanes] + slope_ref[:, lanes] * entering
        )
        row = row_ref[:, lanes] + jnp.sum(terms, axis=0, keepdims=True)
        if final:
            rate_part = rate_part + head_column(row, heads, channels // heads, begin)
        else:
            out_ref[:, lanes] = row
    if final:
        base = parts_ref[...]
        out_ref[...] = jnp.concatenate([base[:1] + to_row(rate_part), base[1:]], axis=0)


def share_kernel(size, pieces, start, *refs):
    states, refs = [refs[3 * i : 3 * i + 3] for i in range(pieces)], refs[3 * pieces :]
    high_ref, low_ref, scaled_ref, sum_b_ref, sum_c_ref = refs[:5]
    rows, channels = pieces * states[0][0].shape[0], scaled_ref.shape[1]
    here = slice(start, start + rows)
    grad_b = sum_b_ref[:, here]
    grad_c = sum_c_ref[:, here]
    for begin in range(0, channels, LANES):
        lanes = pl.ds(begin, LANES)
        entering, after = picked(size, states, lanes)
        enter_high, enter_low = split(entering, 2)
        after_high, after_low = split(after, 2)
        high, low, scaled = high_ref[:, lanes], low_ref[:, lanes], scaled_ref[:, lanes]
        grad_c = grad_c + mm_nt(high, enter_high) + (mm_nt(high, enter_low) + mm_nt(low, enter_high))
        grad_b = grad_b + mm_nt(scaled, after_high) + mm_nt(scaled, after_low)
    refs[-1][...] = jnp.concatenate([grad_b, grad_c], axis=1)


def rest_kernel(size, pieces, *refs):
    states, refs = [refs[3 * i : 3 * i + 3] for i in range(pieces)], refs[3 * pieces :]
    (
        v_ref, b_ref, c_ref, coef_ref, mamba_ref, inner_ref, growth_ref, fall_ref, gy_ref,
        gcum_ref, decay_ref, neg_ref, *_, gv_ref, gg_ref, gs_ref,
    ) = refs
    length, channels = v_ref.shape
    heads = gcum_ref.shape[0]
    width = channels // heads
    block_b, block_c = b_ref[...], c_ref[...]
    grad_cum = gcum_ref[...]
    grad_total = jnp.zeros((heads, 1), F32)
    for first in range(0, channels, LANES):
        here = pl.ds(first, LANES)
        entering, after = picked(size, states, here)
        enter_high, enter_low = split(entering, 2)
        after_high, after_low = split(after, 2)
        inter = growth_ref[:, here] * (mm(block_c, enter_high) + mm(block_c, enter_low))
        outer = fall_ref[:, here] * (mm(block_b, after_high) + mm(block_b, after_low))
        gg_ref[0, :, here] = (coef_ref[:, here] * (mamba_ref[:, here] + inter)).astype(BF16)
        gv_ref[0, :, here] = (inner_ref[:, here] + outer).astype(BF16)
        pulled = v_ref[:, here].astype(F32) * outer
        high, low = split(gy_ref[:, here] * inter - pulled, 2)
        head_rows = jnp.where(head_map(heads, width, first, LANES), 1.0, 0.0).astype(BF16)
        grad_cum = grad_cum + mm_nt(head_rows, high) + mm_nt(head_rows, low)
        total_row = jnp.sum(pulled, axis=0, keepdims=True) + decay_ref[:, here] * jnp.sum(
            after * entering, axis=0, keepdims=True
        )
        grad_total = grad_total + head_column(total_row, heads, width, first)
    gs_ref[0] = neg_ref[...] * (scan_tokens(grad_cum, True) + grad_total)


def tree(values):
    while len(values) > 1:
        values = [sum(values[i + 1 : i + 2], values[i]) for i in range(0, len(values), 2)]
    return values[0]


def add_kernel(x_ref, y_ref, *refs):
    refs[-1][...] = x_ref[...] + y_ref[...]


def last_kernel(*refs):
    refs, (gb_ref, gc_ref, rate_ref, skip_ref) = refs[:-4], refs[-4:]
    *shares, small = [tree([ref[i] for i in range(ref.shape[0])]) for ref in refs]
    start = 0
    for both in shares:
        rows = both.shape[1] // 2
        gb_ref[0, :, start : start + rows] = both[:, :rows]
        gc_ref[0, :, start : start + rows] = both[:, rows:]
        start += rows
    rate_ref[...] = small[:1]
    skip_ref[...] = small[1:]


def call(kernel, outs, scratch=(), flops=0, space=pltpu.VMEM, after=()):
    def run(*args):
        if space == pltpu.HBM:
            args = [pltpu.with_memory_space_constraint(a, space) for a in args]
        specs = [pl.BlockSpec(memory_space=space)] * len(args)
        specs += [pl.BlockSpec(memory_space=pl.ANY)] * len(after)
        args = (*args, *after)
        size = sum(a.size * a.dtype.itemsize for a in (*args, *outs))
        return pl.pallas_call(
            kernel,
            out_shape=tuple(outs),
            in_specs=specs,
            out_specs=tuple(pl.BlockSpec(memory_space=pltpu.VMEM) for _ in outs),
            scratch_shapes=list(scratch),
            compiler_params=pltpu.CompilerParams(vmem_limit_bytes=VMEM_LIMIT),
            cost_estimate=pl.CostEstimate(flops=flops, bytes_accessed=size, transcendentals=0),
        )(*args)

    return run


def swap(x, axis, size, bit):
    return lax.ppermute(x, axis, [(i, i ^ bit) for i in range(size)])


def hop(x, sizes, step):
    size, copies = sizes["seq"], sizes["replica"]
    pairs = []
    for copy in range(copies):
        for place in range(size):
            to = (copy ^ 1 if copies % 2 == 0 else copy, place)
            for low in (step, size - 2 - step):
                if place in (low, low + 1):
                    to = (copy, 2 * low + 1 - place)
            pairs.append((copy * size + place, to[0] * size + to[1]))
    return lax.ppermute(x, ("replica", "seq"), pairs)


def pass_kernel(*refs):
    got_ref, base_ref, decay_ref = refs[:3]
    refs[-1][...] = decay_ref[...] * got_ref[...] + base_ref[...]


def pass_on(got, base, decay, after):
    return call(pass_kernel, [jax.ShapeDtypeStruct(base.shape, F32)], flops=2 * base.size, after=after)(
        got, base, decay
    )[0]


def chain(sizes, mine, other, decay, work):
    chunks = len(mine)
    size = sizes["seq"]
    if size == 1:
        for k in sorted(work):
            work[k](())
        return [(x, x, x) for x in mine]
    if size % 2:
        raise NotImplementedError
    index = lax.axis_index("seq")
    place = jnp.minimum(index, size - 1 - index)
    middle = size // 2 - 1
    got = {(0, c): hop(mine[c], sizes, 0) for c in range(chunks)}
    steps = [
        (at + c + (LAG if at > middle else 0), at, c) for at in range(1, size - 1) for c in range(chunks)
    ]
    token = ()
    for count, (_, at, c) in enumerate(sorted(steps)):
        if count in work:
            token = work[count](token)
        if at > middle and c > 2:
            token = (*token, got[at, c - 3])
        base = mine[c] if at <= middle else other[c]
        pay = pass_on(got[at - 1, c], base, decay, token)
        got[at, c] = hop(pay, sizes, at)
        token = (pay,)
    for k in sorted(work):
        if k >= len(steps):
            token = work[k](token)
    states = []
    for c in range(chunks):
        first, second, last = got[0, c], got[middle, c], got[size - 2, c]
        for at in range(1, middle):
            first = jnp.where(place == at + 1, got[at, c], first)
        for at in range(middle + 1, size - 2):
            second = jnp.where(place == size - 2 - at, got[at, c], second)
        states.append((first, second, last))
    return states


def sum_terms(x, axes, sizes):
    count = math.prod(sizes[axis] for axis in axes)
    if count == 1:
        return x[None]
    return lax.all_to_all(jnp.broadcast_to(x, (count, *x.shape)), axes, 0, 0)


def shards(sizes, values, gate_in, in_b, in_c, step_sizes, log_rates, skip_gain, grad_out):
    like = jax.ShapeDtypeStruct
    length, channels = values.shape[1:]
    heads = step_sizes.shape[1]
    state = in_b.shape[2]
    seq = sizes["seq"]
    rows = state // CHUNKS
    wide = like((length, channels), F32)
    wide_b = like((length, channels), BF16)
    share = like((length, state), F32)
    small = like((heads, length), F32)
    row = like((1, channels), F32)
    piece = like((rows, channels), F32)
    maps = like((length, state), BF16)

    out = call(
        functools.partial(states_kernel, CHUNKS, seq),
        [wide_b, wide_b, wide_b, maps, maps, small, small, row, row, like((1, heads), F32)]
        + [piece] * (2 * CHUNKS),
        [
            pltpu.VMEM((heads, length), F32),
            pltpu.VMEM((1, heads), F32),
            pltpu.SemaphoreType.DMA((8,)),
        ],
        flops=8 * length * channels * state,
        space=pltpu.HBM,
    )(
        values[0], gate_in[0], grad_out[0], in_b[0], in_c[0], step_sizes[0],
        log_rates.reshape(1, heads), skip_gain.reshape(1, heads),
    )
    vals, gate, grad, block_b, block_c, cumulative, negative, decay, slope, skip = out[:10]
    mine, other = out[10 : 10 + CHUNKS], out[10 + CHUNKS :]

    made = {}

    def intra(after):
        made["intra"] = call(
            intra_kernel,
            [wide, wide, share, share],
            [
                pltpu.VMEM((channels, length), BF16),
                pltpu.VMEM((channels, length), F32),
                pltpu.VMEM((length, length), F32),
            ],
            flops=16 * length * length * channels,
        )(vals, gate, grad, block_b, block_c, cumulative)
        return (made["intra"][2],)

    def factors(after):
        made["factors"] = call(
            factors_kernel,
            [wide_b] * 3 + [like((state, channels), F32)] * 2,
            flops=8 * length * state * channels,
        )(vals, gate, grad, block_b, block_c, cumulative, *(after if after else made["intra"][2:3]))
        return (made["factors"][-1],)

    def prepare(after):
        made["prepare"] = call(
            prepare_kernel,
            [wide] * 6 + [small, like((2, heads), F32)],
            flops=8 * length * state * channels,
        )(
            vals, gate, grad, cumulative, skip,
            *made["intra"][:2], *(after if after else made["intra"][2:3]),
        )
        return (made["prepare"][-1],)

    last_middle = (max(seq // 2 - 1, 1) - 1) * CHUNKS + CHUNKS
    states = chain(sizes, mine, other, decay, {0: intra, 1: factors, last_middle + LAG: prepare})
    sum_b, sum_c = made["intra"][2:]
    high, low, scaled, q, r = made["factors"]
    coef, mamba, inner, growth, fall, grad_y, grad_cum, parts = made["prepare"]

    rate_row = jnp.zeros((1, channels), F32)
    terms = []
    for i in range(PARTS):
        final = i == PARTS - 1
        count = CHUNKS // PARTS
        own = [x for group in states[i * count : (i + 1) * count] for x in group]
        rate_row = call(
            functools.partial(rate_kernel, seq, count, i * rows * count, heads, final),
            [like((2, heads), F32) if final else row],
        )(*own, q, r, slope, rate_row, parts)[0]
        share_of = call(
            functools.partial(share_kernel, seq, count, i * rows * count),
            [like((length, 2 * rows * count), F32)],
            flops=10 * length * channels * rows * count,
            after=(rate_row,),
        )(*own, high, low, scaled, sum_b, sum_c)[0]
        terms.append(sum_terms(share_of, ("tensor",), sizes))

    def rest(after):
        made["rest"] = call(
            functools.partial(rest_kernel, seq, CHUNKS),
            [like((1, length, channels), BF16)] * 2 + [like((1, heads, length), F32)],
            flops=10 * length * channels * state,
            after=after,
        )(
            *(x for group in states for x in group),
            vals, block_b, block_c, coef, mamba, inner, growth, fall, grad_y, grad_cum, decay, negative,
        )

    terms.append(sum_terms(rate_row, ("replica", "seq"), sizes))
    rest(())
    grad_values, grad_gate, grad_steps = made["rest"]
    grad_b, grad_c, rate_sum, skip_sum = call(
        last_kernel,
        [like((1, length, state), F32)] * 2 + [like((1, heads), F32)] * 2,
    )(*terms)
    return (
        grad_values,
        grad_gate,
        grad_b,
        grad_c,
        grad_steps,
        rate_sum.reshape(heads),
        skip_sum.reshape(heads),
    )


def solution(mesh):
    in_specs = (
        P("replica", "seq", "tensor"),
        P("replica", "seq", "tensor"),
        P("replica", "seq", None),
        P("replica", "seq", None),
        P("replica", "tensor", "seq"),
        P("tensor"),
        P("tensor"),
        P("replica", "seq", "tensor"),
    )
    out_specs = (
        P("replica", "seq", "tensor"),
        P("replica", "seq", "tensor"),
        P("replica", "seq", None),
        P("replica", "seq", None),
        P("replica", "tensor", "seq"),
        P("tensor"),
        P("tensor"),
    )
    body = functools.partial(shards, dict(mesh.shape))
    return jax.shard_map(body, mesh=mesh, in_specs=in_specs, out_specs=out_specs, check_vma=False)
```

```python
import functools

import jax
import jax.numpy as jnp
from jax import lax
from jax.experimental import pallas as pl
from jax.experimental.pallas import tpu as pltpu
from jax.sharding import PartitionSpec as P

F32 = jnp.float32
BF16 = jnp.bfloat16
VMEM_LIMIT = 24 * 1024 * 1024
LANES = 256
CHUNKS = 4
PARTS = 2
WEIGHTS = {'pass4': 30, 'pass5': 10, 'pass6': 300, 'pass7': 30, 'rate0': 30, 'rate1': 10, 'later': 30, 'sum': 100, 'add1': 100, 'rest': 30}


def split(x, parts):
    terms = []
    for _ in range(parts - 1):
        term = x.astype(BF16)
        terms.append(term)
        x = x - term.astype(F32)
    terms.append(x.astype(BF16))
    return terms


def mm(a, b):
    return lax.dot_general(a, b, (((1,), (0,)), ((), ())), preferred_element_type=F32)


def mm_nt(a, b):
    return lax.dot_general(a, b, (((1,), (1,)), ((), ())), preferred_element_type=F32)


def mm_tn(a, b):
    return lax.dot_general(a, b, (((0,), (0,)), ((), ())), preferred_element_type=F32)


def iota(shape, dim):
    return lax.broadcasted_iota(jnp.int32, shape, dim)


def to_column(row):
    n = row.shape[1]
    eye = iota((n, n), 0) == iota((n, n), 1)
    return jnp.sum(jnp.where(eye, row, 0.0), axis=1, keepdims=True)


def to_row(column):
    n = column.shape[0]
    eye = iota((n, n), 0) == iota((n, n), 1)
    return jnp.sum(jnp.where(eye, column, 0.0), axis=0, keepdims=True)


def head_map(heads, width, first, lanes):
    low = iota((heads, lanes), 0) * width
    channel = iota((heads, lanes), 1) + first
    return (channel >= low) & (channel < low + width)


def spread_map(heads, width, first, lanes):
    one = jnp.where(head_map(heads, width, first, lanes), 1.0, 0.0).astype(BF16)
    return jnp.concatenate([one, one, one], axis=0)


def rows_of_three(per_head):
    return jnp.concatenate(split(per_head, 3), axis=0)


def spread(three, first, lanes, width):
    heads = three.shape[0] // 3
    return mm_tn(three, spread_map(heads, width, first, lanes))


def scan_tokens(per_head, backward):
    heads, length = per_head.shape
    source = iota((length, length), 0)
    target = iota((length, length), 1)
    keep = source >= target if backward else source <= target
    sums = mm(rows_of_three(per_head), jnp.where(keep, 1.0, 0.0).astype(BF16))
    return sums[:heads] + sums[heads : 2 * heads] + sums[2 * heads :]


def channel_row(column, heads, width, first):
    mine = head_map(heads, width, first, LANES)
    return jnp.sum(jnp.where(mine, column, 0.0), axis=0, keepdims=True)


def head_column(row, heads, width, first):
    mine = head_map(heads, width, first, LANES)
    return jnp.sum(jnp.where(mine, row, 0.0), axis=1, keepdims=True)


def gate_parts(gate, grad):
    wide = gate.astype(F32)
    sigmoid = 1.0 / (1.0 + jnp.exp(-wide))
    return wide, sigmoid, grad.astype(F32) * (wide * sigmoid)


def put_rows(refs, here, value):
    start = 0
    for ref in refs:
        rows = ref.shape[0]
        ref[:, here] = value[start : start + rows]
        start += rows


def states_kernel(size, *refs):
    sources, outs, (steps_ref, lr_ref, sems) = refs[:8], refs[8:-3], refs[-3:]
    v_ref, gate_ref, go_ref, b_ref, c_ref = outs[:5]
    cum_ref, neg_ref, decay_ref, slope_ref, skip_ref = outs[5:10]
    mine_refs = outs[10:]
    targets = (v_ref, gate_ref, go_ref, b_ref, c_ref, steps_ref, lr_ref, skip_ref)
    copies = [
        pltpu.make_async_copy(source, target, sems.at[i])
        for i, (source, target) in enumerate(zip(sources, targets))
    ]
    for i in (6, 5, 3, 4, 0, 1, 2, 7):
        copies[i].start()
    copies[6].wait()
    copies[5].wait()
    length, channels = v_ref.shape
    heads = steps_ref.shape[0]
    width = channels // heads
    rates = jnp.exp(to_column(lr_ref[...]))
    cumulative = scan_tokens(-rates * steps_ref[...], False)
    total = cumulative[:, -1:]
    decay = jnp.exp(total)
    cum_ref[...] = cumulative
    neg_ref[...] = jnp.broadcast_to(-rates, (heads, length))
    for first in range(0, channels, LANES):
        here = pl.ds(first, LANES)
        decay_ref[:, here] = channel_row(decay, heads, width, first)
        slope_ref[:, here] = channel_row(total * decay, heads, width, first)

    def local():
        copies[3].wait()
        b_t = b_ref[...].astype(F32).T.astype(BF16)
        fall = rows_of_three(jnp.exp(total - cumulative))
        copies[0].wait()
        for first in range(0, channels, LANES):
            here = pl.ds(first, LANES)
            scaled = spread(fall, first, LANES, width) * v_ref[:, here].astype(F32)
            put_rows(mine_refs, here, mm(b_t, scaled.astype(BF16)))
        for i in (1, 2, 4, 7):
            copies[i].wait()

    def pulled():
        copies[4].wait()
        c_t = c_ref[...].astype(F32).T.astype(BF16)
        growth = rows_of_three(jnp.exp(cumulative))
        copies[1].wait()
        copies[2].wait()
        for first in range(0, channels, LANES):
            here = pl.ds(first, LANES)
            _, _, grad_y = gate_parts(gate_ref[:, here], go_ref[:, here])
            high, low = split(spread(growth, first, LANES, width) * grad_y, 2)
            put_rows(mine_refs, here, mm(c_t, high) + mm(c_t, low))
        for i in (0, 3, 7):
            copies[i].wait()

    if size == 1:
        local()
    else:
        lower = lax.axis_index("seq") < size // 2
        pl.when(lower)(local)
        pl.when(jnp.logical_not(lower))(pulled)


def intra_kernel(
    v_ref, gate_ref, go_ref, b_ref, c_ref, cum_ref,
    intra_ref, inner_ref, sum_b_ref, sum_c_ref, grad_t_ref, inner_t_ref, acc_ref,
):
    length, channels = v_ref.shape
    heads = cum_ref.shape[0]
    width = channels // heads
    half = length // 2
    pair = 2 * width
    cumulative = cum_ref[...]
    columns = cumulative.T
    scores = mm_nt(c_ref[...], b_ref[...])
    causal = iota((half, half), 0) >= iota((half, half), 1)
    left = iota((1, pair), 1) < width
    acc_ref[...] = jnp.zeros_like(acc_ref)

    def blocks(x):
        return x[:half, :half], x[half:, :half], x[half:, half:]

    scores_00, scores_10, scores_11 = blocks(scores)
    for first in range(0, channels, pair):
        here = pl.ds(first, pair)
        _, _, grad_y = gate_parts(gate_ref[:, here], go_ref[:, here])
        grad_t_ref[here, :] = grad_y.T.astype(BF16)
        vals = v_ref[:, here]
        pieces = []
        for side in range(2):
            head = first // width + side
            own = left if side == 0 else jnp.logical_not(left)
            row = cumulative[head : head + 1, :]
            column = columns[:, head : head + 1]
            row_0, row_1 = row[:, :half], row[:, half:]
            column_0, column_1 = column[:half], column[half:]
            decay_00 = jnp.exp(jnp.where(causal, column_0 - row_0, -1e30))
            decay_10 = jnp.exp(column_1 - row_0)
            decay_11 = jnp.exp(jnp.where(causal, column_1 - row_1, -1e30))
            mix_00 = (scores_00 * decay_00).astype(BF16)
            mix_10 = (scores_10 * decay_10).astype(BF16)
            mix_11 = (scores_11 * decay_11).astype(BF16)
            low_rows = jnp.concatenate([mix_10, mix_11], axis=1)
            pieces.append((mm(mix_00, vals[:half]), mm(low_rows, vals)))
            head_grad = jnp.where(own, grad_y, 0.0).astype(BF16)
            mixed_0 = mm_nt(head_grad[:half], vals[:half])
            mixed_1 = mm_nt(head_grad[half:], vals)
            acc_ref[:half, :half] += mixed_0 * decay_00
            acc_ref[half:, :half] += mixed_1[:, :half] * decay_10
            acc_ref[half:, half:] += mixed_1[:, half:] * decay_11
            mine = pl.ds(first + side * width, width)
            grad_t = grad_t_ref[mine, :]
            inner_t_ref[mine, :half] = mm(grad_t[:, :half], mix_00) + mm(grad_t[:, half:], mix_10)
            inner_t_ref[mine, half:] = mm(grad_t[:, half:], mix_11)
        intra_ref[:half, here] = jnp.where(left, pieces[0][0], pieces[1][0])
        intra_ref[half:, here] = jnp.where(left, pieces[0][1], pieces[1][1])
        inner_ref[:, here] = inner_t_ref[here, :].T
    shares = acc_ref[...]
    high, low = split(shares, 2)
    sum_c_ref[...] = mm(high, b_ref[...]) + mm(low, b_ref[...])
    high, low = split(shares.T, 2)
    sum_b_ref[...] = mm(high, c_ref[...]) + mm(low, c_ref[...])


def factors_kernel(
    size, v_ref, gate_ref, go_ref, b_ref, c_ref, cum_ref, after_ref,
    high_ref, low_ref, scaled_ref, q_ref, r_ref, *other_refs,
):
    length, channels = v_ref.shape
    heads = cum_ref.shape[0]
    width = channels // heads
    cumulative = cum_ref[...]
    left_over = cumulative[:, -1:] - cumulative
    growth = rows_of_three(jnp.exp(cumulative))
    fall = rows_of_three(jnp.exp(left_over))
    growth_slope = rows_of_three(cumulative * jnp.exp(cumulative))
    fall_slope = rows_of_three(left_over * jnp.exp(left_over))
    b_t = b_ref[...].astype(F32).T.astype(BF16)
    c_t = c_ref[...].astype(F32).T.astype(BF16)
    for first in range(0, channels, LANES):
        here = pl.ds(first, LANES)
        _, _, grad_y = gate_parts(gate_ref[:, here], go_ref[:, here])
        vals = v_ref[:, here].astype(F32)
        high, low = split(spread(growth, first, LANES, width) * grad_y, 2)
        high_ref[:, here] = high
        low_ref[:, here] = low
        scaled_ref[:, here] = (spread(fall, first, LANES, width) * vals).astype(BF16)
        high, low = split(spread(growth_slope, first, LANES, width) * grad_y, 2)
        q_ref[:, here] = mm(c_t, high) + mm(c_t, low)
        high, low = split(spread(fall_slope, first, LANES, width) * vals, 2)
        r_ref[:, here] = mm(b_t, high) + mm(b_t, low)

    def pulled():
        put_rows(other_refs, slice(None), mm(c_t, high_ref[...]) + mm(c_t, low_ref[...]))

    def local():
        put_rows(other_refs, slice(None), mm(b_t, scaled_ref[...]))

    if size == 1:
        pulled()
    else:
        lower = lax.axis_index("seq") < size // 2
        pl.when(lower)(pulled)
        pl.when(jnp.logical_not(lower))(local)


def prepare_kernel(
    v_ref, gate_ref, go_ref, cum_ref, skip_ref, intra_ref, in_inner_ref, after_ref,
    coef_ref, mamba_ref, inner_ref, growth_ref, fall_ref, gy_ref, gcum_ref, parts_ref,
):
    length, channels = v_ref.shape
    heads = cum_ref.shape[0]
    width = channels // heads
    cumulative = cum_ref[...]
    growth_three = rows_of_three(jnp.exp(cumulative))
    fall_three = rows_of_three(jnp.exp(cumulative[:, -1:] - cumulative))
    skip_column = to_column(skip_ref[...])
    grad_cum = jnp.zeros((heads, length), F32)
    skip_part = jnp.zeros((heads, 1), F32)
    for first in range(0, channels, LANES):
        here = pl.ds(first, LANES)
        wide, sigmoid, grad_y = gate_parts(gate_ref[:, here], go_ref[:, here])
        vals = v_ref[:, here].astype(F32)
        skip = channel_row(skip_column, heads, width, first)
        growth_ref[:, here] = spread(growth_three, first, LANES, width)
        fall_ref[:, here] = spread(fall_three, first, LANES, width)
        gy_ref[:, here] = grad_y
        coef_ref[:, here] = go_ref[:, here].astype(F32) * sigmoid * (1.0 + wide * (1.0 - sigmoid))
        intra = intra_ref[:, here]
        inner = in_inner_ref[:, here]
        mamba_ref[:, here] = intra + skip * vals
        inner_ref[:, here] = inner + skip * grad_y
        high, low = split(grad_y.astype(BF16).astype(F32) * intra - vals * inner, 2)
        head_rows = jnp.where(head_map(heads, width, first, LANES), 1.0, 0.0).astype(BF16)
        grad_cum = grad_cum + mm_nt(head_rows, high) + mm_nt(head_rows, low)
        skip_row = jnp.sum(grad_y * vals, axis=0, keepdims=True)
        skip_part = skip_part + head_column(skip_row, heads, width, first)
    gcum_ref[...] = grad_cum
    rate_part = jnp.sum(grad_cum * cumulative, axis=1, keepdims=True)
    parts_ref[...] = jnp.concatenate([to_row(rate_part), to_row(skip_part)], axis=0)


def pick(size, first, second, last):
    if size == 1:
        return jnp.zeros_like(first), jnp.zeros_like(first)
    if size % 2:
        return first, second
    index = lax.axis_index("seq")
    lower = index < size // 2
    edge = jnp.logical_or(index == 0, index == size - 1)
    first = jnp.where(edge, 0.0, first)
    second = jnp.where(edge, last, second)
    return jnp.where(lower, first, second), jnp.where(lower, second, first)


def picked(size, states, here):
    both = [pick(size, *(ref[:, here] for ref in state)) for state in states]
    return jnp.concatenate([x[0] for x in both], axis=0), jnp.concatenate([x[1] for x in both], axis=0)


def rate_kernel(size, pieces, start, heads, final, *refs):
    states, refs = [refs[3 * i : 3 * i + 3] for i in range(pieces)], refs[3 * pieces :]
    q_ref, r_ref, slope_ref, row_ref, parts_ref, out_ref = *refs[:5], refs[-1]
    rows, channels = pieces * states[0][0].shape[0], q_ref.shape[1]
    here = slice(start, start + rows)
    rate_part = jnp.zeros((heads, 1), F32)
    for begin in range(0, channels, LANES):
        lanes = pl.ds(begin, LANES)
        entering, after = picked(size, states, lanes)
        terms = entering * q_ref[here, lanes] + after * (
            r_ref[here, lanes] + slope_ref[:, lanes] * entering
        )
        row = row_ref[:, lanes] + jnp.sum(terms, axis=0, keepdims=True)
        if final:
            rate_part = rate_part + head_column(row, heads, channels // heads, begin)
        else:
            out_ref[:, lanes] = row
    if final:
        base = parts_ref[...]
        out_ref[...] = jnp.concatenate([base[:1] + to_row(rate_part), base[1:]], axis=0)


def share_kernel(size, pieces, start, *refs):
    states, refs = [refs[3 * i : 3 * i + 3] for i in range(pieces)], refs[3 * pieces :]
    high_ref, low_ref, scaled_ref, sum_b_ref, sum_c_ref = refs[:5]
    rows, channels = pieces * states[0][0].shape[0], scaled_ref.shape[1]
    here = slice(start, start + rows)
    grad_b = sum_b_ref[:, here]
    grad_c = sum_c_ref[:, here]
    for begin in range(0, channels, LANES):
        lanes = pl.ds(begin, LANES)
        entering, after = picked(size, states, lanes)
        enter_high, enter_low = split(entering, 2)
        after_high, after_low = split(after, 2)
        high, low, scaled = high_ref[:, lanes], low_ref[:, lanes], scaled_ref[:, lanes]
        grad_c = grad_c + mm_nt(high, enter_high) + (mm_nt(high, enter_low) + mm_nt(low, enter_high))
        grad_b = grad_b + mm_nt(scaled, after_high) + mm_nt(scaled, after_low)
    refs[-1][...] = jnp.concatenate([grad_b, grad_c], axis=1)


def rest_kernel(size, pieces, *refs):
    states, refs = [refs[3 * i : 3 * i + 3] for i in range(pieces)], refs[3 * pieces :]
    (
        v_ref, b_ref, c_ref, coef_ref, mamba_ref, inner_ref, growth_ref, fall_ref, gy_ref,
        gcum_ref, decay_ref, neg_ref, *_, gv_ref, gg_ref, gs_ref,
    ) = refs
    length, channels = v_ref.shape
    heads = gcum_ref.shape[0]
    width = channels // heads
    block_b, block_c = b_ref[...], c_ref[...]
    grad_cum = gcum_ref[...]
    grad_total = jnp.zeros((heads, 1), F32)
    for first in range(0, channels, LANES):
        here = pl.ds(first, LANES)
        entering, after = picked(size, states, here)
        enter_high, enter_low = split(entering, 2)
        after_high, after_low = split(after, 2)
        inter = growth_ref[:, here] * (mm(block_c, enter_high) + mm(block_c, enter_low))
        outer = fall_ref[:, here] * (mm(block_b, after_high) + mm(block_b, after_low))
        gg_ref[0, :, here] = (coef_ref[:, here] * (mamba_ref[:, here] + inter)).astype(BF16)
        gv_ref[0, :, here] = (inner_ref[:, here] + outer).astype(BF16)
        pulled = v_ref[:, here].astype(F32) * outer
        high, low = split(gy_ref[:, here] * inter - pulled, 2)
        head_rows = jnp.where(head_map(heads, width, first, LANES), 1.0, 0.0).astype(BF16)
        grad_cum = grad_cum + mm_nt(head_rows, high) + mm_nt(head_rows, low)
        total_row = jnp.sum(pulled, axis=0, keepdims=True) + decay_ref[:, here] * jnp.sum(
            after * entering, axis=0, keepdims=True
        )
        grad_total = grad_total + head_column(total_row, heads, width, first)
    gs_ref[0] = neg_ref[...] * (scan_tokens(grad_cum, True) + grad_total)


def tree(values):
    while len(values) > 1:
        values = [sum(values[i + 1 : i + 2], values[i]) for i in range(0, len(values), 2)]
    return values[0]


def copy_kernel(x_ref, *refs):
    refs[-1][...] = x_ref[...]


def add_kernel(x_ref, y_ref, *refs):
    refs[-1][...] = x_ref[...] + y_ref[...]


def sum_kernel(*refs):
    refs[-1][...] = tree([ref[...] for ref in refs[:-1]])


def last_kernel(counts, *refs):
    refs, (gb_ref, gc_ref, rate_ref, skip_ref) = refs[:-4], refs[-4:]
    sums = []
    for count in counts:
        sums.append(tree([ref[...] for ref in refs[:count]]))
        refs = refs[count:]
    *shares, small = sums
    start = 0
    for both in shares:
        rows = both.shape[1] // 2
        gb_ref[0, :, start : start + rows] = both[:, :rows]
        gc_ref[0, :, start : start + rows] = both[:, rows:]
        start += rows
    rate_ref[...] = small[:1]
    skip_ref[...] = small[1:]


def call(kernel, outs, scratch=(), name="", space=pltpu.VMEM, after=()):
    def run(*args):
        if space == pltpu.HBM:
            args = [pltpu.with_memory_space_constraint(a, space) for a in args]
        specs = [pl.BlockSpec(memory_space=space)] * len(args)
        specs += [pl.BlockSpec(memory_space=pl.ANY)] * len(after)
        args = (*args, *after)
        return pl.pallas_call(
            kernel,
            out_shape=tuple(outs),
            in_specs=specs,
            out_specs=tuple(pl.BlockSpec(memory_space=pltpu.VMEM) for _ in outs),
            scratch_shapes=list(scratch),
            compiler_params=pltpu.CompilerParams(vmem_limit_bytes=VMEM_LIMIT),
            cost_estimate=pl.CostEstimate(
                flops=WEIGHTS.get(name, 0) * 10**7, bytes_accessed=0, transcendentals=0
            ),
        )(*args)

    return run


def swap(x, axis, size, bit):
    return lax.ppermute(x, axis, [(i, i ^ bit) for i in range(size)])


def hop(x, sizes, step):
    size, copies = sizes["seq"], sizes["replica"]
    pairs = []
    for copy in range(copies):
        for place in range(size):
            to = (copy ^ 1 if copies % 2 == 0 else copy, place)
            for low in (step, size - 2 - step):
                if place in (low, low + 1):
                    to = (copy, 2 * low + 1 - place)
            pairs.append((copy * size + place, to[0] * size + to[1]))
    return lax.ppermute(x, ("replica", "seq"), pairs)


def pass_kernel(*refs):
    got_ref, base_ref, decay_ref = refs[:3]
    refs[-1][...] = decay_ref[...] * got_ref[...] + base_ref[...]


def pass_on(got, base, decay, after, name):
    return call(pass_kernel, [jax.ShapeDtypeStruct(base.shape, F32)], name=name, after=after)(
        got, base, decay
    )[0]


def chain(sizes, mine, made, decay, work):
    chunks = len(mine)
    size = sizes["seq"]
    if size == 1:
        for k in sorted(work):
            work[k](())
        return [(x, x, x) for x in mine]
    if size % 2:
        raise NotImplementedError
    index = lax.axis_index("seq")
    place = jnp.minimum(index, size - 1 - index)
    middle = size // 2 - 1
    got = {(0, c): hop(mine[c], sizes, 0) for c in range(chunks)}
    steps = [
        (at + c + (1 if at > middle else 0), at, c)
        for at in range(1, size - 1)
        for c in range(chunks)
    ]
    token = ()
    for count, (_, at, c) in enumerate(sorted(steps)):
        if count in work:
            token = work[count](token)
        if at > middle and c > 2:
            token = (*token, got[at, c - 2 - 1])
        base = mine[c] if at <= middle else made["factors"][5 + c]
        pay = pass_on(got[at - 1, c], base, decay, token, f"pass{min(count, 7)}")
        got[at, c] = hop(pay, sizes, at)
        token = (pay,)
    for k in sorted(work):
        if k >= len(steps):
            token = work[k](token)
    states = []
    for c in range(chunks):
        first, second, last = got[0, c], got[middle, c], got[size - 2, c]
        for at in range(1, middle):
            first = jnp.where(place == at + 1, got[at, c], first)
        for at in range(middle + 1, size - 2):
            second = jnp.where(place == size - 2 - at, got[at, c], second)
        states.append((first, second, last))
    return states


def sum_terms(x, later, axis, size):
    if size == 1:
        return [x]
    if size == 4:
        return [x, swap(x, axis, size, 1)] + [swap(later, axis, size, bit) for bit in (2, 3)]
    if size & (size - 1):
        return [lax.psum(x, axis)]
    bit = 1
    while 2 * bit < size:
        x = x + swap(x, axis, size, bit)
        bit *= 2
    return [x, swap(x, axis, size, bit)]


def small_terms(x, axes, sizes, hooks):
    bits = [(axis, 1 << k) for axis in axes for k in range(sizes[axis].bit_length() - 1)]
    if any(sizes[axis] & (sizes[axis] - 1) for axis in axes):
        x, bits = lax.psum(x, tuple(axes)), []
    for count, (axis, bit) in enumerate(bits):
        theirs = swap(x, axis, sizes[axis], bit)
        if count == len(bits) - 1:
            break
        x = call(add_kernel, [jax.ShapeDtypeStruct(x.shape, F32)], name=f"add{count}")(x, theirs)[0]
        if count < len(hooks):
            hooks[count]((x,))
    for hook in hooks[max(len(bits) - 1, 0) :]:
        hook((x,))
    return [x, theirs] if bits else [x]


def shards(sizes, values, gate_in, in_b, in_c, step_sizes, log_rates, skip_gain, grad_out):
    like = jax.ShapeDtypeStruct
    length, channels = values.shape[1:]
    heads = step_sizes.shape[1]
    state = in_b.shape[2]
    seq = sizes["seq"]
    rows = state // CHUNKS
    wide = like((length, channels), F32)
    wide_b = like((length, channels), BF16)
    share = like((length, state), F32)
    small = like((heads, length), F32)
    row = like((1, channels), F32)
    piece = like((rows, channels), F32)
    maps = like((length, state), BF16)

    out = call(
        functools.partial(states_kernel, seq),
        [wide_b, wide_b, wide_b, maps, maps, small, small, row, row, like((1, heads), F32)]
        + [piece] * CHUNKS,
        [
            pltpu.VMEM((heads, length), F32),
            pltpu.VMEM((1, heads), F32),
            pltpu.SemaphoreType.DMA((8,)),
        ],
        space=pltpu.HBM,
    )(
        values[0], gate_in[0], grad_out[0], in_b[0], in_c[0], step_sizes[0],
        log_rates.reshape(1, heads), skip_gain.reshape(1, heads),
    )
    vals, gate, grad, block_b, block_c, cumulative, negative, decay, slope, skip = out[:10]
    mine = out[10:]

    made = {}

    def intra(after):
        made["intra"] = call(
            intra_kernel,
            [wide, wide, share, share],
            [
                pltpu.VMEM((channels, length), BF16),
                pltpu.VMEM((channels, length), F32),
                pltpu.VMEM((length, length), F32),
            ],
            name="intra",
        )(vals, gate, grad, block_b, block_c, cumulative)
        return (made["intra"][2],)

    def factors(after):
        made["factors"] = call(
            functools.partial(factors_kernel, seq),
            [wide_b] * 3 + [like((state, channels), F32)] * 2 + [piece] * CHUNKS,
            name="factors",
        )(vals, gate, grad, block_b, block_c, cumulative, *(after if after else made["intra"][2:3]))
        return made["factors"][5:6]

    def prepare(after):
        made["prepare"] = call(
            prepare_kernel,
            [wide] * 6 + [small, like((2, heads), F32)],
            name="prepare",
        )(
            vals, gate, grad, cumulative, skip,
            *made["intra"][:2], *(after if after else made["intra"][2:3]),
        )
        return (made["prepare"][-1],)

    sums = max(seq - 2, 0) * CHUNKS
    states = chain(sizes, mine, made, decay, {0: intra, 1: factors, max(sums - 2, 2): prepare})
    sum_b, sum_c = made["intra"][2:]
    high, low, scaled, q, r = made["factors"][:5]
    coef, mamba, inner, growth, fall, grad_y, grad_cum, parts = made["prepare"]

    rate_row = jnp.zeros((1, channels), F32)
    terms, counts = [], []
    for i in range(PARTS):
        final = i == PARTS - 1
        count = CHUNKS // PARTS
        own = [x for group in states[i * count : (i + 1) * count] for x in group]
        rate_row = call(
            functools.partial(rate_kernel, seq, count, i * rows * count, heads, final),
            [like((2, heads), F32) if final else row],
            name=f"rate{i}",
        )(*own, q, r, slope, rate_row, parts)[0]
        share_of = call(
            functools.partial(share_kernel, seq, count, i * rows * count),
            [like((length, 2 * rows * count), F32)],
            name=f"share{i}",
            after=(rate_row,),
        )(*own, high, low, scaled, sum_b, sum_c)[0]
        if not final:
            own = sum_terms(share_of, share_of, "tensor", sizes["tensor"])
            terms += call(sum_kernel, [like(share_of.shape, F32)], name="sum")(*own)
            counts.append(1)

    def exchange(after):
        later = call(copy_kernel, [like(share_of.shape, F32)], name="later", after=after)(share_of)[0]
        made["share"] = sum_terms(share_of, later, "tensor", sizes["tensor"])

    def rest(after):
        made["rest"] = call(
            functools.partial(rest_kernel, seq, CHUNKS),
            [like((1, length, channels), BF16)] * 2 + [like((1, heads, length), F32)],
            name="rest",
            after=(*after, *terms),
        )(
            *(x for group in states for x in group),
            vals, block_b, block_c, coef, mamba, inner, growth, fall, grad_y, grad_cum, decay, negative,
        )

    own = small_terms(rate_row, ("replica", "seq"), sizes, (exchange, rest))
    for group in (made["share"], own):
        terms += group
        counts.append(len(group))
    grad_values, grad_gate, grad_steps = made["rest"]
    grad_b, grad_c, rate_sum, skip_sum = call(
        functools.partial(last_kernel, tuple(counts)),
        [like((1, length, state), F32)] * 2 + [like((1, heads), F32)] * 2,
    )(*terms)
    return (
        grad_values,
        grad_gate,
        grad_b,
        grad_c,
        grad_steps,
        rate_sum.reshape(heads),
        skip_sum.reshape(heads),
    )


def solution(mesh):
    in_specs = (
        P("replica", "seq", "tensor"),
        P("replica", "seq", "tensor"),
        P("replica", "seq", None),
        P("replica", "seq", None),
        P("replica", "tensor", "seq"),
        P("tensor"),
        P("tensor"),
        P("replica", "seq", "tensor"),
    )
    out_specs = (
        P("replica", "seq", "tensor"),
        P("replica", "seq", "tensor"),
        P("replica", "seq", None),
        P("replica", "seq", None),
        P("replica", "tensor", "seq"),
        P("tensor"),
        P("tensor"),
    )
    body = functools.partial(shards, dict(mesh.shape))
    return jax.shard_map(body, mesh=mesh, in_specs=in_specs, out_specs=out_specs, check_vma=False)
```

```python
import functools

import jax
import jax.numpy as jnp
from jax import lax
from jax.experimental import pallas as pl
from jax.experimental.pallas import tpu as pltpu
from jax.sharding import PartitionSpec as P

F32 = jnp.float32
BF16 = jnp.bfloat16
VMEM_LIMIT = 24 * 1024 * 1024
LANES = 256
CHUNKS = 4
PARTS = 2
WEIGHTS = {'pass4': 30, 'pass5': 10, 'pass6': 300, 'pass7': 30, 'rate0': 30, 'rate1': 10, 'later': 30, 'sum': 100, 'add1': 100, 'rest': 30}


def split(x, parts):
    terms = []
    for _ in range(parts - 1):
        term = x.astype(BF16)
        terms.append(term)
        x = x - term.astype(F32)
    terms.append(x.astype(BF16))
    return terms


def mm(a, b):
    return lax.dot_general(a, b, (((1,), (0,)), ((), ())), preferred_element_type=F32)


def mm_nt(a, b):
    return lax.dot_general(a, b, (((1,), (1,)), ((), ())), preferred_element_type=F32)


def mm_tn(a, b):
    return lax.dot_general(a, b, (((0,), (0,)), ((), ())), preferred_element_type=F32)


def iota(shape, dim):
    return lax.broadcasted_iota(jnp.int32, shape, dim)


def to_column(row):
    n = row.shape[1]
    eye = iota((n, n), 0) == iota((n, n), 1)
    return jnp.sum(jnp.where(eye, row, 0.0), axis=1, keepdims=True)


def to_row(column):
    n = column.shape[0]
    eye = iota((n, n), 0) == iota((n, n), 1)
    return jnp.sum(jnp.where(eye, column, 0.0), axis=0, keepdims=True)


def head_map(heads, width, first, lanes):
    low = iota((heads, lanes), 0) * width
    channel = iota((heads, lanes), 1) + first
    return (channel >= low) & (channel < low + width)


def spread_map(heads, width, first, lanes):
    one = jnp.where(head_map(heads, width, first, lanes), 1.0, 0.0).astype(BF16)
    return jnp.concatenate([one, one, one], axis=0)


def rows_of_three(per_head):
    return jnp.concatenate(split(per_head, 3), axis=0)


def spread(three, first, lanes, width):
    heads = three.shape[0] // 3
    return mm_tn(three, spread_map(heads, width, first, lanes))


def scan_tokens(per_head, backward):
    heads, length = per_head.shape
    source = iota((length, length), 0)
    target = iota((length, length), 1)
    keep = source >= target if backward else source <= target
    sums = mm(rows_of_three(per_head), jnp.where(keep, 1.0, 0.0).astype(BF16))
    return sums[:heads] + sums[heads : 2 * heads] + sums[2 * heads :]


def channel_row(column, heads, width, first):
    mine = head_map(heads, width, first, LANES)
    return jnp.sum(jnp.where(mine, column, 0.0), axis=0, keepdims=True)


def head_column(row, heads, width, first):
    mine = head_map(heads, width, first, LANES)
    return jnp.sum(jnp.where(mine, row, 0.0), axis=1, keepdims=True)


def gate_parts(gate, grad):
    wide = gate.astype(F32)
    sigmoid = 1.0 / (1.0 + jnp.exp(-wide))
    return wide, sigmoid, grad.astype(F32) * (wide * sigmoid)


def put_rows(refs, here, value):
    start = 0
    for ref in refs:
        rows = ref.shape[0]
        ref[:, here] = value[start : start + rows]
        start += rows


def states_kernel(size, *refs):
    sources, outs, (steps_ref, lr_ref, sems) = refs[:8], refs[8:-3], refs[-3:]
    v_ref, gate_ref, go_ref, b_ref, c_ref = outs[:5]
    cum_ref, neg_ref, decay_ref, slope_ref, skip_ref = outs[5:10]
    mine_refs = outs[10:]
    targets = (v_ref, gate_ref, go_ref, b_ref, c_ref, steps_ref, lr_ref, skip_ref)
    copies = [
        pltpu.make_async_copy(source, target, sems.at[i])
        for i, (source, target) in enumerate(zip(sources, targets))
    ]
    for i in (6, 5, 3, 4, 0, 1, 2, 7):
        copies[i].start()
    copies[6].wait()
    copies[5].wait()
    length, channels = v_ref.shape
    heads = steps_ref.shape[0]
    width = channels // heads
    rates = jnp.exp(to_column(lr_ref[...]))
    cumulative = scan_tokens(-rates * steps_ref[...], False)
    total = cumulative[:, -1:]
    decay = jnp.exp(total)
    cum_ref[...] = cumulative
    neg_ref[...] = jnp.broadcast_to(-rates, (heads, length))
    for first in range(0, channels, LANES):
        here = pl.ds(first, LANES)
        decay_ref[:, here] = channel_row(decay, heads, width, first)
        slope_ref[:, here] = channel_row(total * decay, heads, width, first)

    def local():
        copies[3].wait()
        b_t = b_ref[...].astype(F32).T.astype(BF16)
        fall = rows_of_three(jnp.exp(total - cumulative))
        copies[0].wait()
        for first in range(0, channels, LANES):
            here = pl.ds(first, LANES)
            scaled = spread(fall, first, LANES, width) * v_ref[:, here].astype(F32)
            put_rows(mine_refs, here, mm(b_t, scaled.astype(BF16)))
        for i in (1, 2, 4, 7):
            copies[i].wait()

    def pulled():
        copies[4].wait()
        c_t = c_ref[...].astype(F32).T.astype(BF16)
        growth = rows_of_three(jnp.exp(cumulative))
        copies[1].wait()
        copies[2].wait()
        for first in range(0, channels, LANES):
            here = pl.ds(first, LANES)
            _, _, grad_y = gate_parts(gate_ref[:, here], go_ref[:, here])
            high, low = split(spread(growth, first, LANES, width) * grad_y, 2)
            put_rows(mine_refs, here, mm(c_t, high) + mm(c_t, low))
        for i in (0, 3, 7):
            copies[i].wait()

    if size == 1:
        local()
    else:
        lower = lax.axis_index("seq") < size // 2
        pl.when(lower)(local)
        pl.when(jnp.logical_not(lower))(pulled)


def intra_kernel(
    v_ref, gate_ref, go_ref, b_ref, c_ref, cum_ref,
    intra_ref, inner_ref, sum_b_ref, sum_c_ref, grad_t_ref, inner_t_ref, acc_ref,
):
    length, channels = v_ref.shape
    heads = cum_ref.shape[0]
    width = channels // heads
    half = length // 2
    pair = 2 * width
    cumulative = cum_ref[...]
    columns = cumulative.T
    scores = mm_nt(c_ref[...], b_ref[...])
    causal = iota((half, half), 0) >= iota((half, half), 1)
    left = iota((1, pair), 1) < width
    acc_ref[...] = jnp.zeros_like(acc_ref)

    def blocks(x):
        return x[:half, :half], x[half:, :half], x[half:, half:]

    scores_00, scores_10, scores_11 = blocks(scores)
    for first in range(0, channels, pair):
        here = pl.ds(first, pair)
        _, _, grad_y = gate_parts(gate_ref[:, here], go_ref[:, here])
        grad_t_ref[here, :] = grad_y.T.astype(BF16)
        vals = v_ref[:, here]
        pieces = []
        for side in range(2):
            head = first // width + side
            own = left if side == 0 else jnp.logical_not(left)
            row = cumulative[head : head + 1, :]
            column = columns[:, head : head + 1]
            row_0, row_1 = row[:, :half], row[:, half:]
            column_0, column_1 = column[:half], column[half:]
            decay_00 = jnp.exp(jnp.where(causal, column_0 - row_0, -1e30))
            decay_10 = jnp.exp(column_1 - row_0)
            decay_11 = jnp.exp(jnp.where(causal, column_1 - row_1, -1e30))
            mix_00 = (scores_00 * decay_00).astype(BF16)
            mix_10 = (scores_10 * decay_10).astype(BF16)
            mix_11 = (scores_11 * decay_11).astype(BF16)
            low_rows = jnp.concatenate([mix_10, mix_11], axis=1)
            pieces.append((mm(mix_00, vals[:half]), mm(low_rows, vals)))
            head_grad = jnp.where(own, grad_y, 0.0).astype(BF16)
            mixed_0 = mm_nt(head_grad[:half], vals[:half])
            mixed_1 = mm_nt(head_grad[half:], vals)
            acc_ref[:half, :half] += mixed_0 * decay_00
            acc_ref[half:, :half] += mixed_1[:, :half] * decay_10
            acc_ref[half:, half:] += mixed_1[:, half:] * decay_11
            mine = pl.ds(first + side * width, width)
            grad_t = grad_t_ref[mine, :]
            inner_t_ref[mine, :half] = mm(grad_t[:, :half], mix_00) + mm(grad_t[:, half:], mix_10)
            inner_t_ref[mine, half:] = mm(grad_t[:, half:], mix_11)
        intra_ref[:half, here] = jnp.where(left, pieces[0][0], pieces[1][0])
        intra_ref[half:, here] = jnp.where(left, pieces[0][1], pieces[1][1])
        inner_ref[:, here] = inner_t_ref[here, :].T
    shares = acc_ref[...]
    high, low = split(shares, 2)
    sum_c_ref[...] = mm(high, b_ref[...]) + mm(low, b_ref[...])
    high, low = split(shares.T, 2)
    sum_b_ref[...] = mm(high, c_ref[...]) + mm(low, c_ref[...])


def factors_kernel(
    size, v_ref, gate_ref, go_ref, b_ref, c_ref, cum_ref, after_ref,
    high_ref, low_ref, scaled_ref, q_ref, r_ref, *other_refs,
):
    length, channels = v_ref.shape
    heads = cum_ref.shape[0]
    width = channels // heads
    cumulative = cum_ref[...]
    left_over = cumulative[:, -1:] - cumulative
    growth = rows_of_three(jnp.exp(cumulative))
    fall = rows_of_three(jnp.exp(left_over))
    growth_slope = rows_of_three(cumulative * jnp.exp(cumulative))
    fall_slope = rows_of_three(left_over * jnp.exp(left_over))
    b_t = b_ref[...].astype(F32).T.astype(BF16)
    c_t = c_ref[...].astype(F32).T.astype(BF16)
    for first in range(0, channels, LANES):
        here = pl.ds(first, LANES)
        _, _, grad_y = gate_parts(gate_ref[:, here], go_ref[:, here])
        vals = v_ref[:, here].astype(F32)
        high, low = split(spread(growth, first, LANES, width) * grad_y, 2)
        high_ref[:, here] = high
        low_ref[:, here] = low
        scaled_ref[:, here] = (spread(fall, first, LANES, width) * vals).astype(BF16)
        high, low = split(spread(growth_slope, first, LANES, width) * grad_y, 2)
        q_ref[:, here] = mm(c_t, high) + mm(c_t, low)
        high, low = split(spread(fall_slope, first, LANES, width) * vals, 2)
        r_ref[:, here] = mm(b_t, high) + mm(b_t, low)

    def pulled():
        put_rows(other_refs, slice(None), mm(c_t, high_ref[...]) + mm(c_t, low_ref[...]))

    def local():
        put_rows(other_refs, slice(None), mm(b_t, scaled_ref[...]))

    if size == 1:
        pulled()
    else:
        lower = lax.axis_index("seq") < size // 2
        pl.when(lower)(pulled)
        pl.when(jnp.logical_not(lower))(local)


def prepare_kernel(
    v_ref, gate_ref, go_ref, cum_ref, skip_ref, intra_ref, in_inner_ref, after_ref,
    coef_ref, mamba_ref, inner_ref, growth_ref, fall_ref, gy_ref, gcum_ref, parts_ref,
):
    length, channels = v_ref.shape
    heads = cum_ref.shape[0]
    width = channels // heads
    cumulative = cum_ref[...]
    growth_three = rows_of_three(jnp.exp(cumulative))
    fall_three = rows_of_three(jnp.exp(cumulative[:, -1:] - cumulative))
    skip_column = to_column(skip_ref[...])
    grad_cum = jnp.zeros((heads, length), F32)
    skip_part = jnp.zeros((heads, 1), F32)
    for first in range(0, channels, LANES):
        here = pl.ds(first, LANES)
        wide, sigmoid, grad_y = gate_parts(gate_ref[:, here], go_ref[:, here])
        vals = v_ref[:, here].astype(F32)
        skip = channel_row(skip_column, heads, width, first)
        growth_ref[:, here] = spread(growth_three, first, LANES, width)
        fall_ref[:, here] = spread(fall_three, first, LANES, width)
        gy_ref[:, here] = grad_y
        coef_ref[:, here] = go_ref[:, here].astype(F32) * sigmoid * (1.0 + wide * (1.0 - sigmoid))
        intra = intra_ref[:, here]
        inner = in_inner_ref[:, here]
        mamba_ref[:, here] = intra + skip * vals
        inner_ref[:, here] = inner + skip * grad_y
        high, low = split(grad_y.astype(BF16).astype(F32) * intra - vals * inner, 2)
        head_rows = jnp.where(head_map(heads, width, first, LANES), 1.0, 0.0).astype(BF16)
        grad_cum = grad_cum + mm_nt(head_rows, high) + mm_nt(head_rows, low)
        skip_row = jnp.sum(grad_y * vals, axis=0, keepdims=True)
        skip_part = skip_part + head_column(skip_row, heads, width, first)
    gcum_ref[...] = grad_cum
    rate_part = jnp.sum(grad_cum * cumulative, axis=1, keepdims=True)
    parts_ref[...] = jnp.concatenate([to_row(rate_part), to_row(skip_part)], axis=0)


def pick(size, first, second, last):
    if size == 1:
        return jnp.zeros_like(first), jnp.zeros_like(first)
    if size % 2:
        return first, second
    index = lax.axis_index("seq")
    lower = index < size // 2
    edge = jnp.logical_or(index == 0, index == size - 1)
    first = jnp.where(edge, 0.0, first)
    second = jnp.where(edge, last, second)
    return jnp.where(lower, first, second), jnp.where(lower, second, first)


def picked(size, states, here):
    both = [pick(size, *(ref[:, here] for ref in state)) for state in states]
    return jnp.concatenate([x[0] for x in both], axis=0), jnp.concatenate([x[1] for x in both], axis=0)


def rate_kernel(size, pieces, start, heads, final, *refs):
    states, refs = [refs[3 * i : 3 * i + 3] for i in range(pieces)], refs[3 * pieces :]
    q_ref, r_ref, slope_ref, row_ref, parts_ref, out_ref = *refs[:5], refs[-1]
    rows, channels = pieces * states[0][0].shape[0], q_ref.shape[1]
    here = slice(start, start + rows)
    rate_part = jnp.zeros((heads, 1), F32)
    for begin in range(0, channels, LANES):
        lanes = pl.ds(begin, LANES)
        entering, after = picked(size, states, lanes)
        terms = entering * q_ref[here, lanes] + after * (
            r_ref[here, lanes] + slope_ref[:, lanes] * entering
        )
        row = row_ref[:, lanes] + jnp.sum(terms, axis=0, keepdims=True)
        if final:
            rate_part = rate_part + head_column(row, heads, channels // heads, begin)
        else:
            out_ref[:, lanes] = row
    if final:
        base = parts_ref[...]
        out_ref[...] = jnp.concatenate([base[:1] + to_row(rate_part), base[1:]], axis=0)


def share_kernel(size, pieces, start, *refs):
    states, refs = [refs[3 * i : 3 * i + 3] for i in range(pieces)], refs[3 * pieces :]
    high_ref, low_ref, scaled_ref, sum_b_ref, sum_c_ref = refs[:5]
    rows, channels = pieces * states[0][0].shape[0], scaled_ref.shape[1]
    here = slice(start, start + rows)
    grad_b = sum_b_ref[:, here]
    grad_c = sum_c_ref[:, here]
    pairs_b = pairs_c = jnp.zeros((scaled_ref.shape[0], 2 * rows), F32)
    for begin in range(0, channels, LANES):
        lanes = pl.ds(begin, LANES)
        entering, after = picked(size, states, lanes)
        enter_high, enter_low = split(entering, 2)
        after_high, after_low = split(after, 2)
        high, low, scaled = high_ref[:, lanes], low_ref[:, lanes], scaled_ref[:, lanes]
        pairs_c = pairs_c + mm_nt(high, jnp.concatenate([enter_low, enter_high], axis=0))
        pairs_b = pairs_b + mm_nt(scaled, jnp.concatenate([after_low, after_high], axis=0))
        grad_c = grad_c + mm_nt(low, enter_high)
    grad_b = grad_b + (pairs_b[:, :rows] + pairs_b[:, rows:])
    grad_c = grad_c + (pairs_c[:, :rows] + pairs_c[:, rows:])
    refs[-1][...] = jnp.concatenate([grad_b, grad_c], axis=1)


def rest_kernel(size, pieces, *refs):
    states, refs = [refs[3 * i : 3 * i + 3] for i in range(pieces)], refs[3 * pieces :]
    (
        v_ref, b_ref, c_ref, coef_ref, mamba_ref, inner_ref, growth_ref, fall_ref, gy_ref,
        gcum_ref, decay_ref, neg_ref, *_, gv_ref, gg_ref, gs_ref,
    ) = refs
    length, channels = v_ref.shape
    heads = gcum_ref.shape[0]
    width = channels // heads
    twice_b, twice_c = (jnp.concatenate([ref[...], ref[...]], axis=1) for ref in (b_ref, c_ref))
    grad_cum = gcum_ref[...]
    grad_total = jnp.zeros((heads, 1), F32)
    for first in range(0, channels, LANES):
        here = pl.ds(first, LANES)
        entering, after = picked(size, states, here)
        inter = growth_ref[:, here] * mm(twice_c, jnp.concatenate(split(entering, 2), axis=0))
        outer = fall_ref[:, here] * mm(twice_b, jnp.concatenate(split(after, 2), axis=0))
        gg_ref[0, :, here] = (coef_ref[:, here] * (mamba_ref[:, here] + inter)).astype(BF16)
        gv_ref[0, :, here] = (inner_ref[:, here] + outer).astype(BF16)
        pulled = v_ref[:, here].astype(F32) * outer
        high, low = split(gy_ref[:, here] * inter - pulled, 2)
        head_rows = jnp.where(head_map(heads, width, first, LANES), 1.0, 0.0).astype(BF16)
        grad_cum = grad_cum + mm_nt(head_rows, high) + mm_nt(head_rows, low)
        total_row = jnp.sum(pulled, axis=0, keepdims=True) + decay_ref[:, here] * jnp.sum(
            after * entering, axis=0, keepdims=True
        )
        grad_total = grad_total + head_column(total_row, heads, width, first)
    gs_ref[0] = neg_ref[...] * (scan_tokens(grad_cum, True) + grad_total)


def tree(values):
    while len(values) > 1:
        values = [sum(values[i + 1 : i + 2], values[i]) for i in range(0, len(values), 2)]
    return values[0]


def copy_kernel(x_ref, *refs):
    refs[-1][...] = x_ref[...]


def add_kernel(x_ref, y_ref, *refs):
    refs[-1][...] = x_ref[...] + y_ref[...]


def sum_kernel(*refs):
    refs[-1][...] = tree([ref[...] for ref in refs[:-1]])


def last_kernel(counts, *refs):
    refs, (gb_ref, gc_ref, rate_ref, skip_ref) = refs[:-4], refs[-4:]
    sums = []
    for count in counts:
        sums.append(tree([ref[...] for ref in refs[:count]]))
        refs = refs[count:]
    *shares, small = sums
    start = 0
    for both in shares:
        rows = both.shape[1] // 2
        gb_ref[0, :, start : start + rows] = both[:, :rows]
        gc_ref[0, :, start : start + rows] = both[:, rows:]
        start += rows
    rate_ref[...] = small[:1]
    skip_ref[...] = small[1:]


def call(kernel, outs, scratch=(), name="", space=pltpu.VMEM, after=()):
    def run(*args):
        if space == pltpu.HBM:
            args = [pltpu.with_memory_space_constraint(a, space) for a in args]
        specs = [pl.BlockSpec(memory_space=space)] * len(args)
        specs += [pl.BlockSpec(memory_space=pl.ANY)] * len(after)
        args = (*args, *after)
        return pl.pallas_call(
            kernel,
            out_shape=tuple(outs),
            in_specs=specs,
            out_specs=tuple(pl.BlockSpec(memory_space=pltpu.VMEM) for _ in outs),
            scratch_shapes=list(scratch),
            compiler_params=pltpu.CompilerParams(vmem_limit_bytes=VMEM_LIMIT),
            cost_estimate=pl.CostEstimate(
                flops=WEIGHTS.get(name, 0) * 10**7, bytes_accessed=0, transcendentals=0
            ),
        )(*args)

    return run


def swap(x, axis, size, bit):
    return lax.ppermute(x, axis, [(i, i ^ bit) for i in range(size)])


def hop(x, sizes, step):
    size, copies = sizes["seq"], sizes["replica"]
    pairs = []
    for copy in range(copies):
        for place in range(size):
            to = (copy ^ 1 if copies % 2 == 0 else copy, place)
            for low in (step, size - 2 - step):
                if place in (low, low + 1):
                    to = (copy, 2 * low + 1 - place)
            pairs.append((copy * size + place, to[0] * size + to[1]))
    return lax.ppermute(x, ("replica", "seq"), pairs)


def pass_kernel(*refs):
    got_ref, base_ref, decay_ref = refs[:3]
    refs[-1][...] = decay_ref[...] * got_ref[...] + base_ref[...]


def pass_on(got, base, decay, after, name):
    return call(pass_kernel, [jax.ShapeDtypeStruct(base.shape, F32)], name=name, after=after)(
        got, base, decay
    )[0]


def chain(sizes, mine, made, decay, work):
    chunks = len(mine)
    size = sizes["seq"]
    if size == 1:
        for k in sorted(work):
            work[k](())
        return [(x, x, x) for x in mine]
    if size % 2:
        raise NotImplementedError
    index = lax.axis_index("seq")
    place = jnp.minimum(index, size - 1 - index)
    middle = size // 2 - 1
    got = {(0, c): hop(mine[c], sizes, 0) for c in range(chunks)}
    steps = [
        (at + c + (1 if at > middle else 0), at, c)
        for at in range(1, size - 1)
        for c in range(chunks)
    ]
    token = ()
    for count, (_, at, c) in enumerate(sorted(steps)):
        if count in work:
            token = work[count](token)
        if at > middle and c > 2:
            token = (*token, got[at, c - 2 - 1])
        base = mine[c] if at <= middle else made["factors"][5 + c]
        pay = pass_on(got[at - 1, c], base, decay, token, f"pass{min(count, 7)}")
        got[at, c] = hop(pay, sizes, at)
        token = (pay,)
    for k in sorted(work):
        if k >= len(steps):
            token = work[k](token)
    states = []
    for c in range(chunks):
        first, second, last = got[0, c], got[middle, c], got[size - 2, c]
        for at in range(1, middle):
            first = jnp.where(place == at + 1, got[at, c], first)
        for at in range(middle + 1, size - 2):
            second = jnp.where(place == size - 2 - at, got[at, c], second)
        states.append((first, second, last))
    return states


def sum_terms(x, later, axis, size):
    if size == 1:
        return [x]
    if size == 4:
        return [x, swap(x, axis, size, 1)] + [swap(later, axis, size, bit) for bit in (2, 3)]
    if size & (size - 1):
        return [lax.psum(x, axis)]
    bit = 1
    while 2 * bit < size:
        x = x + swap(x, axis, size, bit)
        bit *= 2
    return [x, swap(x, axis, size, bit)]


def small_terms(x, axes, sizes, hooks):
    bits = [(axis, 1 << k) for axis in axes for k in range(sizes[axis].bit_length() - 1)]
    if any(sizes[axis] & (sizes[axis] - 1) for axis in axes):
        x, bits = lax.psum(x, tuple(axes)), []
    for count, (axis, bit) in enumerate(bits):
        theirs = swap(x, axis, sizes[axis], bit)
        if count == len(bits) - 1:
            break
        x = call(add_kernel, [jax.ShapeDtypeStruct(x.shape, F32)], name=f"add{count}")(x, theirs)[0]
        if count < len(hooks):
            hooks[count]((x,))
    for hook in hooks[max(len(bits) - 1, 0) :]:
        hook((x,))
    return [x, theirs] if bits else [x]


def shards(sizes, values, gate_in, in_b, in_c, step_sizes, log_rates, skip_gain, grad_out):
    like = jax.ShapeDtypeStruct
    length, channels = values.shape[1:]
    heads = step_sizes.shape[1]
    state = in_b.shape[2]
    seq = sizes["seq"]
    rows = state // CHUNKS
    wide = like((length, channels), F32)
    wide_b = like((length, channels), BF16)
    share = like((length, state), F32)
    small = like((heads, length), F32)
    row = like((1, channels), F32)
    piece = like((rows, channels), F32)
    maps = like((length, state), BF16)

    out = call(
        functools.partial(states_kernel, seq),
        [wide_b, wide_b, wide_b, maps, maps, small, small, row, row, like((1, heads), F32)]
        + [piece] * CHUNKS,
        [
            pltpu.VMEM((heads, length), F32),
            pltpu.VMEM((1, heads), F32),
            pltpu.SemaphoreType.DMA((8,)),
        ],
        space=pltpu.HBM,
    )(
        values[0], gate_in[0], grad_out[0], in_b[0], in_c[0], step_sizes[0],
        log_rates.reshape(1, heads), skip_gain.reshape(1, heads),
    )
    vals, gate, grad, block_b, block_c, cumulative, negative, decay, slope, skip = out[:10]
    mine = out[10:]

    made = {}

    def intra(after):
        made["intra"] = call(
            intra_kernel,
            [wide, wide, share, share],
            [
                pltpu.VMEM((channels, length), BF16),
                pltpu.VMEM((channels, length), F32),
                pltpu.VMEM((length, length), F32),
            ],
            name="intra",
        )(vals, gate, grad, block_b, block_c, cumulative)
        return factors((made["intra"][2],))

    def factors(after):
        made["factors"] = call(
            functools.partial(factors_kernel, seq),
            [wide_b] * 3 + [like((state, channels), F32)] * 2 + [piece] * CHUNKS,
            name="factors",
        )(vals, gate, grad, block_b, block_c, cumulative, *(after if after else made["intra"][2:3]))
        return made["factors"][5:6]

    def prepare(after):
        made["prepare"] = call(
            prepare_kernel,
            [wide] * 6 + [small, like((2, heads), F32)],
            name="prepare",
        )(
            vals, gate, grad, cumulative, skip,
            *made["intra"][:2], *(after if after else made["intra"][2:3]),
        )
        return (made["prepare"][-1],)

    sums = max(seq - 2, 0) * CHUNKS
    states = chain(sizes, mine, made, decay, {0: intra, max(sums - 2, 2): prepare})
    sum_b, sum_c = made["intra"][2:]
    high, low, scaled, q, r = made["factors"][:5]
    coef, mamba, inner, growth, fall, grad_y, grad_cum, parts = made["prepare"]

    rate_row = jnp.zeros((1, channels), F32)
    terms, counts = [], []
    for i in range(PARTS):
        final = i == PARTS - 1
        count = CHUNKS // PARTS
        own = [x for group in states[i * count : (i + 1) * count] for x in group]
        rate_row = call(
            functools.partial(rate_kernel, seq, count, i * rows * count, heads, final),
            [like((2, heads), F32) if final else row],
            name=f"rate{i}",
        )(*own, q, r, slope, rate_row, parts)[0]
        share_of = call(
            functools.partial(share_kernel, seq, count, i * rows * count),
            [like((length, 2 * rows * count), F32)],
            name=f"share{i}",
            after=(rate_row,),
        )(*own, high, low, scaled, sum_b, sum_c)[0]
        if not final:
            own = sum_terms(share_of, share_of, "tensor", sizes["tensor"])
            terms += call(sum_kernel, [like(share_of.shape, F32)], name="sum")(*own)
            counts.append(1)

    def exchange(after):
        later = call(copy_kernel, [like(share_of.shape, F32)], name="later", after=after)(share_of)[0]
        made["share"] = sum_terms(share_of, later, "tensor", sizes["tensor"])

    def rest(after):
        made["rest"] = call(
            functools.partial(rest_kernel, seq, CHUNKS),
            [like((1, length, channels), BF16)] * 2 + [like((1, heads, length), F32)],
            name="rest",
            after=(*after, *terms),
        )(
            *(x for group in states for x in group),
            vals, block_b, block_c, coef, mamba, inner, growth, fall, grad_y, grad_cum, decay, negative,
        )

    own = small_terms(rate_row, ("replica", "seq"), sizes, (exchange, rest))
    for group in (made["share"], own):
        terms += group
        counts.append(len(group))
    grad_values, grad_gate, grad_steps = made["rest"]
    grad_b, grad_c, rate_sum, skip_sum = call(
        functools.partial(last_kernel, tuple(counts)),
        [like((1, length, state), F32)] * 2 + [like((1, heads), F32)] * 2,
    )(*terms)
    return (
        grad_values,
        grad_gate,
        grad_b,
        grad_c,
        grad_steps,
        rate_sum.reshape(heads),
        skip_sum.reshape(heads),
    )


def solution(mesh):
    in_specs = (
        P("replica", "seq", "tensor"),
        P("replica", "seq", "tensor"),
        P("replica", "seq", None),
        P("replica", "seq", None),
        P("replica", "tensor", "seq"),
        P("tensor"),
        P("tensor"),
        P("replica", "seq", "tensor"),
    )
    out_specs = (
        P("replica", "seq", "tensor"),
        P("replica", "seq", "tensor"),
        P("replica", "seq", None),
        P("replica", "seq", None),
        P("replica", "tensor", "seq"),
        P("tensor"),
        P("tensor"),
    )
    body = functools.partial(shards, dict(mesh.shape))
    return jax.shard_map(body, mesh=mesh, in_specs=in_specs, out_specs=out_specs, check_vma=False)
```

```python
import functools

import jax
import jax.numpy as jnp
from jax import lax
from jax.experimental import pallas as pl
from jax.experimental.pallas import tpu as pltpu
from jax.sharding import PartitionSpec as P

F32 = jnp.float32
BF16 = jnp.bfloat16
VMEM_LIMIT = 24 * 1024 * 1024
LANES = 256
CHUNKS = 4
PARTS = 2
WEIGHTS = {'pass4': 30, 'pass5': 10, 'pass6': 300, 'pass7': 30, 'rate0': 30, 'rate1': 10, 'later': 30, 'sum': 100, 'add1': 100, 'rest': 30}


def split(x, parts):
    terms = []
    for _ in range(parts - 1):
        term = x.astype(BF16)
        terms.append(term)
        x = x - term.astype(F32)
    terms.append(x.astype(BF16))
    return terms


def mm(a, b):
    return lax.dot_general(a, b, (((1,), (0,)), ((), ())), preferred_element_type=F32)


def mm_nt(a, b):
    return lax.dot_general(a, b, (((1,), (1,)), ((), ())), preferred_element_type=F32)


def mm_tn(a, b):
    return lax.dot_general(a, b, (((0,), (0,)), ((), ())), preferred_element_type=F32)


def iota(shape, dim):
    return lax.broadcasted_iota(jnp.int32, shape, dim)


def to_column(row):
    n = row.shape[1]
    eye = iota((n, n), 0) == iota((n, n), 1)
    return jnp.sum(jnp.where(eye, row, 0.0), axis=1, keepdims=True)


def to_row(column):
    n = column.shape[0]
    eye = iota((n, n), 0) == iota((n, n), 1)
    return jnp.sum(jnp.where(eye, column, 0.0), axis=0, keepdims=True)


def head_map(heads, width, first, lanes):
    low = iota((heads, lanes), 0) * width
    channel = iota((heads, lanes), 1) + first
    return (channel >= low) & (channel < low + width)


def spread_map(heads, width, first, lanes):
    one = jnp.where(head_map(heads, width, first, lanes), 1.0, 0.0).astype(BF16)
    return jnp.concatenate([one, one, one], axis=0)


def rows_of_three(per_head):
    return jnp.concatenate(split(per_head, 3), axis=0)


def spread(three, first, lanes, width):
    heads = three.shape[0] // 3
    return mm_tn(three, spread_map(heads, width, first, lanes))


def scan_tokens(per_head, backward):
    heads, length = per_head.shape
    source = iota((length, length), 0)
    target = iota((length, length), 1)
    keep = source >= target if backward else source <= target
    sums = mm(rows_of_three(per_head), jnp.where(keep, 1.0, 0.0).astype(BF16))
    return sums[:heads] + sums[heads : 2 * heads] + sums[2 * heads :]


def channel_row(column, heads, width, first):
    mine = head_map(heads, width, first, LANES)
    return jnp.sum(jnp.where(mine, column, 0.0), axis=0, keepdims=True)


def head_column(row, heads, width, first):
    mine = head_map(heads, width, first, LANES)
    return jnp.sum(jnp.where(mine, row, 0.0), axis=1, keepdims=True)


def gate_parts(gate, grad):
    wide = gate.astype(F32)
    sigmoid = 1.0 / (1.0 + jnp.exp(-wide))
    return wide, sigmoid, grad.astype(F32) * (wide * sigmoid)


def put_rows(refs, here, value):
    start = 0
    for ref in refs:
        rows = ref.shape[0]
        ref[:, here] = value[start : start + rows]
        start += rows


def states_kernel(size, *refs):
    sources, outs, (steps_ref, lr_ref, sems) = refs[:8], refs[8:-3], refs[-3:]
    v_ref, gate_ref, go_ref, b_ref, c_ref = outs[:5]
    cum_ref, neg_ref, decay_ref, slope_ref, skip_ref = outs[5:10]
    mine_refs = outs[10:]
    targets = (v_ref, gate_ref, go_ref, b_ref, c_ref, steps_ref, lr_ref, skip_ref)
    copies = [
        pltpu.make_async_copy(source, target, sems.at[i])
        for i, (source, target) in enumerate(zip(sources, targets))
    ]
    for i in (6, 5, 3, 4, 0, 1, 2, 7):
        copies[i].start()
    copies[6].wait()
    copies[5].wait()
    length, channels = v_ref.shape
    heads = steps_ref.shape[0]
    width = channels // heads
    rates = jnp.exp(to_column(lr_ref[...]))
    cumulative = scan_tokens(-rates * steps_ref[...], False)
    total = cumulative[:, -1:]
    decay = jnp.exp(total)
    cum_ref[...] = cumulative
    neg_ref[...] = jnp.broadcast_to(-rates, (heads, length))
    for first in range(0, channels, LANES):
        here = pl.ds(first, LANES)
        decay_ref[:, here] = channel_row(decay, heads, width, first)
        slope_ref[:, here] = channel_row(total * decay, heads, width, first)

    def local():
        copies[3].wait()
        b_t = b_ref[...].astype(F32).T.astype(BF16)
        fall = rows_of_three(jnp.exp(total - cumulative))
        copies[0].wait()
        for first in range(0, channels, LANES):
            here = pl.ds(first, LANES)
            scaled = spread(fall, first, LANES, width) * v_ref[:, here].astype(F32)
            put_rows(mine_refs, here, mm(b_t, scaled.astype(BF16)))
        for i in (1, 2, 4, 7):
            copies[i].wait()

    def pulled():
        copies[4].wait()
        c_t = c_ref[...].astype(F32).T.astype(BF16)
        growth = rows_of_three(jnp.exp(cumulative))
        copies[1].wait()
        copies[2].wait()
        for first in range(0, channels, LANES):
            here = pl.ds(first, LANES)
            _, _, grad_y = gate_parts(gate_ref[:, here], go_ref[:, here])
            high, low = split(spread(growth, first, LANES, width) * grad_y, 2)
            put_rows(mine_refs, here, mm(c_t, high) + mm(c_t, low))
        for i in (0, 3, 7):
            copies[i].wait()

    if size == 1:
        local()
    else:
        lower = lax.axis_index("seq") < size // 2
        pl.when(lower)(local)
        pl.when(jnp.logical_not(lower))(pulled)


def intra_kernel(
    v_ref, gate_ref, go_ref, b_ref, c_ref, cum_ref,
    intra_ref, inner_ref, sum_b_ref, sum_c_ref, grad_t_ref, inner_t_ref, acc_ref,
):
    length, channels = v_ref.shape
    heads = cum_ref.shape[0]
    width = channels // heads
    half = length // 2
    pair = 2 * width
    cumulative = cum_ref[...]
    columns = cumulative.T
    scores = mm_nt(c_ref[...], b_ref[...])
    causal = iota((half, half), 0) >= iota((half, half), 1)
    left = iota((1, pair), 1) < width
    acc_ref[...] = jnp.zeros_like(acc_ref)

    def blocks(x):
        return x[:half, :half], x[half:, :half], x[half:, half:]

    scores_00, scores_10, scores_11 = blocks(scores)
    for first in range(0, channels, pair):
        here = pl.ds(first, pair)
        _, _, grad_y = gate_parts(gate_ref[:, here], go_ref[:, here])
        grad_t_ref[here, :] = grad_y.T.astype(BF16)
        vals = v_ref[:, here]
        pieces = []
        for side in range(2):
            head = first // width + side
            own = left if side == 0 else jnp.logical_not(left)
            row = cumulative[head : head + 1, :]
            column = columns[:, head : head + 1]
            row_0, row_1 = row[:, :half], row[:, half:]
            column_0, column_1 = column[:half], column[half:]
            decay_00 = jnp.exp(jnp.where(causal, column_0 - row_0, -1e30))
            decay_10 = jnp.exp(column_1 - row_0)
            decay_11 = jnp.exp(jnp.where(causal, column_1 - row_1, -1e30))
            mix_00 = (scores_00 * decay_00).astype(BF16)
            mix_10 = (scores_10 * decay_10).astype(BF16)
            mix_11 = (scores_11 * decay_11).astype(BF16)
            low_rows = jnp.concatenate([mix_10, mix_11], axis=1)
            pieces.append((mm(mix_00, vals[:half]), mm(low_rows, vals)))
            head_grad = jnp.where(own, grad_y, 0.0).astype(BF16)
            mixed_0 = mm_nt(head_grad[:half], vals[:half])
            mixed_1 = mm_nt(head_grad[half:], vals)
            acc_ref[:half, :half] += mixed_0 * decay_00
            acc_ref[half:, :half] += mixed_1[:, :half] * decay_10
            acc_ref[half:, half:] += mixed_1[:, half:] * decay_11
            mine = pl.ds(first + side * width, width)
            grad_t = grad_t_ref[mine, :]
            inner_t_ref[mine, :half] = mm(grad_t[:, :half], mix_00) + mm(grad_t[:, half:], mix_10)
            inner_t_ref[mine, half:] = mm(grad_t[:, half:], mix_11)
        intra_ref[:half, here] = jnp.where(left, pieces[0][0], pieces[1][0])
        intra_ref[half:, here] = jnp.where(left, pieces[0][1], pieces[1][1])
        inner_ref[:, here] = inner_t_ref[here, :].T
    shares = acc_ref[...]
    high, low = split(shares, 2)
    sum_c_ref[...] = mm(high, b_ref[...]) + mm(low, b_ref[...])
    high, low = split(shares.T, 2)
    sum_b_ref[...] = mm(high, c_ref[...]) + mm(low, c_ref[...])


def factors_kernel(
    size, v_ref, gate_ref, go_ref, b_ref, c_ref, cum_ref, after_ref,
    high_ref, low_ref, scaled_ref, q_ref, r_ref, *other_refs,
):
    length, channels = v_ref.shape
    heads = cum_ref.shape[0]
    width = channels // heads
    cumulative = cum_ref[...]
    left_over = cumulative[:, -1:] - cumulative
    growth = rows_of_three(jnp.exp(cumulative))
    fall = rows_of_three(jnp.exp(left_over))
    growth_slope = rows_of_three(cumulative * jnp.exp(cumulative))
    fall_slope = rows_of_three(left_over * jnp.exp(left_over))
    b_t = b_ref[...].astype(F32).T.astype(BF16)
    c_t = c_ref[...].astype(F32).T.astype(BF16)
    for first in range(0, channels, LANES):
        here = pl.ds(first, LANES)
        _, _, grad_y = gate_parts(gate_ref[:, here], go_ref[:, here])
        vals = v_ref[:, here].astype(F32)
        high, low = split(spread(growth, first, LANES, width) * grad_y, 2)
        high_ref[:, here] = high
        low_ref[:, here] = low
        scaled_ref[:, here] = (spread(fall, first, LANES, width) * vals).astype(BF16)
        high, low = split(spread(growth_slope, first, LANES, width) * grad_y, 2)
        q_ref[:, here] = mm(c_t, high) + mm(c_t, low)
        high, low = split(spread(fall_slope, first, LANES, width) * vals, 2)
        r_ref[:, here] = mm(b_t, high) + mm(b_t, low)

    def pulled():
        put_rows(other_refs, slice(None), mm(c_t, high_ref[...]) + mm(c_t, low_ref[...]))

    def local():
        put_rows(other_refs, slice(None), mm(b_t, scaled_ref[...]))

    if size == 1:
        pulled()
    else:
        lower = lax.axis_index("seq") < size // 2
        pl.when(lower)(pulled)
        pl.when(jnp.logical_not(lower))(local)


def prepare_kernel(
    v_ref, gate_ref, go_ref, cum_ref, skip_ref, intra_ref, in_inner_ref, after_ref,
    coef_ref, mamba_ref, inner_ref, growth_ref, fall_ref, gy_ref, gcum_ref, parts_ref,
):
    length, channels = v_ref.shape
    heads = cum_ref.shape[0]
    width = channels // heads
    cumulative = cum_ref[...]
    growth_three = rows_of_three(jnp.exp(cumulative))
    fall_three = rows_of_three(jnp.exp(cumulative[:, -1:] - cumulative))
    skip_column = to_column(skip_ref[...])
    grad_cum = jnp.zeros((heads, length), F32)
    skip_part = jnp.zeros((heads, 1), F32)
    for first in range(0, channels, LANES):
        here = pl.ds(first, LANES)
        wide, sigmoid, grad_y = gate_parts(gate_ref[:, here], go_ref[:, here])
        vals = v_ref[:, here].astype(F32)
        skip = channel_row(skip_column, heads, width, first)
        growth_ref[:, here] = spread(growth_three, first, LANES, width)
        fall_ref[:, here] = spread(fall_three, first, LANES, width)
        gy_ref[:, here] = grad_y
        coef_ref[:, here] = go_ref[:, here].astype(F32) * sigmoid * (1.0 + wide * (1.0 - sigmoid))
        intra = intra_ref[:, here]
        inner = in_inner_ref[:, here]
        mamba_ref[:, here] = intra + skip * vals
        inner_ref[:, here] = inner + skip * grad_y
        high, low = split(grad_y.astype(BF16).astype(F32) * intra - vals * inner, 2)
        head_rows = jnp.where(head_map(heads, width, first, LANES), 1.0, 0.0).astype(BF16)
        grad_cum = grad_cum + mm_nt(head_rows, high) + mm_nt(head_rows, low)
        skip_row = jnp.sum(grad_y * vals, axis=0, keepdims=True)
        skip_part = skip_part + head_column(skip_row, heads, width, first)
    gcum_ref[...] = grad_cum
    rate_part = jnp.sum(grad_cum * cumulative, axis=1, keepdims=True)
    parts_ref[...] = jnp.concatenate([to_row(rate_part), to_row(skip_part)], axis=0)


def pick(size, first, second, last):
    if size == 1:
        return jnp.zeros_like(first), jnp.zeros_like(first)
    if size % 2:
        return first, second
    index = lax.axis_index("seq")
    lower = index < size // 2
    edge = jnp.logical_or(index == 0, index == size - 1)
    first = jnp.where(edge, 0.0, first)
    second = jnp.where(edge, last, second)
    return jnp.where(lower, first, second), jnp.where(lower, second, first)


def picked(size, states, here):
    both = [pick(size, *(ref[:, here] for ref in state)) for state in states]
    return jnp.concatenate([x[0] for x in both], axis=0), jnp.concatenate([x[1] for x in both], axis=0)


def rate_kernel(size, pieces, start, heads, final, *refs):
    states, refs = [refs[3 * i : 3 * i + 3] for i in range(pieces)], refs[3 * pieces :]
    q_ref, r_ref, slope_ref, row_ref, parts_ref, out_ref = *refs[:5], refs[-1]
    rows, channels = pieces * states[0][0].shape[0], q_ref.shape[1]
    here = slice(start, start + rows)
    rate_part = jnp.zeros((heads, 1), F32)
    for begin in range(0, channels, LANES):
        lanes = pl.ds(begin, LANES)
        entering, after = picked(size, states, lanes)
        terms = entering * q_ref[here, lanes] + after * (
            r_ref[here, lanes] + slope_ref[:, lanes] * entering
        )
        row = row_ref[:, lanes] + jnp.sum(terms, axis=0, keepdims=True)
        if final:
            rate_part = rate_part + head_column(row, heads, channels // heads, begin)
        else:
            out_ref[:, lanes] = row
    if final:
        base = parts_ref[...]
        out_ref[...] = jnp.concatenate([base[:1] + to_row(rate_part), base[1:]], axis=0)


def share_kernel(size, pieces, start, *refs):
    states, refs = [refs[3 * i : 3 * i + 3] for i in range(pieces)], refs[3 * pieces :]
    high_ref, low_ref, scaled_ref, sum_b_ref, sum_c_ref = refs[:5]
    rows, channels = pieces * states[0][0].shape[0], scaled_ref.shape[1]
    here = slice(start, start + rows)
    grad_b = sum_b_ref[:, here]
    grad_c = sum_c_ref[:, here]
    pairs_b = pairs_c = jnp.zeros((scaled_ref.shape[0], 2 * rows), F32)
    for begin in range(0, channels, LANES):
        lanes = pl.ds(begin, LANES)
        entering, after = picked(size, states, lanes)
        enter_high, enter_low = split(entering, 2)
        after_high, after_low = split(after, 2)
        high, low, scaled = high_ref[:, lanes], low_ref[:, lanes], scaled_ref[:, lanes]
        pairs_c = pairs_c + mm_nt(high, jnp.concatenate([enter_low, enter_high], axis=0))
        pairs_b = pairs_b + mm_nt(scaled, jnp.concatenate([after_low, after_high], axis=0))
        grad_c = grad_c + mm_nt(low, enter_high)
    grad_b = grad_b + (pairs_b[:, :rows] + pairs_b[:, rows:])
    grad_c = grad_c + (pairs_c[:, :rows] + pairs_c[:, rows:])
    refs[-1][...] = jnp.concatenate([grad_b, grad_c], axis=1)


def rest_kernel(size, pieces, *refs):
    states, refs = [refs[3 * i : 3 * i + 3] for i in range(pieces)], refs[3 * pieces :]
    (
        v_ref, b_ref, c_ref, coef_ref, mamba_ref, inner_ref, growth_ref, fall_ref, gy_ref,
        gcum_ref, decay_ref, neg_ref, *_, gv_ref, gg_ref, gs_ref, total_ref,
    ) = refs
    length, channels = v_ref.shape
    heads = gcum_ref.shape[0]
    width = channels // heads
    twice_b, twice_c = (jnp.concatenate([ref[...], ref[...]], axis=1) for ref in (b_ref, c_ref))
    grad_cum = gcum_ref[...]
    grad_total = jnp.zeros((heads, 1), F32)
    for first in range(0, channels, LANES):
        here = pl.ds(first, LANES)
        entering, after = picked(size, states, here)
        inter = growth_ref[:, here] * mm(twice_c, jnp.concatenate(split(entering, 2), axis=0))
        outer = fall_ref[:, here] * mm(twice_b, jnp.concatenate(split(after, 2), axis=0))
        gg_ref[0, :, here] = (coef_ref[:, here] * (mamba_ref[:, here] + inter)).astype(BF16)
        gv_ref[0, :, here] = (inner_ref[:, here] + outer).astype(BF16)
        pulled = v_ref[:, here].astype(F32) * outer
        high, low = split(gy_ref[:, here] * inter - pulled, 2)
        head_rows = jnp.where(head_map(heads, width, first, LANES), 1.0, 0.0).astype(BF16)
        grad_cum = grad_cum + mm_nt(head_rows, high) + mm_nt(head_rows, low)
        total_row = jnp.sum(pulled, axis=0, keepdims=True) + decay_ref[:, here] * jnp.sum(
            after * entering, axis=0, keepdims=True
        )
        grad_total = grad_total + head_column(total_row, heads, width, first)
    gs_ref[0] = neg_ref[...] * (scan_tokens(grad_cum, True) + grad_total)
    total_ref[...] = to_row(grad_total)


def tree(values):
    while len(values) > 1:
        values = [sum(values[i + 1 : i + 2], values[i]) for i in range(0, len(values), 2)]
    return values[0]


def copy_kernel(x_ref, *refs):
    refs[-1][...] = x_ref[...]


def add_kernel(x_ref, y_ref, *refs):
    refs[-1][...] = x_ref[...] + y_ref[...]


def sum_kernel(*refs):
    refs[-1][...] = tree([ref[...] for ref in refs[:-1]])


def last_kernel(counts, *refs):
    refs, (gb_ref, gc_ref, rate_ref, skip_ref) = refs[:-4], refs[-4:]
    sums = []
    for count in counts:
        sums.append(tree([ref[...] for ref in refs[:count]]))
        refs = refs[count:]
    *shares, small = sums
    start = 0
    for both in shares:
        rows = both.shape[1] // 2
        gb_ref[0, :, start : start + rows] = both[:, :rows]
        gc_ref[0, :, start : start + rows] = both[:, rows:]
        start += rows
    rate_ref[...] = small[:1]
    skip_ref[...] = small[1:]


def call(kernel, outs, scratch=(), name="", space=pltpu.VMEM, after=()):
    def run(*args):
        if space == pltpu.HBM:
            args = [pltpu.with_memory_space_constraint(a, space) for a in args]
        specs = [pl.BlockSpec(memory_space=space)] * len(args)
        specs += [pl.BlockSpec(memory_space=pl.ANY)] * len(after)
        args = (*args, *after)
        return pl.pallas_call(
            kernel,
            out_shape=tuple(outs),
            in_specs=specs,
            out_specs=tuple(pl.BlockSpec(memory_space=pltpu.VMEM) for _ in outs),
            scratch_shapes=list(scratch),
            compiler_params=pltpu.CompilerParams(vmem_limit_bytes=VMEM_LIMIT),
            cost_estimate=pl.CostEstimate(
                flops=WEIGHTS.get(name, 0) * 10**7, bytes_accessed=0, transcendentals=0
            ),
        )(*args)

    return run


def swap(x, axis, size, bit):
    return lax.ppermute(x, axis, [(i, i ^ bit) for i in range(size)])


def hop(x, sizes, step):
    size, copies = sizes["seq"], sizes["replica"]
    pairs = []
    for copy in range(copies):
        for place in range(size):
            to = (copy ^ 1 if copies % 2 == 0 else copy, place)
            for low in (step, size - 2 - step):
                if place in (low, low + 1):
                    to = (copy, 2 * low + 1 - place)
            pairs.append((copy * size + place, to[0] * size + to[1]))
    return lax.ppermute(x, ("replica", "seq"), pairs)


def pass_kernel(*refs):
    got_ref, base_ref, decay_ref = refs[:3]
    refs[-1][...] = decay_ref[...] * got_ref[...] + base_ref[...]


def pass_on(got, base, decay, after, name):
    return call(pass_kernel, [jax.ShapeDtypeStruct(base.shape, F32)], name=name, after=after)(
        got, base, decay
    )[0]


def chain(sizes, mine, made, decay, work):
    chunks = len(mine)
    size = sizes["seq"]
    if size == 1:
        for k in sorted(work):
            work[k](())
        return [(x, x, x) for x in mine]
    if size % 2:
        raise NotImplementedError
    index = lax.axis_index("seq")
    place = jnp.minimum(index, size - 1 - index)
    middle = size // 2 - 1
    got = {(0, c): hop(mine[c], sizes, 0) for c in range(chunks)}
    steps = [
        (at + c + (1 if at > middle else 0), at, c)
        for at in range(1, size - 1)
        for c in range(chunks)
    ]
    token = ()
    for count, (_, at, c) in enumerate(sorted(steps)):
        if count in work:
            token = work[count](token)
        if at > middle and c > 2:
            token = (*token, got[at, c - 2 - 1])
        base = mine[c] if at <= middle else made["factors"][5 + c]
        pay = pass_on(got[at - 1, c], base, decay, token, f"pass{min(count, 7)}")
        got[at, c] = hop(pay, sizes, at)
        token = (pay,)
    for k in sorted(work):
        if k >= len(steps):
            token = work[k](token)
    states = []
    for c in range(chunks):
        first, second, last = got[0, c], got[middle, c], got[size - 2, c]
        for at in range(1, middle):
            first = jnp.where(place == at + 1, got[at, c], first)
        for at in range(middle + 1, size - 2):
            second = jnp.where(place == size - 2 - at, got[at, c], second)
        states.append((first, second, last))
    return states


def sum_terms(x, later, axis, size):
    if size == 1:
        return [x]
    if size == 4:
        return [x, swap(x, axis, size, 1)] + [swap(later, axis, size, bit) for bit in (2, 3)]
    if size & (size - 1):
        return [lax.psum(x, axis)]
    bit = 1
    while 2 * bit < size:
        x = x + swap(x, axis, size, bit)
        bit *= 2
    return [x, swap(x, axis, size, bit)]


def small_terms(x, axes, sizes, between):
    bits = [(axis, 1 << k) for axis in axes for k in range(sizes[axis].bit_length() - 1)]
    if any(sizes[axis] & (sizes[axis] - 1) for axis in axes):
        x, bits = lax.psum(x, tuple(axes)), []
    after = ()
    for count, (axis, bit) in enumerate(bits):
        theirs = swap(x, axis, sizes[axis], bit)
        if count == len(bits) - 1:
            break
        x = call(add_kernel, [jax.ShapeDtypeStruct(x.shape, F32)], name=f"add{count}", after=after)(x, theirs)[0]
        after = between((x,)) if count == 0 else ()
    if len(bits) < 2:
        between((x,))
    return [x, theirs] if bits else [x]


def shards(sizes, values, gate_in, in_b, in_c, step_sizes, log_rates, skip_gain, grad_out):
    like = jax.ShapeDtypeStruct
    length, channels = values.shape[1:]
    heads = step_sizes.shape[1]
    state = in_b.shape[2]
    seq = sizes["seq"]
    rows = state // CHUNKS
    wide = like((length, channels), F32)
    wide_b = like((length, channels), BF16)
    share = like((length, state), F32)
    small = like((heads, length), F32)
    row = like((1, channels), F32)
    piece = like((rows, channels), F32)
    maps = like((length, state), BF16)

    out = call(
        functools.partial(states_kernel, seq),
        [wide_b, wide_b, wide_b, maps, maps, small, small, row, row, like((1, heads), F32)]
        + [piece] * CHUNKS,
        [
            pltpu.VMEM((heads, length), F32),
            pltpu.VMEM((1, heads), F32),
            pltpu.SemaphoreType.DMA((8,)),
        ],
        space=pltpu.HBM,
    )(
        values[0], gate_in[0], grad_out[0], in_b[0], in_c[0], step_sizes[0],
        log_rates.reshape(1, heads), skip_gain.reshape(1, heads),
    )
    vals, gate, grad, block_b, block_c, cumulative, negative, decay, slope, skip = out[:10]
    mine = out[10:]

    made = {}

    def intra(after):
        made["intra"] = call(
            intra_kernel,
            [wide, wide, share, share],
            [
                pltpu.VMEM((channels, length), BF16),
                pltpu.VMEM((channels, length), F32),
                pltpu.VMEM((length, length), F32),
            ],
            name="intra",
        )(vals, gate, grad, block_b, block_c, cumulative)
        return (made["intra"][2],)

    def factors(after):
        made["factors"] = call(
            functools.partial(factors_kernel, seq),
            [wide_b] * 3 + [like((state, channels), F32)] * 2 + [piece] * CHUNKS,
            name="factors",
        )(vals, gate, grad, block_b, block_c, cumulative, *(after if after else made["intra"][2:3]))
        return made["factors"][5:6]

    def prepare(after):
        made["prepare"] = call(
            prepare_kernel,
            [wide] * 6 + [small, like((2, heads), F32)],
            name="prepare",
        )(
            vals, gate, grad, cumulative, skip,
            *made["intra"][:2], *(after if after else made["intra"][2:3]),
        )
        return (made["prepare"][-1],)

    sums = max(seq - 2, 0) * CHUNKS
    states = chain(sizes, mine, made, decay, {0: intra, 1: factors, max(sums - 2, 2): prepare})
    sum_b, sum_c = made["intra"][2:]
    high, low, scaled, q, r = made["factors"][:5]
    coef, mamba, inner, growth, fall, grad_y, grad_cum, parts = made["prepare"]

    rate_row = jnp.zeros((1, channels), F32)
    terms, counts = [], []
    for i in range(PARTS):
        final = i == PARTS - 1
        count = CHUNKS // PARTS
        own = [x for group in states[i * count : (i + 1) * count] for x in group]
        rate_row = call(
            functools.partial(rate_kernel, seq, count, i * rows * count, heads, final),
            [like((2, heads), F32) if final else row],
            name=f"rate{i}",
        )(*own, q, r, slope, rate_row, parts)[0]
        share_of = call(
            functools.partial(share_kernel, seq, count, i * rows * count),
            [like((length, 2 * rows * count), F32)],
            name=f"share{i}",
            after=(rate_row,),
        )(*own, high, low, scaled, sum_b, sum_c)[0]
        if not final:
            own = sum_terms(share_of, share_of, "tensor", sizes["tensor"])
            terms += call(sum_kernel, [like(share_of.shape, F32)], name="sum")(*own)
            counts.append(1)

    def between(after):
        later = call(copy_kernel, [like(share_of.shape, F32)], name="later", after=after)(share_of)[0]
        made["share"] = sum_terms(share_of, later, "tensor", sizes["tensor"])
        return rest(after)

    def rest(after):
        made["rest"] = call(
            functools.partial(rest_kernel, seq, CHUNKS),
            [like((1, length, channels), BF16)] * 2
            + [like((1, heads, length), F32), like((1, heads), F32)],
            name="rest",
            after=(*after, *terms),
        )(
            *(x for group in states for x in group),
            vals, block_b, block_c, coef, mamba, inner, growth, fall, grad_y, grad_cum, decay, negative,
        )
        return (made["rest"][3],)

    own = small_terms(rate_row, ("seq", "replica"), sizes, between)
    for group in (made["share"], own):
        terms += group
        counts.append(len(group))
    grad_values, grad_gate, grad_steps, _ = made["rest"]
    grad_b, grad_c, rate_sum, skip_sum = call(
        functools.partial(last_kernel, tuple(counts)),
        [like((1, length, state), F32)] * 2 + [like((1, heads), F32)] * 2,
    )(*terms)
    return (
        grad_values,
        grad_gate,
        grad_b,
        grad_c,
        grad_steps,
        rate_sum.reshape(heads),
        skip_sum.reshape(heads),
    )


def solution(mesh):
    in_specs = (
        P("replica", "seq", "tensor"),
        P("replica", "seq", "tensor"),
        P("replica", "seq", None),
        P("replica", "seq", None),
        P("replica", "tensor", "seq"),
        P("tensor"),
        P("tensor"),
        P("replica", "seq", "tensor"),
    )
    out_specs = (
        P("replica", "seq", "tensor"),
        P("replica", "seq", "tensor"),
        P("replica", "seq", None),
        P("replica", "seq", None),
        P("replica", "tensor", "seq"),
        P("tensor"),
        P("tensor"),
    )
    body = functools.partial(shards, dict(mesh.shape))
    return jax.shard_map(body, mesh=mesh, in_specs=in_specs, out_specs=out_specs, check_vma=False)
```

```python
import functools

import jax
import jax.numpy as jnp
from jax import lax
from jax.experimental import pallas as pl
from jax.experimental.pallas import tpu as pltpu
from jax.sharding import PartitionSpec as P

F32 = jnp.float32
BF16 = jnp.bfloat16
VMEM_LIMIT = 24 * 1024 * 1024
LANES = 256
CHUNKS = 4
PARTS = 2
WEIGHTS = {'pass4': 30, 'pass5': 10, 'pass6': 300, 'pass7': 30, 'rate0': 30, 'rate1': 10, 'later': 30, 'sum': 100, 'add1': 100, 'rest': 30}


def split(x, parts):
    terms = []
    for _ in range(parts - 1):
        term = x.astype(BF16)
        terms.append(term)
        x = x - term.astype(F32)
    terms.append(x.astype(BF16))
    return terms


def mm(a, b):
    return lax.dot_general(a, b, (((1,), (0,)), ((), ())), preferred_element_type=F32)


def mm_nt(a, b):
    return lax.dot_general(a, b, (((1,), (1,)), ((), ())), preferred_element_type=F32)


def mm_tn(a, b):
    return lax.dot_general(a, b, (((0,), (0,)), ((), ())), preferred_element_type=F32)


def iota(shape, dim):
    return lax.broadcasted_iota(jnp.int32, shape, dim)


def to_column(row):
    n = row.shape[1]
    eye = iota((n, n), 0) == iota((n, n), 1)
    return jnp.sum(jnp.where(eye, row, 0.0), axis=1, keepdims=True)


def to_row(column):
    n = column.shape[0]
    eye = iota((n, n), 0) == iota((n, n), 1)
    return jnp.sum(jnp.where(eye, column, 0.0), axis=0, keepdims=True)


def head_map(heads, width, first, lanes):
    low = iota((heads, lanes), 0) * width
    channel = iota((heads, lanes), 1) + first
    return (channel >= low) & (channel < low + width)


def spread_map(heads, width, first, lanes):
    one = jnp.where(head_map(heads, width, first, lanes), 1.0, 0.0).astype(BF16)
    return jnp.concatenate([one, one, one], axis=0)


def rows_of_three(per_head):
    return jnp.concatenate(split(per_head, 3), axis=0)


def spread(three, first, lanes, width):
    heads = three.shape[0] // 3
    return mm_tn(three, spread_map(heads, width, first, lanes))


def scan_tokens(per_head, backward):
    heads, length = per_head.shape
    source = iota((length, length), 0)
    target = iota((length, length), 1)
    keep = source >= target if backward else source <= target
    sums = mm(rows_of_three(per_head), jnp.where(keep, 1.0, 0.0).astype(BF16))
    return sums[:heads] + sums[heads : 2 * heads] + sums[2 * heads :]


def channel_row(column, heads, width, first):
    mine = head_map(heads, width, first, LANES)
    return jnp.sum(jnp.where(mine, column, 0.0), axis=0, keepdims=True)


def head_column(row, heads, width, first):
    mine = head_map(heads, width, first, LANES)
    return jnp.sum(jnp.where(mine, row, 0.0), axis=1, keepdims=True)


def gate_parts(gate, grad):
    wide = gate.astype(F32)
    sigmoid = 1.0 / (1.0 + jnp.exp(-wide))
    return wide, sigmoid, grad.astype(F32) * (wide * sigmoid)


def put_rows(refs, here, value):
    start = 0
    for ref in refs:
        rows = ref.shape[0]
        ref[:, here] = value[start : start + rows]
        start += rows


def states_kernel(size, *refs):
    sources, outs, (steps_ref, lr_ref, sems) = refs[:8], refs[8:-3], refs[-3:]
    v_ref, gate_ref, go_ref, b_ref, c_ref = outs[:5]
    cum_ref, neg_ref, decay_ref, slope_ref, skip_ref = outs[5:10]
    mine_refs = outs[10:]
    targets = (v_ref, gate_ref, go_ref, b_ref, c_ref, steps_ref, lr_ref, skip_ref)
    copies = [
        pltpu.make_async_copy(source, target, sems.at[i])
        for i, (source, target) in enumerate(zip(sources, targets))
    ]
    for i in (6, 5, 3, 4, 0, 1, 2, 7):
        copies[i].start()
    length, channels = v_ref.shape
    heads = steps_ref.shape[0]
    width = channels // heads

    def wait(*which):
        for i in which:
            copies[i].wait()

    def scan():
        rates = jnp.exp(to_column(lr_ref[...]))
        cumulative = scan_tokens(-rates * steps_ref[...], False)
        return rates, cumulative, cumulative[:, -1:]

    def keep(rates, cumulative, total):
        decay = jnp.exp(total)
        cum_ref[...] = cumulative
        neg_ref[...] = jnp.broadcast_to(-rates, (heads, length))
        for first in range(0, channels, LANES):
            here = pl.ds(first, LANES)
            decay_ref[:, here] = channel_row(decay, heads, width, first)
            slope_ref[:, here] = channel_row(total * decay, heads, width, first)

    def local():
        wait(6, 5, 3, 0)
        rates, cumulative, total = scan()
        b_t = b_ref[...].astype(F32).T.astype(BF16)
        fall = rows_of_three(jnp.exp(total - cumulative))
        for first in range(0, channels, LANES):
            here = pl.ds(first, LANES)
            scaled = spread(fall, first, LANES, width) * v_ref[:, here].astype(F32)
            put_rows(mine_refs, here, mm(b_t, scaled.astype(BF16)))
        keep(rates, cumulative, total)
        wait(1, 2, 4, 7)

    def pulled():
        wait(6, 5, 4, 1, 2)
        rates, cumulative, total = scan()
        c_t = c_ref[...].astype(F32).T.astype(BF16)
        growth = rows_of_three(jnp.exp(cumulative))
        for first in range(0, channels, LANES):
            here = pl.ds(first, LANES)
            _, _, grad_y = gate_parts(gate_ref[:, here], go_ref[:, here])
            high, low = split(spread(growth, first, LANES, width) * grad_y, 2)
            put_rows(mine_refs, here, mm(c_t, high) + mm(c_t, low))
        keep(rates, cumulative, total)
        wait(0, 3, 7)

    if size == 1:
        local()
    else:
        lower = lax.axis_index("seq") < size // 2
        pl.when(lower)(local)
        pl.when(jnp.logical_not(lower))(pulled)


def intra_kernel(
    v_ref, gate_ref, go_ref, b_ref, c_ref, cum_ref,
    intra_ref, inner_ref, sum_b_ref, sum_c_ref, grad_t_ref, inner_t_ref, acc_ref,
):
    length, channels = v_ref.shape
    heads = cum_ref.shape[0]
    width = channels // heads
    half = length // 2
    pair = 2 * width
    cumulative = cum_ref[...]
    columns = cumulative.T
    scores = mm_nt(c_ref[...], b_ref[...])
    causal = iota((half, half), 0) >= iota((half, half), 1)
    left = iota((1, pair), 1) < width
    acc_ref[...] = jnp.zeros_like(acc_ref)

    def blocks(x):
        return x[:half, :half], x[half:, :half], x[half:, half:]

    scores_00, scores_10, scores_11 = blocks(scores)
    for first in range(0, channels, pair):
        here = pl.ds(first, pair)
        _, _, grad_y = gate_parts(gate_ref[:, here], go_ref[:, here])
        grad_t_ref[here, :] = grad_y.T.astype(BF16)
        vals = v_ref[:, here]
        pieces = []
        for side in range(2):
            head = first // width + side
            own = left if side == 0 else jnp.logical_not(left)
            row = cumulative[head : head + 1, :]
            column = columns[:, head : head + 1]
            row_0, row_1 = row[:, :half], row[:, half:]
            column_0, column_1 = column[:half], column[half:]
            decay_00 = jnp.exp(jnp.where(causal, column_0 - row_0, -1e30))
            decay_10 = jnp.exp(column_1 - row_0)
            decay_11 = jnp.exp(jnp.where(causal, column_1 - row_1, -1e30))
            mix_00 = (scores_00 * decay_00).astype(BF16)
            mix_10 = (scores_10 * decay_10).astype(BF16)
            mix_11 = (scores_11 * decay_11).astype(BF16)
            low_rows = jnp.concatenate([mix_10, mix_11], axis=1)
            pieces.append((mm(mix_00, vals[:half]), mm(low_rows, vals)))
            head_grad = jnp.where(own, grad_y, 0.0).astype(BF16)
            mixed_0 = mm_nt(head_grad[:half], vals[:half])
            mixed_1 = mm_nt(head_grad[half:], vals)
            acc_ref[:half, :half] += mixed_0 * decay_00
            acc_ref[half:, :half] += mixed_1[:, :half] * decay_10
            acc_ref[half:, half:] += mixed_1[:, half:] * decay_11
            mine = pl.ds(first + side * width, width)
            grad_t = grad_t_ref[mine, :]
            inner_t_ref[mine, :half] = mm(grad_t[:, :half], mix_00) + mm(grad_t[:, half:], mix_10)
            inner_t_ref[mine, half:] = mm(grad_t[:, half:], mix_11)
        intra_ref[:half, here] = jnp.where(left, pieces[0][0], pieces[1][0])
        intra_ref[half:, here] = jnp.where(left, pieces[0][1], pieces[1][1])
        inner_ref[:, here] = inner_t_ref[here, :].T
    shares = acc_ref[...]
    high, low = split(shares, 2)
    sum_c_ref[...] = mm(high, b_ref[...]) + mm(low, b_ref[...])
    high, low = split(shares.T, 2)
    sum_b_ref[...] = mm(high, c_ref[...]) + mm(low, c_ref[...])


def factors_kernel(
    size, v_ref, gate_ref, go_ref, b_ref, c_ref, cum_ref, after_ref,
    high_ref, low_ref, scaled_ref, q_ref, r_ref, *other_refs,
):
    length, channels = v_ref.shape
    heads = cum_ref.shape[0]
    width = channels // heads
    cumulative = cum_ref[...]
    left_over = cumulative[:, -1:] - cumulative
    growth = rows_of_three(jnp.exp(cumulative))
    fall = rows_of_three(jnp.exp(left_over))
    growth_slope = rows_of_three(cumulative * jnp.exp(cumulative))
    fall_slope = rows_of_three(left_over * jnp.exp(left_over))
    b_t = b_ref[...].astype(F32).T.astype(BF16)
    c_t = c_ref[...].astype(F32).T.astype(BF16)
    for first in range(0, channels, LANES):
        here = pl.ds(first, LANES)
        _, _, grad_y = gate_parts(gate_ref[:, here], go_ref[:, here])
        vals = v_ref[:, here].astype(F32)
        high, low = split(spread(growth, first, LANES, width) * grad_y, 2)
        high_ref[:, here] = high
        low_ref[:, here] = low
        scaled_ref[:, here] = (spread(fall, first, LANES, width) * vals).astype(BF16)
        high, low = split(spread(growth_slope, first, LANES, width) * grad_y, 2)
        q_ref[:, here] = mm(c_t, high) + mm(c_t, low)
        high, low = split(spread(fall_slope, first, LANES, width) * vals, 2)
        r_ref[:, here] = mm(b_t, high) + mm(b_t, low)

    def pulled():
        put_rows(other_refs, slice(None), mm(c_t, high_ref[...]) + mm(c_t, low_ref[...]))

    def local():
        put_rows(other_refs, slice(None), mm(b_t, scaled_ref[...]))

    if size == 1:
        pulled()
    else:
        lower = lax.axis_index("seq") < size // 2
        pl.when(lower)(pulled)
        pl.when(jnp.logical_not(lower))(local)


def prepare_kernel(
    v_ref, gate_ref, go_ref, cum_ref, skip_ref, intra_ref, in_inner_ref, after_ref,
    coef_ref, mamba_ref, inner_ref, growth_ref, fall_ref, gy_ref, gcum_ref, parts_ref,
):
    length, channels = v_ref.shape
    heads = cum_ref.shape[0]
    width = channels // heads
    cumulative = cum_ref[...]
    growth_three = rows_of_three(jnp.exp(cumulative))
    fall_three = rows_of_three(jnp.exp(cumulative[:, -1:] - cumulative))
    skip_column = to_column(skip_ref[...])
    grad_cum = jnp.zeros((heads, length), F32)
    skip_part = jnp.zeros((heads, 1), F32)
    for first in range(0, channels, LANES):
        here = pl.ds(first, LANES)
        wide, sigmoid, grad_y = gate_parts(gate_ref[:, here], go_ref[:, here])
        vals = v_ref[:, here].astype(F32)
        skip = channel_row(skip_column, heads, width, first)
        growth_ref[:, here] = spread(growth_three, first, LANES, width)
        fall_ref[:, here] = spread(fall_three, first, LANES, width)
        gy_ref[:, here] = grad_y
        coef_ref[:, here] = go_ref[:, here].astype(F32) * sigmoid * (1.0 + wide * (1.0 - sigmoid))
        intra = intra_ref[:, here]
        inner = in_inner_ref[:, here]
        mamba_ref[:, here] = intra + skip * vals
        inner_ref[:, here] = inner + skip * grad_y
        high, low = split(grad_y.astype(BF16).astype(F32) * intra - vals * inner, 2)
        head_rows = jnp.where(head_map(heads, width, first, LANES), 1.0, 0.0).astype(BF16)
        grad_cum = grad_cum + mm_nt(head_rows, high) + mm_nt(head_rows, low)
        skip_row = jnp.sum(grad_y * vals, axis=0, keepdims=True)
        skip_part = skip_part + head_column(skip_row, heads, width, first)
    gcum_ref[...] = grad_cum
    rate_part = jnp.sum(grad_cum * cumulative, axis=1, keepdims=True)
    parts_ref[...] = jnp.concatenate([to_row(rate_part), to_row(skip_part)], axis=0)


def pick(size, first, second, last):
    if size == 1:
        return jnp.zeros_like(first), jnp.zeros_like(first)
    if size % 2:
        return first, second
    index = lax.axis_index("seq")
    lower = index < size // 2
    edge = jnp.logical_or(index == 0, index == size - 1)
    first = jnp.where(edge, 0.0, first)
    second = jnp.where(edge, last, second)
    return jnp.where(lower, first, second), jnp.where(lower, second, first)


def picked(size, states, here):
    both = [pick(size, *(ref[:, here] for ref in state)) for state in states]
    return jnp.concatenate([x[0] for x in both], axis=0), jnp.concatenate([x[1] for x in both], axis=0)


def rate_kernel(size, pieces, start, heads, final, *refs):
    states, refs = [refs[3 * i : 3 * i + 3] for i in range(pieces)], refs[3 * pieces :]
    q_ref, r_ref, slope_ref, row_ref, parts_ref, out_ref = *refs[:5], refs[-1]
    rows, channels = pieces * states[0][0].shape[0], q_ref.shape[1]
    here = slice(start, start + rows)
    rate_part = jnp.zeros((heads, 1), F32)
    for begin in range(0, channels, LANES):
        lanes = pl.ds(begin, LANES)
        entering, after = picked(size, states, lanes)
        terms = entering * q_ref[here, lanes] + after * (
            r_ref[here, lanes] + slope_ref[:, lanes] * entering
        )
        row = row_ref[:, lanes] + jnp.sum(terms, axis=0, keepdims=True)
        if final:
            rate_part = rate_part + head_column(row, heads, channels // heads, begin)
        else:
            out_ref[:, lanes] = row
    if final:
        base = parts_ref[...]
        out_ref[...] = jnp.concatenate([base[:1] + to_row(rate_part), base[1:]], axis=0)


def share_kernel(size, pieces, start, *refs):
    states, refs = [refs[3 * i : 3 * i + 3] for i in range(pieces)], refs[3 * pieces :]
    high_ref, low_ref, scaled_ref, sum_b_ref, sum_c_ref = refs[:5]
    rows, channels = pieces * states[0][0].shape[0], scaled_ref.shape[1]
    here = slice(start, start + rows)
    grad_b = sum_b_ref[:, here]
    grad_c = sum_c_ref[:, here]
    pairs_b = pairs_c = jnp.zeros((scaled_ref.shape[0], 2 * rows), F32)
    for begin in range(0, channels, LANES):
        lanes = pl.ds(begin, LANES)
        entering, after = picked(size, states, lanes)
        enter_high, enter_low = split(entering, 2)
        after_high, after_low = split(after, 2)
        high, low, scaled = high_ref[:, lanes], low_ref[:, lanes], scaled_ref[:, lanes]
        pairs_c = pairs_c + mm_nt(high, jnp.concatenate([enter_low, enter_high], axis=0))
        pairs_b = pairs_b + mm_nt(scaled, jnp.concatenate([after_low, after_high], axis=0))
        grad_c = grad_c + mm_nt(low, enter_high)
    grad_b = grad_b + (pairs_b[:, :rows] + pairs_b[:, rows:])
    grad_c = grad_c + (pairs_c[:, :rows] + pairs_c[:, rows:])
    refs[-1][...] = jnp.concatenate([grad_b, grad_c], axis=1)


def rest_kernel(size, pieces, *refs):
    states, refs = [refs[3 * i : 3 * i + 3] for i in range(pieces)], refs[3 * pieces :]
    (
        v_ref, b_ref, c_ref, coef_ref, mamba_ref, inner_ref, growth_ref, fall_ref, gy_ref,
        gcum_ref, decay_ref, neg_ref, *_, gv_ref, gg_ref, gs_ref, total_ref,
    ) = refs
    length, channels = v_ref.shape
    heads = gcum_ref.shape[0]
    width = channels // heads
    twice_b, twice_c = (jnp.concatenate([ref[...], ref[...]], axis=1) for ref in (b_ref, c_ref))
    grad_cum = gcum_ref[...]
    grad_total = jnp.zeros((heads, 1), F32)
    for first in range(0, channels, LANES):
        here = pl.ds(first, LANES)
        entering, after = picked(size, states, here)
        inter = growth_ref[:, here] * mm(twice_c, jnp.concatenate(split(entering, 2), axis=0))
        outer = fall_ref[:, here] * mm(twice_b, jnp.concatenate(split(after, 2), axis=0))
        gg_ref[0, :, here] = (coef_ref[:, here] * (mamba_ref[:, here] + inter)).astype(BF16)
        gv_ref[0, :, here] = (inner_ref[:, here] + outer).astype(BF16)
        pulled = v_ref[:, here].astype(F32) * outer
        high, low = split(gy_ref[:, here] * inter - pulled, 2)
        head_rows = jnp.where(head_map(heads, width, first, LANES), 1.0, 0.0).astype(BF16)
        grad_cum = grad_cum + mm_nt(head_rows, high) + mm_nt(head_rows, low)
        total_row = jnp.sum(pulled, axis=0, keepdims=True) + decay_ref[:, here] * jnp.sum(
            after * entering, axis=0, keepdims=True
        )
        grad_total = grad_total + head_column(total_row, heads, width, first)
    gs_ref[0] = neg_ref[...] * (scan_tokens(grad_cum, True) + grad_total)
    total_ref[...] = to_row(grad_total)


def tree(values):
    while len(values) > 1:
        values = [sum(values[i + 1 : i + 2], values[i]) for i in range(0, len(values), 2)]
    return values[0]


def copy_kernel(x_ref, *refs):
    refs[-1][...] = x_ref[...]


def add_kernel(x_ref, y_ref, *refs):
    refs[-1][...] = x_ref[...] + y_ref[...]


def sum_kernel(*refs):
    refs[-1][...] = tree([ref[...] for ref in refs[:-1]])


def last_kernel(counts, *refs):
    refs, (gb_ref, gc_ref, rate_ref, skip_ref) = refs[:-4], refs[-4:]
    sums = []
    for count in counts:
        sums.append(tree([ref[...] for ref in refs[:count]]))
        refs = refs[count:]
    *shares, small = sums
    start = 0
    for both in shares:
        rows = both.shape[1] // 2
        gb_ref[0, :, start : start + rows] = both[:, :rows]
        gc_ref[0, :, start : start + rows] = both[:, rows:]
        start += rows
    rate_ref[...] = small[:1]
    skip_ref[...] = small[1:]


def call(kernel, outs, scratch=(), name="", space=pltpu.VMEM, after=()):
    def run(*args):
        if space == pltpu.HBM:
            args = [pltpu.with_memory_space_constraint(a, space) for a in args]
        specs = [pl.BlockSpec(memory_space=space)] * len(args)
        specs += [pl.BlockSpec(memory_space=pl.ANY)] * len(after)
        args = (*args, *after)
        return pl.pallas_call(
            kernel,
            out_shape=tuple(outs),
            in_specs=specs,
            out_specs=tuple(pl.BlockSpec(memory_space=pltpu.VMEM) for _ in outs),
            scratch_shapes=list(scratch),
            compiler_params=pltpu.CompilerParams(vmem_limit_bytes=VMEM_LIMIT),
            cost_estimate=pl.CostEstimate(
                flops=WEIGHTS.get(name, 0) * 10**7, bytes_accessed=0, transcendentals=0
            ),
        )(*args)

    return run


def swap(x, axis, size, bit):
    return lax.ppermute(x, axis, [(i, i ^ bit) for i in range(size)])


def hop(x, sizes, step):
    size, copies = sizes["seq"], sizes["replica"]
    pairs = []
    for copy in range(copies):
        for place in range(size):
            to = (copy ^ 1 if copies % 2 == 0 else copy, place)
            for low in (step, size - 2 - step):
                if place in (low, low + 1):
                    to = (copy, 2 * low + 1 - place)
            pairs.append((copy * size + place, to[0] * size + to[1]))
    return lax.ppermute(x, ("replica", "seq"), pairs)


def pass_kernel(*refs):
    got_ref, base_ref, decay_ref = refs[:3]
    refs[-1][...] = decay_ref[...] * got_ref[...] + base_ref[...]


def pass_on(got, base, decay, after, name):
    return call(pass_kernel, [jax.ShapeDtypeStruct(base.shape, F32)], name=name, after=after)(
        got, base, decay
    )[0]


def chain(sizes, mine, made, decay, work):
    chunks = len(mine)
    size = sizes["seq"]
    if size == 1:
        for k in sorted(work):
            work[k](())
        return [(x, x, x) for x in mine]
    if size % 2:
        raise NotImplementedError
    index = lax.axis_index("seq")
    place = jnp.minimum(index, size - 1 - index)
    middle = size // 2 - 1
    got = {(0, c): hop(mine[c], sizes, 0) for c in range(chunks)}
    steps = [
        (at + c + (1 if at > middle else 0), at, c)
        for at in range(1, size - 1)
        for c in range(chunks)
    ]
    token = ()
    for count, (_, at, c) in enumerate(sorted(steps)):
        if count in work:
            token = work[count](token)
        if at > middle and c > 2:
            token = (*token, got[at, c - 2 - 1])
        base = mine[c] if at <= middle else made["factors"][5 + c]
        pay = pass_on(got[at - 1, c], base, decay, token, f"pass{min(count, 7)}")
        got[at, c] = hop(pay, sizes, at)
        token = (pay,)
    for k in sorted(work):
        if k >= len(steps):
            token = work[k](token)
    states = []
    for c in range(chunks):
        first, second, last = got[0, c], got[middle, c], got[size - 2, c]
        for at in range(1, middle):
            first = jnp.where(place == at + 1, got[at, c], first)
        for at in range(middle + 1, size - 2):
            second = jnp.where(place == size - 2 - at, got[at, c], second)
        states.append((first, second, last))
    return states


def sum_terms(x, later, axis, size):
    if size == 1:
        return [x]
    if size == 4:
        return [x, swap(x, axis, size, 1)] + [swap(later, axis, size, bit) for bit in (2, 3)]
    if size & (size - 1):
        return [lax.psum(x, axis)]
    bit = 1
    while 2 * bit < size:
        x = x + swap(x, axis, size, bit)
        bit *= 2
    return [x, swap(x, axis, size, bit)]


def small_terms(x, axes, sizes, between):
    bits = [(axis, 1 << k) for axis in axes for k in range(sizes[axis].bit_length() - 1)]
    if any(sizes[axis] & (sizes[axis] - 1) for axis in axes):
        x, bits = lax.psum(x, tuple(axes)), []
    after = ()
    for count, (axis, bit) in enumerate(bits):
        theirs = swap(x, axis, sizes[axis], bit)
        if count == len(bits) - 1:
            break
        x = call(add_kernel, [jax.ShapeDtypeStruct(x.shape, F32)], name=f"add{count}", after=after)(x, theirs)[0]
        after = between((x,)) if count == 0 else ()
    if len(bits) < 2:
        between((x,))
    return [x, theirs] if bits else [x]


def shards(sizes, values, gate_in, in_b, in_c, step_sizes, log_rates, skip_gain, grad_out):
    like = jax.ShapeDtypeStruct
    length, channels = values.shape[1:]
    heads = step_sizes.shape[1]
    state = in_b.shape[2]
    seq = sizes["seq"]
    rows = state // CHUNKS
    wide = like((length, channels), F32)
    wide_b = like((length, channels), BF16)
    share = like((length, state), F32)
    small = like((heads, length), F32)
    row = like((1, channels), F32)
    piece = like((rows, channels), F32)
    maps = like((length, state), BF16)

    out = call(
        functools.partial(states_kernel, seq),
        [wide_b, wide_b, wide_b, maps, maps, small, small, row, row, like((1, heads), F32)]
        + [piece] * CHUNKS,
        [
            pltpu.VMEM((heads, length), F32),
            pltpu.VMEM((1, heads), F32),
            pltpu.SemaphoreType.DMA((8,)),
        ],
        space=pltpu.HBM,
    )(
        values[0], gate_in[0], grad_out[0], in_b[0], in_c[0], step_sizes[0],
        log_rates.reshape(1, heads), skip_gain.reshape(1, heads),
    )
    vals, gate, grad, block_b, block_c, cumulative, negative, decay, slope, skip = out[:10]
    mine = out[10:]

    made = {}

    def intra(after):
        made["intra"] = call(
            intra_kernel,
            [wide, wide, share, share],
            [
                pltpu.VMEM((channels, length), BF16),
                pltpu.VMEM((channels, length), F32),
                pltpu.VMEM((length, length), F32),
            ],
            name="intra",
        )(vals, gate, grad, block_b, block_c, cumulative)
        return (made["intra"][2],)

    def factors(after):
        made["factors"] = call(
            functools.partial(factors_kernel, seq),
            [wide_b] * 3 + [like((state, channels), F32)] * 2 + [piece] * CHUNKS,
            name="factors",
        )(vals, gate, grad, block_b, block_c, cumulative, *(after if after else made["intra"][2:3]))
        return made["factors"][5:6]

    def prepare(after):
        made["prepare"] = call(
            prepare_kernel,
            [wide] * 6 + [small, like((2, heads), F32)],
            name="prepare",
        )(
            vals, gate, grad, cumulative, skip,
            *made["intra"][:2], *(after if after else made["intra"][2:3]),
        )
        return (made["prepare"][-1],)

    sums = max(seq - 2, 0) * CHUNKS
    states = chain(sizes, mine, made, decay, {0: intra, 1: factors, max(sums - 2, 2): prepare})
    sum_b, sum_c = made["intra"][2:]
    high, low, scaled, q, r = made["factors"][:5]
    coef, mamba, inner, growth, fall, grad_y, grad_cum, parts = made["prepare"]

    rate_row = jnp.zeros((1, channels), F32)
    terms, counts = [], []
    for i in range(PARTS):
        final = i == PARTS - 1
        count = CHUNKS // PARTS
        own = [x for group in states[i * count : (i + 1) * count] for x in group]
        rate_row = call(
            functools.partial(rate_kernel, seq, count, i * rows * count, heads, final),
            [like((2, heads), F32) if final else row],
            name=f"rate{i}",
        )(*own, q, r, slope, rate_row, parts)[0]
        share_of = call(
            functools.partial(share_kernel, seq, count, i * rows * count),
            [like((length, 2 * rows * count), F32)],
            name=f"share{i}",
            after=(rate_row,),
        )(*own, high, low, scaled, sum_b, sum_c)[0]
        if not final:
            own = sum_terms(share_of, share_of, "tensor", sizes["tensor"])
            terms += call(sum_kernel, [like(share_of.shape, F32)], name="sum")(*own)
            counts.append(1)

    def between(after):
        later = call(copy_kernel, [like(share_of.shape, F32)], name="later", after=after)(share_of)[0]
        made["share"] = sum_terms(share_of, later, "tensor", sizes["tensor"])
        return rest(after)

    def rest(after):
        made["rest"] = call(
            functools.partial(rest_kernel, seq, CHUNKS),
            [like((1, length, channels), BF16)] * 2
            + [like((1, heads, length), F32), like((1, heads), F32)],
            name="rest",
            after=(*after, *terms),
        )(
            *(x for group in states for x in group),
            vals, block_b, block_c, coef, mamba, inner, growth, fall, grad_y, grad_cum, decay, negative,
        )
        return (made["rest"][3],)

    own = small_terms(rate_row, ("seq", "replica"), sizes, between)
    for group in (made["share"], own):
        terms += group
        counts.append(len(group))
    grad_values, grad_gate, grad_steps, _ = made["rest"]
    grad_b, grad_c, rate_sum, skip_sum = call(
        functools.partial(last_kernel, tuple(counts)),
        [like((1, length, state), F32)] * 2 + [like((1, heads), F32)] * 2,
    )(*terms)
    return (
        grad_values,
        grad_gate,
        grad_b,
        grad_c,
        grad_steps,
        rate_sum.reshape(heads),
        skip_sum.reshape(heads),
    )


def solution(mesh):
    in_specs = (
        P("replica", "seq", "tensor"),
        P("replica", "seq", "tensor"),
        P("replica", "seq", None),
        P("replica", "seq", None),
        P("replica", "tensor", "seq"),
        P("tensor"),
        P("tensor"),
        P("replica", "seq", "tensor"),
    )
    out_specs = (
        P("replica", "seq", "tensor"),
        P("replica", "seq", "tensor"),
        P("replica", "seq", None),
        P("replica", "seq", None),
        P("replica", "tensor", "seq"),
        P("tensor"),
        P("tensor"),
    )
    body = functools.partial(shards, dict(mesh.shape))
    return jax.shard_map(body, mesh=mesh, in_specs=in_specs, out_specs=out_specs, check_vma=False)
```

```python
import functools

import jax
import jax.numpy as jnp
from jax import lax
from jax.experimental import pallas as pl
from jax.experimental.pallas import tpu as pltpu
from jax.sharding import PartitionSpec as P

F32 = jnp.float32
BF16 = jnp.bfloat16
VMEM_LIMIT = 24 * 1024 * 1024
LANES = 256
CHUNKS = 4
PARTS = 2
WEIGHTS = {'pass4': 30, 'pass5': 10, 'pass6': 300, 'pass7': 30, 'rate0': 30, 'rate1': 10, 'later': 30, 'sum': 100, 'add1': 100, 'rest': 30}


def split(x, parts):
    terms = []
    for _ in range(parts - 1):
        term = x.astype(BF16)
        terms.append(term)
        x = x - term.astype(F32)
    terms.append(x.astype(BF16))
    return terms


def mm(a, b):
    return lax.dot_general(a, b, (((1,), (0,)), ((), ())), preferred_element_type=F32)


def mm_nt(a, b):
    return lax.dot_general(a, b, (((1,), (1,)), ((), ())), preferred_element_type=F32)


def mm_tn(a, b):
    return lax.dot_general(a, b, (((0,), (0,)), ((), ())), preferred_element_type=F32)


def iota(shape, dim):
    return lax.broadcasted_iota(jnp.int32, shape, dim)


def to_column(row):
    n = row.shape[1]
    eye = iota((n, n), 0) == iota((n, n), 1)
    return jnp.sum(jnp.where(eye, row, 0.0), axis=1, keepdims=True)


def to_row(column):
    n = column.shape[0]
    eye = iota((n, n), 0) == iota((n, n), 1)
    return jnp.sum(jnp.where(eye, column, 0.0), axis=0, keepdims=True)


def head_map(heads, width, first, lanes):
    low = iota((heads, lanes), 0) * width
    channel = iota((heads, lanes), 1) + first
    return (channel >= low) & (channel < low + width)


def spread_map(heads, width, first, lanes):
    one = jnp.where(head_map(heads, width, first, lanes), 1.0, 0.0).astype(BF16)
    return jnp.concatenate([one, one, one], axis=0)


def rows_of_three(per_head):
    return jnp.concatenate(split(per_head, 3), axis=0)


def spread(three, first, lanes, width):
    heads = three.shape[0] // 3
    return mm_tn(three, spread_map(heads, width, first, lanes))


def scan_tokens(per_head, backward):
    heads, length = per_head.shape
    source = iota((length, length), 0)
    target = iota((length, length), 1)
    keep = source >= target if backward else source <= target
    sums = mm(rows_of_three(per_head), jnp.where(keep, 1.0, 0.0).astype(BF16))
    return sums[:heads] + sums[heads : 2 * heads] + sums[2 * heads :]


def channel_row(column, heads, width, first):
    mine = head_map(heads, width, first, LANES)
    return jnp.sum(jnp.where(mine, column, 0.0), axis=0, keepdims=True)


def head_column(row, heads, width, first):
    mine = head_map(heads, width, first, LANES)
    return jnp.sum(jnp.where(mine, row, 0.0), axis=1, keepdims=True)


def gate_parts(gate, grad):
    wide = gate.astype(F32)
    sigmoid = 1.0 / (1.0 + jnp.exp(-wide))
    return wide, sigmoid, grad.astype(F32) * (wide * sigmoid)


def put_rows(refs, here, value):
    start = 0
    for ref in refs:
        rows = ref.shape[0]
        ref[:, here] = value[start : start + rows]
        start += rows


def states_kernel(size, *refs):
    sources, outs, (steps_ref, lr_ref, sems) = refs[:8], refs[8:-3], refs[-3:]
    v_ref, gate_ref, go_ref, b_ref, c_ref = outs[:5]
    cum_ref, neg_ref, decay_ref, slope_ref, skip_ref = outs[5:10]
    mine_refs = outs[10:]
    targets = (v_ref, gate_ref, go_ref, b_ref, c_ref, steps_ref, lr_ref, skip_ref)
    copies = [
        pltpu.make_async_copy(source, target, sems.at[i])
        for i, (source, target) in enumerate(zip(sources, targets))
    ]

    def start(*which):
        for i in which:
            copies[i].start()

    start(6, 5)
    if size == 1:
        start(3, 0, 4, 1, 2, 7)
    else:
        lower = lax.axis_index("seq") < size // 2
        pl.when(lower)(lambda: start(3, 0, 4, 1, 2, 7))
        pl.when(jnp.logical_not(lower))(lambda: start(4, 1, 2, 3, 0, 7))
    copies[6].wait()
    copies[5].wait()
    length, channels = v_ref.shape
    heads = steps_ref.shape[0]
    width = channels // heads
    rates = jnp.exp(to_column(lr_ref[...]))
    cumulative = scan_tokens(-rates * steps_ref[...], False)
    total = cumulative[:, -1:]
    decay = jnp.exp(total)
    cum_ref[...] = cumulative
    neg_ref[...] = jnp.broadcast_to(-rates, (heads, length))
    for first in range(0, channels, LANES):
        here = pl.ds(first, LANES)
        decay_ref[:, here] = channel_row(decay, heads, width, first)
        slope_ref[:, here] = channel_row(total * decay, heads, width, first)

    def local():
        copies[3].wait()
        b_t = b_ref[...].astype(F32).T.astype(BF16)
        fall = rows_of_three(jnp.exp(total - cumulative))
        copies[0].wait()
        for first in range(0, channels, LANES):
            here = pl.ds(first, LANES)
            scaled = spread(fall, first, LANES, width) * v_ref[:, here].astype(F32)
            put_rows(mine_refs, here, mm(b_t, scaled.astype(BF16)))
        for i in (1, 2, 4, 7):
            copies[i].wait()

    def pulled():
        copies[4].wait()
        c_t = c_ref[...].astype(F32).T.astype(BF16)
        growth = rows_of_three(jnp.exp(cumulative))
        copies[1].wait()
        copies[2].wait()
        for first in range(0, channels, LANES):
            here = pl.ds(first, LANES)
            _, _, grad_y = gate_parts(gate_ref[:, here], go_ref[:, here])
            high, low = split(spread(growth, first, LANES, width) * grad_y, 2)
            put_rows(mine_refs, here, mm(c_t, high) + mm(c_t, low))
        for i in (0, 3, 7):
            copies[i].wait()

    if size == 1:
        local()
    else:
        pl.when(lower)(local)
        pl.when(jnp.logical_not(lower))(pulled)


def intra_kernel(
    v_ref, gate_ref, go_ref, b_ref, c_ref, cum_ref,
    intra_ref, inner_ref, sum_b_ref, sum_c_ref, grad_t_ref, inner_t_ref, acc_ref,
):
    length, channels = v_ref.shape
    heads = cum_ref.shape[0]
    width = channels // heads
    half = length // 2
    pair = 2 * width
    cumulative = cum_ref[...]
    columns = cumulative.T
    scores = mm_nt(c_ref[...], b_ref[...])
    causal = iota((half, half), 0) >= iota((half, half), 1)
    left = iota((1, pair), 1) < width
    acc_ref[...] = jnp.zeros_like(acc_ref)

    def blocks(x):
        return x[:half, :half], x[half:, :half], x[half:, half:]

    scores_00, scores_10, scores_11 = blocks(scores)
    for first in range(0, channels, pair):
        here = pl.ds(first, pair)
        _, _, grad_y = gate_parts(gate_ref[:, here], go_ref[:, here])
        grad_t_ref[here, :] = grad_y.T.astype(BF16)
        vals = v_ref[:, here]
        pieces = []
        for side in range(2):
            head = first // width + side
            own = left if side == 0 else jnp.logical_not(left)
            row = cumulative[head : head + 1, :]
            column = columns[:, head : head + 1]
            row_0, row_1 = row[:, :half], row[:, half:]
            column_0, column_1 = column[:half], column[half:]
            decay_00 = jnp.exp(jnp.where(causal, column_0 - row_0, -1e30))
            decay_10 = jnp.exp(column_1 - row_0)
            decay_11 = jnp.exp(jnp.where(causal, column_1 - row_1, -1e30))
            mix_00 = (scores_00 * decay_00).astype(BF16)
            mix_10 = (scores_10 * decay_10).astype(BF16)
            mix_11 = (scores_11 * decay_11).astype(BF16)
            low_rows = jnp.concatenate([mix_10, mix_11], axis=1)
            pieces.append((mm(mix_00, vals[:half]), mm(low_rows, vals)))
            head_grad = jnp.where(own, grad_y, 0.0).astype(BF16)
            mixed_0 = mm_nt(head_grad[:half], vals[:half])
            mixed_1 = mm_nt(head_grad[half:], vals)
            acc_ref[:half, :half] += mixed_0 * decay_00
            acc_ref[half:, :half] += mixed_1[:, :half] * decay_10
            acc_ref[half:, half:] += mixed_1[:, half:] * decay_11
            mine = pl.ds(first + side * width, width)
            grad_t = grad_t_ref[mine, :]
            inner_t_ref[mine, :half] = mm(grad_t[:, :half], mix_00) + mm(grad_t[:, half:], mix_10)
            inner_t_ref[mine, half:] = mm(grad_t[:, half:], mix_11)
        intra_ref[:half, here] = jnp.where(left, pieces[0][0], pieces[1][0])
        intra_ref[half:, here] = jnp.where(left, pieces[0][1], pieces[1][1])
        inner_ref[:, here] = inner_t_ref[here, :].T
    shares = acc_ref[...]
    high, low = split(shares, 2)
    sum_c_ref[...] = mm(high, b_ref[...]) + mm(low, b_ref[...])
    high, low = split(shares.T, 2)
    sum_b_ref[...] = mm(high, c_ref[...]) + mm(low, c_ref[...])


def factors_kernel(
    size, v_ref, gate_ref, go_ref, b_ref, c_ref, cum_ref, after_ref,
    high_ref, low_ref, scaled_ref, q_ref, r_ref, *other_refs,
):
    length, channels = v_ref.shape
    heads = cum_ref.shape[0]
    width = channels // heads
    cumulative = cum_ref[...]
    left_over = cumulative[:, -1:] - cumulative
    growth = rows_of_three(jnp.exp(cumulative))
    fall = rows_of_three(jnp.exp(left_over))
    growth_slope = rows_of_three(cumulative * jnp.exp(cumulative))
    fall_slope = rows_of_three(left_over * jnp.exp(left_over))
    b_t = b_ref[...].astype(F32).T.astype(BF16)
    c_t = c_ref[...].astype(F32).T.astype(BF16)
    for first in range(0, channels, LANES):
        here = pl.ds(first, LANES)
        _, _, grad_y = gate_parts(gate_ref[:, here], go_ref[:, here])
        vals = v_ref[:, here].astype(F32)
        high, low = split(spread(growth, first, LANES, width) * grad_y, 2)
        high_ref[:, here] = high
        low_ref[:, here] = low
        scaled_ref[:, here] = (spread(fall, first, LANES, width) * vals).astype(BF16)
        high, low = split(spread(growth_slope, first, LANES, width) * grad_y, 2)
        q_ref[:, here] = mm(c_t, high) + mm(c_t, low)
        high, low = split(spread(fall_slope, first, LANES, width) * vals, 2)
        r_ref[:, here] = mm(b_t, high) + mm(b_t, low)

    def pulled():
        put_rows(other_refs, slice(None), mm(c_t, high_ref[...]) + mm(c_t, low_ref[...]))

    def local():
        put_rows(other_refs, slice(None), mm(b_t, scaled_ref[...]))

    if size == 1:
        pulled()
    else:
        lower = lax.axis_index("seq") < size // 2
        pl.when(lower)(pulled)
        pl.when(jnp.logical_not(lower))(local)


def prepare_kernel(
    v_ref, gate_ref, go_ref, cum_ref, skip_ref, intra_ref, in_inner_ref, after_ref,
    coef_ref, mamba_ref, inner_ref, growth_ref, fall_ref, gy_ref, gcum_ref, parts_ref,
):
    length, channels = v_ref.shape
    heads = cum_ref.shape[0]
    width = channels // heads
    cumulative = cum_ref[...]
    growth_three = rows_of_three(jnp.exp(cumulative))
    fall_three = rows_of_three(jnp.exp(cumulative[:, -1:] - cumulative))
    skip_column = to_column(skip_ref[...])
    grad_cum = jnp.zeros((heads, length), F32)
    skip_part = jnp.zeros((heads, 1), F32)
    for first in range(0, channels, LANES):
        here = pl.ds(first, LANES)
        wide, sigmoid, grad_y = gate_parts(gate_ref[:, here], go_ref[:, here])
        vals = v_ref[:, here].astype(F32)
        skip = channel_row(skip_column, heads, width, first)
        growth_ref[:, here] = spread(growth_three, first, LANES, width)
        fall_ref[:, here] = spread(fall_three, first, LANES, width)
        gy_ref[:, here] = grad_y
        coef_ref[:, here] = go_ref[:, here].astype(F32) * sigmoid * (1.0 + wide * (1.0 - sigmoid))
        intra = intra_ref[:, here]
        inner = in_inner_ref[:, here]
        mamba_ref[:, here] = intra + skip * vals
        inner_ref[:, here] = inner + skip * grad_y
        high, low = split(grad_y.astype(BF16).astype(F32) * intra - vals * inner, 2)
        head_rows = jnp.where(head_map(heads, width, first, LANES), 1.0, 0.0).astype(BF16)
        grad_cum = grad_cum + mm_nt(head_rows, high) + mm_nt(head_rows, low)
        skip_row = jnp.sum(grad_y * vals, axis=0, keepdims=True)
        skip_part = skip_part + head_column(skip_row, heads, width, first)
    gcum_ref[...] = grad_cum
    rate_part = jnp.sum(grad_cum * cumulative, axis=1, keepdims=True)
    parts_ref[...] = jnp.concatenate([to_row(rate_part), to_row(skip_part)], axis=0)


def pick(size, first, second, last):
    if size == 1:
        return jnp.zeros_like(first), jnp.zeros_like(first)
    if size % 2:
        return first, second
    index = lax.axis_index("seq")
    lower = index < size // 2
    edge = jnp.logical_or(index == 0, index == size - 1)
    first = jnp.where(edge, 0.0, first)
    second = jnp.where(edge, last, second)
    return jnp.where(lower, first, second), jnp.where(lower, second, first)


def picked(size, states, here):
    both = [pick(size, *(ref[:, here] for ref in state)) for state in states]
    return jnp.concatenate([x[0] for x in both], axis=0), jnp.concatenate([x[1] for x in both], axis=0)


def rate_kernel(size, pieces, start, heads, final, *refs):
    states, refs = [refs[3 * i : 3 * i + 3] for i in range(pieces)], refs[3 * pieces :]
    q_ref, r_ref, slope_ref, row_ref, parts_ref, out_ref = *refs[:5], refs[-1]
    rows, channels = pieces * states[0][0].shape[0], q_ref.shape[1]
    here = slice(start, start + rows)
    rate_part = jnp.zeros((heads, 1), F32)
    for begin in range(0, channels, LANES):
        lanes = pl.ds(begin, LANES)
        entering, after = picked(size, states, lanes)
        terms = entering * q_ref[here, lanes] + after * (
            r_ref[here, lanes] + slope_ref[:, lanes] * entering
        )
        row = row_ref[:, lanes] + jnp.sum(terms, axis=0, keepdims=True)
        if final:
            rate_part = rate_part + head_column(row, heads, channels // heads, begin)
        else:
            out_ref[:, lanes] = row
    if final:
        base = parts_ref[...]
        out_ref[...] = jnp.concatenate([base[:1] + to_row(rate_part), base[1:]], axis=0)


def share_kernel(size, pieces, start, *refs):
    states, refs = [refs[3 * i : 3 * i + 3] for i in range(pieces)], refs[3 * pieces :]
    high_ref, low_ref, scaled_ref, sum_b_ref, sum_c_ref = refs[:5]
    rows, channels = pieces * states[0][0].shape[0], scaled_ref.shape[1]
    here = slice(start, start + rows)
    grad_b = sum_b_ref[:, here]
    grad_c = sum_c_ref[:, here]
    pairs_b = pairs_c = jnp.zeros((scaled_ref.shape[0], 2 * rows), F32)
    for begin in range(0, channels, LANES):
        lanes = pl.ds(begin, LANES)
        entering, after = picked(size, states, lanes)
        enter_high, enter_low = split(entering, 2)
        after_high, after_low = split(after, 2)
        high, low, scaled = high_ref[:, lanes], low_ref[:, lanes], scaled_ref[:, lanes]
        pairs_c = pairs_c + mm_nt(high, jnp.concatenate([enter_low, enter_high], axis=0))
        pairs_b = pairs_b + mm_nt(scaled, jnp.concatenate([after_low, after_high], axis=0))
        grad_c = grad_c + mm_nt(low, enter_high)
    grad_b = grad_b + (pairs_b[:, :rows] + pairs_b[:, rows:])
    grad_c = grad_c + (pairs_c[:, :rows] + pairs_c[:, rows:])
    refs[-1][...] = jnp.concatenate([grad_b, grad_c], axis=1)


def rest_kernel(size, pieces, *refs):
    states, refs = [refs[3 * i : 3 * i + 3] for i in range(pieces)], refs[3 * pieces :]
    (
        v_ref, b_ref, c_ref, coef_ref, mamba_ref, inner_ref, growth_ref, fall_ref, gy_ref,
        gcum_ref, decay_ref, neg_ref, *_, gv_ref, gg_ref, gs_ref,
    ) = refs
    length, channels = v_ref.shape
    heads = gcum_ref.shape[0]
    width = channels // heads
    twice_b, twice_c = (jnp.concatenate([ref[...], ref[...]], axis=1) for ref in (b_ref, c_ref))
    grad_cum = gcum_ref[...]
    grad_total = jnp.zeros((heads, 1), F32)
    for first in range(0, channels, LANES):
        here = pl.ds(first, LANES)
        entering, after = picked(size, states, here)
        inter = growth_ref[:, here] * mm(twice_c, jnp.concatenate(split(entering, 2), axis=0))
        outer = fall_ref[:, here] * mm(twice_b, jnp.concatenate(split(after, 2), axis=0))
        gg_ref[0, :, here] = (coef_ref[:, here] * (mamba_ref[:, here] + inter)).astype(BF16)
        gv_ref[0, :, here] = (inner_ref[:, here] + outer).astype(BF16)
        pulled = v_ref[:, here].astype(F32) * outer
        high, low = split(gy_ref[:, here] * inter - pulled, 2)
        head_rows = jnp.where(head_map(heads, width, first, LANES), 1.0, 0.0).astype(BF16)
        grad_cum = grad_cum + mm_nt(head_rows, high) + mm_nt(head_rows, low)
        total_row = jnp.sum(pulled, axis=0, keepdims=True) + decay_ref[:, here] * jnp.sum(
            after * entering, axis=0, keepdims=True
        )
        grad_total = grad_total + head_column(total_row, heads, width, first)
    gs_ref[0] = neg_ref[...] * (scan_tokens(grad_cum, True) + grad_total)


def tree(values):
    while len(values) > 1:
        values = [sum(values[i + 1 : i + 2], values[i]) for i in range(0, len(values), 2)]
    return values[0]


def copy_kernel(x_ref, *refs):
    refs[-1][...] = x_ref[...]


def add_kernel(x_ref, y_ref, *refs):
    refs[-1][...] = x_ref[...] + y_ref[...]


def sum_kernel(*refs):
    refs[-1][...] = tree([ref[...] for ref in refs[:-1]])


def last_kernel(counts, *refs):
    refs, (gb_ref, gc_ref, rate_ref, skip_ref) = refs[:-4], refs[-4:]
    sums = []
    for count in counts:
        sums.append(tree([ref[...] for ref in refs[:count]]))
        refs = refs[count:]
    *shares, small = sums
    start = 0
    for both in shares:
        rows = both.shape[1] // 2
        gb_ref[0, :, start : start + rows] = both[:, :rows]
        gc_ref[0, :, start : start + rows] = both[:, rows:]
        start += rows
    rate_ref[...] = small[:1]
    skip_ref[...] = small[1:]


def call(kernel, outs, scratch=(), name="", space=pltpu.VMEM, after=()):
    def run(*args):
        if space == pltpu.HBM:
            args = [pltpu.with_memory_space_constraint(a, space) for a in args]
        specs = [pl.BlockSpec(memory_space=space)] * len(args)
        specs += [pl.BlockSpec(memory_space=pl.ANY)] * len(after)
        args = (*args, *after)
        return pl.pallas_call(
            kernel,
            out_shape=tuple(outs),
            in_specs=specs,
            out_specs=tuple(pl.BlockSpec(memory_space=pltpu.VMEM) for _ in outs),
            scratch_shapes=list(scratch),
            compiler_params=pltpu.CompilerParams(vmem_limit_bytes=VMEM_LIMIT),
            cost_estimate=pl.CostEstimate(
                flops=WEIGHTS.get(name, 0) * 10**7, bytes_accessed=0, transcendentals=0
            ),
        )(*args)

    return run


def swap(x, axis, size, bit):
    return lax.ppermute(x, axis, [(i, i ^ bit) for i in range(size)])


def hop(x, sizes, step):
    size, copies = sizes["seq"], sizes["replica"]
    pairs = []
    for copy in range(copies):
        for place in range(size):
            to = (copy ^ 1 if copies % 2 == 0 else copy, place)
            for low in (step, size - 2 - step):
                if place in (low, low + 1):
                    to = (copy, 2 * low + 1 - place)
            pairs.append((copy * size + place, to[0] * size + to[1]))
    return lax.ppermute(x, ("replica", "seq"), pairs)


def pass_kernel(*refs):
    got_ref, base_ref, decay_ref = refs[:3]
    refs[-1][...] = decay_ref[...] * got_ref[...] + base_ref[...]


def pass_on(got, base, decay, after, name):
    return call(pass_kernel, [jax.ShapeDtypeStruct(base.shape, F32)], name=name, after=after)(
        got, base, decay
    )[0]


def chain(sizes, mine, made, decay, work):
    chunks = len(mine)
    size = sizes["seq"]
    if size == 1:
        for k in sorted(work):
            work[k](())
        return [(x, x, x) for x in mine]
    if size % 2:
        raise NotImplementedError
    index = lax.axis_index("seq")
    place = jnp.minimum(index, size - 1 - index)
    middle = size // 2 - 1
    got = {(0, c): hop(mine[c], sizes, 0) for c in range(chunks)}
    steps = [
        (at + c + (1 if at > middle else 0), at, c)
        for at in range(1, size - 1)
        for c in range(chunks)
    ]
    token = ()
    for count, (_, at, c) in enumerate(sorted(steps)):
        if count in work:
            token = work[count](token)
        if at > middle and c > 2:
            token = (*token, got[at, c - 2 - 1])
        base = mine[c] if at <= middle else made["factors"][5 + c]
        pay = pass_on(got[at - 1, c], base, decay, token, f"pass{min(count, 7)}")
        got[at, c] = hop(pay, sizes, at)
        token = (pay,)
    for k in sorted(work):
        if k >= len(steps):
            token = work[k](token)
    states = []
    for c in range(chunks):
        first, second, last = got[0, c], got[middle, c], got[size - 2, c]
        for at in range(1, middle):
            first = jnp.where(place == at + 1, got[at, c], first)
        for at in range(middle + 1, size - 2):
            second = jnp.where(place == size - 2 - at, got[at, c], second)
        states.append((first, second, last))
    return states


def sum_terms(x, later, axis, size):
    if size == 1:
        return [x]
    if size == 4:
        return [x, swap(x, axis, size, 1)] + [swap(later, axis, size, bit) for bit in (2, 3)]
    if size & (size - 1):
        return [lax.psum(x, axis)]
    bit = 1
    while 2 * bit < size:
        x = x + swap(x, axis, size, bit)
        bit *= 2
    return [x, swap(x, axis, size, bit)]


def small_terms(x, sizes, hooks):
    axes = ("seq", "replica")
    along, across = ([(axis, 1 << k) for k in range(sizes[axis].bit_length() - 1)] for axis in axes)
    bits = along[:1] + across + along[1:]
    if any(sizes[axis] & (sizes[axis] - 1) for axis in axes):
        x, bits = lax.psum(x, axes), []
    for count, (axis, bit) in enumerate(bits):
        theirs = swap(x, axis, sizes[axis], bit)
        if count == len(bits) - 1:
            break
        x = call(add_kernel, [jax.ShapeDtypeStruct(x.shape, F32)], name=f"add{count}")(x, theirs)[0]
        if count < len(hooks):
            hooks[count]((x,))
    for hook in hooks[max(len(bits) - 1, 0) :]:
        hook((x,))
    return [x, theirs] if bits else [x]


def shards(sizes, values, gate_in, in_b, in_c, step_sizes, log_rates, skip_gain, grad_out):
    like = jax.ShapeDtypeStruct
    length, channels = values.shape[1:]
    heads = step_sizes.shape[1]
    state = in_b.shape[2]
    seq = sizes["seq"]
    rows = state // CHUNKS
    wide = like((length, channels), F32)
    wide_b = like((length, channels), BF16)
    share = like((length, state), F32)
    small = like((heads, length), F32)
    row = like((1, channels), F32)
    piece = like((rows, channels), F32)
    maps = like((length, state), BF16)

    out = call(
        functools.partial(states_kernel, seq),
        [wide_b, wide_b, wide_b, maps, maps, small, small, row, row, like((1, heads), F32)]
        + [piece] * CHUNKS,
        [
            pltpu.VMEM((heads, length), F32),
            pltpu.VMEM((1, heads), F32),
            pltpu.SemaphoreType.DMA((8,)),
        ],
        space=pltpu.HBM,
    )(
        values[0], gate_in[0], grad_out[0], in_b[0], in_c[0], step_sizes[0],
        log_rates.reshape(1, heads), skip_gain.reshape(1, heads),
    )
    vals, gate, grad, block_b, block_c, cumulative, negative, decay, slope, skip = out[:10]
    mine = out[10:]

    made = {}

    def intra(after):
        made["intra"] = call(
            intra_kernel,
            [wide, wide, share, share],
            [
                pltpu.VMEM((channels, length), BF16),
                pltpu.VMEM((channels, length), F32),
                pltpu.VMEM((length, length), F32),
            ],
            name="intra",
        )(vals, gate, grad, block_b, block_c, cumulative)
        return (made["intra"][2],)

    def factors(after):
        made["factors"] = call(
            functools.partial(factors_kernel, seq),
            [wide_b] * 3 + [like((state, channels), F32)] * 2 + [piece] * CHUNKS,
            name="factors",
        )(vals, gate, grad, block_b, block_c, cumulative, *(after if after else made["intra"][2:3]))
        return made["factors"][5:6]

    def prepare(after):
        made["prepare"] = call(
            prepare_kernel,
            [wide] * 6 + [small, like((2, heads), F32)],
            name="prepare",
        )(
            vals, gate, grad, cumulative, skip,
            *made["intra"][:2], *(after if after else made["intra"][2:3]),
        )
        return (made["prepare"][-1],)

    sums = max(seq - 2, 0) * CHUNKS
    states = chain(sizes, mine, made, decay, {0: intra, 1: factors, max(sums - 2, 2): prepare})
    sum_b, sum_c = made["intra"][2:]
    high, low, scaled, q, r = made["factors"][:5]
    coef, mamba, inner, growth, fall, grad_y, grad_cum, parts = made["prepare"]

    rate_row = jnp.zeros((1, channels), F32)
    terms, counts = [], []
    for i in range(PARTS):
        final = i == PARTS - 1
        count = CHUNKS // PARTS
        own = [x for group in states[i * count : (i + 1) * count] for x in group]
        rate_row = call(
            functools.partial(rate_kernel, seq, count, i * rows * count, heads, final),
            [like((2, heads), F32) if final else row],
            name=f"rate{i}",
        )(*own, q, r, slope, rate_row, parts)[0]
        share_of = call(
            functools.partial(share_kernel, seq, count, i * rows * count),
            [like((length, 2 * rows * count), F32)],
            name=f"share{i}",
            after=(rate_row,),
        )(*own, high, low, scaled, sum_b, sum_c)[0]
        if not final:
            own = sum_terms(share_of, share_of, "tensor", sizes["tensor"])
            terms += call(sum_kernel, [like(share_of.shape, F32)], name="sum")(*own)
            counts.append(1)

    def exchange(after):
        later = call(copy_kernel, [like(share_of.shape, F32)], name="later", after=after)(share_of)[0]
        made["share"] = sum_terms(share_of, later, "tensor", sizes["tensor"])

    def rest(after):
        made["rest"] = call(
            functools.partial(rest_kernel, seq, CHUNKS),
            [like((1, length, channels), BF16)] * 2 + [like((1, heads, length), F32)],
            name="rest",
            after=(*after, *terms),
        )(
            *(x for group in states for x in group),
            vals, block_b, block_c, coef, mamba, inner, growth, fall, grad_y, grad_cum, decay, negative,
        )

    own = small_terms(rate_row, sizes, (exchange, rest))
    for group in (made["share"], own):
        terms += group
        counts.append(len(group))
    grad_values, grad_gate, grad_steps = made["rest"]
    grad_b, grad_c, rate_sum, skip_sum = call(
        functools.partial(last_kernel, tuple(counts)),
        [like((1, length, state), F32)] * 2 + [like((1, heads), F32)] * 2,
    )(*terms)
    return (
        grad_values,
        grad_gate,
        grad_b,
        grad_c,
        grad_steps,
        rate_sum.reshape(heads),
        skip_sum.reshape(heads),
    )


def solution(mesh):
    in_specs = (
        P("replica", "seq", "tensor"),
        P("replica", "seq", "tensor"),
        P("replica", "seq", None),
        P("replica", "seq", None),
        P("replica", "tensor", "seq"),
        P("tensor"),
        P("tensor"),
        P("replica", "seq", "tensor"),
    )
    out_specs = (
        P("replica", "seq", "tensor"),
        P("replica", "seq", "tensor"),
        P("replica", "seq", None),
        P("replica", "seq", None),
        P("replica", "tensor", "seq"),
        P("tensor"),
        P("tensor"),
    )
    body = functools.partial(shards, dict(mesh.shape))
    return jax.shard_map(body, mesh=mesh, in_specs=in_specs, out_specs=out_specs, check_vma=False)
```

```python
import functools

import jax
import jax.numpy as jnp
from jax import lax
from jax.experimental import pallas as pl
from jax.experimental.pallas import tpu as pltpu
from jax.sharding import PartitionSpec as P

F32 = jnp.float32
BF16 = jnp.bfloat16
VMEM_LIMIT = 24 * 1024 * 1024
LANES = 256
CHUNKS = 4
PARTS = 2
WEIGHTS = {'pass4': 30, 'pass5': 10, 'pass6': 300, 'pass7': 30, 'rate0': 30, 'rate1': 10, 'later': 30, 'sum': 100, 'add1': 100, 'rest': 30}


def split(x, parts):
    terms = []
    for _ in range(parts - 1):
        term = x.astype(BF16)
        terms.append(term)
        x = x - term.astype(F32)
    terms.append(x.astype(BF16))
    return terms


def mm(a, b):
    return lax.dot_general(a, b, (((1,), (0,)), ((), ())), preferred_element_type=F32)


def mm_nt(a, b):
    return lax.dot_general(a, b, (((1,), (1,)), ((), ())), preferred_element_type=F32)


def mm_tn(a, b):
    return lax.dot_general(a, b, (((0,), (0,)), ((), ())), preferred_element_type=F32)


def iota(shape, dim):
    return lax.broadcasted_iota(jnp.int32, shape, dim)


def to_column(row):
    n = row.shape[1]
    eye = iota((n, n), 0) == iota((n, n), 1)
    return jnp.sum(jnp.where(eye, row, 0.0), axis=1, keepdims=True)


def to_row(column):
    n = column.shape[0]
    eye = iota((n, n), 0) == iota((n, n), 1)
    return jnp.sum(jnp.where(eye, column, 0.0), axis=0, keepdims=True)


def head_map(heads, width, first, lanes):
    low = iota((heads, lanes), 0) * width
    channel = iota((heads, lanes), 1) + first
    return (channel >= low) & (channel < low + width)


def spread_map(heads, width, first, lanes):
    one = jnp.where(head_map(heads, width, first, lanes), 1.0, 0.0).astype(BF16)
    return jnp.concatenate([one, one, one], axis=0)


def rows_of_three(per_head):
    return jnp.concatenate(split(per_head, 3), axis=0)


def spread(three, first, lanes, width):
    heads = three.shape[0] // 3
    return mm_tn(three, spread_map(heads, width, first, lanes))


def scan_tokens(per_head, backward):
    heads, length = per_head.shape
    source = iota((length, length), 0)
    target = iota((length, length), 1)
    keep = source >= target if backward else source <= target
    sums = mm(rows_of_three(per_head), jnp.where(keep, 1.0, 0.0).astype(BF16))
    return sums[:heads] + sums[heads : 2 * heads] + sums[2 * heads :]


def channel_row(column, heads, width, first):
    mine = head_map(heads, width, first, LANES)
    return jnp.sum(jnp.where(mine, column, 0.0), axis=0, keepdims=True)


def head_column(row, heads, width, first):
    mine = head_map(heads, width, first, LANES)
    return jnp.sum(jnp.where(mine, row, 0.0), axis=1, keepdims=True)


def gate_parts(gate, grad):
    wide = gate.astype(F32)
    sigmoid = 1.0 / (1.0 + jnp.exp(-wide))
    return wide, sigmoid, grad.astype(F32) * (wide * sigmoid)


def put_rows(refs, here, value):
    start = 0
    for ref in refs:
        rows = ref.shape[0]
        ref[:, here] = value[start : start + rows]
        start += rows


def states_kernel(size, *refs):
    sources, outs, (steps_ref, lr_ref, sems) = refs[:8], refs[8:-3], refs[-3:]
    v_ref, gate_ref, go_ref, b_ref, c_ref = outs[:5]
    cum_ref, neg_ref, decay_ref, slope_ref, skip_ref = outs[5:10]
    mine_refs = outs[10:]
    targets = (v_ref, gate_ref, go_ref, b_ref, c_ref, steps_ref, lr_ref, skip_ref)
    copies = [
        pltpu.make_async_copy(source, target, sems.at[i])
        for i, (source, target) in enumerate(zip(sources, targets))
    ]

    def start(*which):
        for i in which:
            copies[i].start()

    start(6, 5)
    if size == 1:
        start(3, 0, 4, 1, 2, 7)
    else:
        lower = lax.axis_index("seq") < size // 2
        pl.when(lower)(lambda: start(3, 0, 4, 1, 2, 7))
        pl.when(jnp.logical_not(lower))(lambda: start(4, 1, 2, 3, 0, 7))
    copies[6].wait()
    copies[5].wait()
    length, channels = v_ref.shape
    heads = steps_ref.shape[0]
    width = channels // heads
    rates = jnp.exp(to_column(lr_ref[...]))
    cumulative = scan_tokens(-rates * steps_ref[...], False)
    total = cumulative[:, -1:]
    decay = jnp.exp(total)
    cum_ref[...] = cumulative
    neg_ref[...] = jnp.broadcast_to(-rates, (heads, length))
    for first in range(0, channels, LANES):
        here = pl.ds(first, LANES)
        decay_ref[:, here] = channel_row(decay, heads, width, first)
        slope_ref[:, here] = channel_row(total * decay, heads, width, first)

    def local():
        copies[3].wait()
        b_t = b_ref[...].astype(F32).T.astype(BF16)
        fall = rows_of_three(jnp.exp(total - cumulative))
        copies[0].wait()
        for first in range(0, channels, LANES):
            here = pl.ds(first, LANES)
            scaled = spread(fall, first, LANES, width) * v_ref[:, here].astype(F32)
            put_rows(mine_refs, here, mm(b_t, scaled.astype(BF16)))
        for i in (1, 2, 4, 7):
            copies[i].wait()

    def pulled():
        copies[4].wait()
        c_t = c_ref[...].astype(F32).T.astype(BF16)
        growth = rows_of_three(jnp.exp(cumulative))
        copies[1].wait()
        copies[2].wait()
        for first in range(0, channels, LANES):
            here = pl.ds(first, LANES)
            _, _, grad_y = gate_parts(gate_ref[:, here], go_ref[:, here])
            high, low = split(spread(growth, first, LANES, width) * grad_y, 2)
            put_rows(mine_refs, here, mm(c_t, high) + mm(c_t, low))
        for i in (0, 3, 7):
            copies[i].wait()

    if size == 1:
        local()
    else:
        pl.when(lower)(local)
        pl.when(jnp.logical_not(lower))(pulled)


def intra_kernel(
    v_ref, gate_ref, go_ref, b_ref, c_ref, cum_ref,
    intra_ref, inner_ref, sum_b_ref, sum_c_ref, grad_t_ref, inner_t_ref, acc_ref,
):
    length, channels = v_ref.shape
    heads = cum_ref.shape[0]
    width = channels // heads
    half = length // 2
    pair = 2 * width
    cumulative = cum_ref[...]
    columns = cumulative.T
    scores = mm_nt(c_ref[...], b_ref[...])
    causal = iota((half, half), 0) >= iota((half, half), 1)
    left = iota((1, pair), 1) < width
    acc_ref[...] = jnp.zeros_like(acc_ref)

    def blocks(x):
        return x[:half, :half], x[half:, :half], x[half:, half:]

    scores_00, scores_10, scores_11 = blocks(scores)
    for first in range(0, channels, pair):
        here = pl.ds(first, pair)
        _, _, grad_y = gate_parts(gate_ref[:, here], go_ref[:, here])
        grad_t_ref[here, :] = grad_y.T.astype(BF16)
        vals = v_ref[:, here]
        pieces = []
        for side in range(2):
            head = first // width + side
            own = left if side == 0 else jnp.logical_not(left)
            row = cumulative[head : head + 1, :]
            column = columns[:, head : head + 1]
            row_0, row_1 = row[:, :half], row[:, half:]
            column_0, column_1 = column[:half], column[half:]
            decay_00 = jnp.exp(jnp.where(causal, column_0 - row_0, -1e30))
            decay_10 = jnp.exp(column_1 - row_0)
            decay_11 = jnp.exp(jnp.where(causal, column_1 - row_1, -1e30))
            mix_00 = (scores_00 * decay_00).astype(BF16)
            mix_10 = (scores_10 * decay_10).astype(BF16)
            mix_11 = (scores_11 * decay_11).astype(BF16)
            low_rows = jnp.concatenate([mix_10, mix_11], axis=1)
            pieces.append((mm(mix_00, vals[:half]), mm(low_rows, vals)))
            head_grad = jnp.where(own, grad_y, 0.0).astype(BF16)
            mixed_0 = mm_nt(head_grad[:half], vals[:half])
            mixed_1 = mm_nt(head_grad[half:], vals)
            acc_ref[:half, :half] += mixed_0 * decay_00
            acc_ref[half:, :half] += mixed_1[:, :half] * decay_10
            acc_ref[half:, half:] += mixed_1[:, half:] * decay_11
            mine = pl.ds(first + side * width, width)
            grad_t = grad_t_ref[mine, :]
            inner_t_ref[mine, :half] = mm(grad_t[:, :half], mix_00) + mm(grad_t[:, half:], mix_10)
            inner_t_ref[mine, half:] = mm(grad_t[:, half:], mix_11)
        intra_ref[:half, here] = jnp.where(left, pieces[0][0], pieces[1][0])
        intra_ref[half:, here] = jnp.where(left, pieces[0][1], pieces[1][1])
        inner_ref[:, here] = inner_t_ref[here, :].T
    shares = acc_ref[...]
    high, low = split(shares, 2)
    sum_c_ref[...] = mm(high, b_ref[...]) + mm(low, b_ref[...])
    high, low = split(shares.T, 2)
    sum_b_ref[...] = mm(high, c_ref[...]) + mm(low, c_ref[...])


def factors_kernel(
    size, v_ref, gate_ref, go_ref, b_ref, c_ref, cum_ref, after_ref,
    high_ref, low_ref, scaled_ref, *other_refs,
):
    length, channels = v_ref.shape
    heads = cum_ref.shape[0]
    width = channels // heads
    cumulative = cum_ref[...]
    left_over = cumulative[:, -1:] - cumulative
    growth = rows_of_three(jnp.exp(cumulative))
    fall = rows_of_three(jnp.exp(left_over))
    b_t = b_ref[...].astype(F32).T.astype(BF16)
    c_t = c_ref[...].astype(F32).T.astype(BF16)
    for first in range(0, channels, LANES):
        here = pl.ds(first, LANES)
        _, _, grad_y = gate_parts(gate_ref[:, here], go_ref[:, here])
        vals = v_ref[:, here].astype(F32)
        high, low = split(spread(growth, first, LANES, width) * grad_y, 2)
        high_ref[:, here] = high
        low_ref[:, here] = low
        scaled_ref[:, here] = (spread(fall, first, LANES, width) * vals).astype(BF16)

    def pulled():
        put_rows(other_refs, slice(None), mm(c_t, high_ref[...]) + mm(c_t, low_ref[...]))

    def local():
        put_rows(other_refs, slice(None), mm(b_t, scaled_ref[...]))

    if size == 1:
        pulled()
    else:
        lower = lax.axis_index("seq") < size // 2
        pl.when(lower)(pulled)
        pl.when(jnp.logical_not(lower))(local)


def slopes_kernel(v_ref, gate_ref, go_ref, b_ref, c_ref, cum_ref, after_ref, q_ref, r_ref):
    length, channels = v_ref.shape
    width = channels // cum_ref.shape[0]
    cumulative = cum_ref[...]
    left_over = cumulative[:, -1:] - cumulative
    growth_slope = rows_of_three(cumulative * jnp.exp(cumulative))
    fall_slope = rows_of_three(left_over * jnp.exp(left_over))
    b_t = b_ref[...].astype(F32).T.astype(BF16)
    c_t = c_ref[...].astype(F32).T.astype(BF16)
    for first in range(0, channels, LANES):
        here = pl.ds(first, LANES)
        _, _, grad_y = gate_parts(gate_ref[:, here], go_ref[:, here])
        high, low = split(spread(growth_slope, first, LANES, width) * grad_y, 2)
        q_ref[:, here] = mm(c_t, high) + mm(c_t, low)
        high, low = split(spread(fall_slope, first, LANES, width) * v_ref[:, here].astype(F32), 2)
        r_ref[:, here] = mm(b_t, high) + mm(b_t, low)


def prepare_kernel(
    v_ref, gate_ref, go_ref, cum_ref, skip_ref, intra_ref, in_inner_ref, after_ref,
    coef_ref, mamba_ref, inner_ref, growth_ref, fall_ref, gy_ref, gcum_ref, parts_ref,
):
    length, channels = v_ref.shape
    heads = cum_ref.shape[0]
    width = channels // heads
    cumulative = cum_ref[...]
    growth_three = rows_of_three(jnp.exp(cumulative))
    fall_three = rows_of_three(jnp.exp(cumulative[:, -1:] - cumulative))
    skip_column = to_column(skip_ref[...])
    grad_cum = jnp.zeros((heads, length), F32)
    skip_part = jnp.zeros((heads, 1), F32)
    for first in range(0, channels, LANES):
        here = pl.ds(first, LANES)
        wide, sigmoid, grad_y = gate_parts(gate_ref[:, here], go_ref[:, here])
        vals = v_ref[:, here].astype(F32)
        skip = channel_row(skip_column, heads, width, first)
        growth_ref[:, here] = spread(growth_three, first, LANES, width)
        fall_ref[:, here] = spread(fall_three, first, LANES, width)
        gy_ref[:, here] = grad_y
        coef_ref[:, here] = go_ref[:, here].astype(F32) * sigmoid * (1.0 + wide * (1.0 - sigmoid))
        intra = intra_ref[:, here]
        inner = in_inner_ref[:, here]
        mamba_ref[:, here] = intra + skip * vals
        inner_ref[:, here] = inner + skip * grad_y
        high, low = split(grad_y.astype(BF16).astype(F32) * intra - vals * inner, 2)
        head_rows = jnp.where(head_map(heads, width, first, LANES), 1.0, 0.0).astype(BF16)
        grad_cum = grad_cum + mm_nt(head_rows, high) + mm_nt(head_rows, low)
        skip_row = jnp.sum(grad_y * vals, axis=0, keepdims=True)
        skip_part = skip_part + head_column(skip_row, heads, width, first)
    gcum_ref[...] = grad_cum
    rate_part = jnp.sum(grad_cum * cumulative, axis=1, keepdims=True)
    parts_ref[...] = jnp.concatenate([to_row(rate_part), to_row(skip_part)], axis=0)


def pick(size, first, second, last):
    if size == 1:
        return jnp.zeros_like(first), jnp.zeros_like(first)
    if size % 2:
        return first, second
    index = lax.axis_index("seq")
    lower = index < size // 2
    edge = jnp.logical_or(index == 0, index == size - 1)
    first = jnp.where(edge, 0.0, first)
    second = jnp.where(edge, last, second)
    return jnp.where(lower, first, second), jnp.where(lower, second, first)


def picked(size, states, here):
    both = [pick(size, *(ref[:, here] for ref in state)) for state in states]
    return jnp.concatenate([x[0] for x in both], axis=0), jnp.concatenate([x[1] for x in both], axis=0)


def rate_kernel(size, pieces, start, heads, final, *refs):
    states, refs = [refs[3 * i : 3 * i + 3] for i in range(pieces)], refs[3 * pieces :]
    q_ref, r_ref, slope_ref, row_ref, parts_ref, out_ref = *refs[:5], refs[-1]
    rows, channels = pieces * states[0][0].shape[0], q_ref.shape[1]
    here = slice(start, start + rows)
    rate_part = jnp.zeros((heads, 1), F32)
    for begin in range(0, channels, LANES):
        lanes = pl.ds(begin, LANES)
        entering, after = picked(size, states, lanes)
        terms = entering * q_ref[here, lanes] + after * (
            r_ref[here, lanes] + slope_ref[:, lanes] * entering
        )
        row = row_ref[:, lanes] + jnp.sum(terms, axis=0, keepdims=True)
        if final:
            rate_part = rate_part + head_column(row, heads, channels // heads, begin)
        else:
            out_ref[:, lanes] = row
    if final:
        base = parts_ref[...]
        out_ref[...] = jnp.concatenate([base[:1] + to_row(rate_part), base[1:]], axis=0)


def share_kernel(size, pieces, start, *refs):
    states, refs = [refs[3 * i : 3 * i + 3] for i in range(pieces)], refs[3 * pieces :]
    high_ref, low_ref, scaled_ref, sum_b_ref, sum_c_ref = refs[:5]
    rows, channels = pieces * states[0][0].shape[0], scaled_ref.shape[1]
    here = slice(start, start + rows)
    grad_b = sum_b_ref[:, here]
    grad_c = sum_c_ref[:, here]
    pairs_b = pairs_c = jnp.zeros((scaled_ref.shape[0], 2 * rows), F32)
    for begin in range(0, channels, LANES):
        lanes = pl.ds(begin, LANES)
        entering, after = picked(size, states, lanes)
        enter_high, enter_low = split(entering, 2)
        after_high, after_low = split(after, 2)
        high, low, scaled = high_ref[:, lanes], low_ref[:, lanes], scaled_ref[:, lanes]
        pairs_c = pairs_c + mm_nt(high, jnp.concatenate([enter_low, enter_high], axis=0))
        pairs_b = pairs_b + mm_nt(scaled, jnp.concatenate([after_low, after_high], axis=0))
        grad_c = grad_c + mm_nt(low, enter_high)
    grad_b = grad_b + (pairs_b[:, :rows] + pairs_b[:, rows:])
    grad_c = grad_c + (pairs_c[:, :rows] + pairs_c[:, rows:])
    refs[-1][...] = jnp.concatenate([grad_b, grad_c], axis=1)


def rest_kernel(size, pieces, *refs):
    states, refs = [refs[3 * i : 3 * i + 3] for i in range(pieces)], refs[3 * pieces :]
    (
        v_ref, b_ref, c_ref, coef_ref, mamba_ref, inner_ref, growth_ref, fall_ref, gy_ref,
        gcum_ref, decay_ref, neg_ref, *_, gv_ref, gg_ref, gs_ref,
    ) = refs
    length, channels = v_ref.shape
    heads = gcum_ref.shape[0]
    width = channels // heads
    twice_b, twice_c = (jnp.concatenate([ref[...], ref[...]], axis=1) for ref in (b_ref, c_ref))
    grad_cum = gcum_ref[...]
    grad_total = jnp.zeros((heads, 1), F32)
    for first in range(0, channels, LANES):
        here = pl.ds(first, LANES)
        entering, after = picked(size, states, here)
        inter = growth_ref[:, here] * mm(twice_c, jnp.concatenate(split(entering, 2), axis=0))
        outer = fall_ref[:, here] * mm(twice_b, jnp.concatenate(split(after, 2), axis=0))
        gg_ref[0, :, here] = (coef_ref[:, here] * (mamba_ref[:, here] + inter)).astype(BF16)
        gv_ref[0, :, here] = (inner_ref[:, here] + outer).astype(BF16)
        pulled = v_ref[:, here].astype(F32) * outer
        high, low = split(gy_ref[:, here] * inter - pulled, 2)
        head_rows = jnp.where(head_map(heads, width, first, LANES), 1.0, 0.0).astype(BF16)
        grad_cum = grad_cum + mm_nt(head_rows, high) + mm_nt(head_rows, low)
        total_row = jnp.sum(pulled, axis=0, keepdims=True) + decay_ref[:, here] * jnp.sum(
            after * entering, axis=0, keepdims=True
        )
        grad_total = grad_total + head_column(total_row, heads, width, first)
    gs_ref[0] = neg_ref[...] * (scan_tokens(grad_cum, True) + grad_total)


def tree(values):
    while len(values) > 1:
        values = [sum(values[i + 1 : i + 2], values[i]) for i in range(0, len(values), 2)]
    return values[0]


def copy_kernel(x_ref, *refs):
    refs[-1][...] = x_ref[...]


def add_kernel(x_ref, y_ref, *refs):
    refs[-1][...] = x_ref[...] + y_ref[...]


def sum_kernel(*refs):
    refs[-1][...] = tree([ref[...] for ref in refs[:-1]])


def last_kernel(counts, *refs):
    refs, (gb_ref, gc_ref, rate_ref, skip_ref) = refs[:-4], refs[-4:]
    sums = []
    for count in counts:
        sums.append(tree([ref[...] for ref in refs[:count]]))
        refs = refs[count:]
    *shares, small = sums
    start = 0
    for both in shares:
        rows = both.shape[1] // 2
        gb_ref[0, :, start : start + rows] = both[:, :rows]
        gc_ref[0, :, start : start + rows] = both[:, rows:]
        start += rows
    rate_ref[...] = small[:1]
    skip_ref[...] = small[1:]


def call(kernel, outs, scratch=(), name="", space=pltpu.VMEM, after=()):
    def run(*args):
        if space == pltpu.HBM:
            args = [pltpu.with_memory_space_constraint(a, space) for a in args]
        specs = [pl.BlockSpec(memory_space=space)] * len(args)
        specs += [pl.BlockSpec(memory_space=pl.ANY)] * len(after)
        args = (*args, *after)
        return pl.pallas_call(
            kernel,
            out_shape=tuple(outs),
            in_specs=specs,
            out_specs=tuple(pl.BlockSpec(memory_space=pltpu.VMEM) for _ in outs),
            scratch_shapes=list(scratch),
            compiler_params=pltpu.CompilerParams(vmem_limit_bytes=VMEM_LIMIT),
            cost_estimate=pl.CostEstimate(
                flops=WEIGHTS.get(name, 0) * 10**7, bytes_accessed=0, transcendentals=0
            ),
        )(*args)

    return run


def swap(x, axis, size, bit):
    return lax.ppermute(x, axis, [(i, i ^ bit) for i in range(size)])


def hop(x, sizes, step):
    size, copies = sizes["seq"], sizes["replica"]
    pairs = []
    for copy in range(copies):
        for place in range(size):
            to = (copy ^ 1 if copies % 2 == 0 else copy, place)
            for low in (step, size - 2 - step):
                if place in (low, low + 1):
                    to = (copy, 2 * low + 1 - place)
            pairs.append((copy * size + place, to[0] * size + to[1]))
    return lax.ppermute(x, ("replica", "seq"), pairs)


def pass_kernel(*refs):
    got_ref, base_ref, decay_ref = refs[:3]
    refs[-1][...] = decay_ref[...] * got_ref[...] + base_ref[...]


def pass_on(got, base, decay, after, name):
    return call(pass_kernel, [jax.ShapeDtypeStruct(base.shape, F32)], name=name, after=after)(
        got, base, decay
    )[0]


def chain(sizes, mine, made, decay, work):
    chunks = len(mine)
    size = sizes["seq"]
    if size == 1:
        for k in sorted(work):
            work[k](())
        return [(x, x, x) for x in mine]
    if size % 2:
        raise NotImplementedError
    index = lax.axis_index("seq")
    place = jnp.minimum(index, size - 1 - index)
    middle = size // 2 - 1
    got = {(0, c): hop(mine[c], sizes, 0) for c in range(chunks)}
    steps = [
        (at + c + (1 if at > middle else 0), at, c)
        for at in range(1, size - 1)
        for c in range(chunks)
    ]
    token = ()
    for count, (_, at, c) in enumerate(sorted(steps)):
        if count in work:
            token = work[count](token)
        if at > middle and c > 2:
            token = (*token, got[at, c - 2 - 1])
        base = mine[c] if at <= middle else made["factors"][3 + c]
        pay = pass_on(got[at - 1, c], base, decay, token, f"pass{min(count, 7)}")
        got[at, c] = hop(pay, sizes, at)
        token = (pay,)
    for k in sorted(work):
        if k >= len(steps):
            token = work[k](token)
    states = []
    for c in range(chunks):
        first, second, last = got[0, c], got[middle, c], got[size - 2, c]
        for at in range(1, middle):
            first = jnp.where(place == at + 1, got[at, c], first)
        for at in range(middle + 1, size - 2):
            second = jnp.where(place == size - 2 - at, got[at, c], second)
        states.append((first, second, last))
    return states


def sum_terms(x, later, axis, size):
    if size == 1:
        return [x]
    if size == 4:
        return [x, swap(x, axis, size, 1)] + [swap(later, axis, size, bit) for bit in (2, 3)]
    if size & (size - 1):
        return [lax.psum(x, axis)]
    bit = 1
    while 2 * bit < size:
        x = x + swap(x, axis, size, bit)
        bit *= 2
    return [x, swap(x, axis, size, bit)]


def small_terms(x, sizes, hooks):
    axes = ("seq", "replica")
    along, across = ([(axis, 1 << k) for k in range(sizes[axis].bit_length() - 1)] for axis in axes)
    bits = along[:1] + across + along[1:]
    if any(sizes[axis] & (sizes[axis] - 1) for axis in axes):
        x, bits = lax.psum(x, axes), []
    for count, (axis, bit) in enumerate(bits):
        theirs = swap(x, axis, sizes[axis], bit)
        if count == len(bits) - 1:
            break
        x = call(add_kernel, [jax.ShapeDtypeStruct(x.shape, F32)], name=f"add{count}")(x, theirs)[0]
        if count < len(hooks):
            hooks[count]((x,))
    for hook in hooks[max(len(bits) - 1, 0) :]:
        hook((x,))
    return [x, theirs] if bits else [x]


def shards(sizes, values, gate_in, in_b, in_c, step_sizes, log_rates, skip_gain, grad_out):
    like = jax.ShapeDtypeStruct
    length, channels = values.shape[1:]
    heads = step_sizes.shape[1]
    state = in_b.shape[2]
    seq = sizes["seq"]
    rows = state // CHUNKS
    wide = like((length, channels), F32)
    wide_b = like((length, channels), BF16)
    share = like((length, state), F32)
    small = like((heads, length), F32)
    row = like((1, channels), F32)
    piece = like((rows, channels), F32)
    maps = like((length, state), BF16)

    out = call(
        functools.partial(states_kernel, seq),
        [wide_b, wide_b, wide_b, maps, maps, small, small, row, row, like((1, heads), F32)]
        + [piece] * CHUNKS,
        [
            pltpu.VMEM((heads, length), F32),
            pltpu.VMEM((1, heads), F32),
            pltpu.SemaphoreType.DMA((8,)),
        ],
        space=pltpu.HBM,
    )(
        values[0], gate_in[0], grad_out[0], in_b[0], in_c[0], step_sizes[0],
        log_rates.reshape(1, heads), skip_gain.reshape(1, heads),
    )
    vals, gate, grad, block_b, block_c, cumulative, negative, decay, slope, skip = out[:10]
    mine = out[10:]

    made = {}

    def intra(after):
        made["intra"] = call(
            intra_kernel,
            [wide, wide, share, share],
            [
                pltpu.VMEM((channels, length), BF16),
                pltpu.VMEM((channels, length), F32),
                pltpu.VMEM((length, length), F32),
            ],
            name="intra",
        )(vals, gate, grad, block_b, block_c, cumulative)
        return (made["intra"][2],)

    def factors(after):
        made["factors"] = call(
            functools.partial(factors_kernel, seq),
            [wide_b] * 3 + [piece] * CHUNKS,
            name="factors",
        )(vals, gate, grad, block_b, block_c, cumulative, *(after if after else made["intra"][2:3]))
        return made["factors"][3:4]

    def slopes(after):
        made["slopes"] = call(slopes_kernel, [like((state, channels), F32)] * 2, name="slopes")(
            vals, gate, grad, block_b, block_c, cumulative, *(after if after else made["intra"][2:3])
        )
        return made["slopes"][:1]

    def prepare(after):
        made["prepare"] = call(
            prepare_kernel,
            [wide] * 6 + [small, like((2, heads), F32)],
            name="prepare",
        )(
            vals, gate, grad, cumulative, skip,
            *made["intra"][:2], *(after if after else made["intra"][2:3]),
        )
        return (made["prepare"][-1],)

    sums = max(seq - 2, 0) * CHUNKS
    states = chain(sizes, mine, made, decay, {0: intra, 1: factors, 2: slopes, max(sums - 2, 3): prepare})
    sum_b, sum_c = made["intra"][2:]
    high, low, scaled = made["factors"][:3]
    q, r = made["slopes"]
    coef, mamba, inner, growth, fall, grad_y, grad_cum, parts = made["prepare"]

    rate_row = jnp.zeros((1, channels), F32)
    terms, counts = [], []
    for i in range(PARTS):
        final = i == PARTS - 1
        count = CHUNKS // PARTS
        own = [x for group in states[i * count : (i + 1) * count] for x in group]
        rate_row = call(
            functools.partial(rate_kernel, seq, count, i * rows * count, heads, final),
            [like((2, heads), F32) if final else row],
            name=f"rate{i}",
        )(*own, q, r, slope, rate_row, parts)[0]
        share_of = call(
            functools.partial(share_kernel, seq, count, i * rows * count),
            [like((length, 2 * rows * count), F32)],
            name=f"share{i}",
            after=(rate_row,),
        )(*own, high, low, scaled, sum_b, sum_c)[0]
        if not final:
            own = sum_terms(share_of, share_of, "tensor", sizes["tensor"])
            terms += call(sum_kernel, [like(share_of.shape, F32)], name="sum")(*own)
            counts.append(1)

    def exchange(after):
        later = call(copy_kernel, [like(share_of.shape, F32)], name="later", after=after)(share_of)[0]
        made["share"] = sum_terms(share_of, later, "tensor", sizes["tensor"])

    def rest(after):
        made["rest"] = call(
            functools.partial(rest_kernel, seq, CHUNKS),
            [like((1, length, channels), BF16)] * 2 + [like((1, heads, length), F32)],
            name="rest",
            after=(*after, *terms),
        )(
            *(x for group in states for x in group),
            vals, block_b, block_c, coef, mamba, inner, growth, fall, grad_y, grad_cum, decay, negative,
        )

    own = small_terms(rate_row, sizes, (exchange, rest))
    for group in (made["share"], own):
        terms += group
        counts.append(len(group))
    grad_values, grad_gate, grad_steps = made["rest"]
    grad_b, grad_c, rate_sum, skip_sum = call(
        functools.partial(last_kernel, tuple(counts)),
        [like((1, length, state), F32)] * 2 + [like((1, heads), F32)] * 2,
    )(*terms)
    return (
        grad_values,
        grad_gate,
        grad_b,
        grad_c,
        grad_steps,
        rate_sum.reshape(heads),
        skip_sum.reshape(heads),
    )


def solution(mesh):
    in_specs = (
        P("replica", "seq", "tensor"),
        P("replica", "seq", "tensor"),
        P("replica", "seq", None),
        P("replica", "seq", None),
        P("replica", "tensor", "seq"),
        P("tensor"),
        P("tensor"),
        P("replica", "seq", "tensor"),
    )
    out_specs = (
        P("replica", "seq", "tensor"),
        P("replica", "seq", "tensor"),
        P("replica", "seq", None),
        P("replica", "seq", None),
        P("replica", "tensor", "seq"),
        P("tensor"),
        P("tensor"),
    )
    body = functools.partial(shards, dict(mesh.shape))
    return jax.shard_map(body, mesh=mesh, in_specs=in_specs, out_specs=out_specs, check_vma=False)
```

```python
import functools

import jax
import jax.numpy as jnp
from jax import lax
from jax.experimental import pallas as pl
from jax.experimental.pallas import tpu as pltpu
from jax.sharding import PartitionSpec as P

F32 = jnp.float32
BF16 = jnp.bfloat16
VMEM_LIMIT = 24 * 1024 * 1024
LANES = 256
CHUNKS = 4
PARTS = 2
WEIGHTS = {'pass4': 30, 'pass5': 10, 'pass6': 300, 'pass7': 30, 'rate0': 30, 'rate1': 10, 'later': 30, 'sum': 100, 'add1': 100, 'rest': 30, 'share1': 0}


def split(x, parts):
    terms = []
    for _ in range(parts - 1):
        term = x.astype(BF16)
        terms.append(term)
        x = x - term.astype(F32)
    terms.append(x.astype(BF16))
    return terms


def mm(a, b):
    return lax.dot_general(a, b, (((1,), (0,)), ((), ())), preferred_element_type=F32)


def mm_nt(a, b):
    return lax.dot_general(a, b, (((1,), (1,)), ((), ())), preferred_element_type=F32)


def mm_tn(a, b):
    return lax.dot_general(a, b, (((0,), (0,)), ((), ())), preferred_element_type=F32)


def iota(shape, dim):
    return lax.broadcasted_iota(jnp.int32, shape, dim)


def to_column(row):
    n = row.shape[1]
    eye = iota((n, n), 0) == iota((n, n), 1)
    return jnp.sum(jnp.where(eye, row, 0.0), axis=1, keepdims=True)


def to_row(column):
    n = column.shape[0]
    eye = iota((n, n), 0) == iota((n, n), 1)
    return jnp.sum(jnp.where(eye, column, 0.0), axis=0, keepdims=True)


def head_map(heads, width, first, lanes):
    low = iota((heads, lanes), 0) * width
    channel = iota((heads, lanes), 1) + first
    return (channel >= low) & (channel < low + width)


def spread_map(heads, width, first, lanes):
    one = jnp.where(head_map(heads, width, first, lanes), 1.0, 0.0).astype(BF16)
    return jnp.concatenate([one, one, one], axis=0)


def rows_of_three(per_head):
    return jnp.concatenate(split(per_head, 3), axis=0)


def spread(three, first, lanes, width):
    heads = three.shape[0] // 3
    return mm_tn(three, spread_map(heads, width, first, lanes))


def scan_tokens(per_head, backward):
    heads, length = per_head.shape
    source = iota((length, length), 0)
    target = iota((length, length), 1)
    keep = source >= target if backward else source <= target
    sums = mm(rows_of_three(per_head), jnp.where(keep, 1.0, 0.0).astype(BF16))
    return sums[:heads] + sums[heads : 2 * heads] + sums[2 * heads :]


def channel_row(column, heads, width, first):
    mine = head_map(heads, width, first, LANES)
    return jnp.sum(jnp.where(mine, column, 0.0), axis=0, keepdims=True)


def head_column(row, heads, width, first):
    mine = head_map(heads, width, first, LANES)
    return jnp.sum(jnp.where(mine, row, 0.0), axis=1, keepdims=True)


def gate_parts(gate, grad):
    wide = gate.astype(F32)
    sigmoid = 1.0 / (1.0 + jnp.exp(-wide))
    return wide, sigmoid, grad.astype(F32) * (wide * sigmoid)


def put_rows(refs, here, value):
    start = 0
    for ref in refs:
        rows = ref.shape[0]
        ref[:, here] = value[start : start + rows]
        start += rows


def states_kernel(size, *refs):
    sources, outs, (steps_ref, lr_ref, sems) = refs[:8], refs[8:-3], refs[-3:]
    v_ref, gate_ref, go_ref, b_ref, c_ref = outs[:5]
    cum_ref, neg_ref, decay_ref, slope_ref, skip_ref = outs[5:10]
    mine_refs = outs[10:]
    targets = (v_ref, gate_ref, go_ref, b_ref, c_ref, steps_ref, lr_ref, skip_ref)
    copies = [
        pltpu.make_async_copy(source, target, sems.at[i])
        for i, (source, target) in enumerate(zip(sources, targets))
    ]

    def start(*which):
        for i in which:
            copies[i].start()

    start(6, 5)
    if size == 1:
        start(3, 0, 4, 1, 2, 7)
    else:
        lower = lax.axis_index("seq") < size // 2
        pl.when(lower)(lambda: start(3, 0, 4, 1, 2, 7))
        pl.when(jnp.logical_not(lower))(lambda: start(4, 1, 2, 3, 0, 7))
    copies[6].wait()
    copies[5].wait()
    length, channels = v_ref.shape
    heads = steps_ref.shape[0]
    width = channels // heads
    rates = jnp.exp(to_column(lr_ref[...]))
    cumulative = scan_tokens(-rates * steps_ref[...], False)
    total = cumulative[:, -1:]
    decay = jnp.exp(total)
    cum_ref[...] = cumulative
    neg_ref[...] = jnp.broadcast_to(-rates, (heads, length))
    for first in range(0, channels, LANES):
        here = pl.ds(first, LANES)
        decay_ref[:, here] = channel_row(decay, heads, width, first)
        slope_ref[:, here] = channel_row(total * decay, heads, width, first)

    def local():
        copies[3].wait()
        b_t = b_ref[...].astype(F32).T.astype(BF16)
        fall = rows_of_three(jnp.exp(total - cumulative))
        copies[0].wait()
        for first in range(0, channels, LANES):
            here = pl.ds(first, LANES)
            scaled = spread(fall, first, LANES, width) * v_ref[:, here].astype(F32)
            put_rows(mine_refs, here, mm(b_t, scaled.astype(BF16)))
        for i in (1, 2, 4, 7):
            copies[i].wait()

    def pulled():
        copies[4].wait()
        c_t = c_ref[...].astype(F32).T.astype(BF16)
        growth = rows_of_three(jnp.exp(cumulative))
        copies[1].wait()
        copies[2].wait()
        for first in range(0, channels, LANES):
            here = pl.ds(first, LANES)
            _, _, grad_y = gate_parts(gate_ref[:, here], go_ref[:, here])
            high, low = split(spread(growth, first, LANES, width) * grad_y, 2)
            put_rows(mine_refs, here, mm(c_t, high) + mm(c_t, low))
        for i in (0, 3, 7):
            copies[i].wait()

    if size == 1:
        local()
    else:
        pl.when(lower)(local)
        pl.when(jnp.logical_not(lower))(pulled)


def intra_kernel(
    v_ref, gate_ref, go_ref, b_ref, c_ref, cum_ref,
    intra_ref, inner_ref, sum_b_ref, sum_c_ref, grad_t_ref, inner_t_ref, acc_ref,
):
    length, channels = v_ref.shape
    heads = cum_ref.shape[0]
    width = channels // heads
    half = length // 2
    pair = 2 * width
    cumulative = cum_ref[...]
    columns = cumulative.T
    scores = mm_nt(c_ref[...], b_ref[...])
    causal = iota((half, half), 0) >= iota((half, half), 1)
    left = iota((1, pair), 1) < width
    acc_ref[...] = jnp.zeros_like(acc_ref)

    def blocks(x):
        return x[:half, :half], x[half:, :half], x[half:, half:]

    scores_00, scores_10, scores_11 = blocks(scores)
    for first in range(0, channels, pair):
        here = pl.ds(first, pair)
        _, _, grad_y = gate_parts(gate_ref[:, here], go_ref[:, here])
        grad_t_ref[here, :] = grad_y.T.astype(BF16)
        vals = v_ref[:, here]
        pieces = []
        for side in range(2):
            head = first // width + side
            own = left if side == 0 else jnp.logical_not(left)
            row = cumulative[head : head + 1, :]
            column = columns[:, head : head + 1]
            row_0, row_1 = row[:, :half], row[:, half:]
            column_0, column_1 = column[:half], column[half:]
            decay_00 = jnp.exp(jnp.where(causal, column_0 - row_0, -1e30))
            decay_10 = jnp.exp(column_1 - row_0)
            decay_11 = jnp.exp(jnp.where(causal, column_1 - row_1, -1e30))
            mix_00 = (scores_00 * decay_00).astype(BF16)
            mix_10 = (scores_10 * decay_10).astype(BF16)
            mix_11 = (scores_11 * decay_11).astype(BF16)
            low_rows = jnp.concatenate([mix_10, mix_11], axis=1)
            pieces.append((mm(mix_00, vals[:half]), mm(low_rows, vals)))
            head_grad = jnp.where(own, grad_y, 0.0).astype(BF16)
            mixed_0 = mm_nt(head_grad[:half], vals[:half])
            mixed_1 = mm_nt(head_grad[half:], vals)
            acc_ref[:half, :half] += mixed_0 * decay_00
            acc_ref[half:, :half] += mixed_1[:, :half] * decay_10
            acc_ref[half:, half:] += mixed_1[:, half:] * decay_11
            mine = pl.ds(first + side * width, width)
            grad_t = grad_t_ref[mine, :]
            inner_t_ref[mine, :half] = mm(grad_t[:, :half], mix_00) + mm(grad_t[:, half:], mix_10)
            inner_t_ref[mine, half:] = mm(grad_t[:, half:], mix_11)
        intra_ref[:half, here] = jnp.where(left, pieces[0][0], pieces[1][0])
        intra_ref[half:, here] = jnp.where(left, pieces[0][1], pieces[1][1])
        inner_ref[:, here] = inner_t_ref[here, :].T
    shares = acc_ref[...]
    high, low = split(shares, 2)
    sum_c_ref[...] = mm(high, b_ref[...]) + mm(low, b_ref[...])
    high, low = split(shares.T, 2)
    sum_b_ref[...] = mm(high, c_ref[...]) + mm(low, c_ref[...])


def factors_kernel(
    size, v_ref, gate_ref, go_ref, b_ref, c_ref, cum_ref, after_ref,
    high_ref, low_ref, scaled_ref, *other_refs,
):
    length, channels = v_ref.shape
    heads = cum_ref.shape[0]
    width = channels // heads
    cumulative = cum_ref[...]
    left_over = cumulative[:, -1:] - cumulative
    growth = rows_of_three(jnp.exp(cumulative))
    fall = rows_of_three(jnp.exp(left_over))
    b_t = b_ref[...].astype(F32).T.astype(BF16)
    c_t = c_ref[...].astype(F32).T.astype(BF16)
    for first in range(0, channels, LANES):
        here = pl.ds(first, LANES)
        _, _, grad_y = gate_parts(gate_ref[:, here], go_ref[:, here])
        vals = v_ref[:, here].astype(F32)
        high, low = split(spread(growth, first, LANES, width) * grad_y, 2)
        high_ref[:, here] = high
        low_ref[:, here] = low
        scaled_ref[:, here] = (spread(fall, first, LANES, width) * vals).astype(BF16)

    def pulled():
        put_rows(other_refs, slice(None), mm(c_t, high_ref[...]) + mm(c_t, low_ref[...]))

    def local():
        put_rows(other_refs, slice(None), mm(b_t, scaled_ref[...]))

    if size == 1:
        pulled()
    else:
        lower = lax.axis_index("seq") < size // 2
        pl.when(lower)(pulled)
        pl.when(jnp.logical_not(lower))(local)


def slopes_kernel(v_ref, gate_ref, go_ref, b_ref, c_ref, cum_ref, after_ref, q_ref, r_ref):
    length, channels = v_ref.shape
    width = channels // cum_ref.shape[0]
    cumulative = cum_ref[...]
    left_over = cumulative[:, -1:] - cumulative
    growth_slope = rows_of_three(cumulative * jnp.exp(cumulative))
    fall_slope = rows_of_three(left_over * jnp.exp(left_over))
    b_t = b_ref[...].astype(F32).T.astype(BF16)
    c_t = c_ref[...].astype(F32).T.astype(BF16)
    for first in range(0, channels, LANES):
        here = pl.ds(first, LANES)
        _, _, grad_y = gate_parts(gate_ref[:, here], go_ref[:, here])
        high, low = split(spread(growth_slope, first, LANES, width) * grad_y, 2)
        q_ref[:, here] = mm(c_t, high) + mm(c_t, low)
        high, low = split(spread(fall_slope, first, LANES, width) * v_ref[:, here].astype(F32), 2)
        r_ref[:, here] = mm(b_t, high) + mm(b_t, low)


def prepare_kernel(
    v_ref, gate_ref, go_ref, cum_ref, skip_ref, intra_ref, in_inner_ref, after_ref,
    coef_ref, mamba_ref, inner_ref, growth_ref, fall_ref, gy_ref, gcum_ref, parts_ref,
):
    length, channels = v_ref.shape
    heads = cum_ref.shape[0]
    width = channels // heads
    cumulative = cum_ref[...]
    growth_three = rows_of_three(jnp.exp(cumulative))
    fall_three = rows_of_three(jnp.exp(cumulative[:, -1:] - cumulative))
    skip_column = to_column(skip_ref[...])
    grad_cum = jnp.zeros((heads, length), F32)
    skip_part = jnp.zeros((heads, 1), F32)
    for first in range(0, channels, LANES):
        here = pl.ds(first, LANES)
        wide, sigmoid, grad_y = gate_parts(gate_ref[:, here], go_ref[:, here])
        vals = v_ref[:, here].astype(F32)
        skip = channel_row(skip_column, heads, width, first)
        growth_ref[:, here] = spread(growth_three, first, LANES, width)
        fall_ref[:, here] = spread(fall_three, first, LANES, width)
        gy_ref[:, here] = grad_y
        coef_ref[:, here] = go_ref[:, here].astype(F32) * sigmoid * (1.0 + wide * (1.0 - sigmoid))
        intra = intra_ref[:, here]
        inner = in_inner_ref[:, here]
        mamba_ref[:, here] = intra + skip * vals
        inner_ref[:, here] = inner + skip * grad_y
        high, low = split(grad_y.astype(BF16).astype(F32) * intra - vals * inner, 2)
        head_rows = jnp.where(head_map(heads, width, first, LANES), 1.0, 0.0).astype(BF16)
        grad_cum = grad_cum + mm_nt(head_rows, high) + mm_nt(head_rows, low)
        skip_row = jnp.sum(grad_y * vals, axis=0, keepdims=True)
        skip_part = skip_part + head_column(skip_row, heads, width, first)
    gcum_ref[...] = grad_cum
    rate_part = jnp.sum(grad_cum * cumulative, axis=1, keepdims=True)
    parts_ref[...] = jnp.concatenate([to_row(rate_part), to_row(skip_part)], axis=0)


def pick(size, first, second, last):
    if size == 1:
        return jnp.zeros_like(first), jnp.zeros_like(first)
    if size % 2:
        return first, second
    index = lax.axis_index("seq")
    lower = index < size // 2
    edge = jnp.logical_or(index == 0, index == size - 1)
    first = jnp.where(edge, 0.0, first)
    second = jnp.where(edge, last, second)
    return jnp.where(lower, first, second), jnp.where(lower, second, first)


def picked(size, states, here):
    both = [pick(size, *(ref[:, here] for ref in state)) for state in states]
    return jnp.concatenate([x[0] for x in both], axis=0), jnp.concatenate([x[1] for x in both], axis=0)


def rate_kernel(size, pieces, start, heads, final, *refs):
    states, refs = [refs[3 * i : 3 * i + 3] for i in range(pieces)], refs[3 * pieces :]
    q_ref, r_ref, slope_ref, row_ref, parts_ref, out_ref = *refs[:5], refs[-1]
    rows, channels = pieces * states[0][0].shape[0], q_ref.shape[1]
    here = slice(start, start + rows)
    rate_part = jnp.zeros((heads, 1), F32)
    for begin in range(0, channels, LANES):
        lanes = pl.ds(begin, LANES)
        entering, after = picked(size, states, lanes)
        terms = entering * q_ref[here, lanes] + after * (
            r_ref[here, lanes] + slope_ref[:, lanes] * entering
        )
        row = row_ref[:, lanes] + jnp.sum(terms, axis=0, keepdims=True)
        if final:
            rate_part = rate_part + head_column(row, heads, channels // heads, begin)
        else:
            out_ref[:, lanes] = row
    if final:
        base = parts_ref[...]
        out_ref[...] = jnp.concatenate([base[:1] + to_row(rate_part), base[1:]], axis=0)


def share_kernel(size, pieces, start, *refs):
    states, refs = [refs[3 * i : 3 * i + 3] for i in range(pieces)], refs[3 * pieces :]
    high_ref, low_ref, scaled_ref, sum_b_ref, sum_c_ref = refs[:5]
    rows, channels = pieces * states[0][0].shape[0], scaled_ref.shape[1]
    here = slice(start, start + rows)
    grad_b = sum_b_ref[:, here]
    grad_c = sum_c_ref[:, here]
    pairs_b = pairs_c = jnp.zeros((scaled_ref.shape[0], 2 * rows), F32)
    for begin in range(0, channels, LANES):
        lanes = pl.ds(begin, LANES)
        entering, after = picked(size, states, lanes)
        enter_high, enter_low = split(entering, 2)
        after_high, after_low = split(after, 2)
        high, low, scaled = high_ref[:, lanes], low_ref[:, lanes], scaled_ref[:, lanes]
        pairs_c = pairs_c + mm_nt(high, jnp.concatenate([enter_low, enter_high], axis=0))
        pairs_b = pairs_b + mm_nt(scaled, jnp.concatenate([after_low, after_high], axis=0))
        grad_c = grad_c + mm_nt(low, enter_high)
    grad_b = grad_b + (pairs_b[:, :rows] + pairs_b[:, rows:])
    grad_c = grad_c + (pairs_c[:, :rows] + pairs_c[:, rows:])
    refs[-1][...] = jnp.concatenate([grad_b, grad_c], axis=1)


def rest_kernel(size, pieces, *refs):
    states, refs = [refs[3 * i : 3 * i + 3] for i in range(pieces)], refs[3 * pieces :]
    (
        v_ref, b_ref, c_ref, coef_ref, mamba_ref, inner_ref, growth_ref, fall_ref, gy_ref,
        gcum_ref, decay_ref, neg_ref, *_, gv_ref, gg_ref, gs_ref,
    ) = refs
    length, channels = v_ref.shape
    heads = gcum_ref.shape[0]
    width = channels // heads
    twice_b, twice_c = (jnp.concatenate([ref[...], ref[...]], axis=1) for ref in (b_ref, c_ref))
    grad_cum = gcum_ref[...]
    grad_total = jnp.zeros((heads, 1), F32)
    for first in range(0, channels, LANES):
        here = pl.ds(first, LANES)
        entering, after = picked(size, states, here)
        inter = growth_ref[:, here] * mm(twice_c, jnp.concatenate(split(entering, 2), axis=0))
        outer = fall_ref[:, here] * mm(twice_b, jnp.concatenate(split(after, 2), axis=0))
        gg_ref[0, :, here] = (coef_ref[:, here] * (mamba_ref[:, here] + inter)).astype(BF16)
        gv_ref[0, :, here] = (inner_ref[:, here] + outer).astype(BF16)
        pulled = v_ref[:, here].astype(F32) * outer
        high, low = split(gy_ref[:, here] * inter - pulled, 2)
        head_rows = jnp.where(head_map(heads, width, first, LANES), 1.0, 0.0).astype(BF16)
        grad_cum = grad_cum + mm_nt(head_rows, high) + mm_nt(head_rows, low)
        total_row = jnp.sum(pulled, axis=0, keepdims=True) + decay_ref[:, here] * jnp.sum(
            after * entering, axis=0, keepdims=True
        )
        grad_total = grad_total + head_column(total_row, heads, width, first)
    gs_ref[0] = neg_ref[...] * (scan_tokens(grad_cum, True) + grad_total)


def tree(values):
    while len(values) > 1:
        values = [sum(values[i + 1 : i + 2], values[i]) for i in range(0, len(values), 2)]
    return values[0]


def copy_kernel(x_ref, *refs):
    refs[-1][...] = x_ref[...]


def add_kernel(x_ref, y_ref, *refs):
    refs[-1][...] = x_ref[...] + y_ref[...]


def sum_kernel(*refs):
    refs[-1][...] = tree([ref[...] for ref in refs[:-1]])


def last_kernel(counts, *refs):
    refs, (gb_ref, gc_ref, rate_ref, skip_ref) = refs[:-4], refs[-4:]
    sums = []
    for count in counts:
        sums.append(tree([ref[...] for ref in refs[:count]]))
        refs = refs[count:]
    *shares, small = sums
    start = 0
    for both in shares:
        rows = both.shape[1] // 2
        gb_ref[0, :, start : start + rows] = both[:, :rows]
        gc_ref[0, :, start : start + rows] = both[:, rows:]
        start += rows
    rate_ref[...] = small[:1]
    skip_ref[...] = small[1:]


def call(kernel, outs, scratch=(), name="", space=pltpu.VMEM, after=()):
    def run(*args):
        if space == pltpu.HBM:
            args = [pltpu.with_memory_space_constraint(a, space) for a in args]
        specs = [pl.BlockSpec(memory_space=space)] * len(args)
        specs += [pl.BlockSpec(memory_space=pl.ANY)] * len(after)
        args = (*args, *after)
        return pl.pallas_call(
            kernel,
            out_shape=tuple(outs),
            in_specs=specs,
            out_specs=tuple(pl.BlockSpec(memory_space=pltpu.VMEM) for _ in outs),
            scratch_shapes=list(scratch),
            compiler_params=pltpu.CompilerParams(vmem_limit_bytes=VMEM_LIMIT),
            cost_estimate=pl.CostEstimate(
                flops=WEIGHTS.get(name, 0) * 10**7, bytes_accessed=0, transcendentals=0
            ),
        )(*args)

    return run


def swap(x, axis, size, bit):
    return lax.ppermute(x, axis, [(i, i ^ bit) for i in range(size)])


def hop(x, sizes, step):
    size, copies = sizes["seq"], sizes["replica"]
    pairs = []
    for copy in range(copies):
        for place in range(size):
            to = (copy ^ 1 if copies % 2 == 0 else copy, place)
            for low in (step, size - 2 - step):
                if place in (low, low + 1):
                    to = (copy, 2 * low + 1 - place)
            pairs.append((copy * size + place, to[0] * size + to[1]))
    return lax.ppermute(x, ("replica", "seq"), pairs)


def pass_kernel(*refs):
    got_ref, base_ref, decay_ref = refs[:3]
    refs[-1][...] = decay_ref[...] * got_ref[...] + base_ref[...]


def pass_on(got, base, decay, after, name):
    return call(pass_kernel, [jax.ShapeDtypeStruct(base.shape, F32)], name=name, after=after)(
        got, base, decay
    )[0]


def chain(sizes, mine, made, decay, work):
    chunks = len(mine)
    size = sizes["seq"]
    if size == 1:
        for k in sorted(work):
            work[k](())
        return [(x, x, x) for x in mine]
    if size % 2:
        raise NotImplementedError
    index = lax.axis_index("seq")
    place = jnp.minimum(index, size - 1 - index)
    middle = size // 2 - 1
    got = {(0, c): hop(mine[c], sizes, 0) for c in range(chunks)}
    steps = [
        (at + c + (1 if at > middle else 0), at, c)
        for at in range(1, size - 1)
        for c in range(chunks)
    ]
    token = ()
    for count, (_, at, c) in enumerate(sorted(steps)):
        if count in work:
            token = work[count](token)
        if at > middle and c > 2:
            token = (*token, got[at, c - 2 - 1])
        base = mine[c] if at <= middle else made["factors"][3 + c]
        pay = pass_on(got[at - 1, c], base, decay, token, f"pass{min(count, 7)}")
        got[at, c] = hop(pay, sizes, at)
        token = (pay,)
    for k in sorted(work):
        if k >= len(steps):
            token = work[k](token)
    states = []
    for c in range(chunks):
        first, second, last = got[0, c], got[middle, c], got[size - 2, c]
        for at in range(1, middle):
            first = jnp.where(place == at + 1, got[at, c], first)
        for at in range(middle + 1, size - 2):
            second = jnp.where(place == size - 2 - at, got[at, c], second)
        states.append((first, second, last))
    return states


def sum_terms(x, later, axis, size):
    if size == 1:
        return [x]
    if size == 4:
        return [x, swap(x, axis, size, 1), swap(x, axis, size, 2), swap(later, axis, size, 3)]
    if size & (size - 1):
        return [lax.psum(x, axis)]
    bit = 1
    while 2 * bit < size:
        x = x + swap(x, axis, size, bit)
        bit *= 2
    return [x, swap(x, axis, size, bit)]


def small_terms(x, sizes, hooks):
    axes = ("seq", "replica")
    along, across = ([(axis, 1 << k) for k in range(sizes[axis].bit_length() - 1)] for axis in axes)
    bits = along[:1] + across + along[1:]
    if any(sizes[axis] & (sizes[axis] - 1) for axis in axes):
        x, bits = lax.psum(x, axes), []
    for count, (axis, bit) in enumerate(bits):
        theirs = swap(x, axis, sizes[axis], bit)
        if count == len(bits) - 1:
            break
        x = call(add_kernel, [jax.ShapeDtypeStruct(x.shape, F32)], name=f"add{count}")(x, theirs)[0]
        if count < len(hooks):
            hooks[count]((x,))
    for hook in hooks[max(len(bits) - 1, 0) :]:
        hook((x,))
    return [x, theirs] if bits else [x]


def shards(sizes, values, gate_in, in_b, in_c, step_sizes, log_rates, skip_gain, grad_out):
    like = jax.ShapeDtypeStruct
    length, channels = values.shape[1:]
    heads = step_sizes.shape[1]
    state = in_b.shape[2]
    seq = sizes["seq"]
    rows = state // CHUNKS
    wide = like((length, channels), F32)
    wide_b = like((length, channels), BF16)
    share = like((length, state), F32)
    small = like((heads, length), F32)
    row = like((1, channels), F32)
    piece = like((rows, channels), F32)
    maps = like((length, state), BF16)

    out = call(
        functools.partial(states_kernel, seq),
        [wide_b, wide_b, wide_b, maps, maps, small, small, row, row, like((1, heads), F32)]
        + [piece] * CHUNKS,
        [
            pltpu.VMEM((heads, length), F32),
            pltpu.VMEM((1, heads), F32),
            pltpu.SemaphoreType.DMA((8,)),
        ],
        space=pltpu.HBM,
    )(
        values[0], gate_in[0], grad_out[0], in_b[0], in_c[0], step_sizes[0],
        log_rates.reshape(1, heads), skip_gain.reshape(1, heads),
    )
    vals, gate, grad, block_b, block_c, cumulative, negative, decay, slope, skip = out[:10]
    mine = out[10:]

    made = {}

    def intra(after):
        made["intra"] = call(
            intra_kernel,
            [wide, wide, share, share],
            [
                pltpu.VMEM((channels, length), BF16),
                pltpu.VMEM((channels, length), F32),
                pltpu.VMEM((length, length), F32),
            ],
            name="intra",
        )(vals, gate, grad, block_b, block_c, cumulative)
        return (made["intra"][2],)

    def factors(after):
        made["factors"] = call(
            functools.partial(factors_kernel, seq),
            [wide_b] * 3 + [piece] * CHUNKS,
            name="factors",
        )(vals, gate, grad, block_b, block_c, cumulative, *(after if after else made["intra"][2:3]))
        return made["factors"][3:4]

    def slopes(after):
        made["slopes"] = call(slopes_kernel, [like((state, channels), F32)] * 2, name="slopes")(
            vals, gate, grad, block_b, block_c, cumulative, *(after if after else made["intra"][2:3])
        )
        return made["slopes"][:1]

    def prepare(after):
        made["prepare"] = call(
            prepare_kernel,
            [wide] * 6 + [small, like((2, heads), F32)],
            name="prepare",
        )(
            vals, gate, grad, cumulative, skip,
            *made["intra"][:2], *(after if after else made["intra"][2:3]),
        )
        return (made["prepare"][-1],)

    sums = max(seq - 2, 0) * CHUNKS
    states = chain(sizes, mine, made, decay, {0: intra, 1: factors, 2: slopes, max(sums - 2, 3): prepare})
    sum_b, sum_c = made["intra"][2:]
    high, low, scaled = made["factors"][:3]
    q, r = made["slopes"]
    coef, mamba, inner, growth, fall, grad_y, grad_cum, parts = made["prepare"]

    rate_row = jnp.zeros((1, channels), F32)
    terms, counts = [], []
    for i in range(PARTS):
        final = i == PARTS - 1
        count = CHUNKS // PARTS
        own = [x for group in states[i * count : (i + 1) * count] for x in group]
        rate_row = call(
            functools.partial(rate_kernel, seq, count, i * rows * count, heads, final),
            [like((2, heads), F32) if final else row],
            name=f"rate{i}",
        )(*own, q, r, slope, rate_row, parts)[0]
        share_of = call(
            functools.partial(share_kernel, seq, count, i * rows * count),
            [like((length, 2 * rows * count), F32)],
            name=f"share{i}",
            after=(rate_row,),
        )(*own, high, low, scaled, sum_b, sum_c)[0]
        if not final:
            own = sum_terms(share_of, share_of, "tensor", sizes["tensor"])
            terms += call(sum_kernel, [like(share_of.shape, F32)], name="sum")(*own)
            counts.append(1)

    def exchange(after):
        later = call(copy_kernel, [like(share_of.shape, F32)], name="later", after=after)(share_of)[0]
        made["share"] = sum_terms(share_of, later, "tensor", sizes["tensor"])

    def rest(after):
        made["rest"] = call(
            functools.partial(rest_kernel, seq, CHUNKS),
            [like((1, length, channels), BF16)] * 2 + [like((1, heads, length), F32)],
            name="rest",
            after=(*after, *terms),
        )(
            *(x for group in states for x in group),
            vals, block_b, block_c, coef, mamba, inner, growth, fall, grad_y, grad_cum, decay, negative,
        )

    own = small_terms(rate_row, sizes, (exchange, rest))
    for group in (made["share"], own):
        terms += group
        counts.append(len(group))
    grad_values, grad_gate, grad_steps = made["rest"]
    grad_b, grad_c, rate_sum, skip_sum = call(
        functools.partial(last_kernel, tuple(counts)),
        [like((1, length, state), F32)] * 2 + [like((1, heads), F32)] * 2,
    )(*terms)
    return (
        grad_values,
        grad_gate,
        grad_b,
        grad_c,
        grad_steps,
        rate_sum.reshape(heads),
        skip_sum.reshape(heads),
    )


def solution(mesh):
    in_specs = (
        P("replica", "seq", "tensor"),
        P("replica", "seq", "tensor"),
        P("replica", "seq", None),
        P("replica", "seq", None),
        P("replica", "tensor", "seq"),
        P("tensor"),
        P("tensor"),
        P("replica", "seq", "tensor"),
    )
    out_specs = (
        P("replica", "seq", "tensor"),
        P("replica", "seq", "tensor"),
        P("replica", "seq", None),
        P("replica", "seq", None),
        P("replica", "tensor", "seq"),
        P("tensor"),
        P("tensor"),
    )
    body = functools.partial(shards, dict(mesh.shape))
    return jax.shard_map(body, mesh=mesh, in_specs=in_specs, out_specs=out_specs, check_vma=False)
```
